32 devices in a mesh: dp: 2 (over x), fsdp: 16 (over z, y, core).
Axes of the slice: x: 2, y: 2, z: 4, core: 2. Of those that a mesh axis runs over, the one named last changes fastest.
Arguments:
- layer_input: bfloat16 [4096, 2048], P(('dp', 'fsdp')), may hold values from -12 to 12
- first_gain: bfloat16 [2048], P('fsdp'), may hold values from 0.25 to 1.75
- in_weight: bfloat16 [2048, 6144], P('fsdp'), may hold values from -0.125 to 0.125
- out_weight: bfloat16 [2048, 2048], P('fsdp'), may hold values from -0.5 to 0.5
- mix_gate: bfloat16 [2048], P('fsdp'), may hold values from -2 to 2
- second_gain: bfloat16 [2048], P('fsdp'), may hold values from 0.25 to 1.75
- gate_up: bfloat16 [2048, 16384], P('fsdp'), may hold values from -0.125 to 0.125
- down_weight: bfloat16 [2048, 8192], P('fsdp'), may hold values from -0.0625 to 0.0625
- document_starts: int32 [2, 2], P('dp'), may hold values from 0 to 1, as said below
- cotangent: bfloat16 [4096, 2048], P(('dp', 'fsdp')), may hold values from -6 to 6
Outputs:
- layer_output: bfloat16 [4096, 2048], P(('dp', 'fsdp'))
- input_grad: float32 [4096, 2048], P(('dp', 'fsdp'))
- first_gain_grad: float32 [2048], P('fsdp')
- in_weight_grad: float32 [2048, 6144], P('fsdp')
- out_weight_grad: float32 [2048, 2048], P('fsdp')
- mix_gate_grad: float32 [2048], P('fsdp')
- second_gain_grad: float32 [2048], P('fsdp')
- gate_up_grad: float32 [2048, 16384], P('fsdp')
- down_weight_grad: float32 [2048, 8192], P('fsdp')
The draws below stay inside these ranges and needn't reach their ends.
Inputs may be any that keep to these rules, and one draw needn't show every extreme that they name: document_starts[n, 0] is 0; one packed sequence, which one drawn from the seed, has no 1 at all (a single document); every other packed sequence has at least one 1.
All inputs are finite; a program needn't handle non-finite values.
Results may differ from the reference program's by a relative error of at most 0.013.
Values may be sent and summed in bfloat16 or wider, within the bound.
A program may use at most 832 MiB of HBM per device.

```python
import math
import jax
import jax.numpy as jnp
from jax import lax

D = 2048
H = 16
DH = 128
FF = 8192
SEG = 1024
TOK_DEV = 128
ROW = 2048
NSEG = 2
TOKENS = 4096
N_DP = 2


def draw_layer_input(key, part):
    key = jax.random.fold_in(key, 11)
    noise_key, shift_key = jax.random.split(key, 2)
    blocks = TOKENS // TOK_DEV
    noise = jax.random.normal(noise_key, (TOKENS, D), jnp.float32)
    shifts = 0.8 * jax.random.normal(shift_key, (blocks, 1, D), jnp.float32)
    values = noise.reshape(blocks, TOK_DEV, D) + shifts
    return values.reshape(TOKENS, D).astype(jnp.bfloat16)


def draw_document_starts(key, part):
    key = jax.random.fold_in(key, 23)
    bits_key, place_key, whole_key = jax.random.split(key, 3)
    bits = jax.random.randint(bits_key, (N_DP, NSEG), 0, 2, dtype=jnp.int32)
    places = jax.random.randint(place_key, (N_DP, 1), 1, NSEG, dtype=jnp.int32)
    single = jax.random.randint(whole_key, (), 0, N_DP, dtype=jnp.int32)
    columns = jnp.arange(NSEG, dtype=jnp.int32)[None, :]
    rows = jnp.arange(N_DP, dtype=jnp.int32)[:, None]
    marks = jnp.where(columns == places, 1, bits)
    marks = jnp.where(columns == 0, 0, marks)
    marks = jnp.where(rows == single, 0, marks)
    return marks.astype(jnp.int32)


def shard_levels(key, dims, pieces, smallest, high):
    def one(dim, shards_of):
        draws = jax.random.uniform(jax.random.fold_in(jax.random.fold_in(key, 6), dim), (shards_of,), jnp.float32, smallest / len(pieces), high / len(pieces))
        return jnp.repeat(jnp.exp(draws), dims[dim] // shards_of).reshape((-1,) + (1,) * (len(dims) - dim - 1))

    factor_of = one(*pieces[0])
    for cut in pieces[1:]:
        factor_of = factor_of * one(*cut)
    return factor_of


def normal_values(own_key, dims, spread, limit, cuts=(), kind=jnp.bfloat16):
    level = shard_levels(own_key, dims, cuts, -0.22, 0.18) if cuts else 1.0
    result = jax.random.normal(own_key, dims, jnp.float32) * spread * level
    return jnp.minimum(jnp.maximum(result, -limit), limit).astype(kind)


def setup_inputs(seed: int = 0) -> dict:
    seeds = jax.random.split(jax.random.key(seed), 11)
    return {
        "layer_input": draw_layer_input(jax.random.fold_in(seeds[10], 71), 0),
        "first_gain": jnp.clip(1.0 + 0.15 * jax.random.normal(seeds[1], (D,), jnp.float32), 0.25, 1.75).astype(jnp.bfloat16),
        "in_weight": normal_values(seeds[2], (D, 3 * D), D ** -0.5, 0.125, ((0, 16),)),
        "out_weight": normal_values(seeds[3], (D, D), (D // 16) ** -0.5, 0.5, ((0, 16),)),
        "mix_gate": jnp.clip(jax.random.uniform(seeds[4], (D,), jnp.float32, -2.0, 2.0) * shard_levels(seeds[4], (D,), ((0, 16),), -0.4, 0.0), -2.0, 2.0).astype(jnp.bfloat16),
        "second_gain": jnp.clip(1.0 + 0.15 * jax.random.normal(seeds[5], (D,), jnp.float32), 0.25, 1.75).astype(jnp.bfloat16),
        "gate_up": normal_values(seeds[6], (D, 2 * FF), D ** -0.5, 0.125, ((0, 16),)),
        "down_weight": normal_values(seeds[7], (D, FF), FF ** -0.5, 0.0625, ((0, 16),)),
        "document_starts": draw_document_starts(jax.random.fold_in(seeds[10], 71), 0),
        "cotangent": normal_values(seeds[9], (TOKENS, D), 1.0, 6.0, ((0, 32),)),
    }


highest_precision = lax.Precision.HIGHEST
epsilon = 1e-06

@jax.custom_vjp
def low(v):
    return lax.optimization_barrier(v.astype(jnp.bfloat16)).astype(jnp.float32)

@jax.custom_vjp
def low_back(v):
    return v

def low_keep(v):
    return (low(v), None)

def low_pass(kept, grad):
    return (grad,)

def back_keep(v):
    return (v, None)

def back_low(kept, grad):
    return (low(grad),)
low.defvjp(low_keep, low_pass)
low_back.defvjp(back_keep, back_low)

def rms_scale(values, gain):
    factor = lax.rsqrt(lax.optimization_barrier(jnp.mean(values * values, axis=-1, keepdims=True)) + epsilon)
    return values * factor * gain

def feature(values):
    return jax.nn.elu(values) + 1.0

def segment_attention(query, key, value):
    rows = min(SEG, 512)
    count = SEG // rows
    positions = jnp.arange(SEG, dtype=jnp.int32)

    def block(index):
        start = index * rows
        part = lax.dynamic_slice_in_dim(query, start, rows, 0)
        scores = jnp.einsum('qhc,khc->hqk', part, key, precision=highest_precision) * (1.0 / math.sqrt(DH))
        scores = low_back(scores)
        query_pos = start + jnp.arange(rows, dtype=jnp.int32)
        allowed = positions[None, :] <= query_pos[:, None]
        scores = jnp.where(allowed[None], scores, -1e+30)
        weights = low(jax.nn.softmax(scores, axis=-1))
        return jnp.einsum('hqk,khc->qhc', weights, value, precision=highest_precision)
    outputs = lax.map(jax.checkpoint(block), jnp.arange(count, dtype=jnp.int32))
    return outputs.reshape(SEG, H, DH)

def carry_step(state, inputs_seg):
    memory_matrix, normal = state
    memory_update, total, reset = inputs_seg
    memory_matrix = jnp.where(reset, jnp.zeros_like(memory_matrix), memory_matrix)
    normal = jnp.where(reset, jnp.zeros_like(normal), normal)
    return ((memory_matrix + memory_update, normal + total), (memory_matrix, normal))

def row_memory(delta_row, total_row, reset_row):
    start_state = (jnp.zeros((H, DH, DH), jnp.float32), jnp.zeros((H, DH), jnp.float32))
    ended, (before, before_norm) = lax.scan(carry_step, start_state, (delta_row, total_row, reset_row))
    return (before, before_norm)

def layer(inputs, first_gain, in_weight, out_weight, mix_gate, second_gain, gate_up, down_weight, document_starts):
    segments = N_DP * NSEG
    normed = low(rms_scale(inputs, first_gain))
    projected = low_back(low(jnp.dot(normed, in_weight, precision=highest_precision)))
    query = projected[:, :D].reshape(segments, SEG, H, DH)
    key = projected[:, D:2 * D].reshape(segments, SEG, H, DH)
    value = projected[:, 2 * D:].reshape(segments, SEG, H, DH)
    attend = jax.checkpoint(segment_attention)
    local_out = low_back(lax.map(lambda trio: attend(trio[0], trio[1], trio[2]), (query, key, value)))
    query_feature = low(feature(query))
    key_feature_map = low(feature(key))
    deltas = jnp.einsum('sthk,sthv->shkv', key_feature_map, value, precision=highest_precision)
    totals = lax.optimization_barrier(jnp.sum(key_feature_map, axis=1))
    first_segment = (jnp.arange(NSEG, dtype=jnp.int32) == 0)[None, :]
    fresh = jnp.logical_or(document_starts > 0, first_segment)
    before, before_norm = jax.vmap(row_memory)(deltas.reshape(N_DP, NSEG, H, DH, DH), totals.reshape(N_DP, NSEG, H, DH), fresh)
    before = before.reshape(segments, H, DH, DH)
    before_norm = before_norm.reshape(segments, H, DH)
    numerator = jnp.einsum('sthk,shkv->sthv', query_feature, before, precision=highest_precision)
    denom = jnp.maximum(jnp.einsum('sthk,shk->sth', query_feature, before_norm, precision=highest_precision), 1.0)
    memory_out = numerator / denom[..., None]
    mix = jax.nn.sigmoid(mix_gate).reshape(H, DH)
    combined = low((mix * memory_out + (1.0 - mix) * local_out).reshape(N_DP * ROW, D))
    attended = low_back(jnp.dot(combined, out_weight, precision=highest_precision))
    middle = inputs + attended
    hidden = low(rms_scale(middle, second_gain))
    both = low_back(jnp.dot(hidden, gate_up, precision=highest_precision))
    activated = low(jax.nn.silu(both[:, :FF]) * both[:, FF:])
    feed_out = low_back(jnp.dot(activated, down_weight.T, precision=highest_precision))
    return middle + feed_out

def reference(layer_input, first_gain, in_weight, out_weight, mix_gate, second_gain, gate_up, down_weight, document_starts, cotangent):
    params = tuple((item.astype(jnp.float32) for item in (layer_input, first_gain, in_weight, out_weight, mix_gate, second_gain, gate_up, down_weight)))

    def forward(inputs, gain_one, weight_in, weight_out, gate_mix, gain_two, weight_gate_up, weight_down):
        return layer(inputs, gain_one, weight_in, weight_out, gate_mix, gain_two, weight_gate_up, weight_down, document_starts)
    output, pullback = jax.vjp(forward, *params)
    grads = pullback(cotangent.astype(jnp.float32))
    return (output.astype(jnp.bfloat16), grads[0], grads[1], grads[2], grads[3], grads[4], grads[5], grads[6], grads[7])
```

```python
import math

import jax
import jax.numpy as jnp
from jax import lax
from jax.sharding import PartitionSpec as P

H = 16
DH = 128
FF = 8192
SEG = 1024

highest = lax.Precision.HIGHEST
epsilon = 1e-06
f32 = jnp.float32
bf16 = jnp.bfloat16
AXIS = "fsdp"


def feature(values):
    return jax.nn.elu(values) + 1.0


def feature_slope(values):
    return jnp.where(values > 0, 1.0, jnp.exp(jnp.minimum(values, 0.0)))


def norm_forward(values, gain):
    factor = lax.rsqrt(jnp.mean(values * values, axis=-1, keepdims=True) + epsilon)
    return (values * factor * gain, factor)


def norm_backward(values, factor, gain, upstream):
    scaled = upstream * gain
    gain_grad = jnp.sum(upstream * values * factor, axis=0)
    value_grad = factor * scaled - values * (factor * factor * factor) * jnp.mean(
        scaled * values, axis=-1, keepdims=True
    )
    return (value_grad, gain_grad)


def dot(left, right, dims):
    return lax.dot_general(left, right, ((dims[0], dims[1]), ((), ())), preferred_element_type=f32)


def rows_dot(left, right):
    return dot(left, right, ((0,), (0,)))


def cols_dot(left, right):
    return dot(left, right, ((1,), (1,)))


class Layout:
    def __init__(self):
        self.count = lax.axis_size(AXIS)
        self.groups = self.count // H
        self.place = lax.axis_index(AXIS)
        self.head = self.place % H
        self.group = self.place // H
        self.inside = None
        self.across = None
        if self.groups > 1:
            self.inside = [[g * H + j for j in range(H)] for g in range(self.groups)]
            self.across = [[g * H + j for g in range(self.groups)] for j in range(H)]

    def gather(self, block):
        return lax.all_gather(block, AXIS, axis=0, tiled=True, axis_index_groups=self.inside)

    def gather_all(self, block):
        return lax.all_gather(block, AXIS, axis=0, tiled=True)

    def scatter_sum(self, whole):
        return lax.psum_scatter(
            whole, AXIS, scatter_dimension=0, tiled=True, axis_index_groups=self.inside
        )

    def columns(self, block, parts):
        rows, width = block.shape
        each = width // (parts * H)
        if self.groups == 1:
            split = block.reshape(rows, parts, H, each)
            out = lax.all_to_all(split, AXIS, 2, 0, tiled=True)
            return out.reshape(rows * self.count, parts * each)
        whole = self.gather_all(block).reshape(rows * self.count, parts, H, each)
        out = lax.dynamic_index_in_dim(whole, self.head, 2, False)
        return out.reshape(rows * self.count, parts * each)

    def own_rows(self, grad, parts):
        rows, width = grad.shape
        each = width // parts
        if self.groups == 1:
            split = grad.astype(bf16).reshape(rows, parts, 1, each)
            out = lax.all_to_all(split, AXIS, 0, 2, tiled=True)
            return out.reshape(rows // self.count, parts * H * each)
        whole = jnp.zeros((rows, parts, H, each), f32)
        whole = lax.dynamic_update_slice_in_dim(
            whole, grad.reshape(rows, parts, 1, each), self.head, 2
        )
        return lax.psum_scatter(
            whole.reshape(rows, parts * H * each), AXIS, scatter_dimension=0, tiled=True
        )

    def to_tokens(self, by_head):
        tokens, each = by_head.shape
        out = lax.all_to_all(
            by_head.reshape(H, tokens // H, each), AXIS, 0, 0, tiled=False,
            axis_index_groups=self.inside,
        )
        return out.transpose(1, 0, 2).reshape(tokens // H, H * each)

    def to_heads(self, by_token):
        tokens, width = by_token.shape
        split = by_token.reshape(tokens, H, width // H).transpose(1, 0, 2)
        out = lax.all_to_all(
            split, AXIS, 0, 0, tiled=False, axis_index_groups=self.inside
        )
        return out.reshape(H * tokens, width // H)


def carry_forward(layout, delta, count, fresh):
    segments = delta.shape[0]

    def walk(state):
        before = []
        for s in range(segments):
            state = jax.tree.map(lambda a: jnp.where(fresh[s], jnp.zeros_like(a), a), state)
            before.append(state)
            state = (state[0] + delta[s], state[1] + count[s])
        return before, state

    state = (jnp.zeros_like(delta[0]), jnp.zeros_like(count[0]))
    if layout.groups > 1:
        _, last = walk(state)
        renewed = jnp.any(fresh).astype(f32)
        every = jax.tree.map(
            lambda a: lax.all_gather(a, AXIS, axis_index_groups=layout.across), last + (renewed,)
        )
        for g in range(layout.groups - 1):
            keep = every[2][g] < 0.5
            after = jax.tree.map(lambda a, e: jnp.where(keep, a, 0.0) + e[g], state, every[:2])
            state = jax.tree.map(lambda a, b: jnp.where(g < layout.group, b, a), state, after)
    before, _ = walk(state)
    return jnp.stack([b[0] for b in before]), jnp.stack([b[1] for b in before])


def carry_backward(layout, state_grad, norm_grad, fresh):
    segments = state_grad.shape[0]

    def walk(state):
        after = [None] * segments
        for s in reversed(range(segments)):
            after[s] = state
            state = (state[0] + state_grad[s], state[1] + norm_grad[s])
            state = jax.tree.map(lambda a: jnp.where(fresh[s], jnp.zeros_like(a), a), state)
        return after, state

    state = (jnp.zeros_like(state_grad[0]), jnp.zeros_like(norm_grad[0]))
    if layout.groups > 1:
        _, first = walk(state)
        renewed = jnp.any(fresh).astype(f32)
        every = jax.tree.map(
            lambda a: lax.all_gather(a, AXIS, axis_index_groups=layout.across), first + (renewed,)
        )
        for g in reversed(range(1, layout.groups)):
            keep = every[2][g] < 0.5
            before = jax.tree.map(lambda a, e: jnp.where(keep, a, 0.0) + e[g], state, every[:2])
            state = jax.tree.map(lambda a, b: jnp.where(g > layout.group, b, a), state, before)
    after, _ = walk(state)
    return jnp.stack([a[0] for a in after]), jnp.stack([a[1] for a in after])


def body(
    layer_input,
    first_gain,
    in_weight,
    out_weight,
    mix_gate,
    second_gain,
    gate_up,
    down_weight,
    document_starts,
    cotangent,
):
    layout = Layout()
    tokens, width = layer_input.shape
    group_tokens = tokens * H
    segments = group_tokens // SEG
    scale = 1.0 / math.sqrt(DH)

    gains = jnp.stack([first_gain, second_gain])
    gains = lax.all_gather(gains, AXIS, axis=1, tiled=True).astype(f32)
    first_all, second_all = gains[0], gains[1]
    if layout.groups == 1:
        mix_own = mix_gate
    else:
        mix_own = lax.dynamic_slice_in_dim(layout.gather_all(mix_gate), layout.head * DH, DH)
    mix = jax.nn.sigmoid(mix_own.astype(f32))[None]

    inputs = layer_input.astype(f32)
    normed, first_factor = norm_forward(inputs, first_all)
    normed_all = layout.gather(normed.astype(bf16))
    in_cols = layout.columns(in_weight, 3)
    out_all = layout.gather_all(out_weight)
    cot_all = layout.gather(cotangent)
    gate_up_cols = layout.columns(gate_up, 2)
    down_cols = layout.columns(down_weight, 1)

    projected = jnp.dot(normed_all, in_cols, preferred_element_type=f32).astype(bf16)
    by_segment = projected.reshape(segments, SEG, 3, DH)
    query, key, value = by_segment[:, :, 0], by_segment[:, :, 1], by_segment[:, :, 2]
    index = jnp.arange(SEG, dtype=jnp.int32)
    allowed = index[None, :] <= index[:, None]

    def attention_scores():
        raw = jnp.einsum("sqc,skc->sqk", query, key, preferred_element_type=f32) * scale
        return jnp.where(allowed[None], raw, -1e30)

    scores = attention_scores()
    top = jnp.max(scores, axis=-1, keepdims=True)
    expo = jnp.exp(scores - top)
    total = jnp.sum(expo, axis=-1, keepdims=True)
    log_total = top + jnp.log(total)
    probs_low = (expo / total).astype(bf16)
    local_out = jnp.einsum("sqk,skc->sqc", probs_low, value, preferred_element_type=f32)

    query_f, key_f, value_f = query.astype(f32), key.astype(f32), value.astype(f32)
    query_feature = feature(query_f).astype(bf16)
    key_feature = feature(key_f).astype(bf16)
    delta = jnp.einsum("slc,sla->sca", key_feature, value, preferred_element_type=f32)
    count = jnp.sum(key_feature.astype(f32), axis=1)
    numbers = layout.group * segments + jnp.arange(segments)
    fresh = (numbers == 0) | (
        lax.dynamic_slice_in_dim(document_starts[0], layout.group * segments, segments) > 0
    )
    memory, normal = carry_forward(layout, delta, count, fresh)
    query_feature_f = query_feature.astype(f32)
    numerator = jnp.einsum("sie,sej->sij", query_feature_f, memory, precision=highest)
    raw_denom = jnp.einsum("sik,sk->si", query_feature_f, normal, precision=highest)[..., None]
    denom = jnp.maximum(raw_denom, 1.0)
    memory_out = numerator / denom
    combined = mix * memory_out + (1.0 - mix) * local_out
    combined_head = combined.reshape(group_tokens, DH).astype(bf16)
    combined_low = layout.to_tokens(combined_head)
    attended = jnp.dot(combined_low, out_all, preferred_element_type=f32)
    middle = inputs + attended

    hidden, second_factor = norm_forward(middle, second_all)
    hidden_all = layout.gather(hidden.astype(bf16))
    act_grad = jnp.dot(cot_all, down_cols, preferred_element_type=f32)
    both = jnp.dot(hidden_all, gate_up_cols, preferred_element_type=f32)
    half = both.shape[1] // 2
    gate_part, up_part = both[:, :half], both[:, half:]
    sigma = jax.nn.sigmoid(gate_part)
    silu = gate_part * sigma
    activated = (silu * up_part).astype(bf16)
    silu_slope = sigma * (1.0 + gate_part * (1.0 - sigma))
    feed_grad = jnp.concatenate(
        [act_grad * up_part * silu_slope, act_grad * silu], axis=1
    ).astype(bf16)
    feed_out = layout.scatter_sum(cols_dot(activated, down_cols).astype(bf16))
    hidden_grad = layout.scatter_sum(cols_dot(feed_grad, gate_up_cols).astype(bf16))
    layer_output = (middle + feed_out.astype(f32)).astype(bf16)
    gate_up_part = layout.own_rows(rows_dot(hidden_all, feed_grad), 2)
    down_part = layout.own_rows(rows_dot(cot_all, activated), 1)

    upstream = cotangent.astype(f32)
    middle_norm_grad, second_local = norm_backward(
        middle, second_factor, second_all, hidden_grad.astype(f32)
    )
    middle_grad = upstream + middle_norm_grad
    attended_grad = middle_grad.astype(bf16)
    attended_grad_all = layout.gather(attended_grad)
    combined_grad = layout.to_heads(cols_dot(attended_grad, out_all).astype(bf16))
    combined_grad = combined_grad.astype(f32).reshape(segments, SEG, DH)
    out_rows_grad = rows_dot(combined_head, attended_grad_all)
    if layout.groups == 1:
        out_part = out_rows_grad
    else:
        whole = jnp.zeros((H * DH, width), f32)
        whole = lax.dynamic_update_slice_in_dim(whole, out_rows_grad, layout.head * DH, 0)
        out_part = lax.psum_scatter(whole, AXIS, scatter_dimension=0, tiled=True)
    mix_local = jnp.sum(combined_grad * (memory_out - local_out), axis=(0, 1)) * (
        mix * (1.0 - mix)
    ).reshape(DH)

    memory_grad = combined_grad * mix
    local_grad = (combined_grad * (1.0 - mix)).astype(bf16)
    numer_grad = memory_grad / denom
    denom_grad = -jnp.sum(memory_grad * memory_out, axis=-1, keepdims=True) / denom
    raw_grad = jnp.where(raw_denom > 1.0, denom_grad, 0.0)
    query_feature_grad = (
        jnp.einsum("sij,sej->sie", numer_grad, memory, precision=highest)
        + raw_grad * normal[:, None]
    )
    state_grad = jnp.einsum("sie,sij->sej", query_feature_f, numer_grad, precision=highest)
    norm_grad = jnp.sum(raw_grad * query_feature_f, axis=1)
    delta_grad, count_grad = carry_backward(layout, state_grad, norm_grad, fresh)
    key_feature_grad = (
        jnp.einsum("sij,sej->sie", value_f, delta_grad, precision=highest) + count_grad[:, None]
    )
    value_memory_grad = jnp.einsum(
        "sie,sej->sij", key_feature.astype(f32), delta_grad, precision=highest
    )
    query_memory_grad = query_feature_grad * feature_slope(query_f)
    key_memory_grad = key_feature_grad * feature_slope(key_f)

    probs = jnp.exp(attention_scores() - log_total)
    prob_grad = jnp.einsum("sqc,skc->sqk", local_grad, value, preferred_element_type=f32)
    row_term = jnp.sum(probs * prob_grad, axis=-1, keepdims=True)
    score_grad = (probs * (prob_grad - row_term)).astype(bf16)
    query_grad = query_memory_grad + scale * jnp.einsum(
        "sqk,skc->sqc", score_grad, key, preferred_element_type=f32
    )
    key_grad = key_memory_grad + scale * jnp.einsum(
        "sqk,sqc->skc", score_grad, query, preferred_element_type=f32
    )
    value_grad = value_memory_grad + jnp.einsum(
        "sqk,sqc->skc", probs.astype(bf16), local_grad, preferred_element_type=f32
    )
    projected_grad = (
        jnp.stack([query_grad, key_grad, value_grad], axis=2)
        .reshape(group_tokens, 3 * DH)
        .astype(bf16)
    )
    normed_grad = layout.scatter_sum(cols_dot(projected_grad, in_cols).astype(bf16))
    in_part = layout.own_rows(rows_dot(normed_all, projected_grad), 3)
    input_norm_grad, first_local = norm_backward(
        inputs, first_factor, first_all, normed_grad.astype(f32)
    )
    input_grad = middle_grad + input_norm_grad

    gains_part = lax.psum_scatter(
        jnp.stack([first_local, second_local]), AXIS, scatter_dimension=1, tiled=True
    )
    if layout.groups == 1:
        mix_part = mix_local
    else:
        whole = jnp.zeros((H * DH,), f32)
        whole = lax.dynamic_update_slice_in_dim(whole, mix_local, layout.head * DH, 0)
        mix_part = lax.psum_scatter(whole, AXIS, scatter_dimension=0, tiled=True)

    def over_sequences(part):
        return lax.psum(part.astype(bf16), "dp").astype(f32)

    small = over_sequences(jnp.concatenate([gains_part, mix_part[None]]))
    return (
        layer_output,
        input_grad,
        small[0],
        over_sequences(in_part),
        over_sequences(out_part),
        small[2],
        small[1],
        over_sequences(gate_up_part),
        over_sequences(down_part),
    )


def solution(mesh):
    return jax.shard_map(
        body,
        mesh=mesh,
        in_specs=(
            P(("dp", "fsdp"), None),
            P("fsdp"),
            P("fsdp", None),
            P("fsdp", None),
            P("fsdp"),
            P("fsdp"),
            P("fsdp", None),
            P("fsdp", None),
            P("dp", None),
            P(("dp", "fsdp"), None),
        ),
        out_specs=(
            P(("dp", "fsdp"), None),
            P(("dp", "fsdp"), None),
            P("fsdp"),
            P("fsdp", None),
            P("fsdp", None),
            P("fsdp"),
            P("fsdp"),
            P("fsdp", None),
            P("fsdp", None),
        ),
        check_vma=False,
    )
```

```python
import functools
import math

import jax
import jax.numpy as jnp
from jax import lax
from jax.experimental import pallas as pl
from jax.experimental.pallas import tpu as pltpu
from jax.sharding import PartitionSpec as P

H = 16
DH = 128
FF = 8192
SEG = 1024

highest = lax.Precision.HIGHEST
epsilon = 1e-06
f32 = jnp.float32
bf16 = jnp.bfloat16
AXIS = "fsdp"


def feature(values):
    return jax.nn.elu(values) + 1.0


def feature_slope(values):
    return jnp.where(values > 0, 1.0, jnp.exp(jnp.minimum(values, 0.0)))


def norm_forward(values, gain):
    factor = lax.rsqrt(jnp.mean(values * values, axis=-1, keepdims=True) + epsilon)
    return (values * factor * gain, factor)


def norm_backward(values, factor, gain, upstream):
    scaled = upstream * gain
    gain_grad = jnp.sum(upstream * values * factor, axis=0)
    value_grad = factor * scaled - values * (factor * factor * factor) * jnp.mean(
        scaled * values, axis=-1, keepdims=True
    )
    return (value_grad, gain_grad)


def dot(left, right, dims):
    return lax.dot_general(left, right, ((dims[0], dims[1]), ((), ())), preferred_element_type=f32)


def rows_dot(left, right):
    return dot(left, right, ((0,), (0,)))


def cols_dot(left, right):
    return dot(left, right, ((1,), (1,)))


class Layout:
    def __init__(self):
        self.count = lax.axis_size(AXIS)
        self.groups = self.count // H
        self.place = lax.axis_index(AXIS)
        self.head = self.place % H
        self.group = self.place // H
        self.inside = None
        self.across = None
        if self.groups > 1:
            self.inside = [[g * H + j for j in range(H)] for g in range(self.groups)]
            self.across = [[g * H + j for g in range(self.groups)] for j in range(H)]

    def gather(self, block):
        return lax.all_gather(block, AXIS, axis=0, tiled=True, axis_index_groups=self.inside)

    def gather_all(self, block):
        return lax.all_gather(block, AXIS, axis=0, tiled=True)

    def scatter_sum(self, whole):
        return lax.psum_scatter(
            whole, AXIS, scatter_dimension=0, tiled=True, axis_index_groups=self.inside
        )

    def columns(self, block, parts):
        rows, width = block.shape
        each = width // (parts * H)
        if self.groups == 1:
            split = block.reshape(rows, parts, H, each)
            out = lax.all_to_all(split, AXIS, 2, 0, tiled=True)
            return out.reshape(rows * self.count, parts * each)
        whole = self.gather_all(block).reshape(rows * self.count, parts, H, each)
        out = lax.dynamic_index_in_dim(whole, self.head, 2, False)
        return out.reshape(rows * self.count, parts * each)

    def own_rows(self, grad, parts):
        rows, width = grad.shape
        each = width // parts
        if self.groups == 1:
            split = grad.astype(bf16).reshape(rows, parts, 1, each)
            out = lax.all_to_all(split, AXIS, 0, 2, tiled=True)
            return out.reshape(rows // self.count, parts * H * each)
        whole = jnp.zeros((rows, parts, H, each), f32)
        whole = lax.dynamic_update_slice_in_dim(
            whole, grad.reshape(rows, parts, 1, each), self.head, 2
        )
        return lax.psum_scatter(
            whole.reshape(rows, parts * H * each), AXIS, scatter_dimension=0, tiled=True
        )

    def to_tokens(self, by_head):
        tokens, each = by_head.shape
        out = lax.all_to_all(
            by_head.reshape(H, tokens // H, each), AXIS, 0, 0, tiled=False,
            axis_index_groups=self.inside,
        )
        return out.transpose(1, 0, 2).reshape(tokens // H, H * each)

    def to_heads(self, by_token):
        tokens, width = by_token.shape
        split = by_token.reshape(tokens, H, width // H).transpose(1, 0, 2)
        out = lax.all_to_all(
            split, AXIS, 0, 0, tiled=False, axis_index_groups=self.inside
        )
        return out.reshape(H * tokens, width // H)


def carry_forward(layout, delta, count, fresh):
    segments = delta.shape[0]

    def walk(state):
        before = []
        for s in range(segments):
            state = jax.tree.map(lambda a: jnp.where(fresh[s], jnp.zeros_like(a), a), state)
            before.append(state)
            state = (state[0] + delta[s], state[1] + count[s])
        return before, state

    state = (jnp.zeros_like(delta[0]), jnp.zeros_like(count[0]))
    if layout.groups > 1:
        _, last = walk(state)
        renewed = jnp.any(fresh).astype(f32)
        every = jax.tree.map(
            lambda a: lax.all_gather(a, AXIS, axis_index_groups=layout.across), last + (renewed,)
        )
        for g in range(layout.groups - 1):
            keep = every[2][g] < 0.5
            after = jax.tree.map(lambda a, e: jnp.where(keep, a, 0.0) + e[g], state, every[:2])
            state = jax.tree.map(lambda a, b: jnp.where(g < layout.group, b, a), state, after)
    before, _ = walk(state)
    return jnp.stack([b[0] for b in before]), jnp.stack([b[1] for b in before])


def carry_backward(layout, state_grad, norm_grad, fresh):
    segments = state_grad.shape[0]

    def walk(state):
        after = [None] * segments
        for s in reversed(range(segments)):
            after[s] = state
            state = (state[0] + state_grad[s], state[1] + norm_grad[s])
            state = jax.tree.map(lambda a: jnp.where(fresh[s], jnp.zeros_like(a), a), state)
        return after, state

    state = (jnp.zeros_like(state_grad[0]), jnp.zeros_like(norm_grad[0]))
    if layout.groups > 1:
        _, first = walk(state)
        renewed = jnp.any(fresh).astype(f32)
        every = jax.tree.map(
            lambda a: lax.all_gather(a, AXIS, axis_index_groups=layout.across), first + (renewed,)
        )
        for g in reversed(range(1, layout.groups)):
            keep = every[2][g] < 0.5
            before = jax.tree.map(lambda a, e: jnp.where(keep, a, 0.0) + e[g], state, every[:2])
            state = jax.tree.map(lambda a, b: jnp.where(g > layout.group, b, a), state, before)
    after, _ = walk(state)
    return jnp.stack([a[0] for a in after]), jnp.stack([a[1] for a in after])


def body_groups(
    layer_input,
    first_gain,
    in_weight,
    out_weight,
    mix_gate,
    second_gain,
    gate_up,
    down_weight,
    document_starts,
    cotangent,
):
    layout = Layout()
    tokens, width = layer_input.shape
    group_tokens = tokens * H
    segments = group_tokens // SEG
    scale = 1.0 / math.sqrt(DH)

    gains = jnp.stack([first_gain, second_gain])
    gains = lax.all_gather(gains, AXIS, axis=1, tiled=True).astype(f32)
    first_all, second_all = gains[0], gains[1]
    if layout.groups == 1:
        mix_own = mix_gate
    else:
        mix_own = lax.dynamic_slice_in_dim(layout.gather_all(mix_gate), layout.head * DH, DH)
    mix = jax.nn.sigmoid(mix_own.astype(f32))[None]

    inputs = layer_input.astype(f32)
    normed, first_factor = norm_forward(inputs, first_all)
    normed_all = layout.gather(normed.astype(bf16))
    in_cols = layout.columns(in_weight, 3)
    out_all = layout.gather_all(out_weight)
    cot_all = layout.gather(cotangent)
    gate_up_cols = layout.columns(gate_up, 2)
    down_cols = layout.columns(down_weight, 1)

    projected = jnp.dot(normed_all, in_cols, preferred_element_type=f32).astype(bf16)
    by_segment = projected.reshape(segments, SEG, 3, DH)
    query, key, value = by_segment[:, :, 0], by_segment[:, :, 1], by_segment[:, :, 2]
    index = jnp.arange(SEG, dtype=jnp.int32)
    allowed = index[None, :] <= index[:, None]

    def attention_scores():
        raw = jnp.einsum("sqc,skc->sqk", query, key, preferred_element_type=f32) * scale
        return jnp.where(allowed[None], raw, -1e30)

    scores = attention_scores()
    top = jnp.max(scores, axis=-1, keepdims=True)
    expo = jnp.exp(scores - top)
    total = jnp.sum(expo, axis=-1, keepdims=True)
    log_total = top + jnp.log(total)
    probs_low = (expo / total).astype(bf16)
    local_out = jnp.einsum("sqk,skc->sqc", probs_low, value, preferred_element_type=f32)

    query_f, key_f, value_f = query.astype(f32), key.astype(f32), value.astype(f32)
    query_feature = feature(query_f).astype(bf16)
    key_feature = feature(key_f).astype(bf16)
    delta = jnp.einsum("slc,sla->sca", key_feature, value, preferred_element_type=f32)
    count = jnp.sum(key_feature.astype(f32), axis=1)
    numbers = layout.group * segments + jnp.arange(segments)
    fresh = (numbers == 0) | (
        lax.dynamic_slice_in_dim(document_starts[0], layout.group * segments, segments) > 0
    )
    memory, normal = carry_forward(layout, delta, count, fresh)
    query_feature_f = query_feature.astype(f32)
    numerator = jnp.einsum("sie,sej->sij", query_feature_f, memory, precision=highest)
    raw_denom = jnp.einsum("sik,sk->si", query_feature_f, normal, precision=highest)[..., None]
    denom = jnp.maximum(raw_denom, 1.0)
    memory_out = numerator / denom
    combined = mix * memory_out + (1.0 - mix) * local_out
    combined_head = combined.reshape(group_tokens, DH).astype(bf16)
    combined_low = layout.to_tokens(combined_head)
    attended = jnp.dot(combined_low, out_all, preferred_element_type=f32)
    middle = inputs + attended

    hidden, second_factor = norm_forward(middle, second_all)
    hidden_all = layout.gather(hidden.astype(bf16))
    act_grad = jnp.dot(cot_all, down_cols, preferred_element_type=f32)
    both = jnp.dot(hidden_all, gate_up_cols, preferred_element_type=f32)
    half = both.shape[1] // 2
    gate_part, up_part = both[:, :half], both[:, half:]
    sigma = jax.nn.sigmoid(gate_part)
    silu = gate_part * sigma
    activated = (silu * up_part).astype(bf16)
    silu_slope = sigma * (1.0 + gate_part * (1.0 - sigma))
    feed_grad = jnp.concatenate(
        [act_grad * up_part * silu_slope, act_grad * silu], axis=1
    ).astype(bf16)
    feed_out = layout.scatter_sum(cols_dot(activated, down_cols).astype(bf16))
    hidden_grad = layout.scatter_sum(cols_dot(feed_grad, gate_up_cols).astype(bf16))
    layer_output = (middle + feed_out.astype(f32)).astype(bf16)
    gate_up_part = layout.own_rows(rows_dot(hidden_all, feed_grad), 2)
    down_part = layout.own_rows(rows_dot(cot_all, activated), 1)

    upstream = cotangent.astype(f32)
    middle_norm_grad, second_local = norm_backward(
        middle, second_factor, second_all, hidden_grad.astype(f32)
    )
    middle_grad = upstream + middle_norm_grad
    attended_grad = middle_grad.astype(bf16)
    attended_grad_all = layout.gather(attended_grad)
    combined_grad = layout.to_heads(cols_dot(attended_grad, out_all).astype(bf16))
    combined_grad = combined_grad.astype(f32).reshape(segments, SEG, DH)
    out_rows_grad = rows_dot(combined_head, attended_grad_all)
    if layout.groups == 1:
        out_part = out_rows_grad
    else:
        whole = jnp.zeros((H * DH, width), f32)
        whole = lax.dynamic_update_slice_in_dim(whole, out_rows_grad, layout.head * DH, 0)
        out_part = lax.psum_scatter(whole, AXIS, scatter_dimension=0, tiled=True)
    mix_local = jnp.sum(combined_grad * (memory_out - local_out), axis=(0, 1)) * (
        mix * (1.0 - mix)
    ).reshape(DH)

    memory_grad = combined_grad * mix
    local_grad = (combined_grad * (1.0 - mix)).astype(bf16)
    numer_grad = memory_grad / denom
    denom_grad = -jnp.sum(memory_grad * memory_out, axis=-1, keepdims=True) / denom
    raw_grad = jnp.where(raw_denom > 1.0, denom_grad, 0.0)
    query_feature_grad = (
        jnp.einsum("sij,sej->sie", numer_grad, memory, precision=highest)
        + raw_grad * normal[:, None]
    )
    state_grad = jnp.einsum("sie,sij->sej", query_feature_f, numer_grad, precision=highest)
    norm_grad = jnp.sum(raw_grad * query_feature_f, axis=1)
    delta_grad, count_grad = carry_backward(layout, state_grad, norm_grad, fresh)
    key_feature_grad = (
        jnp.einsum("sij,sej->sie", value_f, delta_grad, precision=highest) + count_grad[:, None]
    )
    value_memory_grad = jnp.einsum(
        "sie,sej->sij", key_feature.astype(f32), delta_grad, precision=highest
    )
    query_memory_grad = query_feature_grad * feature_slope(query_f)
    key_memory_grad = key_feature_grad * feature_slope(key_f)

    probs = jnp.exp(attention_scores() - log_total)
    prob_grad = jnp.einsum("sqc,skc->sqk", local_grad, value, preferred_element_type=f32)
    row_term = jnp.sum(probs * prob_grad, axis=-1, keepdims=True)
    score_grad = (probs * (prob_grad - row_term)).astype(bf16)
    query_grad = query_memory_grad + scale * jnp.einsum(
        "sqk,skc->sqc", score_grad, key, preferred_element_type=f32
    )
    key_grad = key_memory_grad + scale * jnp.einsum(
        "sqk,sqc->skc", score_grad, query, preferred_element_type=f32
    )
    value_grad = value_memory_grad + jnp.einsum(
        "sqk,sqc->skc", probs.astype(bf16), local_grad, preferred_element_type=f32
    )
    projected_grad = (
        jnp.stack([query_grad, key_grad, value_grad], axis=2)
        .reshape(group_tokens, 3 * DH)
        .astype(bf16)
    )
    normed_grad = layout.scatter_sum(cols_dot(projected_grad, in_cols).astype(bf16))
    in_part = layout.own_rows(rows_dot(normed_all, projected_grad), 3)
    input_norm_grad, first_local = norm_backward(
        inputs, first_factor, first_all, normed_grad.astype(f32)
    )
    input_grad = middle_grad + input_norm_grad

    gains_part = lax.psum_scatter(
        jnp.stack([first_local, second_local]), AXIS, scatter_dimension=1, tiled=True
    )
    if layout.groups == 1:
        mix_part = mix_local
    else:
        whole = jnp.zeros((H * DH,), f32)
        whole = lax.dynamic_update_slice_in_dim(whole, mix_local, layout.head * DH, 0)
        mix_part = lax.psum_scatter(whole, AXIS, scatter_dimension=0, tiled=True)

    def over_sequences(part):
        return lax.psum(part.astype(bf16), "dp").astype(f32)

    small = over_sequences(jnp.concatenate([gains_part, mix_part[None]]))
    return (
        layer_output,
        input_grad,
        small[0],
        over_sequences(in_part),
        over_sequences(out_part),
        small[2],
        small[1],
        over_sequences(gate_up_part),
        over_sequences(down_part),
    )


MESH = pl.DeviceIdType.MESH
LIMIT = 60 * 2**20
CHUNKS = 4
QUARTERS = 4
ROWS = 256
dma = pltpu.SemaphoreType.DMA
VM = pltpu.VMEM


def vmem():
    return pl.BlockSpec(memory_space=pltpu.VMEM)


def anywhere():
    return pl.BlockSpec(memory_space=pl.ANY)


class Spot:
    def __init__(self):
        self.dp = lax.axis_index("dp")
        self.me = lax.axis_index(AXIS)
        self.z = self.me // 4
        self.y = (self.me // 2) % 2
        self.c = self.me % 2

    def at(self, z, y, c):
        return z * 4 + y * 2 + c

    def arrival(self, j):
        if j == 0:
            return self.z
        ends = jnp.where(self.z == 0, j, 3 - j)
        middle = {1: (0, 3), 2: (2, 1), 3: (3, 0)}[j]
        inner = jnp.where(self.z == 1, middle[0], middle[1])
        return jnp.where((self.z == 0) | (self.z == 3), ends, inner)


def greet(s, plane=True, other=True):
    ids = []
    if plane:
        ids += [{AXIS: (s.me + k) % 16} for k in range(1, 16)]
    else:
        ids += [{AXIS: s.at((s.z + k) % 4, s.y, s.c)} for k in (1, 2, 3)]
        ids += [{AXIS: s.at(s.z, 1 - s.y, s.c)}, {AXIS: s.at(s.z, s.y, 1 - s.c)}]
    if other:
        ids += [{"dp": 1 - s.dp}]
    barrier = pltpu.get_barrier_semaphore()
    for d in ids:
        pl.semaphore_signal(barrier, inc=1, device_id=d, device_id_type=MESH)
    pl.semaphore_wait(barrier, len(ids))


def send(src, dst, ssem, rsem, to):
    return pltpu.make_async_remote_copy(
        src_ref=src, dst_ref=dst, send_sem=ssem, recv_sem=rsem,
        device_id={AXIS: to}, device_id_type=MESH,
    )


def send_over(src, dst, ssem, rsem, s):
    return pltpu.make_async_remote_copy(
        src_ref=src, dst_ref=dst, send_sem=ssem, recv_sem=rsem,
        device_id={"dp": 1 - s.dp}, device_id_type=MESH,
    )


def merged(*lists):
    keyed = []
    for n, tasks in enumerate(lists):
        keyed += [((i + 0.5) / len(tasks), n, i, t) for i, t in enumerate(tasks)]
    for _, _, _, t in sorted(keyed, key=lambda e: e[:3]):
        t()


class Gather:
    @staticmethod
    def sems():
        return [dma((CHUNKS, 4))] * 5 + [dma((CHUNKS, 8))] * 2

    def __init__(self, s, src, dst, sems):
        self.s, self.src, self.dst = s, src, dst
        self.zr, self.zu, self.zd, self.ys, self.yr, self.ss, self.sr = sems
        self.rows = 128 // CHUNKS

    def block(self, ch, z, y, c):
        start = pl.multiple_of(self.s.at(z, y, c) * 128 + ch * self.rows, self.rows)
        return self.dst.at[pl.ds(start, self.rows)]

    def own(self, ch):
        return self.src.at[pl.ds(ch * self.rows, self.rows)]

    def zcopy(self, ch, zo, up, own=False):
        s = self.s
        dst = self.block(ch, zo, s.y, s.c)
        to = s.at(s.z + 1 if up else s.z - 1, s.y, s.c)
        return send(
            self.own(ch) if own else dst, dst,
            (self.zu if up else self.zd).at[ch, zo], self.zr.at[ch, zo], to,
        )

    def ycopy(self, ch, zo, own=False):
        s = self.s
        dst = self.block(ch, zo, s.y, s.c)
        src = self.own(ch) if own else dst
        return send(src, dst, self.ys.at[ch, zo], self.yr.at[ch, zo], s.at(s.z, 1 - s.y, s.c))

    def scopy(self, ch, zo, yo, own=False):
        s = self.s
        dst = self.block(ch, zo, yo, s.c)
        n = zo * 2 + yo
        src = self.own(ch) if own else dst
        return send(src, dst, self.ss.at[ch, n], self.sr.at[ch, n], s.at(s.z, s.y, 1 - s.c))

    def start(self):
        s = self.s
        for ch in range(CHUNKS):
            pl.when(s.z < 3)(lambda: self.zcopy(ch, s.z, True, True).start())
            pl.when(s.z > 0)(lambda: self.zcopy(ch, s.z, False, True).start())
            self.ycopy(ch, s.z, True).start()
            self.scopy(ch, s.z, s.y, True).start()

    def z_arrive(self, ch, j):
        s = self.s
        zo = s.arrival(j)
        self.zcopy(ch, zo, True).wait_recv()
        pl.when((zo < s.z) & (s.z < 3))(lambda: self.zcopy(ch, zo, True).start())
        pl.when((zo > s.z) & (s.z > 0))(lambda: self.zcopy(ch, zo, False).start())
        self.ycopy(ch, zo).start()
        self.scopy(ch, zo, s.y).start()

    def y_arrive(self, ch, j):
        s = self.s
        zo = s.arrival(j)
        b = self.block(ch, zo, 1 - s.y, s.c)
        send(b, b, self.ys.at[ch, zo], self.yr.at[ch, zo], s.me).wait_recv()
        self.scopy(ch, zo, 1 - s.y).start()

    def s_arrive(self, j):
        s = self.s
        zo = s.arrival(j)
        for ch in range(CHUNKS):
            for yo in range(2):
                n = zo * 2 + yo
                b = self.block(ch, zo, yo, 1 - s.c)
                send(b, b, self.ss.at[ch, n], self.sr.at[ch, n], s.me).wait_recv()

    def tasks(self, use=None):
        out = []
        for step in range(5):
            for ch in range(CHUNKS):
                if 0 < step < 4:
                    out.append(functools.partial(self.z_arrive, ch, step))
                if step > 0:
                    out.append(functools.partial(self.y_arrive, ch, step - 1))
            if step > 0:
                out.append(functools.partial(self.s_arrive, step - 1))
                if use is not None:
                    out.append(functools.partial(use, step - 1))
        return out

    def drain(self):
        s = self.s
        for ch in range(CHUNKS):
            for zo in range(4):
                pl.when((s.z < 3) & (zo <= s.z))(lambda: self.zcopy(ch, zo, True).wait_send())
                pl.when((s.z > 0) & (zo >= s.z))(lambda: self.zcopy(ch, zo, False).wait_send())
                self.ycopy(ch, zo).wait_send()
                for yo in range(2):
                    self.scopy(ch, zo, yo).wait_send()


class Columns:
    @staticmethod
    def sems(parts):
        return [dma((16, parts)), dma((16, parts)), dma((16,)), dma((16,)), dma((parts,))]

    def __init__(self, s, w, dst, parts, sems):
        self.s, self.w, self.dst, self.parts = s, w, dst, parts
        self.e = dst.shape[1] // parts
        self.ps, self.pr, self.xs, self.xr, self.own = sems

    def rows(self, src, half):
        return pl.ds(pl.multiple_of(src * 128 + half * 64, 64), 64)

    def cols(self, p, h):
        return pl.ds(pl.multiple_of(p * 16 * self.e + h * self.e, 128), self.e)

    def copy(self, k, p):
        s = self.s
        to = (s.me + k) % 16
        half = pl.ds(pl.multiple_of(s.dp * 64, 64), 64)
        return send(
            self.w.at[half, self.cols(p, to)],
            self.dst.at[self.rows(s.me, s.dp), pl.ds(p * self.e, self.e)],
            self.ps.at[k, p], self.pr.at[s.me, p], to,
        )

    def local(self, p):
        s = self.s
        return pltpu.make_async_copy(
            self.w.at[:, self.cols(p, s.me)],
            self.dst.at[pl.ds(pl.multiple_of(s.me * 128, 128), 128), pl.ds(p * self.e, self.e)],
            self.own.at[p],
        )

    def start(self):
        for k in range(1, 16):
            for p in range(self.parts):
                self.copy(k, p).start()
        for p in range(self.parts):
            self.local(p).start()

    def over(self, src):
        s = self.s
        b = self.dst.at[self.rows(src, s.dp)]
        return send_over(b, b, self.xs.at[src], self.xr.at[src], s)

    def arrive(self, k):
        s = self.s
        src = (s.me + 16 - k) % 16
        for p in range(self.parts):
            b = self.dst.at[self.rows(src, s.dp), pl.ds(p * self.e, self.e)]
            send(b, b, self.ps.at[k, p], self.pr.at[src, p], s.me).wait_recv()
        self.over(src).start()

    def tasks(self):
        return [functools.partial(self.arrive, k) for k in range(1, 16)]

    def finish(self):
        s = self.s
        for k in range(1, 16):
            src = (s.me + 16 - k) % 16
            b = self.dst.at[self.rows(src, 1 - s.dp)]
            send_over(b, b, self.xs.at[src], self.xr.at[src], s).wait_recv()
        for p in range(self.parts):
            self.local(p).wait()

    def drain(self):
        s = self.s
        for k in range(1, 16):
            for p in range(self.parts):
                self.copy(k, p).wait_send()
            self.over((s.me + 16 - k) % 16).wait_send()


class Return:
    @staticmethod
    def sems(parts):
        return [dma((16, parts))] * 4 + [dma((parts,))]

    def __init__(self, s, src, dst, parts, sems, other=None):
        self.s, self.src, self.dst, self.parts, self.other = s, src, dst, parts, other
        self.e = src.shape[2] // parts
        self.ps, self.pr, self.xs, self.xr, self.own = sems

    def place(self, ref, p, h):
        return ref.at[:, pl.ds(pl.multiple_of(p * 16 * self.e + h * self.e, 128), self.e)]

    def copy(self, k, p):
        s = self.s
        to = (s.me + k) % 16
        return send(
            self.src.at[to, :, pl.ds(p * self.e, self.e)], self.place(self.dst, p, s.me),
            self.ps.at[k, p], self.pr.at[s.me, p], to,
        )

    def local(self, p):
        s = self.s
        return pltpu.make_async_copy(
            self.src.at[s.me, :, pl.ds(p * self.e, self.e)], self.place(self.dst, p, s.me),
            self.own.at[p],
        )

    def start(self):
        for p in range(self.parts):
            self.local(p).start()
        for k in range(1, 16):
            for p in range(self.parts):
                self.copy(k, p).start()
        if self.other is not None:
            for p in range(self.parts):
                self.over(self.s.me, p, own=True).start()

    def over(self, h, p, own=False):
        s = self.s
        src = self.src.at[s.me, :, pl.ds(p * self.e, self.e)] if own else self.place(self.dst, p, h)
        return send_over(src, self.place(self.other, p, h), self.xs.at[h, p], self.xr.at[h, p], s)

    def arrive(self, k):
        s = self.s
        h = (s.me + 16 - k) % 16
        for p in range(self.parts):
            b = self.place(self.dst, p, h)
            send(b, b, self.ps.at[k, p], self.pr.at[h, p], s.me).wait_recv()
            if self.other is not None:
                self.over(h, p).start()

    def tasks(self):
        return [functools.partial(self.arrive, k) for k in range(1, 16)]

    def finish(self):
        s = self.s
        for p in range(self.parts):
            self.local(p).wait()
        if self.other is not None:
            for k in range(16):
                h = (s.me + 16 - k) % 16
                for p in range(self.parts):
                    b = self.place(self.other, p, h)
                    send_over(b, b, self.xs.at[h, p], self.xr.at[h, p], s).wait_recv()
        for k in range(1, 16):
            for p in range(self.parts):
                self.copy(k, p).wait_send()
        if self.other is not None:
            for k in range(16):
                for p in range(self.parts):
                    self.over((s.me + 16 - k) % 16, p).wait_send()


class Scatter:
    @staticmethod
    def scratch(width):
        q = QUARTERS
        return [
            VM((4, 2, 256, width), bf16), VM((4, 2, 128, width), bf16), VM((4, 2, 128, width), bf16),
            VM((4, 128, width), bf16), VM((3, 128, width), bf16),
            dma((4, q, 2)), dma((4, q, 2)), dma((4, q)), dma((4, q)), dma((3, q)), dma((3, q)),
        ]

    def __init__(self, s, left, right, out, scratch):
        self.s, self.left, self.right, self.out = s, left, right, out
        self.part, self.sib, self.mid, self.got_y, self.got_z = scratch[:5]
        self.ss, self.sr, self.ys, self.yr, self.zs, self.zr = scratch[5:]
        self.cols = right.shape[0] // QUARTERS
        self.order = [(s.z + 2) % 4, 3 - s.z, s.z + 1 - 2 * (s.z % 2), s.z]

    def w(self, h):
        return pl.ds(h * self.cols, self.cols)

    def compute(self, k, h, yd, slot):
        tok = pl.multiple_of((self.order[k] * 2 + yd) * 256, 256)
        p = cols_dot(self.left[pl.ds(tok, 256), :], self.right[self.w(h), :])
        self.part[k, slot, :, self.w(h)] = p.astype(bf16)

    def sib_copy(self, k, h, slot):
        s = self.s
        src = self.part.at[k, slot, pl.ds(pl.multiple_of((1 - s.c) * 128, 128), 128), self.w(h)]
        return send(
            src, self.sib.at[k, slot, :, self.w(h)],
            self.ss.at[k, h, slot], self.sr.at[k, h, slot], s.at(s.z, s.y, 1 - s.c),
        )

    def y_copy(self, k, h):
        s = self.s
        return send(
            self.mid.at[k, 0, :, self.w(h)], self.got_y.at[k, :, self.w(h)],
            self.ys.at[k, h], self.yr.at[k, h], s.at(s.z, 1 - s.y, s.c),
        )

    def z_copy(self, k, h):
        s = self.s
        return send(
            self.mid.at[k, 1, :, self.w(h)], self.got_z.at[k, :, self.w(h)],
            self.zs.at[k, h], self.zr.at[k, h], s.at(self.order[k], s.y, s.c),
        )

    def fold(self, k, h, slot):
        s = self.s
        self.sib_copy(k, h, slot).wait_recv()
        own = self.part[k, slot, pl.ds(pl.multiple_of(s.c * 128, 128), 128), self.w(h)]
        total = own.astype(f32) + self.sib[k, slot, :, self.w(h)].astype(f32)
        self.mid[k, slot, :, self.w(h)] = total.astype(bf16)

    def after_y(self, k, h):
        self.y_copy(k, h).wait_recv()
        w = self.w(h)
        total = self.mid[k, 1, :, w].astype(f32) + self.got_y[k, :, w].astype(f32)
        if k < 3:
            self.mid[k, 1, :, w] = total.astype(bf16)
            self.z_copy(k, h).start()
        else:
            self.out[:, w] = total

    def tasks(self):
        steps = [(k, h) for k in range(4) for h in range(QUARTERS)]
        s = self.s

        def step(i):
            k, h = steps[i]
            self.compute(k, h, 1 - s.y, 0)
            self.sib_copy(k, h, 0).start()
            self.compute(k, h, s.y, 1)
            self.sib_copy(k, h, 1).start()
            self.fold(k, h, 0)
            self.y_copy(k, h).start()
            self.fold(k, h, 1)
            if i >= 2:
                self.after_y(*steps[i - 2])

        out = [functools.partial(step, i) for i in range(len(steps))]
        out += [functools.partial(self.after_y, *steps[i]) for i in (len(steps) - 2, len(steps) - 1)]
        return out

    def finish(self):
        for k in range(3):
            for h in range(QUARTERS):
                self.z_copy(k, h).wait_recv()
                self.out[:, self.w(h)] += self.got_z[k, :, self.w(h)].astype(f32)
        for k in range(4):
            for h in range(QUARTERS):
                self.sib_copy(k, h, 0).wait_send()
                self.sib_copy(k, h, 1).wait_send()
                self.y_copy(k, h).wait_send()
                if k < 3:
                    self.z_copy(k, h).wait_send()


def halves_of(refs, counts):
    out, at = [], 0
    for n in counts:
        out.append(refs[at:at + n])
        at += n
    return out


def communicate(kernel, name, number, ins, in_specs, outs, out_specs, scratch, flops=0):
    return pl.pallas_call(
        kernel, out_shape=outs, in_specs=in_specs, out_specs=out_specs, scratch_shapes=scratch,
        compiler_params=pltpu.CompilerParams(
            collective_id=number, has_side_effects=True, vmem_limit_bytes=LIMIT
        ),
        cost_estimate=pl.CostEstimate(flops=flops, bytes_accessed=2**24, transcendentals=0),
        name=name,
    )(*ins)


def project_kernel(x, gains, in_w, normed_all, in_cols, gains_all, projected, normed, *rest):
    g_s, g_r = rest[:2]
    gather_sems, col_sems = halves_of(rest[2:], [7, 5])
    s = Spot()
    greet(s)

    def gain_copy(k):
        return send(gains, gains_all.at[s.me], g_s.at[k], g_r.at[s.me], (s.me + k) % 16)

    for k in range(1, 16):
        gain_copy(k).start()
    columns = Columns(s, in_w, in_cols, 3, col_sems)
    columns.start()
    gains_all[s.me] = gains[...]
    values = x[...].astype(f32)
    factor = lax.rsqrt(jnp.mean(values * values, axis=-1, keepdims=True) + epsilon)
    for k in range(1, 16):
        src = (s.me + 16 - k) % 16
        b = gains_all.at[src]
        send(b, b, g_s.at[k], g_r.at[src], s.me).wait_recv()
    mine = pl.ds(pl.multiple_of(s.me * 128, 128), 128)
    for j in range(16):
        w = pl.ds(j * 128, 128)
        part = (x[:, w].astype(f32) * factor * gains_all[j, 0:1, :]).astype(bf16)
        normed[:, w] = part
        normed_all[mine, w] = part
    gather = Gather(s, normed, normed_all, gather_sems)
    gather.start()

    def use(j):
        if j == 3:
            columns.finish()
            for i in range(4):
                tok = pl.ds(pl.multiple_of(s.arrival(i) * 512, 512), 512)
                out = jnp.dot(normed_all[tok, :], in_cols[...], preferred_element_type=f32)
                projected[tok, :] = out.astype(bf16)

    merged(gather.tasks(use), columns.tasks() + [lambda: None] * 6)
    gather.drain()
    columns.drain()
    for k in range(1, 16):
        gain_copy(k).wait_send()


def project(x, gains, in_weight, number):
    tokens, width = x.shape
    return communicate(
        project_kernel, "project", number, (x, gains, in_weight), [vmem(), vmem(), anywhere()],
        [
            jax.ShapeDtypeStruct((16 * tokens, width), bf16),
            jax.ShapeDtypeStruct((width, 3 * DH), bf16),
            jax.ShapeDtypeStruct((16, 8, 128), f32),
            jax.ShapeDtypeStruct((16 * tokens, 3 * DH), bf16),
        ],
        [vmem()] * 4,
        [VM((tokens, width), bf16), dma((16,)), dma((16,))] + Gather.sems() + Columns.sems(3),
    )


def kernel_feature(t):
    return jnp.where(t > 0, t + 1.0, jnp.exp(jnp.minimum(t, 0.0)))


def dot_high(left, right, dims=((1,), (0,))):
    return lax.dot_general(
        left, right, (dims, ((), ())), preferred_element_type=f32, precision=highest
    )


def scores_of(query, keys, first):
    raw = cols_dot(query, keys) * (1.0 / math.sqrt(DH))
    row = lax.broadcasted_iota(jnp.int32, raw.shape, 0) + first
    col = lax.broadcasted_iota(jnp.int32, raw.shape, 1)
    return jnp.where(col <= row, raw, -1e30)


class Attend:
    def __init__(self, qkv, keep, mix, local, mem_out, lse, combined, memory, normal):
        self.qkv, self.keep, self.mix = qkv, keep, mix
        self.local, self.mem_out, self.lse, self.combined = local, mem_out, lse, combined
        self.memory, self.normal = memory, normal
        self.segments = qkv.shape[0] // SEG

    def states(self):
        state = jnp.zeros((DH, DH), f32)
        norm = jnp.zeros((1, DH), f32)
        for n in range(self.segments):
            keep = self.keep[n, 0:1, :]
            state, norm = state * keep, norm * keep
            self.memory[n] = state
            self.normal[n, 0:1, :] = norm
            if n + 1 < self.segments:
                rows = pl.ds(n * SEG, SEG)
                fk = kernel_feature(self.qkv[rows, DH:2 * DH].astype(f32)).astype(bf16)
                state = state + rows_dot(fk, self.qkv[rows, 2 * DH:])
                norm = norm + jnp.sum(fk.astype(f32), axis=0, keepdims=True)

    def block(self, n, i):
        rows = pl.ds(n * SEG + i * ROWS, ROWS)
        seen = pl.ds(n * SEG, (i + 1) * ROWS)
        query = self.qkv[rows, :DH]
        scores = scores_of(query, self.qkv[seen, DH:2 * DH], i * ROWS)
        top = jnp.max(scores, axis=-1, keepdims=True)
        expo = jnp.exp(scores - top)
        total = jnp.sum(expo, axis=-1, keepdims=True)
        probs = (expo * (1.0 / total)).astype(bf16)
        local = jnp.dot(probs, self.qkv[seen, 2 * DH:], preferred_element_type=f32)
        fq = kernel_feature(query.astype(f32)).astype(bf16).astype(f32)
        den = jnp.maximum(jnp.sum(fq * self.normal[n, 0:1, :], axis=-1, keepdims=True), 1.0)
        mem_out = dot_high(fq, self.memory[n]) / den
        mix = self.mix[0:1, :]
        self.local[rows, :] = local
        self.mem_out[rows, :] = mem_out
        self.lse[rows, :] = jnp.broadcast_to(top + jnp.log(total), (ROWS, DH))
        self.combined[rows, :] = (mix * mem_out + (1.0 - mix) * local).astype(bf16)

    def blocks(self):
        return [(n, i) for n in range(self.segments) for i in range(SEG // ROWS)]


class AttendBack:
    def __init__(self, qkv, keep, mix, local, mem_out, lse, memory, normal, upstream, grad,
                 mix_grad, dk, dv, state_grad, norm_grad):
        self.qkv, self.keep, self.mix = qkv, keep, mix
        self.local, self.mem_out, self.lse = local, mem_out, lse
        self.memory, self.normal, self.upstream, self.grad = memory, normal, upstream, grad
        self.mix_grad, self.dk, self.dv = mix_grad, dk, dv
        self.state_grad, self.norm_grad = state_grad, norm_grad
        self.segments = qkv.shape[0] // SEG

    def clear(self):
        self.mix_grad[...] = jnp.zeros_like(self.mix_grad)
        self.dk[...] = jnp.zeros_like(self.dk)
        self.dv[...] = jnp.zeros_like(self.dv)
        self.state_grad[...] = jnp.zeros_like(self.state_grad)
        self.norm_grad[...] = jnp.zeros_like(self.norm_grad)

    def block(self, n, i):
        scale = 1.0 / math.sqrt(DH)
        rows = pl.ds(n * SEG + i * ROWS, ROWS)
        seen = pl.ds(n * SEG, (i + 1) * ROWS)
        query = self.qkv[rows, :DH]
        keys = self.qkv[seen, DH:2 * DH]
        values = self.qkv[seen, 2 * DH:]
        up = self.upstream[rows, :].astype(f32)
        mem_out = self.mem_out[rows, :]
        mix = self.mix[0:1, :]
        mixed = jnp.sum(up * (mem_out - self.local[rows, :]), axis=0, keepdims=True)
        self.mix_grad[0:1, :] += mixed * mix * (1.0 - mix)
        memory_grad = up * mix
        local_grad = (up * (1.0 - mix)).astype(bf16)
        query_f = query.astype(f32)
        fq = kernel_feature(query_f).astype(bf16).astype(f32)
        normal = self.normal[n, 0:1, :]
        raw = jnp.sum(fq * normal, axis=-1, keepdims=True)
        den = jnp.maximum(raw, 1.0)
        numer_grad = memory_grad / den
        den_grad = -jnp.sum(memory_grad * mem_out, axis=-1, keepdims=True) / den
        raw_grad = jnp.where(raw > 1.0, den_grad, 0.0)
        fq_grad = dot_high(numer_grad, self.memory[n], ((1,), (1,))) + raw_grad * normal
        if n > 0:
            self.state_grad[n] += dot_high(fq, numer_grad, ((0,), (0,)))
            self.norm_grad[n, 0:1, :] += jnp.sum(raw_grad * fq, axis=0, keepdims=True)
        scores = scores_of(query, keys, i * ROWS)
        probs = jnp.exp(scores - self.lse[rows, 0:1])
        prob_grad = cols_dot(local_grad, values)
        row_term = jnp.sum(probs * prob_grad, axis=-1, keepdims=True)
        score_grad = (probs * (prob_grad - row_term)).astype(bf16)
        query_grad = jnp.dot(score_grad, keys, preferred_element_type=f32) * scale
        query_grad = query_grad + fq_grad * feature_slope(query_f)
        self.grad[rows, :DH] = query_grad.astype(bf16)
        self.dk[seen, :] += rows_dot(score_grad, query) * scale
        self.dv[seen, :] += rows_dot(probs.astype(bf16), local_grad)

    def states(self):
        state = jnp.zeros((DH, DH), f32)
        norm = jnp.zeros((1, DH), f32)
        for n in reversed(range(self.segments)):
            rows = pl.ds(n * SEG, SEG)
            key = self.qkv[rows, DH:2 * DH].astype(f32)
            key_grad = self.dk[rows, :]
            value_grad = self.dv[rows, :]
            if n + 1 < self.segments:
                fk = kernel_feature(key).astype(bf16).astype(f32)
                value = self.qkv[rows, 2 * DH:].astype(f32)
                fk_grad = dot_high(value, state, ((1,), (1,))) + norm
                key_grad = key_grad + fk_grad * feature_slope(key)
                value_grad = value_grad + dot_high(fk, state)
            self.grad[rows, DH:2 * DH] = key_grad.astype(bf16)
            self.grad[rows, 2 * DH:] = value_grad.astype(bf16)
            if n > 0:
                keep = self.keep[n, 0:1, :]
                state = (state + self.state_grad[n]) * keep
                norm = (norm + self.norm_grad[n, 0:1, :]) * keep

    def blocks(self):
        return [(n, i) for n in range(self.segments) for i in range(SEG // ROWS)]


def attend_kernel(qkv, keep, mix, out_w, cot, gate_up, down,
                  local, mem_out, lse, combined, memory, normal, mixed_tokens, out_all, cot_all,
                  gate_up_cols, down_cols, copies, t_s, t_r, *rest):
    sems_o, sems_c, sems_g, sems_d = halves_of(rest, [7, 7, 5, 5])
    s = Spot()
    mine = pl.ds(pl.multiple_of(s.me * 128, 128), 128)
    own = [
        pltpu.make_async_copy(out_w, out_all.at[mine], copies.at[0]),
        pltpu.make_async_copy(cot, cot_all.at[mine], copies.at[1]),
    ]
    for cp in own:
        cp.start()
    greet(s)
    gather_o = Gather(s, out_w, out_all, sems_o)
    gather_c = Gather(s, cot, cot_all, sems_c)
    columns_g = Columns(s, gate_up, gate_up_cols, 2, sems_g)
    columns_d = Columns(s, down, down_cols, 1, sems_d)
    gather_o.start()
    columns_g.start()
    attend = Attend(qkv, keep, mix, local, mem_out, lse, combined, memory, normal)

    def token_copy(j):
        return send(
            combined.at[pl.ds(j * 128, 128)],
            mixed_tokens.at[:, pl.ds(pl.multiple_of(s.me * DH, DH), DH)],
            t_s.at[j], t_r.at[s.me], j,
        )

    def block(n, i):
        attend.block(n, i)
        for j in range((n * SEG + i * ROWS) // 128, (n * SEG + (i + 1) * ROWS) // 128):
            pl.when(s.me != j)(lambda: token_copy(j).start())

    def late():
        gather_c.start()
        columns_d.start()

    compute = [attend.states] + [functools.partial(block, n, i) for n, i in attend.blocks()]
    merged(
        gather_o.tasks() + [late] + gather_c.tasks(),
        compute + [lambda: None] * len(compute),
        [lambda: None] * 3 + columns_g.tasks() + [lambda: None] * 3 + columns_d.tasks(),
    )
    mixed_tokens[:, pl.ds(pl.multiple_of(s.me * DH, DH), DH)] = combined[mine, :]
    columns_g.finish()
    columns_d.finish()
    for k in range(1, 16):
        src = (s.me + 16 - k) % 16
        b = mixed_tokens.at[:, pl.ds(pl.multiple_of(src * DH, DH), DH)]
        send(b, b, t_s.at[0], t_r.at[src], s.me).wait_recv()
    for j in range(16):
        pl.when(s.me != j)(lambda: token_copy(j).wait_send())
    gather_o.drain()
    gather_c.drain()
    columns_g.drain()
    columns_d.drain()
    for cp in own:
        cp.wait()


def attend_forward(qkv, keep, mix, out_weight, cotangent, gate_up, down, number):
    tokens, width = cotangent.shape
    total = qkv.shape[0]
    segments = total // SEG
    shape = jax.ShapeDtypeStruct
    return communicate(
        attend_kernel, "attend", number, (qkv, keep, mix, out_weight, cotangent, gate_up, down),
        [vmem()] * 3 + [anywhere()] * 4,
        [
            shape((total, DH), f32), shape((total, DH), f32), shape((total, DH), f32),
            shape((total, DH), bf16), shape((segments, DH, DH), f32), shape((segments, 8, DH), f32),
            shape((tokens, width), bf16),
            shape((total, width), bf16), shape((total, width), bf16),
            shape((width, gate_up.shape[1] // 16), bf16), shape((width, down.shape[1] // 16), bf16),
        ],
        [vmem()] * 7 + [anywhere()] * 4,
        [dma((2,)), dma((16,)), dma((16,))] + Gather.sems() * 2 + Columns.sems(2) + Columns.sems(1),
    )


def feed_kernel(combined, x, gains_all, out_all, cot_all, gate_up_cols, down_cols,
                middle, hidden_all, act, feed_grad, out_v, cot_v, gate_up_v, down_v, hidden, copies,
                *sems):
    s = Spot()
    loads = [
        pltpu.make_async_copy(a, b, copies.at[i])
        for i, (a, b) in enumerate(
            [(out_all, out_v), (gate_up_cols, gate_up_v), (cot_all, cot_v), (down_cols, down_v)]
        )
    ]
    for cp in loads:
        cp.start()
    greet(s, plane=False, other=False)
    loads[0].wait()
    width = x.shape[1]
    squares = jnp.zeros((x.shape[0], 1), f32)
    for j in range(4):
        w = pl.ds(j * 512, 512)
        got = jnp.dot(combined[...], out_v[:, w], preferred_element_type=f32)
        got = got + x[:, w].astype(f32)
        middle[:, w] = got
        squares = squares + jnp.sum(got * got, axis=-1, keepdims=True)
    factor = lax.rsqrt(squares * (1.0 / width) + epsilon)
    mine = pl.ds(pl.multiple_of(s.me * 128, 128), 128)
    for j in range(16):
        w = pl.ds(j * 128, 128)
        part = (middle[:, w] * factor * gains_all[j, 1:2, :]).astype(bf16)
        hidden[:, w] = part
        hidden_all[mine, w] = part
    gather = Gather(s, hidden, hidden_all, sems)
    gather.start()
    half = act.shape[1]

    def use(j):
        if j == 0:
            for cp in loads[1:]:
                cp.wait()
        tok = pl.ds(pl.multiple_of(s.arrival(j) * 512, 512), 512)
        act_grad = jnp.dot(cot_v[tok, :], down_v[...], preferred_element_type=f32)
        gate = jnp.dot(hidden_all[tok, :], gate_up_v[:, :half], preferred_element_type=f32)
        up = jnp.dot(hidden_all[tok, :], gate_up_v[:, half:], preferred_element_type=f32)
        sigma = jax.nn.sigmoid(gate)
        silu = gate * sigma
        act[tok, :] = (silu * up).astype(bf16)
        slope = sigma * (1.0 + gate * (1.0 - sigma))
        feed_grad[tok, :half] = (act_grad * up * slope).astype(bf16)
        feed_grad[tok, half:] = (act_grad * silu).astype(bf16)

    merged(gather.tasks(use))
    gather.drain()


def feed(combined, x, gains_all, out_all, cot_all, gate_up_cols, down_cols, number):
    tokens, width = x.shape
    total = cot_all.shape[0]
    half = down_cols.shape[1]
    shape = jax.ShapeDtypeStruct
    return communicate(
        feed_kernel, "feed", number,
        (combined, x, gains_all, out_all, cot_all, gate_up_cols, down_cols),
        [vmem()] * 3 + [anywhere()] * 4,
        [
            shape((tokens, width), f32), shape((total, width), bf16),
            shape((total, half), bf16), shape((total, 2 * half), bf16),
        ],
        [vmem()] * 4,
        [
            VM(out_all.shape, bf16), VM(cot_all.shape, bf16), VM(gate_up_cols.shape, bf16),
            VM(down_cols.shape, bf16), VM((tokens, width), bf16), dma((4,)),
        ] + Gather.sems(),
    )


def scatter_kernel(exchanges, left, right, *rest):
    sent = rest[:exchanges]
    out = rest[exchanges]
    got = rest[exchanges + 1:2 * exchanges + 1]
    x_s, x_r = rest[2 * exchanges + 1:2 * exchanges + 3]
    s = Spot()
    greet(s, plane=False)
    overs = [send_over(a, b, x_s.at[i], x_r.at[i], s) for i, (a, b) in enumerate(zip(sent, got))]
    scatter = Scatter(s, left, right, out, rest[2 * exchanges + 3:])
    for cp in overs:
        cp.start()
    merged(scatter.tasks())
    scatter.finish()
    for cp in overs:
        cp.wait()


def scatter_dot(left, right, sent, name, number):
    shape = jax.ShapeDtypeStruct
    width = right.shape[0]
    n = len(sent)
    return communicate(
        functools.partial(scatter_kernel, n), name, number, (left, right, *sent),
        [vmem()] * 2 + [anywhere()] * n,
        [shape((left.shape[0] // 16, width), f32)] + [shape(a.shape, a.dtype) for a in sent],
        [vmem()] + [anywhere()] * n,
        [dma((max(n, 1),)), dma((max(n, 1),))] + Scatter.scratch(width),
    )


def attend_back_kernel(attended, out_all, qkv, keep, mix, local, mem_out, lse, memory, normal,
                       gate_up_half, down_half,
                       attended_all, grad, mix_grad, gate_up_rows, down_rows,
                       out_v, by_token, upstream, dk, dv, state_grad, norm_grad, copies, h_s, h_r,
                       *rest):
    sems_a, sems_g, sems_d = halves_of(rest, [7, 5, 5])
    s = Spot()
    mine = pl.ds(pl.multiple_of(s.me * 128, 128), 128)
    load = pltpu.make_async_copy(out_all, out_v, copies.at[0])
    load.start()
    own = pltpu.make_async_copy(attended, attended_all.at[mine], copies.at[1])
    own.start()
    greet(s, other=False)
    gather = Gather(s, attended, attended_all, sems_a)
    back_g = Return(s, gate_up_half, gate_up_rows, 2, sems_g)
    back_d = Return(s, down_half, down_rows, 1, sems_d)
    attend = AttendBack(qkv, keep, mix, local, mem_out, lse, memory, normal, upstream, grad,
                        mix_grad, dk, dv, state_grad, norm_grad)
    attend.clear()
    load.wait()

    def head_copy(j):
        return send(by_token.at[:, pl.ds(j * DH, DH)], upstream.at[mine], h_s.at[j], h_r.at[s.me], j)

    for j in range(4):
        w = pl.ds(j * 512, 512)
        by_token[:, w] = cols_dot(attended[...], out_v[w, :]).astype(bf16)
        for h in range(4 * j, 4 * j + 4):
            pl.when(s.me != h)(lambda: head_copy(h).start())
    upstream[mine, :] = by_token[:, pl.ds(pl.multiple_of(s.me * DH, DH), DH)]
    gather.start()
    back_g.start()
    back_d.start()

    def arrive(j):
        b = upstream.at[pl.ds(j * 128, 128)]
        pl.when(s.me != j)(lambda: send(b, b, h_s.at[j], h_r.at[j], s.me).wait_recv())

    def block(n, i):
        for j in range((n * SEG + i * ROWS) // 128, (n * SEG + (i + 1) * ROWS) // 128):
            arrive(j)
        attend.block(n, i)

    compute = [functools.partial(block, n, i) for n, i in attend.blocks()] + [attend.states]
    merged(
        gather.tasks(),
        [lambda: None] * 2 + compute,
        [lambda: None] * 10 + back_g.tasks() + back_d.tasks(),
    )
    back_g.finish()
    back_d.finish()
    for j in range(16):
        pl.when(s.me != j)(lambda: head_copy(j).wait_send())
    gather.drain()
    own.wait()


def attend_backward(attended, out_all, qkv, keep, mix, saved, gate_up_half, down_half, number):
    tokens, width = attended.shape
    total = qkv.shape[0]
    segments = total // SEG
    shape = jax.ShapeDtypeStruct
    local, mem_out, lse, memory, normal = saved
    return communicate(
        attend_back_kernel, "attend_back", number,
        (attended, out_all, qkv, keep, mix, local, mem_out, lse, memory, normal,
         gate_up_half, down_half),
        [vmem(), anywhere()] + [vmem()] * 8 + [anywhere()] * 2,
        [
            shape((total, width), bf16), shape((total, 3 * DH), bf16), shape((8, DH), f32),
            shape((64, 16 * gate_up_half.shape[2]), bf16), shape((64, 16 * down_half.shape[2]), bf16),
        ],
        [anywhere(), vmem(), vmem(), anywhere(), anywhere()],
        [
            VM(out_all.shape, bf16), VM((tokens, width), bf16), VM((total, DH), bf16),
            VM((total, DH), f32), VM((total, DH), f32), VM((segments, DH, DH), f32),
            VM((segments, 8, DH), f32), dma((2,)), dma((16,)), dma((16,)),
        ] + Gather.sems() + Return.sems(2) + Return.sems(1),
    )


def last_kernel(act, down_cols, in_half, gate_up_rows, down_rows, out_rows, gains,
                feed_out, in_mine, in_other, gate_up_other, down_other, out_other, gains_out,
                got, total, theirs, x_s, x_r, g_s, g_r, *rest):
    sems_i, scratch = rest[:5], rest[5:]
    s = Spot()
    greet(s)

    def gain_copy(k):
        to = (s.me + k) % 16
        return send(gains.at[to], got.at[s.me], g_s.at[k], g_r.at[s.me], to)

    back = Return(s, in_half, in_mine, 3, sems_i, other=in_other)
    back.start()
    for k in range(1, 16):
        gain_copy(k).start()
    pairs = [(gate_up_rows, gate_up_other), (down_rows, down_other), (out_rows, out_other)]
    overs = [send_over(a, b, x_s.at[i], x_r.at[i], s) for i, (a, b) in enumerate(pairs)]
    scatter = Scatter(s, act, down_cols, feed_out, scratch)
    for cp in overs:
        cp.start()

    def sum_gains():
        for k in range(1, 16):
            src = (s.me + 16 - k) % 16
            b = got.at[src]
            send(b, b, g_s.at[k], g_r.at[src], s.me).wait_recv()
        got[s.me] = gains[s.me]
        acc = got[0]
        for k in range(1, 16):
            acc = acc + got[k]
        total[...] = acc
        send_over(total, theirs, x_s.at[3], x_r.at[3], s).start()

    merged(scatter.tasks(), [lambda: None] * 3 + back.tasks() + [sum_gains])
    scatter.finish()
    back.finish()
    cp = send_over(total, theirs, x_s.at[3], x_r.at[3], s)
    cp.wait()
    gains_out[...] = total[...] + theirs[...]
    for cp in overs:
        cp.wait()
    for k in range(1, 16):
        gain_copy(k).wait_send()


def last(act, down_cols, in_half, gate_up_rows, down_rows, out_rows, gains, number):
    shape = jax.ShapeDtypeStruct
    total = act.shape[0]
    width = down_cols.shape[0]
    in_rows = shape((64, 16 * in_half.shape[2]), bf16)
    like = [shape(a.shape, a.dtype) for a in (gate_up_rows, down_rows, out_rows)]
    return communicate(
        last_kernel, "last", number,
        (act, down_cols, in_half, gate_up_rows, down_rows, out_rows, gains),
        [vmem()] * 2 + [anywhere()] * 4 + [vmem()],
        [shape((total // 16, width), f32), in_rows, in_rows] + like + [shape((8, 128), f32)],
        [vmem()] + [anywhere()] * 5 + [vmem()],
        [VM((16, 8, 128), f32), VM((8, 128), f32), VM((8, 128), f32),
         dma((4,)), dma((4,)), dma((16,)), dma((16,))] + Return.sems(3) + Scatter.scratch(width),
    )


def body(
    layer_input,
    first_gain,
    in_weight,
    out_weight,
    mix_gate,
    second_gain,
    gate_up,
    down_weight,
    document_starts,
    cotangent,
):
    tokens, width = layer_input.shape
    total = tokens * H
    segments = total // SEG
    dp = lax.axis_index("dp")

    own_gains = jnp.zeros((8, tokens), f32)
    own_gains = own_gains.at[0].set(first_gain.astype(f32)).at[1].set(second_gain.astype(f32))
    mix = jnp.broadcast_to(jax.nn.sigmoid(mix_gate.astype(f32))[None], (8, DH))
    numbers = jnp.arange(segments)
    fresh = (numbers == 0) | (document_starts[0] > 0)
    keep = jnp.broadcast_to(jnp.where(fresh, 0.0, 1.0)[:, None, None], (segments, 8, DH))

    normed_all, in_cols, gains_all, qkv = project(layer_input, own_gains, in_weight, 0)
    (local, mem_out, lse, combined, memory, normal, mixed_tokens, out_all, cot_all, gate_up_cols,
     down_cols) = attend_forward(qkv, keep, mix, out_weight, cotangent, gate_up, down_weight, 1)
    middle, hidden_all, act, feed_grad = feed(
        mixed_tokens, layer_input, gains_all, out_all, cot_all, gate_up_cols, down_cols, 2
    )

    def own_and_other(grad):
        split = grad.reshape(16, 2, 64, grad.shape[1])
        mine = lax.dynamic_index_in_dim(split, dp, 1, False)
        other = lax.dynamic_index_in_dim(split, 1 - dp, 1, False)
        return mine, other.astype(bf16)

    gate_up_mine, gate_up_sent = own_and_other(rows_dot(hidden_all, feed_grad))
    down_mine, down_sent = own_and_other(rows_dot(cot_all, act))
    hidden_grad, gate_up_got, down_got = scatter_dot(
        feed_grad, gate_up_cols, (gate_up_sent, down_sent), "hidden_grad", 3
    )
    gate_up_half = (gate_up_mine + gate_up_got.astype(f32)).astype(bf16)
    down_half = (down_mine + down_got.astype(f32)).astype(bf16)

    first_all = gains_all[:, 0].reshape(width)
    second_all = gains_all[:, 1].reshape(width)
    upstream = cotangent.astype(f32)
    second_factor = lax.rsqrt(jnp.mean(middle * middle, axis=-1, keepdims=True) + epsilon)
    middle_norm_grad, second_local = norm_backward(middle, second_factor, second_all, hidden_grad)
    middle_grad = upstream + middle_norm_grad
    attended_all, projected_grad, mix_grad, gate_up_rows, down_rows = attend_backward(
        middle_grad.astype(bf16), out_all, qkv, keep, mix, (local, mem_out, lse, memory, normal),
        gate_up_half, down_half, 4,
    )
    out_rows = rows_dot(combined, attended_all).astype(bf16)
    in_mine, in_sent = own_and_other(rows_dot(normed_all, projected_grad))
    normed_grad, in_got = scatter_dot(projected_grad, in_cols, (in_sent,), "normed_grad", 5)
    in_half = (in_mine + in_got.astype(f32)).astype(bf16)
    inputs = layer_input.astype(f32)
    first_factor = lax.rsqrt(jnp.mean(inputs * inputs, axis=-1, keepdims=True) + epsilon)
    input_norm_grad, first_local = norm_backward(inputs, first_factor, first_all, normed_grad)
    input_grad = middle_grad + input_norm_grad

    mix_rows = jnp.where((jnp.arange(H) == lax.axis_index(AXIS))[:, None], mix_grad[0:1], 0.0)
    gain_grads = jnp.stack(
        [first_local.reshape(16, 128), second_local.reshape(16, 128), mix_rows], axis=1
    )
    gain_grads = jnp.pad(gain_grads, ((0, 0), (0, 5), (0, 0)))
    (feed_out, in_mine_rows, in_other_rows, gate_up_other, down_other, out_other, gains_out) = last(
        act, down_cols, in_half, gate_up_rows, down_rows, out_rows, gain_grads, 6
    )
    layer_output = (middle + feed_out).astype(bf16)

    def both_halves(mine, other):
        low = jnp.where(dp == 0, mine, other)
        high = jnp.where(dp == 0, other, mine)
        return jnp.concatenate([low, high]).astype(f32)

    return (
        layer_output,
        input_grad,
        gains_out[0],
        both_halves(in_mine_rows, in_other_rows),
        out_rows.astype(f32) + out_other.astype(f32),
        gains_out[2],
        gains_out[1],
        both_halves(gate_up_rows, gate_up_other),
        both_halves(down_rows, down_other),
    )


def solution(mesh):
    one_group = mesh.shape[AXIS] == H and mesh.shape["dp"] == 2
    return jax.shard_map(
        body if one_group else body_groups,
        mesh=mesh,
        in_specs=(
            P(("dp", "fsdp"), None),
            P("fsdp"),
            P("fsdp", None),
            P("fsdp", None),
            P("fsdp"),
            P("fsdp"),
            P("fsdp", None),
            P("fsdp", None),
            P("dp", None),
            P(("dp", "fsdp"), None),
        ),
        out_specs=(
            P(("dp", "fsdp"), None),
            P(("dp", "fsdp"), None),
            P("fsdp"),
            P("fsdp", None),
            P("fsdp", None),
            P("fsdp"),
            P("fsdp"),
            P("fsdp", None),
            P("fsdp", None),
        ),
        check_vma=False,
    )
```

```python
import functools
import math

import jax
import jax.numpy as jnp
from jax import lax
from jax.experimental import pallas as pl
from jax.experimental.pallas import tpu as pltpu
from jax.sharding import PartitionSpec as P

H = 16
DH = 128
FF = 8192
SEG = 1024

highest = lax.Precision.HIGHEST
epsilon = 1e-06
f32 = jnp.float32
bf16 = jnp.bfloat16
AXIS = "fsdp"


def feature(values):
    return jax.nn.elu(values) + 1.0


def feature_slope(values):
    return jnp.where(values > 0, 1.0, jnp.exp(jnp.minimum(values, 0.0)))


def norm_forward(values, gain):
    factor = lax.rsqrt(jnp.mean(values * values, axis=-1, keepdims=True) + epsilon)
    return (values * factor * gain, factor)


def norm_backward(values, factor, gain, upstream):
    scaled = upstream * gain
    gain_grad = jnp.sum(upstream * values * factor, axis=0)
    value_grad = factor * scaled - values * (factor * factor * factor) * jnp.mean(
        scaled * values, axis=-1, keepdims=True
    )
    return (value_grad, gain_grad)


def dot(left, right, dims):
    return lax.dot_general(left, right, ((dims[0], dims[1]), ((), ())), preferred_element_type=f32)


def rows_dot(left, right):
    return dot(left, right, ((0,), (0,)))


def cols_dot(left, right):
    return dot(left, right, ((1,), (1,)))


class Layout:
    def __init__(self):
        self.count = lax.axis_size(AXIS)
        self.groups = self.count // H
        self.place = lax.axis_index(AXIS)
        self.head = self.place % H
        self.group = self.place // H
        self.inside = None
        self.across = None
        if self.groups > 1:
            self.inside = [[g * H + j for j in range(H)] for g in range(self.groups)]
            self.across = [[g * H + j for g in range(self.groups)] for j in range(H)]

    def gather(self, block):
        return lax.all_gather(block, AXIS, axis=0, tiled=True, axis_index_groups=self.inside)

    def gather_all(self, block):
        return lax.all_gather(block, AXIS, axis=0, tiled=True)

    def scatter_sum(self, whole):
        return lax.psum_scatter(
            whole, AXIS, scatter_dimension=0, tiled=True, axis_index_groups=self.inside
        )

    def columns(self, block, parts):
        rows, width = block.shape
        each = width // (parts * H)
        if self.groups == 1:
            split = block.reshape(rows, parts, H, each)
            out = lax.all_to_all(split, AXIS, 2, 0, tiled=True)
            return out.reshape(rows * self.count, parts * each)
        whole = self.gather_all(block).reshape(rows * self.count, parts, H, each)
        out = lax.dynamic_index_in_dim(whole, self.head, 2, False)
        return out.reshape(rows * self.count, parts * each)

    def own_rows(self, grad, parts):
        rows, width = grad.shape
        each = width // parts
        if self.groups == 1:
            split = grad.astype(bf16).reshape(rows, parts, 1, each)
            out = lax.all_to_all(split, AXIS, 0, 2, tiled=True)
            return out.reshape(rows // self.count, parts * H * each)
        whole = jnp.zeros((rows, parts, H, each), f32)
        whole = lax.dynamic_update_slice_in_dim(
            whole, grad.reshape(rows, parts, 1, each), self.head, 2
        )
        return lax.psum_scatter(
            whole.reshape(rows, parts * H * each), AXIS, scatter_dimension=0, tiled=True
        )

    def to_tokens(self, by_head):
        tokens, each = by_head.shape
        out = lax.all_to_all(
            by_head.reshape(H, tokens // H, each), AXIS, 0, 0, tiled=False,
            axis_index_groups=self.inside,
        )
        return out.transpose(1, 0, 2).reshape(tokens // H, H * each)

    def to_heads(self, by_token):
        tokens, width = by_token.shape
        split = by_token.reshape(tokens, H, width // H).transpose(1, 0, 2)
        out = lax.all_to_all(
            split, AXIS, 0, 0, tiled=False, axis_index_groups=self.inside
        )
        return out.reshape(H * tokens, width // H)


def carry_forward(layout, delta, count, fresh):
    segments = delta.shape[0]

    def walk(state):
        before = []
        for s in range(segments):
            state = jax.tree.map(lambda a: jnp.where(fresh[s], jnp.zeros_like(a), a), state)
            before.append(state)
            state = (state[0] + delta[s], state[1] + count[s])
        return before, state

    state = (jnp.zeros_like(delta[0]), jnp.zeros_like(count[0]))
    if layout.groups > 1:
        _, last = walk(state)
        renewed = jnp.any(fresh).astype(f32)
        every = jax.tree.map(
            lambda a: lax.all_gather(a, AXIS, axis_index_groups=layout.across), last + (renewed,)
        )
        for g in range(layout.groups - 1):
            keep = every[2][g] < 0.5
            after = jax.tree.map(lambda a, e: jnp.where(keep, a, 0.0) + e[g], state, every[:2])
            state = jax.tree.map(lambda a, b: jnp.where(g < layout.group, b, a), state, after)
    before, _ = walk(state)
    return jnp.stack([b[0] for b in before]), jnp.stack([b[1] for b in before])


def carry_backward(layout, state_grad, norm_grad, fresh):
    segments = state_grad.shape[0]

    def walk(state):
        after = [None] * segments
        for s in reversed(range(segments)):
            after[s] = state
            state = (state[0] + state_grad[s], state[1] + norm_grad[s])
            state = jax.tree.map(lambda a: jnp.where(fresh[s], jnp.zeros_like(a), a), state)
        return after, state

    state = (jnp.zeros_like(state_grad[0]), jnp.zeros_like(norm_grad[0]))
    if layout.groups > 1:
        _, first = walk(state)
        renewed = jnp.any(fresh).astype(f32)
        every = jax.tree.map(
            lambda a: lax.all_gather(a, AXIS, axis_index_groups=layout.across), first + (renewed,)
        )
        for g in reversed(range(1, layout.groups)):
            keep = every[2][g] < 0.5
            before = jax.tree.map(lambda a, e: jnp.where(keep, a, 0.0) + e[g], state, every[:2])
            state = jax.tree.map(lambda a, b: jnp.where(g > layout.group, b, a), state, before)
    after, _ = walk(state)
    return jnp.stack([a[0] for a in after]), jnp.stack([a[1] for a in after])


def body_groups(
    layer_input,
    first_gain,
    in_weight,
    out_weight,
    mix_gate,
    second_gain,
    gate_up,
    down_weight,
    document_starts,
    cotangent,
):
    layout = Layout()
    tokens, width = layer_input.shape
    group_tokens = tokens * H
    segments = group_tokens // SEG
    scale = 1.0 / math.sqrt(DH)

    gains = jnp.stack([first_gain, second_gain])
    gains = lax.all_gather(gains, AXIS, axis=1, tiled=True).astype(f32)
    first_all, second_all = gains[0], gains[1]
    if layout.groups == 1:
        mix_own = mix_gate
    else:
        mix_own = lax.dynamic_slice_in_dim(layout.gather_all(mix_gate), layout.head * DH, DH)
    mix = jax.nn.sigmoid(mix_own.astype(f32))[None]

    inputs = layer_input.astype(f32)
    normed, first_factor = norm_forward(inputs, first_all)
    normed_all = layout.gather(normed.astype(bf16))
    in_cols = layout.columns(in_weight, 3)
    out_all = layout.gather_all(out_weight)
    cot_all = layout.gather(cotangent)
    gate_up_cols = layout.columns(gate_up, 2)
    down_cols = layout.columns(down_weight, 1)

    projected = jnp.dot(normed_all, in_cols, preferred_element_type=f32).astype(bf16)
    by_segment = projected.reshape(segments, SEG, 3, DH)
    query, key, value = by_segment[:, :, 0], by_segment[:, :, 1], by_segment[:, :, 2]
    index = jnp.arange(SEG, dtype=jnp.int32)
    allowed = index[None, :] <= index[:, None]

    def attention_scores():
        raw = jnp.einsum("sqc,skc->sqk", query, key, preferred_element_type=f32) * scale
        return jnp.where(allowed[None], raw, -1e30)

    scores = attention_scores()
    top = jnp.max(scores, axis=-1, keepdims=True)
    expo = jnp.exp(scores - top)
    total = jnp.sum(expo, axis=-1, keepdims=True)
    log_total = top + jnp.log(total)
    probs_low = (expo / total).astype(bf16)
    local_out = jnp.einsum("sqk,skc->sqc", probs_low, value, preferred_element_type=f32)

    query_f, key_f, value_f = query.astype(f32), key.astype(f32), value.astype(f32)
    query_feature = feature(query_f).astype(bf16)
    key_feature = feature(key_f).astype(bf16)
    delta = jnp.einsum("slc,sla->sca", key_feature, value, preferred_element_type=f32)
    count = jnp.sum(key_feature.astype(f32), axis=1)
    numbers = layout.group * segments + jnp.arange(segments)
    fresh = (numbers == 0) | (
        lax.dynamic_slice_in_dim(document_starts[0], layout.group * segments, segments) > 0
    )
    memory, normal = carry_forward(layout, delta, count, fresh)
    query_feature_f = query_feature.astype(f32)
    numerator = jnp.einsum("sie,sej->sij", query_feature_f, memory, precision=highest)
    raw_denom = jnp.einsum("sik,sk->si", query_feature_f, normal, precision=highest)[..., None]
    denom = jnp.maximum(raw_denom, 1.0)
    memory_out = numerator / denom
    combined = mix * memory_out + (1.0 - mix) * local_out
    combined_head = combined.reshape(group_tokens, DH).astype(bf16)
    combined_low = layout.to_tokens(combined_head)
    attended = jnp.dot(combined_low, out_all, preferred_element_type=f32)
    middle = inputs + attended

    hidden, second_factor = norm_forward(middle, second_all)
    hidden_all = layout.gather(hidden.astype(bf16))
    act_grad = jnp.dot(cot_all, down_cols, preferred_element_type=f32)
    both = jnp.dot(hidden_all, gate_up_cols, preferred_element_type=f32)
    half = both.shape[1] // 2
    gate_part, up_part = both[:, :half], both[:, half:]
    sigma = jax.nn.sigmoid(gate_part)
    silu = gate_part * sigma
    activated = (silu * up_part).astype(bf16)
    silu_slope = sigma * (1.0 + gate_part * (1.0 - sigma))
    feed_grad = jnp.concatenate(
        [act_grad * up_part * silu_slope, act_grad * silu], axis=1
    ).astype(bf16)
    feed_out = layout.scatter_sum(cols_dot(activated, down_cols).astype(bf16))
    hidden_grad = layout.scatter_sum(cols_dot(feed_grad, gate_up_cols).astype(bf16))
    layer_output = (middle + feed_out.astype(f32)).astype(bf16)
    gate_up_part = layout.own_rows(rows_dot(hidden_all, feed_grad), 2)
    down_part = layout.own_rows(rows_dot(cot_all, activated), 1)

    upstream = cotangent.astype(f32)
    middle_norm_grad, second_local = norm_backward(
        middle, second_factor, second_all, hidden_grad.astype(f32)
    )
    middle_grad = upstream + middle_norm_grad
    attended_grad = middle_grad.astype(bf16)
    attended_grad_all = layout.gather(attended_grad)
    combined_grad = layout.to_heads(cols_dot(attended_grad, out_all).astype(bf16))
    combined_grad = combined_grad.astype(f32).reshape(segments, SEG, DH)
    out_rows_grad = rows_dot(combined_head, attended_grad_all)
    if layout.groups == 1:
        out_part = out_rows_grad
    else:
        whole = jnp.zeros((H * DH, width), f32)
        whole = lax.dynamic_update_slice_in_dim(whole, out_rows_grad, layout.head * DH, 0)
        out_part = lax.psum_scatter(whole, AXIS, scatter_dimension=0, tiled=True)
    mix_local = jnp.sum(combined_grad * (memory_out - local_out), axis=(0, 1)) * (
        mix * (1.0 - mix)
    ).reshape(DH)

    memory_grad = combined_grad * mix
    local_grad = (combined_grad * (1.0 - mix)).astype(bf16)
    numer_grad = memory_grad / denom
    denom_grad = -jnp.sum(memory_grad * memory_out, axis=-1, keepdims=True) / denom
    raw_grad = jnp.where(raw_denom > 1.0, denom_grad, 0.0)
    query_feature_grad = (
        jnp.einsum("sij,sej->sie", numer_grad, memory, precision=highest)
        + raw_grad * normal[:, None]
    )
    state_grad = jnp.einsum("sie,sij->sej", query_feature_f, numer_grad, precision=highest)
    norm_grad = jnp.sum(raw_grad * query_feature_f, axis=1)
    delta_grad, count_grad = carry_backward(layout, state_grad, norm_grad, fresh)
    key_feature_grad = (
        jnp.einsum("sij,sej->sie", value_f, delta_grad, precision=highest) + count_grad[:, None]
    )
    value_memory_grad = jnp.einsum(
        "sie,sej->sij", key_feature.astype(f32), delta_grad, precision=highest
    )
    query_memory_grad = query_feature_grad * feature_slope(query_f)
    key_memory_grad = key_feature_grad * feature_slope(key_f)

    probs = jnp.exp(attention_scores() - log_total)
    prob_grad = jnp.einsum("sqc,skc->sqk", local_grad, value, preferred_element_type=f32)
    row_term = jnp.sum(probs * prob_grad, axis=-1, keepdims=True)
    score_grad = (probs * (prob_grad - row_term)).astype(bf16)
    query_grad = query_memory_grad + scale * jnp.einsum(
        "sqk,skc->sqc", score_grad, key, preferred_element_type=f32
    )
    key_grad = key_memory_grad + scale * jnp.einsum(
        "sqk,sqc->skc", score_grad, query, preferred_element_type=f32
    )
    value_grad = value_memory_grad + jnp.einsum(
        "sqk,sqc->skc", probs.astype(bf16), local_grad, preferred_element_type=f32
    )
    projected_grad = (
        jnp.stack([query_grad, key_grad, value_grad], axis=2)
        .reshape(group_tokens, 3 * DH)
        .astype(bf16)
    )
    normed_grad = layout.scatter_sum(cols_dot(projected_grad, in_cols).astype(bf16))
    in_part = layout.own_rows(rows_dot(normed_all, projected_grad), 3)
    input_norm_grad, first_local = norm_backward(
        inputs, first_factor, first_all, normed_grad.astype(f32)
    )
    input_grad = middle_grad + input_norm_grad

    gains_part = lax.psum_scatter(
        jnp.stack([first_local, second_local]), AXIS, scatter_dimension=1, tiled=True
    )
    if layout.groups == 1:
        mix_part = mix_local
    else:
        whole = jnp.zeros((H * DH,), f32)
        whole = lax.dynamic_update_slice_in_dim(whole, mix_local, layout.head * DH, 0)
        mix_part = lax.psum_scatter(whole, AXIS, scatter_dimension=0, tiled=True)

    def over_sequences(part):
        return lax.psum(part.astype(bf16), "dp").astype(f32)

    small = over_sequences(jnp.concatenate([gains_part, mix_part[None]]))
    return (
        layer_output,
        input_grad,
        small[0],
        over_sequences(in_part),
        over_sequences(out_part),
        small[2],
        small[1],
        over_sequences(gate_up_part),
        over_sequences(down_part),
    )


MESH = pl.DeviceIdType.MESH
LIMIT = 60 * 2**20
CHUNKS = 4
QUARTERS = 4
ROWS = 256
dma = pltpu.SemaphoreType.DMA
VM = pltpu.VMEM


def vmem():
    return pl.BlockSpec(memory_space=pltpu.VMEM)


def anywhere():
    return pl.BlockSpec(memory_space=pl.ANY)


class Spot:
    def __init__(self):
        self.dp = lax.axis_index("dp")
        self.me = lax.axis_index(AXIS)
        self.z = self.me // 4
        self.y = (self.me // 2) % 2
        self.c = self.me % 2

    def at(self, z, y, c):
        return z * 4 + y * 2 + c

    def arrival(self, j):
        if j == 0:
            return self.z
        ends = jnp.where(self.z == 0, j, 3 - j)
        middle = {1: (0, 3), 2: (2, 1), 3: (3, 0)}[j]
        inner = jnp.where(self.z == 1, middle[0], middle[1])
        return jnp.where((self.z == 0) | (self.z == 3), ends, inner)


def greet(s, plane=True, other=True):
    ids = []
    if plane:
        ids += [{AXIS: (s.me + k) % 16} for k in range(1, 16)]
    else:
        ids += [{AXIS: s.at((s.z + k) % 4, s.y, s.c)} for k in (1, 2, 3)]
        ids += [{AXIS: s.at(s.z, 1 - s.y, s.c)}, {AXIS: s.at(s.z, s.y, 1 - s.c)}]
    if other:
        ids += [{"dp": 1 - s.dp}]
    barrier = pltpu.get_barrier_semaphore()
    for d in ids:
        pl.semaphore_signal(barrier, inc=1, device_id=d, device_id_type=MESH)
    pl.semaphore_wait(barrier, len(ids))


def send(src, dst, ssem, rsem, to):
    return pltpu.make_async_remote_copy(
        src_ref=src, dst_ref=dst, send_sem=ssem, recv_sem=rsem,
        device_id={AXIS: to}, device_id_type=MESH,
    )


def send_over(src, dst, ssem, rsem, s):
    return pltpu.make_async_remote_copy(
        src_ref=src, dst_ref=dst, send_sem=ssem, recv_sem=rsem,
        device_id={"dp": 1 - s.dp}, device_id_type=MESH,
    )


def merged(*lists):
    keyed = []
    for n, tasks in enumerate(lists):
        keyed += [((i + 0.5) / len(tasks), n, i, t) for i, t in enumerate(tasks)]
    for _, _, _, t in sorted(keyed, key=lambda e: e[:3]):
        t()


class Gather:
    chunks = 4

    @classmethod
    def sems(cls):
        return [dma((cls.chunks, 4))] * 5 + [dma((cls.chunks, 8))] * 2

    def __init__(self, s, src, dst, sems):
        self.s, self.src, self.dst = s, src, dst
        self.zr, self.zu, self.zd, self.ys, self.yr, self.ss, self.sr = sems[:7]
        self.rows = 128 // self.chunks
        self.skip = 0

    def block(self, ch, z, y, c):
        start = self.s.at(z, y, c) * 128 + self.skip + ch * self.rows
        return self.dst.at[pl.ds(pl.multiple_of(start, self.rows), self.rows)]

    def own(self, ch):
        start = pl.multiple_of(self.skip + ch * self.rows, self.rows)
        return self.src.at[pl.ds(start, self.rows)]

    def zcopy(self, ch, zo, up, own=False):
        s = self.s
        dst = self.block(ch, zo, s.y, s.c)
        to = s.at(s.z + 1 if up else s.z - 1, s.y, s.c)
        return send(
            self.own(ch) if own else dst, dst,
            (self.zu if up else self.zd).at[ch, zo], self.zr.at[ch, zo], to,
        )

    def ycopy(self, ch, zo, own=False):
        s = self.s
        dst = self.block(ch, zo, s.y, s.c)
        src = self.own(ch) if own else dst
        return send(src, dst, self.ys.at[ch, zo], self.yr.at[ch, zo], s.at(s.z, 1 - s.y, s.c))

    def scopy(self, ch, zo, yo, own=False):
        s = self.s
        dst = self.block(ch, zo, yo, s.c)
        n = zo * 2 + yo
        src = self.own(ch) if own else dst
        return send(src, dst, self.ss.at[ch, n], self.sr.at[ch, n], s.at(s.z, s.y, 1 - s.c))

    def start(self):
        s = self.s
        for ch in range(self.chunks):
            pl.when(s.z < 3)(lambda: self.zcopy(ch, s.z, True, True).start())
            pl.when(s.z > 0)(lambda: self.zcopy(ch, s.z, False, True).start())
            self.ycopy(ch, s.z, True).start()
            self.scopy(ch, s.z, s.y, True).start()

    def passed_on(self, ch, zo, yo):
        self.scopy(ch, zo, yo).start()

    def z_arrive(self, ch, j):
        s = self.s
        zo = s.arrival(j)
        self.zcopy(ch, zo, True).wait_recv()
        pl.when((zo < s.z) & (s.z < 3))(lambda: self.zcopy(ch, zo, True).start())
        pl.when((zo > s.z) & (s.z > 0))(lambda: self.zcopy(ch, zo, False).start())
        self.ycopy(ch, zo).start()
        self.passed_on(ch, zo, s.y)

    def y_arrive(self, ch, j):
        s = self.s
        zo = s.arrival(j)
        b = self.block(ch, zo, 1 - s.y, s.c)
        send(b, b, self.ys.at[ch, zo], self.yr.at[ch, zo], s.me).wait_recv()
        self.passed_on(ch, zo, 1 - s.y)

    def s_arrive(self, j):
        s = self.s
        zo = s.arrival(j)
        for ch in range(self.chunks):
            for yo in range(2):
                n = zo * 2 + yo
                b = self.block(ch, zo, yo, 1 - s.c)
                send(b, b, self.ss.at[ch, n], self.sr.at[ch, n], s.me).wait_recv()

    def tasks(self, use=None):
        out = []
        for step in range(5):
            for ch in range(self.chunks):
                if 0 < step < 4:
                    out.append(functools.partial(self.z_arrive, ch, step))
                if step > 0:
                    out.append(functools.partial(self.y_arrive, ch, step - 1))
            if step > 0:
                out.append(functools.partial(self.s_arrive, step - 1))
                if use is not None:
                    out.append(functools.partial(use, step - 1))
        return out

    def drain(self):
        s = self.s
        for ch in range(self.chunks):
            for zo in range(4):
                pl.when((s.z < 3) & (zo <= s.z))(lambda: self.zcopy(ch, zo, True).wait_send())
                pl.when((s.z > 0) & (zo >= s.z))(lambda: self.zcopy(ch, zo, False).wait_send())
                self.ycopy(ch, zo).wait_send()
                for yo in range(2):
                    self.scopy(ch, zo, yo).wait_send()


class SharedGather(Gather):
    chunks = 2

    @classmethod
    def sems(cls):
        return Gather.sems.__func__(cls) + [dma((cls.chunks, 8))] * 4

    def __init__(self, s, src, dst, sems):
        super().__init__(s, src, dst, sems)
        self.xs, self.xr, self.ts, self.tr = sems[7:]
        self.rows = 64 // self.chunks
        self.skip = s.dp * 64

    def other(self, ch, z, y, c):
        start = self.s.at(z, y, c) * 128 + (1 - self.s.dp) * 64 + ch * self.rows
        return self.dst.at[pl.ds(pl.multiple_of(start, self.rows), self.rows)]

    def xcopy(self, ch, zo, yo):
        s = self.s
        b = self.block(ch, zo, yo, s.c)
        n = zo * 2 + yo
        return send_over(b, b, self.xs.at[ch, n], self.xr.at[ch, n], s)

    def tcopy(self, ch, zo, yo, own=False):
        s = self.s
        b = self.other(ch, zo, yo, s.c)
        n = zo * 2 + yo
        src = b
        if own:
            start = pl.multiple_of((1 - s.dp) * 64 + ch * self.rows, self.rows)
            src = self.src.at[pl.ds(start, self.rows)]
        return send(src, b, self.ts.at[ch, n], self.tr.at[ch, n], s.at(s.z, s.y, 1 - s.c))

    def start(self):
        super().start()
        for ch in range(self.chunks):
            self.tcopy(ch, self.s.z, self.s.y, True).start()

    def passed_on(self, ch, zo, yo):
        self.xcopy(ch, zo, yo).start()
        self.scopy(ch, zo, yo).start()

    def x_arrive(self, j, yo):
        s = self.s
        zo = s.arrival(j)
        row = s.y if yo == 0 else 1 - s.y
        for ch in range(self.chunks):
            b = self.other(ch, zo, row, s.c)
            n = zo * 2 + row
            send_over(b, b, self.xs.at[ch, n], self.xr.at[ch, n], s).wait_recv()
            self.tcopy(ch, zo, row).start()

    def tasks(self, use=None):
        out = super().tasks(use)
        for j in range(4):
            for yo in range(2):
                if j + yo > 0:
                    out.append(functools.partial(self.x_arrive, j, yo))
        return out

    def drain(self):
        s = self.s
        super().drain()
        for ch in range(self.chunks):
            for zo in range(4):
                for yo in range(2):
                    n = zo * 2 + yo
                    b = self.other(ch, zo, yo, 1 - s.c)
                    send(b, b, self.ts.at[ch, n], self.tr.at[ch, n], s.me).wait_recv()
                    self.tcopy(ch, zo, yo).wait_send()
                    far = (s.z != zo) | (s.y != yo)
                    pl.when(far)(lambda: self.xcopy(ch, zo, yo).wait_send())


class Columns:
    @staticmethod
    def sems(parts):
        return [dma((16, parts)), dma((16, parts)), dma((16,)), dma((16,)), dma((parts,))]

    def __init__(self, s, w, dst, parts, sems):
        self.s, self.w, self.dst, self.parts = s, w, dst, parts
        self.e = dst.shape[1] // parts
        self.ps, self.pr, self.xs, self.xr, self.own = sems

    def rows(self, src, half):
        return pl.ds(pl.multiple_of(src * 128 + half * 64, 64), 64)

    def cols(self, p, h):
        return pl.ds(pl.multiple_of(p * 16 * self.e + h * self.e, 128), self.e)

    def copy(self, k, p):
        s = self.s
        to = (s.me + k) % 16
        half = pl.ds(pl.multiple_of(s.dp * 64, 64), 64)
        return send(
            self.w.at[half, self.cols(p, to)],
            self.dst.at[self.rows(s.me, s.dp), pl.ds(p * self.e, self.e)],
            self.ps.at[k, p], self.pr.at[s.me, p], to,
        )

    def local(self, p):
        s = self.s
        return pltpu.make_async_copy(
            self.w.at[:, self.cols(p, s.me)],
            self.dst.at[pl.ds(pl.multiple_of(s.me * 128, 128), 128), pl.ds(p * self.e, self.e)],
            self.own.at[p],
        )

    def start(self):
        for k in range(1, 16):
            for p in range(self.parts):
                self.copy(k, p).start()
        for p in range(self.parts):
            self.local(p).start()

    def over(self, src):
        s = self.s
        b = self.dst.at[self.rows(src, s.dp)]
        return send_over(b, b, self.xs.at[src], self.xr.at[src], s)

    def arrive(self, k):
        s = self.s
        src = (s.me + 16 - k) % 16
        for p in range(self.parts):
            b = self.dst.at[self.rows(src, s.dp), pl.ds(p * self.e, self.e)]
            send(b, b, self.ps.at[k, p], self.pr.at[src, p], s.me).wait_recv()
        self.over(src).start()

    def tasks(self):
        return [functools.partial(self.arrive, k) for k in range(1, 16)]

    def finish(self):
        s = self.s
        for k in range(1, 16):
            src = (s.me + 16 - k) % 16
            b = self.dst.at[self.rows(src, 1 - s.dp)]
            send_over(b, b, self.xs.at[src], self.xr.at[src], s).wait_recv()
        for p in range(self.parts):
            self.local(p).wait()

    def drain(self):
        s = self.s
        for k in range(1, 16):
            for p in range(self.parts):
                self.copy(k, p).wait_send()
            self.over((s.me + 16 - k) % 16).wait_send()


class Return:
    @staticmethod
    def sems(parts):
        return [dma((16, parts))] * 4 + [dma((parts,))]

    def __init__(self, s, src, dst, parts, sems, other=None):
        self.s, self.src, self.dst, self.parts, self.other = s, src, dst, parts, other
        self.e = src.shape[2] // parts
        self.ps, self.pr, self.xs, self.xr, self.own = sems

    def place(self, ref, p, h):
        return ref.at[:, pl.ds(pl.multiple_of(p * 16 * self.e + h * self.e, 128), self.e)]

    def copy(self, k, p):
        s = self.s
        to = (s.me + k) % 16
        return send(
            self.src.at[to, :, pl.ds(p * self.e, self.e)], self.place(self.dst, p, s.me),
            self.ps.at[k, p], self.pr.at[s.me, p], to,
        )

    def local(self, p):
        s = self.s
        return pltpu.make_async_copy(
            self.src.at[s.me, :, pl.ds(p * self.e, self.e)], self.place(self.dst, p, s.me),
            self.own.at[p],
        )

    def start(self):
        for p in range(self.parts):
            self.local(p).start()
        for k in range(1, 16):
            for p in range(self.parts):
                self.copy(k, p).start()
        if self.other is not None:
            for p in range(self.parts):
                self.over(self.s.me, p, own=True).start()

    def over(self, h, p, own=False):
        s = self.s
        src = self.src.at[s.me, :, pl.ds(p * self.e, self.e)] if own else self.place(self.dst, p, h)
        return send_over(src, self.place(self.other, p, h), self.xs.at[h, p], self.xr.at[h, p], s)

    def arrive(self, k):
        s = self.s
        h = (s.me + 16 - k) % 16
        for p in range(self.parts):
            b = self.place(self.dst, p, h)
            send(b, b, self.ps.at[k, p], self.pr.at[h, p], s.me).wait_recv()
            if self.other is not None:
                self.over(h, p).start()

    def tasks(self):
        return [functools.partial(self.arrive, k) for k in range(1, 16)]

    def finish(self):
        s = self.s
        for p in range(self.parts):
            self.local(p).wait()
        if self.other is not None:
            for k in range(16):
                h = (s.me + 16 - k) % 16
                for p in range(self.parts):
                    b = self.place(self.other, p, h)
                    send_over(b, b, self.xs.at[h, p], self.xr.at[h, p], s).wait_recv()
        for k in range(1, 16):
            for p in range(self.parts):
                self.copy(k, p).wait_send()
        if self.other is not None:
            for k in range(16):
                for p in range(self.parts):
                    self.over((s.me + 16 - k) % 16, p).wait_send()


class Scatter:
    lag = 3

    @staticmethod
    def scratch(width):
        q = QUARTERS
        return [
            VM((4, 2, 256, width), bf16), VM((4, 2, 128, width), bf16), VM((4, 2, 128, width), bf16),
            VM((4, 128, width), bf16), VM((5, 128, width), bf16),
            dma((4, q, 2)), dma((4, q, 2)), dma((4, q)), dma((4, q)), dma((4, q)), dma((5, q)),
        ]

    def __init__(self, s, left, right, out, scratch):
        self.s, self.left, self.right, self.out = s, left, right, out
        self.part, self.sib, self.mid, self.got_y, self.got_z = scratch[:5]
        self.ss, self.sr, self.ys, self.yr, self.zs, self.zr = scratch[5:]
        self.cols = right.shape[0] // QUARTERS
        self.order = [s.arrival(j) for j in (3, 2, 1, 0)]

    def w(self, h):
        return pl.ds(h * self.cols, self.cols)

    def compute(self, k, h, yd, slot):
        tok = pl.multiple_of((self.order[k] * 2 + yd) * 256, 256)
        p = cols_dot(self.left[pl.ds(tok, 256), :], self.right[self.w(h), :])
        self.part[k, slot, :, self.w(h)] = p.astype(bf16)

    def sib_copy(self, k, h, slot):
        s = self.s
        src = self.part.at[k, slot, pl.ds(pl.multiple_of((1 - s.c) * 128, 128), 128), self.w(h)]
        return send(
            src, self.sib.at[k, slot, :, self.w(h)],
            self.ss.at[k, h, slot], self.sr.at[k, h, slot], s.at(s.z, s.y, 1 - s.c),
        )

    def y_copy(self, k, h):
        s = self.s
        return send(
            self.mid.at[k, 0, :, self.w(h)], self.got_y.at[k, :, self.w(h)],
            self.ys.at[k, h], self.yr.at[k, h], s.at(s.z, 1 - s.y, s.c),
        )

    def z_copy(self, k, h):
        s = self.s
        to = self.order[k]
        up = to > s.z
        hop = jnp.where(up, s.z + 1, s.z - 1)
        slot = jnp.where(up | (hop != to), to, 4)
        return send(
            self.mid.at[k, 1, :, self.w(h)], self.got_z.at[slot, :, self.w(h)],
            self.zs.at[k, h], self.zr.at[slot, h], s.at(hop, s.y, s.c),
        )

    def z_wait(self, slot, h):
        b = self.got_z.at[slot, :, self.w(h)]
        send(b, b, self.zs.at[0, h], self.zr.at[slot, h], self.s.me).wait_recv()

    def fold(self, k, h, slot):
        s = self.s
        self.sib_copy(k, h, slot).wait_recv()
        own = self.part[k, slot, pl.ds(pl.multiple_of(s.c * 128, 128), 128), self.w(h)]
        total = own.astype(f32) + self.sib[k, slot, :, self.w(h)].astype(f32)
        self.mid[k, slot, :, self.w(h)] = total.astype(bf16)

    def after_y(self, k, h):
        s = self.s
        w = self.w(h)
        self.y_copy(k, h).wait_recv()
        total = self.mid[k, 1, :, w].astype(f32) + self.got_y[k, :, w].astype(f32)
        if k == 3:
            self.out[:, w] = total
            return
        to = self.order[k]
        first = jnp.where(to > s.z, s.z == 0, s.z == 3)

        @pl.when(first)
        def _():
            self.mid[k, 1, :, w] = total.astype(bf16)

        @pl.when(jnp.logical_not(first))
        def _():
            self.z_wait(to, h)
            self.mid[k, 1, :, w] = (total + self.got_z[to, :, w].astype(f32)).astype(bf16)

        self.z_copy(k, h).start()

    def tasks(self):
        steps = [(k, h) for k in range(4) for h in range(QUARTERS)]
        s = self.s

        def step(i):
            k, h = steps[i]
            self.compute(k, h, 1 - s.y, 0)
            self.sib_copy(k, h, 0).start()
            self.compute(k, h, s.y, 1)
            self.sib_copy(k, h, 1).start()
            self.fold(k, h, 0)
            self.y_copy(k, h).start()
            self.fold(k, h, 1)

        out = []
        for i in range(len(steps) + self.lag):
            if i < len(steps):
                out.append(functools.partial(step, i))
            if i >= self.lag:
                out.append(functools.partial(self.after_y, *steps[i - self.lag]))
        return out

    def finish(self):
        s = self.s
        for h in range(QUARTERS):
            w = self.w(h)

            @pl.when(s.z > 0)
            def _():
                self.z_wait(s.z, h)
                self.out[:, w] += self.got_z[s.z, :, w].astype(f32)

            @pl.when(s.z < 3)
            def _():
                self.z_wait(4, h)
                self.out[:, w] += self.got_z[4, :, w].astype(f32)

        for k in range(4):
            for h in range(QUARTERS):
                self.sib_copy(k, h, 0).wait_send()
                self.sib_copy(k, h, 1).wait_send()
                self.y_copy(k, h).wait_send()
                if k < 3:
                    self.z_copy(k, h).wait_send()


class Weigh:
    steps = 8

    @classmethod
    def scratch(cls, cols):
        return [
            VM((16, 64, cols), f32), VM((16, 64, cols), bf16), VM((16, 64, cols), bf16),
            dma((cls.steps,)), dma((cls.steps,)),
        ]

    def __init__(self, s, left, right, half, scratch):
        self.s, self.left, self.right, self.half = s, left, right, half
        self.mine, self.sent, self.got, self.xs, self.xr = scratch

    def copy(self, i):
        w = pl.ds(2 * i, 2)
        return send_over(self.sent.at[w], self.got.at[w], self.xs.at[i], self.xr.at[i], self.s)

    def compute(self, i):
        low = self.s.dp == 0
        got = rows_dot(self.left[:, pl.ds(i * 256, 256)], self.right[...])
        for n in range(2):
            a, b = got[n * 128:n * 128 + 64], got[n * 128 + 64:n * 128 + 128]
            self.mine[2 * i + n] = jnp.where(low, a, b)
            self.sent[2 * i + n] = jnp.where(low, b, a).astype(bf16)
        self.copy(i).start()

    def fold(self, i):
        self.copy(i).wait_recv()
        w = pl.ds(2 * i, 2)
        self.half[w] = (self.mine[w] + self.got[w].astype(f32)).astype(bf16)

    def products(self):
        return [functools.partial(self.compute, i) for i in range(self.steps)]

    def folds(self):
        return [functools.partial(self.fold, i) for i in range(self.steps)]

    def drain(self):
        for i in range(self.steps):
            self.copy(i).wait_send()


def nothing(n):
    return [lambda: None] * n


def halves_of(refs, counts):
    out, at = [], 0
    for n in counts:
        out.append(refs[at:at + n])
        at += n
    return out


def communicate(kernel, name, number, ins, in_specs, outs, out_specs, scratch, flops=0):
    return pl.pallas_call(
        kernel, out_shape=outs, in_specs=in_specs, out_specs=out_specs, scratch_shapes=scratch,
        compiler_params=pltpu.CompilerParams(
            collective_id=number, has_side_effects=True, vmem_limit_bytes=LIMIT
        ),
        cost_estimate=pl.CostEstimate(flops=flops, bytes_accessed=2**24, transcendentals=0),
        name=name,
    )(*ins)


def project_kernel(x, gains, in_w, normed_all, in_cols, gains_all, projected, normed, *rest):
    g_s, g_r = rest[:2]
    gather_sems, col_sems = halves_of(rest[2:], [7, 5])
    s = Spot()
    greet(s)

    def gain_copy(k):
        return send(gains, gains_all.at[s.me], g_s.at[k], g_r.at[s.me], (s.me + k) % 16)

    for k in range(1, 16):
        gain_copy(k).start()
    columns = Columns(s, in_w, in_cols, 3, col_sems)
    columns.start()
    gains_all[s.me] = gains[...]
    values = x[...].astype(f32)
    factor = lax.rsqrt(jnp.mean(values * values, axis=-1, keepdims=True) + epsilon)
    for k in range(1, 16):
        src = (s.me + 16 - k) % 16
        b = gains_all.at[src]
        send(b, b, g_s.at[k], g_r.at[src], s.me).wait_recv()
    mine = pl.ds(pl.multiple_of(s.me * 128, 128), 128)
    for j in range(16):
        w = pl.ds(j * 128, 128)
        part = (x[:, w].astype(f32) * factor * gains_all[j, 0:1, :]).astype(bf16)
        normed[:, w] = part
        normed_all[mine, w] = part
    gather = Gather(s, normed, normed_all, gather_sems)
    gather.start()

    def use(j):
        if j == 1:
            columns.finish()
        for i in {0: (), 1: (0, 1), 2: (2,), 3: (3,)}[j]:
            tok = pl.ds(pl.multiple_of(s.arrival(i) * 512, 512), 512)
            out = jnp.dot(normed_all[tok, :], in_cols[...], preferred_element_type=f32)
            projected[tok, :] = out.astype(bf16)

    merged(gather.tasks(use), nothing(2) + columns.tasks() + nothing(22))
    gather.drain()
    columns.drain()
    for k in range(1, 16):
        gain_copy(k).wait_send()


def project(x, gains, in_weight, number):
    tokens, width = x.shape
    return communicate(
        project_kernel, "project", number, (x, gains, in_weight), [vmem(), vmem(), anywhere()],
        [
            jax.ShapeDtypeStruct((16 * tokens, width), bf16),
            jax.ShapeDtypeStruct((width, 3 * DH), bf16),
            jax.ShapeDtypeStruct((16, 8, 128), f32),
            jax.ShapeDtypeStruct((16 * tokens, 3 * DH), bf16),
        ],
        [vmem()] * 4,
        [VM((tokens, width), bf16), dma((16,)), dma((16,))] + Gather.sems() + Columns.sems(3),
    )


def kernel_feature(t):
    return jnp.where(t > 0, t + 1.0, jnp.exp(jnp.minimum(t, 0.0)))


def dot_high(left, right, dims=((1,), (0,))):
    return lax.dot_general(
        left, right, (dims, ((), ())), preferred_element_type=f32, precision=highest
    )


def scores_of(query, keys, first):
    raw = cols_dot(query, keys) * (1.0 / math.sqrt(DH))
    row = lax.broadcasted_iota(jnp.int32, raw.shape, 0) + first
    col = lax.broadcasted_iota(jnp.int32, raw.shape, 1)
    return jnp.where(col <= row, raw, -1e30)


class Attend:
    def __init__(self, qkv, keep, mix, local, mem_out, lse, combined, memory, normal):
        self.qkv, self.keep, self.mix = qkv, keep, mix
        self.local, self.mem_out, self.lse, self.combined = local, mem_out, lse, combined
        self.memory, self.normal = memory, normal
        self.segments = qkv.shape[0] // SEG

    def states(self):
        state = jnp.zeros((DH, DH), f32)
        norm = jnp.zeros((1, DH), f32)
        for n in range(self.segments):
            keep = self.keep[n, 0:1, :]
            state, norm = state * keep, norm * keep
            self.memory[n] = state
            self.normal[n, 0:1, :] = norm
            if n + 1 < self.segments:
                rows = pl.ds(n * SEG, SEG)
                fk = kernel_feature(self.qkv[rows, DH:2 * DH].astype(f32)).astype(bf16)
                state = state + rows_dot(fk, self.qkv[rows, 2 * DH:])
                norm = norm + jnp.sum(fk.astype(f32), axis=0, keepdims=True)

    def block(self, n, i):
        rows = pl.ds(n * SEG + i * ROWS, ROWS)
        seen = pl.ds(n * SEG, (i + 1) * ROWS)
        query = self.qkv[rows, :DH]
        scores = scores_of(query, self.qkv[seen, DH:2 * DH], i * ROWS)
        top = jnp.max(scores, axis=-1, keepdims=True)
        expo = jnp.exp(scores - top)
        total = jnp.sum(expo, axis=-1, keepdims=True)
        probs = (expo * (1.0 / total)).astype(bf16)
        local = jnp.dot(probs, self.qkv[seen, 2 * DH:], preferred_element_type=f32)
        fq = kernel_feature(query.astype(f32)).astype(bf16).astype(f32)
        den = jnp.maximum(jnp.sum(fq * self.normal[n, 0:1, :], axis=-1, keepdims=True), 1.0)
        mem_out = dot_high(fq, self.memory[n]) / den
        mix = self.mix[0:1, :]
        self.local[rows, :] = local
        self.mem_out[rows, :] = mem_out
        self.lse[rows, :] = jnp.broadcast_to(top + jnp.log(total), (ROWS, DH))
        self.combined[rows, :] = (mix * mem_out + (1.0 - mix) * local).astype(bf16)

    def blocks(self):
        return [(n, i) for n in range(self.segments) for i in range(SEG // ROWS)]


class AttendBack:
    def __init__(self, qkv, keep, mix, local, mem_out, lse, memory, normal, upstream, grad,
                 mix_grad, dk, dv, state_grad, norm_grad):
        self.qkv, self.keep, self.mix = qkv, keep, mix
        self.local, self.mem_out, self.lse = local, mem_out, lse
        self.memory, self.normal, self.upstream, self.grad = memory, normal, upstream, grad
        self.mix_grad, self.dk, self.dv = mix_grad, dk, dv
        self.state_grad, self.norm_grad = state_grad, norm_grad
        self.segments = qkv.shape[0] // SEG

    def clear(self):
        self.mix_grad[...] = jnp.zeros_like(self.mix_grad)
        self.dk[...] = jnp.zeros_like(self.dk)
        self.dv[...] = jnp.zeros_like(self.dv)
        self.state_grad[...] = jnp.zeros_like(self.state_grad)
        self.norm_grad[...] = jnp.zeros_like(self.norm_grad)

    def block(self, n, i):
        scale = 1.0 / math.sqrt(DH)
        rows = pl.ds(n * SEG + i * ROWS, ROWS)
        seen = pl.ds(n * SEG, (i + 1) * ROWS)
        query = self.qkv[rows, :DH]
        keys = self.qkv[seen, DH:2 * DH]
        values = self.qkv[seen, 2 * DH:]
        up = self.upstream[rows, :].astype(f32)
        mem_out = self.mem_out[rows, :]
        mix = self.mix[0:1, :]
        mixed = jnp.sum(up * (mem_out - self.local[rows, :]), axis=0, keepdims=True)
        self.mix_grad[0:1, :] += mixed * mix * (1.0 - mix)
        memory_grad = up * mix
        local_grad = (up * (1.0 - mix)).astype(bf16)
        query_f = query.astype(f32)
        fq = kernel_feature(query_f).astype(bf16).astype(f32)
        normal = self.normal[n, 0:1, :]
        raw = jnp.sum(fq * normal, axis=-1, keepdims=True)
        den = jnp.maximum(raw, 1.0)
        numer_grad = memory_grad / den
        den_grad = -jnp.sum(memory_grad * mem_out, axis=-1, keepdims=True) / den
        raw_grad = jnp.where(raw > 1.0, den_grad, 0.0)
        fq_grad = dot_high(numer_grad, self.memory[n], ((1,), (1,))) + raw_grad * normal
        if n > 0:
            self.state_grad[n] += dot_high(fq, numer_grad, ((0,), (0,)))
            self.norm_grad[n, 0:1, :] += jnp.sum(raw_grad * fq, axis=0, keepdims=True)
        scores = scores_of(query, keys, i * ROWS)
        probs = jnp.exp(scores - self.lse[rows, 0:1])
        prob_grad = cols_dot(local_grad, values)
        row_term = jnp.sum(probs * prob_grad, axis=-1, keepdims=True)
        score_grad = (probs * (prob_grad - row_term)).astype(bf16)
        query_grad = jnp.dot(score_grad, keys, preferred_element_type=f32) * scale
        query_grad = query_grad + fq_grad * feature_slope(query_f)
        self.grad[rows, :DH] = query_grad.astype(bf16)
        self.dk[seen, :] += rows_dot(score_grad, query) * scale
        self.dv[seen, :] += rows_dot(probs.astype(bf16), local_grad)

    def states(self):
        state = jnp.zeros((DH, DH), f32)
        norm = jnp.zeros((1, DH), f32)
        for n in reversed(range(self.segments)):
            rows = pl.ds(n * SEG, SEG)
            key = self.qkv[rows, DH:2 * DH].astype(f32)
            key_grad = self.dk[rows, :]
            value_grad = self.dv[rows, :]
            if n + 1 < self.segments:
                fk = kernel_feature(key).astype(bf16).astype(f32)
                value = self.qkv[rows, 2 * DH:].astype(f32)
                fk_grad = dot_high(value, state, ((1,), (1,))) + norm
                key_grad = key_grad + fk_grad * feature_slope(key)
                value_grad = value_grad + dot_high(fk, state)
            self.grad[rows, DH:2 * DH] = key_grad.astype(bf16)
            self.grad[rows, 2 * DH:] = value_grad.astype(bf16)
            if n > 0:
                keep = self.keep[n, 0:1, :]
                state = (state + self.state_grad[n]) * keep
                norm = (norm + self.norm_grad[n, 0:1, :]) * keep

    def blocks(self):
        return [(n, i) for n in range(self.segments) for i in range(SEG // ROWS)]


def attend_kernel(qkv, keep, mix, out_w, cot, gate_up, down,
                  local, mem_out, lse, combined, memory, normal, mixed_tokens, out_all, cot_all,
                  gate_up_cols, down_cols, copies, t_s, t_r, *rest):
    sems_o, sems_c, sems_g, sems_d = halves_of(rest, [11, 7, 5, 5])
    s = Spot()
    mine = pl.ds(pl.multiple_of(s.me * 128, 128), 128)
    own = [
        pltpu.make_async_copy(out_w, out_all.at[mine], copies.at[0]),
        pltpu.make_async_copy(cot, cot_all.at[mine], copies.at[1]),
    ]
    for cp in own:
        cp.start()
    greet(s)
    gather_o = SharedGather(s, out_w, out_all, sems_o)
    gather_c = Gather(s, cot, cot_all, sems_c)
    columns_g = Columns(s, gate_up, gate_up_cols, 2, sems_g)
    columns_d = Columns(s, down, down_cols, 1, sems_d)
    gather_o.start()
    gather_c.start()
    columns_g.start()
    columns_d.start()
    attend = Attend(qkv, keep, mix, local, mem_out, lse, combined, memory, normal)

    def token_copy(j):
        return send(
            combined.at[pl.ds(j * 128, 128)],
            mixed_tokens.at[:, pl.ds(pl.multiple_of(s.me * DH, DH), DH)],
            t_s.at[j], t_r.at[s.me], j,
        )

    def block(n, i):
        attend.block(n, i)
        for j in range((n * SEG + i * ROWS) // 128, (n * SEG + (i + 1) * ROWS) // 128):
            pl.when(s.me != j)(lambda: token_copy(j).start())

    compute = [attend.states] + [functools.partial(block, n, i) for n, i in attend.blocks()]
    merged(
        gather_o.tasks() + nothing(4),
        gather_c.tasks(),
        compute + nothing(len(compute)),
        nothing(2) + columns_g.tasks() + columns_d.tasks(),
    )
    mixed_tokens[:, pl.ds(pl.multiple_of(s.me * DH, DH), DH)] = combined[mine, :]
    columns_g.finish()
    columns_d.finish()
    for k in range(1, 16):
        src = (s.me + 16 - k) % 16
        b = mixed_tokens.at[:, pl.ds(pl.multiple_of(src * DH, DH), DH)]
        send(b, b, t_s.at[0], t_r.at[src], s.me).wait_recv()
    for j in range(16):
        pl.when(s.me != j)(lambda: token_copy(j).wait_send())
    gather_o.drain()
    gather_c.drain()
    columns_g.drain()
    columns_d.drain()
    for cp in own:
        cp.wait()


def attend_forward(qkv, keep, mix, out_weight, cotangent, gate_up, down, number):
    tokens, width = cotangent.shape
    total = qkv.shape[0]
    segments = total // SEG
    shape = jax.ShapeDtypeStruct
    return communicate(
        attend_kernel, "attend", number, (qkv, keep, mix, out_weight, cotangent, gate_up, down),
        [vmem()] * 3 + [anywhere()] * 4,
        [
            shape((total, DH), f32), shape((total, DH), f32), shape((total, DH), f32),
            shape((total, DH), bf16), shape((segments, DH, DH), f32), shape((segments, 8, DH), f32),
            shape((tokens, width), bf16),
            shape((total, width), bf16), shape((total, width), bf16),
            shape((width, gate_up.shape[1] // 16), bf16), shape((width, down.shape[1] // 16), bf16),
        ],
        [vmem()] * 7 + [anywhere()] * 4,
        [dma((2,)), dma((16,)), dma((16,))] + SharedGather.sems() + Gather.sems() + Columns.sems(2) + Columns.sems(1),
    )


def feed_kernel(combined, x, gains_all, out_all, cot_all, gate_up_cols, down_cols,
                middle, hidden_all, act, feed_grad, out_v, cot_v, gate_up_v, down_v, hidden, copies,
                *sems):
    s = Spot()
    loads = [
        pltpu.make_async_copy(a, b, copies.at[i])
        for i, (a, b) in enumerate(
            [(out_all, out_v), (gate_up_cols, gate_up_v), (cot_all, cot_v), (down_cols, down_v)]
        )
    ]
    for cp in loads:
        cp.start()
    greet(s, plane=False, other=False)
    loads[0].wait()
    width = x.shape[1]
    squares = jnp.zeros((x.shape[0], 1), f32)
    for j in range(4):
        w = pl.ds(j * 512, 512)
        got = jnp.dot(combined[...], out_v[:, w], preferred_element_type=f32)
        got = got + x[:, w].astype(f32)
        middle[:, w] = got
        squares = squares + jnp.sum(got * got, axis=-1, keepdims=True)
    factor = lax.rsqrt(squares * (1.0 / width) + epsilon)
    mine = pl.ds(pl.multiple_of(s.me * 128, 128), 128)
    for j in range(16):
        w = pl.ds(j * 128, 128)
        part = (middle[:, w] * factor * gains_all[j, 1:2, :]).astype(bf16)
        hidden[:, w] = part
        hidden_all[mine, w] = part
    gather = Gather(s, hidden, hidden_all, sems)
    gather.start()
    half = act.shape[1]

    def use(j):
        if j == 0:
            for cp in loads[1:]:
                cp.wait()
        tok = pl.ds(pl.multiple_of(s.arrival(j) * 512, 512), 512)
        act_grad = jnp.dot(cot_v[tok, :], down_v[...], preferred_element_type=f32)
        gate = jnp.dot(hidden_all[tok, :], gate_up_v[:, :half], preferred_element_type=f32)
        up = jnp.dot(hidden_all[tok, :], gate_up_v[:, half:], preferred_element_type=f32)
        sigma = jax.nn.sigmoid(gate)
        silu = gate * sigma
        act[tok, :] = (silu * up).astype(bf16)
        slope = sigma * (1.0 + gate * (1.0 - sigma))
        feed_grad[tok, :half] = (act_grad * up * slope).astype(bf16)
        feed_grad[tok, half:] = (act_grad * silu).astype(bf16)

    merged(gather.tasks(use))
    gather.drain()


def feed(combined, x, gains_all, out_all, cot_all, gate_up_cols, down_cols, number):
    tokens, width = x.shape
    total = cot_all.shape[0]
    half = down_cols.shape[1]
    shape = jax.ShapeDtypeStruct
    return communicate(
        feed_kernel, "feed", number,
        (combined, x, gains_all, out_all, cot_all, gate_up_cols, down_cols),
        [vmem()] * 3 + [anywhere()] * 4,
        [
            shape((tokens, width), f32), shape((total, width), bf16),
            shape((total, half), bf16), shape((total, 2 * half), bf16),
        ],
        [vmem()] * 4,
        [
            VM(out_all.shape, bf16), VM(cot_all.shape, bf16), VM(gate_up_cols.shape, bf16),
            VM(down_cols.shape, bf16), VM((tokens, width), bf16), dma((4,)),
        ] + Gather.sems(),
    )


def hidden_grad_kernel(feed_grad, gate_up_cols, hidden_all, out, half, *rest):
    s = Spot()
    greet(s, plane=False)
    weigh = Weigh(s, hidden_all, feed_grad, half, rest[:5])
    scatter = Scatter(s, feed_grad, gate_up_cols, out, rest[5:])
    products = weigh.products()
    merged(
        scatter.tasks(),
        products + nothing(16),
        nothing(20) + weigh.folds(),
    )
    scatter.finish()
    weigh.drain()


def hidden_grad_of(feed_grad, gate_up_cols, hidden_all, number):
    shape = jax.ShapeDtypeStruct
    total, cols = feed_grad.shape
    width = gate_up_cols.shape[0]
    return communicate(
        hidden_grad_kernel, "hidden_grad", number, (feed_grad, gate_up_cols, hidden_all),
        [vmem()] * 3, [shape((total // 16, width), f32), shape((16, 64, cols), bf16)], [vmem()] * 2,
        Weigh.scratch(cols) + Scatter.scratch(width),
    )


def normed_grad_kernel(grad, in_cols, normed_all, down_half, gate_up_rows,
                       out, half, down_rows, gate_up_other, x_s, x_r, *rest):
    sems_d, sems_w, scratch = halves_of(rest, [5, 5, 11])
    s = Spot()
    greet(s)
    weigh = Weigh(s, normed_all, grad, half, sems_w)
    back = Return(s, down_half, down_rows, 1, sems_d)
    scatter = Scatter(s, grad, in_cols, out, scratch)
    over = send_over(gate_up_rows, gate_up_other, x_s.at[0], x_r.at[0], s)
    back.start()
    merged(
        scatter.tasks(),
        weigh.products() + [over.start] + nothing(20),
        nothing(20) + weigh.folds(),
    )
    scatter.finish()
    for task in back.tasks():
        task()
    back.finish()
    weigh.drain()
    over.wait()


def normed_grad_of(grad, in_cols, normed_all, down_half, gate_up_rows, number):
    shape = jax.ShapeDtypeStruct
    total, cols = grad.shape
    width = in_cols.shape[0]
    return communicate(
        normed_grad_kernel, "normed_grad", number,
        (grad, in_cols, normed_all, down_half, gate_up_rows), [vmem()] * 3 + [anywhere()] * 2,
        [
            shape((total // 16, width), f32), shape((16, 64, cols), bf16),
            shape((64, 16 * down_half.shape[2]), bf16), shape(gate_up_rows.shape, bf16),
        ],
        [vmem()] * 2 + [anywhere()] * 2,
        [dma((1,)), dma((1,))] + Return.sems(1) + Weigh.scratch(cols) + Scatter.scratch(width),
    )


def attend_back_kernel(attended, out_all, qkv, keep, mix, local, mem_out, lse, memory, normal,
                       gate_up_half, cot_all, act,
                       attended_all, grad, mix_grad, gate_up_rows, down_half,
                       out_v, cot_v, by_token, upstream, dk, dv, state_grad, norm_grad, copies, h_s, h_r,
                       *rest):
    sems_a, sems_g, sems_w = halves_of(rest, [7, 5, 5])
    s = Spot()
    mine = pl.ds(pl.multiple_of(s.me * 128, 128), 128)
    cot_load = pltpu.make_async_copy(cot_all, cot_v, copies.at[2])
    load = pltpu.make_async_copy(out_all, out_v, copies.at[0])
    load.start()
    own = pltpu.make_async_copy(attended, attended_all.at[mine], copies.at[1])
    own.start()
    cot_load.start()
    greet(s)
    gather = Gather(s, attended, attended_all, sems_a)
    back_g = Return(s, gate_up_half, gate_up_rows, 2, sems_g)
    weigh = Weigh(s, cot_v, act, down_half, sems_w)
    attend = AttendBack(qkv, keep, mix, local, mem_out, lse, memory, normal, upstream, grad,
                        mix_grad, dk, dv, state_grad, norm_grad)
    attend.clear()
    load.wait()

    def head_copy(j):
        return send(by_token.at[:, pl.ds(j * DH, DH)], upstream.at[mine], h_s.at[j], h_r.at[s.me], j)

    for j in range(4):
        w = pl.ds(j * 512, 512)
        by_token[:, w] = cols_dot(attended[...], out_v[w, :]).astype(bf16)
        for h in range(4 * j, 4 * j + 4):
            pl.when(s.me != h)(lambda: head_copy(h).start())
    upstream[mine, :] = by_token[:, pl.ds(pl.multiple_of(s.me * DH, DH), DH)]
    gather.start()
    back_g.start()
    cot_load.wait()

    def arrive(j):
        b = upstream.at[pl.ds(j * 128, 128)]
        pl.when(s.me != j)(lambda: send(b, b, h_s.at[j], h_r.at[j], s.me).wait_recv())

    def block(n, i):
        for j in range((n * SEG + i * ROWS) // 128, (n * SEG + (i + 1) * ROWS) // 128):
            arrive(j)
        attend.block(n, i)

    compute = [functools.partial(block, n, i) for n, i in attend.blocks()] + [attend.states]
    merged(
        gather.tasks(),
        nothing(2) + compute,
        weigh.products() + weigh.folds(),
        nothing(10) + back_g.tasks(),
    )
    back_g.finish()
    weigh.drain()
    for j in range(16):
        pl.when(s.me != j)(lambda: head_copy(j).wait_send())
    gather.drain()
    own.wait()


def attend_backward(attended, out_all, qkv, keep, mix, saved, gate_up_half, cot_all, act, number):
    tokens, width = attended.shape
    total = qkv.shape[0]
    segments = total // SEG
    shape = jax.ShapeDtypeStruct
    local, mem_out, lse, memory, normal = saved
    return communicate(
        attend_back_kernel, "attend_back", number,
        (attended, out_all, qkv, keep, mix, local, mem_out, lse, memory, normal,
         gate_up_half, cot_all, act),
        [vmem(), anywhere()] + [vmem()] * 8 + [anywhere()] * 2 + [vmem()],
        [
            shape((total, width), bf16), shape((total, 3 * DH), bf16), shape((8, DH), f32),
            shape((64, 16 * gate_up_half.shape[2]), bf16), shape((16, 64, act.shape[1]), bf16),
        ],
        [anywhere(), vmem(), vmem(), anywhere(), vmem()],
        [
            VM(out_all.shape, bf16), VM(cot_all.shape, bf16), VM((tokens, width), bf16),
            VM((total, DH), bf16),
            VM((total, DH), f32), VM((total, DH), f32), VM((segments, DH, DH), f32),
            VM((segments, 8, DH), f32), dma((3,)), dma((16,)), dma((16,)),
        ] + Gather.sems() + Return.sems(2) + Weigh.scratch(act.shape[1]),
    )


def last_kernel(act, down_cols, in_half, down_rows, out_rows, gains,
                feed_out, in_mine, in_other, down_other, out_other, gains_out,
                got, total, theirs, x_s, x_r, g_s, g_r, *rest):
    sems_i, scratch = rest[:5], rest[5:]
    s = Spot()
    greet(s)

    def gain_copy(k):
        to = (s.me + k) % 16
        return send(gains.at[to], got.at[s.me], g_s.at[k], g_r.at[s.me], to)

    back = Return(s, in_half, in_mine, 3, sems_i, other=in_other)
    back.start()
    for k in range(1, 16):
        gain_copy(k).start()
    pairs = [(down_rows, down_other), (out_rows, out_other)]
    overs = [send_over(a, b, x_s.at[i], x_r.at[i], s) for i, (a, b) in enumerate(pairs)]
    scatter = Scatter(s, act, down_cols, feed_out, scratch)
    for cp in overs:
        cp.start()

    def sum_gains():
        for k in range(1, 16):
            src = (s.me + 16 - k) % 16
            b = got.at[src]
            send(b, b, g_s.at[k], g_r.at[src], s.me).wait_recv()
        got[s.me] = gains[s.me]
        acc = got[0]
        for k in range(1, 16):
            acc = acc + got[k]
        total[...] = acc
        send_over(total, theirs, x_s.at[3], x_r.at[3], s).start()

    merged(scatter.tasks(), [lambda: None] * 3 + back.tasks() + [sum_gains])
    scatter.finish()
    back.finish()
    cp = send_over(total, theirs, x_s.at[3], x_r.at[3], s)
    cp.wait()
    gains_out[...] = total[...] + theirs[...]
    for cp in overs:
        cp.wait()
    for k in range(1, 16):
        gain_copy(k).wait_send()


def last(act, down_cols, in_half, down_rows, out_rows, gains, number):
    shape = jax.ShapeDtypeStruct
    total = act.shape[0]
    width = down_cols.shape[0]
    in_rows = shape((64, 16 * in_half.shape[2]), bf16)
    like = [shape(a.shape, a.dtype) for a in (down_rows, out_rows)]
    return communicate(
        last_kernel, "last", number,
        (act, down_cols, in_half, down_rows, out_rows, gains),
        [vmem()] * 2 + [anywhere()] * 3 + [vmem()],
        [shape((total // 16, width), f32), in_rows, in_rows] + like + [shape((8, 128), f32)],
        [vmem()] + [anywhere()] * 4 + [vmem()],
        [VM((16, 8, 128), f32), VM((8, 128), f32), VM((8, 128), f32),
         dma((4,)), dma((4,)), dma((16,)), dma((16,))] + Return.sems(3) + Scatter.scratch(width),
    )


def body(
    layer_input,
    first_gain,
    in_weight,
    out_weight,
    mix_gate,
    second_gain,
    gate_up,
    down_weight,
    document_starts,
    cotangent,
):
    tokens, width = layer_input.shape
    total = tokens * H
    segments = total // SEG
    dp = lax.axis_index("dp")

    own_gains = jnp.zeros((8, tokens), f32)
    own_gains = own_gains.at[0].set(first_gain.astype(f32)).at[1].set(second_gain.astype(f32))
    mix = jnp.broadcast_to(jax.nn.sigmoid(mix_gate.astype(f32))[None], (8, DH))
    numbers = jnp.arange(segments)
    fresh = (numbers == 0) | (document_starts[0] > 0)
    keep = jnp.broadcast_to(jnp.where(fresh, 0.0, 1.0)[:, None, None], (segments, 8, DH))

    normed_all, in_cols, gains_all, qkv = project(layer_input, own_gains, in_weight, 0)
    (local, mem_out, lse, combined, memory, normal, mixed_tokens, out_all, cot_all, gate_up_cols,
     down_cols) = attend_forward(qkv, keep, mix, out_weight, cotangent, gate_up, down_weight, 1)
    middle, hidden_all, act, feed_grad = feed(
        mixed_tokens, layer_input, gains_all, out_all, cot_all, gate_up_cols, down_cols, 2
    )

    hidden_grad, gate_up_half = hidden_grad_of(feed_grad, gate_up_cols, hidden_all, 3)

    first_all = gains_all[:, 0].reshape(width)
    second_all = gains_all[:, 1].reshape(width)
    upstream = cotangent.astype(f32)
    second_factor = lax.rsqrt(jnp.mean(middle * middle, axis=-1, keepdims=True) + epsilon)
    middle_norm_grad, second_local = norm_backward(middle, second_factor, second_all, hidden_grad)
    middle_grad = upstream + middle_norm_grad
    attended_all, projected_grad, mix_grad, gate_up_rows, down_half = attend_backward(
        middle_grad.astype(bf16), out_all, qkv, keep, mix, (local, mem_out, lse, memory, normal),
        gate_up_half, cot_all, act, 4,
    )
    out_rows = rows_dot(combined, attended_all).astype(bf16)
    normed_grad, in_half, down_rows, gate_up_other = normed_grad_of(
        projected_grad, in_cols, normed_all, down_half, gate_up_rows, 5
    )
    inputs = layer_input.astype(f32)
    first_factor = lax.rsqrt(jnp.mean(inputs * inputs, axis=-1, keepdims=True) + epsilon)
    input_norm_grad, first_local = norm_backward(inputs, first_factor, first_all, normed_grad)
    input_grad = middle_grad + input_norm_grad

    mix_rows = jnp.where((jnp.arange(H) == lax.axis_index(AXIS))[:, None], mix_grad[0:1], 0.0)
    gain_grads = jnp.stack(
        [first_local.reshape(16, 128), second_local.reshape(16, 128), mix_rows], axis=1
    )
    gain_grads = jnp.pad(gain_grads, ((0, 0), (0, 5), (0, 0)))
    feed_out, in_mine_rows, in_other_rows, down_other, out_other, gains_out = last(
        act, down_cols, in_half, down_rows, out_rows, gain_grads, 6
    )
    layer_output = (middle + feed_out).astype(bf16)

    def both_halves(mine, other):
        low = jnp.where(dp == 0, mine, other)
        high = jnp.where(dp == 0, other, mine)
        return jnp.concatenate([low, high]).astype(f32)

    return (
        layer_output,
        input_grad,
        gains_out[0],
        both_halves(in_mine_rows, in_other_rows),
        out_rows.astype(f32) + out_other.astype(f32),
        gains_out[2],
        gains_out[1],
        both_halves(gate_up_rows, gate_up_other),
        both_halves(down_rows, down_other),
    )


def solution(mesh):
    one_group = mesh.shape[AXIS] == H and mesh.shape["dp"] == 2
    return jax.shard_map(
        body if one_group else body_groups,
        mesh=mesh,
        in_specs=(
            P(("dp", "fsdp"), None),
            P("fsdp"),
            P("fsdp", None),
            P("fsdp", None),
            P("fsdp"),
            P("fsdp"),
            P("fsdp", None),
            P("fsdp", None),
            P("dp", None),
            P(("dp", "fsdp"), None),
        ),
        out_specs=(
            P(("dp", "fsdp"), None),
            P(("dp", "fsdp"), None),
            P("fsdp"),
            P("fsdp", None),
            P("fsdp", None),
            P("fsdp"),
            P("fsdp"),
            P("fsdp", None),
            P("fsdp", None),
        ),
        check_vma=False,
    )
```

```python
import functools
import math

import jax
import jax.numpy as jnp
from jax import lax
from jax.experimental import pallas as pl
from jax.experimental.pallas import tpu as pltpu
from jax.sharding import PartitionSpec as P

H = 16
DH = 128
FF = 8192
SEG = 1024

highest = lax.Precision.HIGHEST
epsilon = 1e-06
f32 = jnp.float32
bf16 = jnp.bfloat16
AXIS = "fsdp"


def feature(values):
    return jax.nn.elu(values) + 1.0


def feature_slope(values):
    return jnp.where(values > 0, 1.0, jnp.exp(jnp.minimum(values, 0.0)))


def norm_forward(values, gain):
    factor = lax.rsqrt(jnp.mean(values * values, axis=-1, keepdims=True) + epsilon)
    return (values * factor * gain, factor)


def norm_backward(values, factor, gain, upstream):
    scaled = upstream * gain
    gain_grad = jnp.sum(upstream * values * factor, axis=0)
    value_grad = factor * scaled - values * (factor * factor * factor) * jnp.mean(
        scaled * values, axis=-1, keepdims=True
    )
    return (value_grad, gain_grad)


def dot(left, right, dims):
    return lax.dot_general(left, right, ((dims[0], dims[1]), ((), ())), preferred_element_type=f32)


def rows_dot(left, right):
    return dot(left, right, ((0,), (0,)))


def cols_dot(left, right):
    return dot(left, right, ((1,), (1,)))


class Layout:
    def __init__(self):
        self.count = lax.axis_size(AXIS)
        self.groups = self.count // H
        self.place = lax.axis_index(AXIS)
        self.head = self.place % H
        self.group = self.place // H
        self.inside = None
        self.across = None
        if self.groups > 1:
            self.inside = [[g * H + j for j in range(H)] for g in range(self.groups)]
            self.across = [[g * H + j for g in range(self.groups)] for j in range(H)]

    def gather(self, block):
        return lax.all_gather(block, AXIS, axis=0, tiled=True, axis_index_groups=self.inside)

    def gather_all(self, block):
        return lax.all_gather(block, AXIS, axis=0, tiled=True)

    def scatter_sum(self, whole):
        return lax.psum_scatter(
            whole, AXIS, scatter_dimension=0, tiled=True, axis_index_groups=self.inside
        )

    def columns(self, block, parts):
        rows, width = block.shape
        each = width // (parts * H)
        if self.groups == 1:
            split = block.reshape(rows, parts, H, each)
            out = lax.all_to_all(split, AXIS, 2, 0, tiled=True)
            return out.reshape(rows * self.count, parts * each)
        whole = self.gather_all(block).reshape(rows * self.count, parts, H, each)
        out = lax.dynamic_index_in_dim(whole, self.head, 2, False)
        return out.reshape(rows * self.count, parts * each)

    def own_rows(self, grad, parts):
        rows, width = grad.shape
        each = width // parts
        if self.groups == 1:
            split = grad.astype(bf16).reshape(rows, parts, 1, each)
            out = lax.all_to_all(split, AXIS, 0, 2, tiled=True)
            return out.reshape(rows // self.count, parts * H * each)
        whole = jnp.zeros((rows, parts, H, each), f32)
        whole = lax.dynamic_update_slice_in_dim(
            whole, grad.reshape(rows, parts, 1, each), self.head, 2
        )
        return lax.psum_scatter(
            whole.reshape(rows, parts * H * each), AXIS, scatter_dimension=0, tiled=True
        )

    def to_tokens(self, by_head):
        tokens, each = by_head.shape
        out = lax.all_to_all(
            by_head.reshape(H, tokens // H, each), AXIS, 0, 0, tiled=False,
            axis_index_groups=self.inside,
        )
        return out.transpose(1, 0, 2).reshape(tokens // H, H * each)

    def to_heads(self, by_token):
        tokens, width = by_token.shape
        split = by_token.reshape(tokens, H, width // H).transpose(1, 0, 2)
        out = lax.all_to_all(
            split, AXIS, 0, 0, tiled=False, axis_index_groups=self.inside
        )
        return out.reshape(H * tokens, width // H)


def carry_forward(layout, delta, count, fresh):
    segments = delta.shape[0]

    def walk(state):
        before = []
        for s in range(segments):
            state = jax.tree.map(lambda a: jnp.where(fresh[s], jnp.zeros_like(a), a), state)
            before.append(state)
            state = (state[0] + delta[s], state[1] + count[s])
        return before, state

    state = (jnp.zeros_like(delta[0]), jnp.zeros_like(count[0]))
    if layout.groups > 1:
        _, last = walk(state)
        renewed = jnp.any(fresh).astype(f32)
        every = jax.tree.map(
            lambda a: lax.all_gather(a, AXIS, axis_index_groups=layout.across), last + (renewed,)
        )
        for g in range(layout.groups - 1):
            keep = every[2][g] < 0.5
            after = jax.tree.map(lambda a, e: jnp.where(keep, a, 0.0) + e[g], state, every[:2])
            state = jax.tree.map(lambda a, b: jnp.where(g < layout.group, b, a), state, after)
    before, _ = walk(state)
    return jnp.stack([b[0] for b in before]), jnp.stack([b[1] for b in before])


def carry_backward(layout, state_grad, norm_grad, fresh):
    segments = state_grad.shape[0]

    def walk(state):
        after = [None] * segments
        for s in reversed(range(segments)):
            after[s] = state
            state = (state[0] + state_grad[s], state[1] + norm_grad[s])
            state = jax.tree.map(lambda a: jnp.where(fresh[s], jnp.zeros_like(a), a), state)
        return after, state

    state = (jnp.zeros_like(state_grad[0]), jnp.zeros_like(norm_grad[0]))
    if layout.groups > 1:
        _, first = walk(state)
        renewed = jnp.any(fresh).astype(f32)
        every = jax.tree.map(
            lambda a: lax.all_gather(a, AXIS, axis_index_groups=layout.across), first + (renewed,)
        )
        for g in reversed(range(1, layout.groups)):
            keep = every[2][g] < 0.5
            before = jax.tree.map(lambda a, e: jnp.where(keep, a, 0.0) + e[g], state, every[:2])
            state = jax.tree.map(lambda a, b: jnp.where(g > layout.group, b, a), state, before)
    after, _ = walk(state)
    return jnp.stack([a[0] for a in after]), jnp.stack([a[1] for a in after])


def body_groups(
    layer_input,
    first_gain,
    in_weight,
    out_weight,
    mix_gate,
    second_gain,
    gate_up,
    down_weight,
    document_starts,
    cotangent,
):
    layout = Layout()
    tokens, width = layer_input.shape
    group_tokens = tokens * H
    segments = group_tokens // SEG
    scale = 1.0 / math.sqrt(DH)

    gains = jnp.stack([first_gain, second_gain])
    gains = lax.all_gather(gains, AXIS, axis=1, tiled=True).astype(f32)
    first_all, second_all = gains[0], gains[1]
    if layout.groups == 1:
        mix_own = mix_gate
    else:
        mix_own = lax.dynamic_slice_in_dim(layout.gather_all(mix_gate), layout.head * DH, DH)
    mix = jax.nn.sigmoid(mix_own.astype(f32))[None]

    inputs = layer_input.astype(f32)
    normed, first_factor = norm_forward(inputs, first_all)
    normed_all = layout.gather(normed.astype(bf16))
    in_cols = layout.columns(in_weight, 3)
    out_all = layout.gather_all(out_weight)
    cot_all = layout.gather(cotangent)
    gate_up_cols = layout.columns(gate_up, 2)
    down_cols = layout.columns(down_weight, 1)

    projected = jnp.dot(normed_all, in_cols, preferred_element_type=f32).astype(bf16)
    by_segment = projected.reshape(segments, SEG, 3, DH)
    query, key, value = by_segment[:, :, 0], by_segment[:, :, 1], by_segment[:, :, 2]
    index = jnp.arange(SEG, dtype=jnp.int32)
    allowed = index[None, :] <= index[:, None]

    def attention_scores():
        raw = jnp.einsum("sqc,skc->sqk", query, key, preferred_element_type=f32) * scale
        return jnp.where(allowed[None], raw, -1e30)

    scores = attention_scores()
    top = jnp.max(scores, axis=-1, keepdims=True)
    expo = jnp.exp(scores - top)
    total = jnp.sum(expo, axis=-1, keepdims=True)
    log_total = top + jnp.log(total)
    probs_low = (expo / total).astype(bf16)
    local_out = jnp.einsum("sqk,skc->sqc", probs_low, value, preferred_element_type=f32)

    query_f, key_f, value_f = query.astype(f32), key.astype(f32), value.astype(f32)
    query_feature = feature(query_f).astype(bf16)
    key_feature = feature(key_f).astype(bf16)
    delta = jnp.einsum("slc,sla->sca", key_feature, value, preferred_element_type=f32)
    count = jnp.sum(key_feature.astype(f32), axis=1)
    numbers = layout.group * segments + jnp.arange(segments)
    fresh = (numbers == 0) | (
        lax.dynamic_slice_in_dim(document_starts[0], layout.group * segments, segments) > 0
    )
    memory, normal = carry_forward(layout, delta, count, fresh)
    query_feature_f = query_feature.astype(f32)
    numerator = jnp.einsum("sie,sej->sij", query_feature_f, memory, precision=highest)
    raw_denom = jnp.einsum("sik,sk->si", query_feature_f, normal, precision=highest)[..., None]
    denom = jnp.maximum(raw_denom, 1.0)
    memory_out = numerator / denom
    combined = mix * memory_out + (1.0 - mix) * local_out
    combined_head = combined.reshape(group_tokens, DH).astype(bf16)
    combined_low = layout.to_tokens(combined_head)
    attended = jnp.dot(combined_low, out_all, preferred_element_type=f32)
    middle = inputs + attended

    hidden, second_factor = norm_forward(middle, second_all)
    hidden_all = layout.gather(hidden.astype(bf16))
    act_grad = jnp.dot(cot_all, down_cols, preferred_element_type=f32)
    both = jnp.dot(hidden_all, gate_up_cols, preferred_element_type=f32)
    half = both.shape[1] // 2
    gate_part, up_part = both[:, :half], both[:, half:]
    sigma = jax.nn.sigmoid(gate_part)
    silu = gate_part * sigma
    activated = (silu * up_part).astype(bf16)
    silu_slope = sigma * (1.0 + gate_part * (1.0 - sigma))
    feed_grad = jnp.concatenate(
        [act_grad * up_part * silu_slope, act_grad * silu], axis=1
    ).astype(bf16)
    feed_out = layout.scatter_sum(cols_dot(activated, down_cols).astype(bf16))
    hidden_grad = layout.scatter_sum(cols_dot(feed_grad, gate_up_cols).astype(bf16))
    layer_output = (middle + feed_out.astype(f32)).astype(bf16)
    gate_up_part = layout.own_rows(rows_dot(hidden_all, feed_grad), 2)
    down_part = layout.own_rows(rows_dot(cot_all, activated), 1)

    upstream = cotangent.astype(f32)
    middle_norm_grad, second_local = norm_backward(
        middle, second_factor, second_all, hidden_grad.astype(f32)
    )
    middle_grad = upstream + middle_norm_grad
    attended_grad = middle_grad.astype(bf16)
    attended_grad_all = layout.gather(attended_grad)
    combined_grad = layout.to_heads(cols_dot(attended_grad, out_all).astype(bf16))
    combined_grad = combined_grad.astype(f32).reshape(segments, SEG, DH)
    out_rows_grad = rows_dot(combined_head, attended_grad_all)
    if layout.groups == 1:
        out_part = out_rows_grad
    else:
        whole = jnp.zeros((H * DH, width), f32)
        whole = lax.dynamic_update_slice_in_dim(whole, out_rows_grad, layout.head * DH, 0)
        out_part = lax.psum_scatter(whole, AXIS, scatter_dimension=0, tiled=True)
    mix_local = jnp.sum(combined_grad * (memory_out - local_out), axis=(0, 1)) * (
        mix * (1.0 - mix)
    ).reshape(DH)

    memory_grad = combined_grad * mix
    local_grad = (combined_grad * (1.0 - mix)).astype(bf16)
    numer_grad = memory_grad / denom
    denom_grad = -jnp.sum(memory_grad * memory_out, axis=-1, keepdims=True) / denom
    raw_grad = jnp.where(raw_denom > 1.0, denom_grad, 0.0)
    query_feature_grad = (
        jnp.einsum("sij,sej->sie", numer_grad, memory, precision=highest)
        + raw_grad * normal[:, None]
    )
    state_grad = jnp.einsum("sie,sij->sej", query_feature_f, numer_grad, precision=highest)
    norm_grad = jnp.sum(raw_grad * query_feature_f, axis=1)
    delta_grad, count_grad = carry_backward(layout, state_grad, norm_grad, fresh)
    key_feature_grad = (
        jnp.einsum("sij,sej->sie", value_f, delta_grad, precision=highest) + count_grad[:, None]
    )
    value_memory_grad = jnp.einsum(
        "sie,sej->sij", key_feature.astype(f32), delta_grad, precision=highest
    )
    query_memory_grad = query_feature_grad * feature_slope(query_f)
    key_memory_grad = key_feature_grad * feature_slope(key_f)

    probs = jnp.exp(attention_scores() - log_total)
    prob_grad = jnp.einsum("sqc,skc->sqk", local_grad, value, preferred_element_type=f32)
    row_term = jnp.sum(probs * prob_grad, axis=-1, keepdims=True)
    score_grad = (probs * (prob_grad - row_term)).astype(bf16)
    query_grad = query_memory_grad + scale * jnp.einsum(
        "sqk,skc->sqc", score_grad, key, preferred_element_type=f32
    )
    key_grad = key_memory_grad + scale * jnp.einsum(
        "sqk,sqc->skc", score_grad, query, preferred_element_type=f32
    )
    value_grad = value_memory_grad + jnp.einsum(
        "sqk,sqc->skc", probs.astype(bf16), local_grad, preferred_element_type=f32
    )
    projected_grad = (
        jnp.stack([query_grad, key_grad, value_grad], axis=2)
        .reshape(group_tokens, 3 * DH)
        .astype(bf16)
    )
    normed_grad = layout.scatter_sum(cols_dot(projected_grad, in_cols).astype(bf16))
    in_part = layout.own_rows(rows_dot(normed_all, projected_grad), 3)
    input_norm_grad, first_local = norm_backward(
        inputs, first_factor, first_all, normed_grad.astype(f32)
    )
    input_grad = middle_grad + input_norm_grad

    gains_part = lax.psum_scatter(
        jnp.stack([first_local, second_local]), AXIS, scatter_dimension=1, tiled=True
    )
    if layout.groups == 1:
        mix_part = mix_local
    else:
        whole = jnp.zeros((H * DH,), f32)
        whole = lax.dynamic_update_slice_in_dim(whole, mix_local, layout.head * DH, 0)
        mix_part = lax.psum_scatter(whole, AXIS, scatter_dimension=0, tiled=True)

    def over_sequences(part):
        return lax.psum(part.astype(bf16), "dp").astype(f32)

    small = over_sequences(jnp.concatenate([gains_part, mix_part[None]]))
    return (
        layer_output,
        input_grad,
        small[0],
        over_sequences(in_part),
        over_sequences(out_part),
        small[2],
        small[1],
        over_sequences(gate_up_part),
        over_sequences(down_part),
    )


MESH = pl.DeviceIdType.MESH
LIMIT = 60 * 2**20
FILL = ((0, 512), (512, 1024), (1536, 512))
ROWS = 256
dma = pltpu.SemaphoreType.DMA
VM = pltpu.VMEM


def vmem():
    return pl.BlockSpec(memory_space=pltpu.VMEM)


def anywhere():
    return pl.BlockSpec(memory_space=pl.ANY)


class Spot:
    def __init__(self):
        self.dp = lax.axis_index("dp")
        self.me = lax.axis_index(AXIS)
        self.z = self.me // 4
        self.y = (self.me // 2) % 2
        self.c = self.me % 2

    def at(self, z, y, c):
        return z * 4 + y * 2 + c

    def partner(self, k):
        out = self.me
        for bit in (1, 2, 4, 8):
            if k & bit:
                out = out + bit - 2 * bit * ((self.me // bit) % 2)
        return out

    def arrival(self, j):
        if j == 0:
            return self.z
        ends = jnp.where(self.z == 0, j, 3 - j)
        middle = {1: (0, 3), 2: (2, 1), 3: (3, 0)}[j]
        inner = jnp.where(self.z == 1, middle[0], middle[1])
        return jnp.where((self.z == 0) | (self.z == 3), ends, inner)


def greet(s, plane=True, other=True):
    ids = []
    if plane:
        ids += [{AXIS: (s.me + k) % 16} for k in range(1, 16)]
    else:
        ids += [{AXIS: s.at((s.z + k) % 4, s.y, s.c)} for k in (1, 2, 3)]
        ids += [{AXIS: s.at(s.z, 1 - s.y, s.c)}, {AXIS: s.at(s.z, s.y, 1 - s.c)}]
    if other:
        ids += [{"dp": 1 - s.dp}]
    barrier = pltpu.get_barrier_semaphore()
    for d in ids:
        pl.semaphore_signal(barrier, inc=1, device_id=d, device_id_type=MESH)
    pl.semaphore_wait(barrier, len(ids))


def send(src, dst, ssem, rsem, to):
    return pltpu.make_async_remote_copy(
        src_ref=src, dst_ref=dst, send_sem=ssem, recv_sem=rsem,
        device_id={AXIS: to}, device_id_type=MESH,
    )


def send_over(src, dst, ssem, rsem, s):
    return pltpu.make_async_remote_copy(
        src_ref=src, dst_ref=dst, send_sem=ssem, recv_sem=rsem,
        device_id={"dp": 1 - s.dp}, device_id_type=MESH,
    )


def merged(*lists):
    keyed = []
    for n, tasks in enumerate(lists):
        keyed += [((i + 0.5) / len(tasks), n, i, t) for i, t in enumerate(tasks)]
    for _, _, _, t in sorted(keyed, key=lambda e: e[:3]):
        t()


class Gather:
    chunks = 4

    @classmethod
    def sems(cls):
        return [dma((cls.chunks, 4))] * 5 + [dma((cls.chunks, 8))] * 2

    def __init__(self, s, src, dst, sems):
        self.s, self.src, self.dst = s, src, dst
        self.zr, self.zu, self.zd, self.ys, self.yr, self.ss, self.sr = sems[:7]
        self.rows = 128 // self.chunks
        self.skip = 0

    def block(self, ch, z, y, c):
        start = self.s.at(z, y, c) * 128 + self.skip + ch * self.rows
        return self.dst.at[pl.ds(pl.multiple_of(start, self.rows), self.rows)]

    def own(self, ch):
        start = pl.multiple_of(self.skip + ch * self.rows, self.rows)
        return self.src.at[pl.ds(start, self.rows)]

    def zcopy(self, ch, zo, up, own=False):
        s = self.s
        dst = self.block(ch, zo, s.y, s.c)
        to = s.at(s.z + 1 if up else s.z - 1, s.y, s.c)
        return send(
            self.own(ch) if own else dst, dst,
            (self.zu if up else self.zd).at[ch, zo], self.zr.at[ch, zo], to,
        )

    def ycopy(self, ch, zo, own=False):
        s = self.s
        dst = self.block(ch, zo, s.y, s.c)
        src = self.own(ch) if own else dst
        return send(src, dst, self.ys.at[ch, zo], self.yr.at[ch, zo], s.at(s.z, 1 - s.y, s.c))

    def scopy(self, ch, zo, yo, own=False):
        s = self.s
        dst = self.block(ch, zo, yo, s.c)
        n = zo * 2 + yo
        src = self.own(ch) if own else dst
        return send(src, dst, self.ss.at[ch, n], self.sr.at[ch, n], s.at(s.z, s.y, 1 - s.c))

    def start(self):
        s = self.s
        for ch in range(self.chunks):
            pl.when(s.z < 3)(lambda: self.zcopy(ch, s.z, True, True).start())
            pl.when(s.z > 0)(lambda: self.zcopy(ch, s.z, False, True).start())
            self.ycopy(ch, s.z, True).start()
            self.scopy(ch, s.z, s.y, True).start()

    def passed_on(self, ch, zo, yo):
        self.scopy(ch, zo, yo).start()

    def z_arrive(self, ch, j):
        s = self.s
        zo = s.arrival(j)
        self.zcopy(ch, zo, True).wait_recv()
        pl.when((zo < s.z) & (s.z < 3))(lambda: self.zcopy(ch, zo, True).start())
        pl.when((zo > s.z) & (s.z > 0))(lambda: self.zcopy(ch, zo, False).start())
        self.ycopy(ch, zo).start()
        self.passed_on(ch, zo, s.y)

    def y_arrive(self, ch, j):
        s = self.s
        zo = s.arrival(j)
        b = self.block(ch, zo, 1 - s.y, s.c)
        send(b, b, self.ys.at[ch, zo], self.yr.at[ch, zo], s.me).wait_recv()
        self.passed_on(ch, zo, 1 - s.y)

    def s_arrive(self, j):
        s = self.s
        zo = s.arrival(j)
        for ch in range(self.chunks):
            for yo in range(2):
                n = zo * 2 + yo
                b = self.block(ch, zo, yo, 1 - s.c)
                send(b, b, self.ss.at[ch, n], self.sr.at[ch, n], s.me).wait_recv()

    def tasks(self, use=None):
        out = []
        for step in range(1, 5):
            for ch in range(self.chunks):
                if step < 4:
                    out.append(functools.partial(self.z_arrive, ch, step))
                out.append(functools.partial(self.y_arrive, ch, step - 1))
                if step == 4 and ch < 3 and use is not None:
                    out.append(functools.partial(use, ch))
            out.append(functools.partial(self.s_arrive, step - 1))
        if use is not None:
            out.append(functools.partial(use, 3))
        return out

    def drain(self):
        s = self.s
        for ch in range(self.chunks):
            for zo in range(4):
                pl.when((s.z < 3) & (zo <= s.z))(lambda: self.zcopy(ch, zo, True).wait_send())
                pl.when((s.z > 0) & (zo >= s.z))(lambda: self.zcopy(ch, zo, False).wait_send())
                self.ycopy(ch, zo).wait_send()
                for yo in range(2):
                    self.scopy(ch, zo, yo).wait_send()


class SharedGather(Gather):
    chunks = 2

    @classmethod
    def sems(cls):
        return Gather.sems.__func__(cls) + [dma((cls.chunks, 8))] * 4

    def __init__(self, s, src, dst, sems):
        super().__init__(s, src, dst, sems)
        self.xs, self.xr, self.ts, self.tr = sems[7:]
        self.rows = 64 // self.chunks
        self.skip = s.dp * 64

    def other(self, ch, z, y, c):
        start = self.s.at(z, y, c) * 128 + (1 - self.s.dp) * 64 + ch * self.rows
        return self.dst.at[pl.ds(pl.multiple_of(start, self.rows), self.rows)]

    def xcopy(self, ch, zo, yo):
        s = self.s
        b = self.block(ch, zo, yo, s.c)
        n = zo * 2 + yo
        return send_over(b, b, self.xs.at[ch, n], self.xr.at[ch, n], s)

    def tcopy(self, ch, zo, yo, own=False):
        s = self.s
        b = self.other(ch, zo, yo, s.c)
        n = zo * 2 + yo
        src = b
        if own:
            start = pl.multiple_of((1 - s.dp) * 64 + ch * self.rows, self.rows)
            src = self.src.at[pl.ds(start, self.rows)]
        return send(src, b, self.ts.at[ch, n], self.tr.at[ch, n], s.at(s.z, s.y, 1 - s.c))

    def start(self):
        super().start()
        for ch in range(self.chunks):
            self.tcopy(ch, self.s.z, self.s.y, True).start()

    def passed_on(self, ch, zo, yo):
        self.xcopy(ch, zo, yo).start()
        self.scopy(ch, zo, yo).start()

    def x_arrive(self, j, yo):
        s = self.s
        zo = s.arrival(j)
        row = s.y if yo == 0 else 1 - s.y
        for ch in range(self.chunks):
            b = self.other(ch, zo, row, s.c)
            n = zo * 2 + row
            send_over(b, b, self.xs.at[ch, n], self.xr.at[ch, n], s).wait_recv()
            self.tcopy(ch, zo, row).start()

    def tasks(self):
        out = super().tasks()
        for j in range(4):
            for yo in range(2):
                if j + yo > 0:
                    out.append(functools.partial(self.x_arrive, j, yo))
        return out

    def drain(self):
        s = self.s
        super().drain()
        for ch in range(self.chunks):
            for zo in range(4):
                for yo in range(2):
                    n = zo * 2 + yo
                    b = self.other(ch, zo, yo, 1 - s.c)
                    send(b, b, self.ts.at[ch, n], self.tr.at[ch, n], s.me).wait_recv()
                    self.tcopy(ch, zo, yo).wait_send()
                    far = (s.z != zo) | (s.y != yo)
                    pl.when(far)(lambda: self.xcopy(ch, zo, yo).wait_send())


class Columns:
    @staticmethod
    def sems(parts):
        return [dma((16, parts)), dma((16, parts)), dma((16,)), dma((16,)), dma((parts,))]

    def __init__(self, s, w, dst, parts, sems):
        self.s, self.w, self.dst, self.parts = s, w, dst, parts
        self.e = dst.shape[1] // parts
        self.ps, self.pr, self.xs, self.xr, self.own = sems

    def rows(self, src, half):
        return pl.ds(pl.multiple_of(src * 128 + half * 64, 64), 64)

    def cols(self, p, h):
        return pl.ds(pl.multiple_of(p * 16 * self.e + h * self.e, 128), self.e)

    def copy(self, k, p):
        s = self.s
        to = s.partner(k)
        half = pl.ds(pl.multiple_of(s.dp * 64, 64), 64)
        return send(
            self.w.at[half, self.cols(p, to)],
            self.dst.at[self.rows(s.me, s.dp), pl.ds(p * self.e, self.e)],
            self.ps.at[k, p], self.pr.at[s.me, p], to,
        )

    def local(self, p):
        s = self.s
        return pltpu.make_async_copy(
            self.w.at[:, self.cols(p, s.me)],
            self.dst.at[pl.ds(pl.multiple_of(s.me * 128, 128), 128), pl.ds(p * self.e, self.e)],
            self.own.at[p],
        )

    def begin(self, k):
        for p in range(self.parts):
            (self.copy(k, p) if k else self.local(p)).start()

    def start(self, ahead=16):
        self.ahead = ahead
        for k in range(ahead):
            self.begin(k)

    def over(self, src):
        s = self.s
        b = self.dst.at[self.rows(src, s.dp)]
        return send_over(b, b, self.xs.at[src], self.xr.at[src], s)

    def arrive(self, k):
        s = self.s
        if k + self.ahead - 1 < 16:
            self.begin(k + self.ahead - 1)
        src = s.partner(k)
        for p in range(self.parts):
            b = self.dst.at[self.rows(src, s.dp), pl.ds(p * self.e, self.e)]
            send(b, b, self.ps.at[k, p], self.pr.at[src, p], s.me).wait_recv()
        self.over(src).start()

    def tasks(self):
        return [functools.partial(self.arrive, k) for k in range(1, 16)]

    def finish(self):
        s = self.s
        for k in range(1, 16):
            src = s.partner(k)
            b = self.dst.at[self.rows(src, 1 - s.dp)]
            send_over(b, b, self.xs.at[src], self.xr.at[src], s).wait_recv()
        for p in range(self.parts):
            self.local(p).wait()

    def drain(self):
        s = self.s
        for k in range(1, 16):
            for p in range(self.parts):
                self.copy(k, p).wait_send()
            self.over(s.partner(k)).wait_send()


class Return:
    @staticmethod
    def sems(parts):
        return [dma((16, parts))] * 4 + [dma((parts,))]

    ahead = 16

    def __init__(self, s, src, dst, parts, sems, other=None):
        self.s, self.src, self.dst, self.parts, self.other = s, src, dst, parts, other
        self.e = src.shape[2] // parts
        self.ps, self.pr, self.xs, self.xr, self.own = sems

    def place(self, ref, p, h):
        return ref.at[:, pl.ds(pl.multiple_of(p * 16 * self.e + h * self.e, 128), self.e)]

    def copy(self, k, p):
        s = self.s
        to = s.partner(k)
        return send(
            self.src.at[to, :, pl.ds(p * self.e, self.e)], self.place(self.dst, p, s.me),
            self.ps.at[k, p], self.pr.at[s.me, p], to,
        )

    def local(self, p):
        s = self.s
        return pltpu.make_async_copy(
            self.src.at[s.me, :, pl.ds(p * self.e, self.e)], self.place(self.dst, p, s.me),
            self.own.at[p],
        )

    def begin(self, k):
        for p in range(self.parts):
            if k:
                self.copy(k, p).start()
                continue
            self.local(p).start()
            if self.other is not None:
                self.over(self.s.me, p, own=True).start()

    def start(self, ahead=16):
        self.ahead = ahead
        for k in range(ahead):
            self.begin(k)

    def over(self, h, p, own=False):
        s = self.s
        src = self.src.at[s.me, :, pl.ds(p * self.e, self.e)] if own else self.place(self.dst, p, h)
        return send_over(src, self.place(self.other, p, h), self.xs.at[h, p], self.xr.at[h, p], s)

    def arrive(self, k):
        s = self.s
        if k + self.ahead - 1 < 16:
            self.begin(k + self.ahead - 1)
        h = s.partner(k)
        for p in range(self.parts):
            b = self.place(self.dst, p, h)
            send(b, b, self.ps.at[k, p], self.pr.at[h, p], s.me).wait_recv()
            if self.other is not None:
                self.over(h, p).start()

    def tasks(self):
        return [functools.partial(self.arrive, k) for k in range(1, 16)]

    def finish(self):
        s = self.s
        for p in range(self.parts):
            self.local(p).wait()
        if self.other is not None:
            for k in range(16):
                h = s.partner(k)
                for p in range(self.parts):
                    b = self.place(self.other, p, h)
                    send_over(b, b, self.xs.at[h, p], self.xr.at[h, p], s).wait_recv()
        for k in range(1, 16):
            for p in range(self.parts):
                self.copy(k, p).wait_send()
        if self.other is not None:
            for k in range(16):
                for p in range(self.parts):
                    self.over(s.partner(k), p).wait_send()


class Scatter:
    lag = 3

    @staticmethod
    def scratch(width):
        q = width // 512
        return [
            VM((4, 2, 256, width), bf16), VM((4, 2, 128, width), bf16), VM((4, 2, 128, width), bf16),
            VM((4, 128, width), bf16), VM((5, 128, width), bf16),
            dma((4, q, 2)), dma((4, q, 2)), dma((4, q)), dma((4, q)), dma((4, q)), dma((5, q)),
        ]

    def __init__(self, s, left, right, out, scratch, first=0):
        self.s, self.left, self.right, self.out, self.first = s, left, right, out, first
        self.part, self.sib, self.mid, self.got_y, self.got_z = scratch[:5]
        self.ss, self.sr, self.ys, self.yr, self.zs, self.zr = scratch[5:]
        self.cols = 512
        self.pieces = out.shape[1] // 512
        self.order = [s.arrival(j) for j in (3, 2, 1, 0)]

    def w(self, h):
        return pl.ds(h * self.cols, self.cols)

    def compute(self, k, h, yd, slot):
        tok = pl.multiple_of((self.order[k] * 2 + yd) * 256, 256)
        p = cols_dot(self.left[pl.ds(tok, 256), :], self.right[pl.ds(self.first + h * self.cols, self.cols), :])
        self.part[k, slot, :, self.w(h)] = p.astype(bf16)

    def sib_copy(self, k, h, slot):
        s = self.s
        src = self.part.at[k, slot, pl.ds(pl.multiple_of((1 - s.c) * 128, 128), 128), self.w(h)]
        return send(
            src, self.sib.at[k, slot, :, self.w(h)],
            self.ss.at[k, h, slot], self.sr.at[k, h, slot], s.at(s.z, s.y, 1 - s.c),
        )

    def y_copy(self, k, h):
        s = self.s
        return send(
            self.mid.at[k, 0, :, self.w(h)], self.got_y.at[k, :, self.w(h)],
            self.ys.at[k, h], self.yr.at[k, h], s.at(s.z, 1 - s.y, s.c),
        )

    def z_copy(self, k, h):
        s = self.s
        to = self.order[k]
        up = to > s.z
        hop = jnp.where(up, s.z + 1, s.z - 1)
        slot = jnp.where(up | (hop != to), to, 4)
        return send(
            self.mid.at[k, 1, :, self.w(h)], self.got_z.at[slot, :, self.w(h)],
            self.zs.at[k, h], self.zr.at[slot, h], s.at(hop, s.y, s.c),
        )

    def z_wait(self, slot, h):
        b = self.got_z.at[slot, :, self.w(h)]
        send(b, b, self.zs.at[0, h], self.zr.at[slot, h], self.s.me).wait_recv()

    def fold(self, k, h, slot):
        s = self.s
        self.sib_copy(k, h, slot).wait_recv()
        own = self.part[k, slot, pl.ds(pl.multiple_of(s.c * 128, 128), 128), self.w(h)]
        total = own.astype(f32) + self.sib[k, slot, :, self.w(h)].astype(f32)
        self.mid[k, slot, :, self.w(h)] = total.astype(bf16)

    def after_y(self, k, h):
        s = self.s
        w = self.w(h)
        self.y_copy(k, h).wait_recv()
        total = self.mid[k, 1, :, w].astype(f32) + self.got_y[k, :, w].astype(f32)
        if k == 3:
            self.out[:, w] = total
            return
        to = self.order[k]
        first = jnp.where(to > s.z, s.z == 0, s.z == 3)

        @pl.when(first)
        def _():
            self.mid[k, 1, :, w] = total.astype(bf16)

        @pl.when(jnp.logical_not(first))
        def _():
            self.z_wait(to, h)
            self.mid[k, 1, :, w] = (total + self.got_z[to, :, w].astype(f32)).astype(bf16)

        self.z_copy(k, h).start()

    def tasks(self):
        steps = [(k, h) for k in range(4) for h in range(self.pieces)]
        s = self.s

        def step(i):
            k, h = steps[i]
            self.compute(k, h, 1 - s.y, 0)
            self.sib_copy(k, h, 0).start()
            self.compute(k, h, s.y, 1)
            self.sib_copy(k, h, 1).start()
            self.fold(k, h, 0)
            self.y_copy(k, h).start()
            self.fold(k, h, 1)

        out = []
        for i in range(len(steps) + self.lag):
            if i < len(steps):
                out.append(functools.partial(step, i))
            if i >= self.lag:
                out.append(functools.partial(self.after_y, *steps[i - self.lag]))
        return out

    def finish(self):
        s = self.s
        for h in range(self.pieces):
            w = self.w(h)

            @pl.when(s.z > 0)
            def _():
                self.z_wait(s.z, h)
                self.out[:, w] += self.got_z[s.z, :, w].astype(f32)

            @pl.when(s.z < 3)
            def _():
                self.z_wait(4, h)
                self.out[:, w] += self.got_z[4, :, w].astype(f32)

        for k in range(4):
            for h in range(self.pieces):
                self.sib_copy(k, h, 0).wait_send()
                self.sib_copy(k, h, 1).wait_send()
                self.y_copy(k, h).wait_send()
                if k < 3:
                    self.z_copy(k, h).wait_send()


class Weigh:
    steps = 8

    @classmethod
    def scratch(cls, cols):
        return [
            VM((16, 64, cols), f32), VM((16, 64, cols), bf16), VM((16, 64, cols), bf16),
            dma((cls.steps,)), dma((cls.steps,)),
        ]

    def __init__(self, s, left, right, half, scratch, back=None):
        self.s, self.left, self.right, self.half, self.back = s, left, right, half, back
        self.mine, self.sent, self.got, self.xs, self.xr = scratch

    def at(self, n):
        return self.s.partner(2 * n) // 2

    def copy(self, n):
        i = self.at(n)
        w = pl.ds(2 * i, 2)
        return send_over(self.sent.at[w], self.got.at[w], self.xs.at[i], self.xr.at[i], self.s)

    def compute(self, n):
        i = self.at(n)
        low = self.s.dp == 0
        cols = pl.ds(pl.multiple_of(i * 256, 256), 256)
        got = rows_dot(self.left[:, cols], self.right[...])
        for m in range(2):
            a, b = got[m * 128:m * 128 + 64], got[m * 128 + 64:m * 128 + 128]
            self.mine[2 * i + m] = jnp.where(low, a, b)
            self.sent[2 * i + m] = jnp.where(low, b, a).astype(bf16)
        self.copy(n).start()

    def fold(self, n):
        self.copy(n).wait_recv()
        w = pl.ds(2 * self.at(n), 2)
        self.half[w] = (self.mine[w] + self.got[w].astype(f32)).astype(bf16)
        if self.back is not None:
            self.back.begin(2 * n)
            self.back.begin(2 * n + 1)

    def products(self):
        return [functools.partial(self.compute, i) for i in range(self.steps)]

    def folds(self):
        return [functools.partial(self.fold, i) for i in range(self.steps)]

    def drain(self):
        for i in range(self.steps):
            self.copy(i).wait_send()


def nothing(n):
    return [lambda: None] * n


def halves_of(refs, counts):
    out, at = [], 0
    for n in counts:
        out.append(refs[at:at + n])
        at += n
    return out


def communicate(kernel, name, number, ins, in_specs, outs, out_specs, scratch, flops=0):
    return pl.pallas_call(
        kernel, out_shape=outs, in_specs=in_specs, out_specs=out_specs, scratch_shapes=scratch,
        compiler_params=pltpu.CompilerParams(
            collective_id=number, has_side_effects=True, vmem_limit_bytes=LIMIT
        ),
        cost_estimate=pl.CostEstimate(flops=flops, bytes_accessed=2**24, transcendentals=0),
        name=name,
    )(*ins)


def project_kernel(x, gains, in_w, normed_all, in_cols, gains_all, projected, normed, *rest):
    g_s, g_r = rest[:2]
    gather_sems, col_sems = halves_of(rest[2:], [7, 5])
    s = Spot()
    greet(s)

    def gain_copy(k):
        return send(gains, gains_all.at[s.me], g_s.at[k], g_r.at[s.me], (s.me + k) % 16)

    for k in range(1, 16):
        gain_copy(k).start()
    columns = Columns(s, in_w, in_cols, 3, col_sems)
    columns.start()
    gains_all[s.me] = gains[...]
    values = x[...].astype(f32)
    factor = lax.rsqrt(jnp.mean(values * values, axis=-1, keepdims=True) + epsilon)
    for k in range(1, 16):
        src = (s.me + 16 - k) % 16
        b = gains_all.at[src]
        send(b, b, g_s.at[k], g_r.at[src], s.me).wait_recv()
    mine = pl.ds(pl.multiple_of(s.me * 128, 128), 128)
    for j in range(16):
        w = pl.ds(j * 128, 128)
        part = (x[:, w].astype(f32) * factor * gains_all[j, 0:1, :]).astype(bf16)
        normed[:, w] = part
        normed_all[mine, w] = part
    gather = Gather(s, normed, normed_all, gather_sems)
    gather.start()

    def use(j):
        if j == 0:
            columns.finish()
        tok = pl.ds(pl.multiple_of(s.arrival(j) * 512, 512), 512)
        out = jnp.dot(normed_all[tok, :], in_cols[...], preferred_element_type=f32)
        projected[tok, :] = out.astype(bf16)

    merged(gather.tasks(use), nothing(2) + columns.tasks() + nothing(8))
    gather.drain()
    columns.drain()
    for k in range(1, 16):
        gain_copy(k).wait_send()


def project(x, gains, in_weight, number):
    tokens, width = x.shape
    return communicate(
        project_kernel, "project", number, (x, gains, in_weight), [vmem(), vmem(), anywhere()],
        [
            jax.ShapeDtypeStruct((16 * tokens, width), bf16),
            jax.ShapeDtypeStruct((width, 3 * DH), bf16),
            jax.ShapeDtypeStruct((16, 8, 128), f32),
            jax.ShapeDtypeStruct((16 * tokens, 3 * DH), bf16),
        ],
        [vmem()] * 4,
        [VM((tokens, width), bf16), dma((16,)), dma((16,))] + Gather.sems() + Columns.sems(3),
    )


def kernel_feature(t):
    return jnp.where(t > 0, t + 1.0, jnp.exp(jnp.minimum(t, 0.0)))


def dot_high(left, right, dims=((1,), (0,))):
    return lax.dot_general(
        left, right, (dims, ((), ())), preferred_element_type=f32, precision=highest
    )


def scores_of(query, keys, first):
    raw = cols_dot(query, keys) * (1.0 / math.sqrt(DH))
    row = lax.broadcasted_iota(jnp.int32, raw.shape, 0) + first
    col = lax.broadcasted_iota(jnp.int32, raw.shape, 1)
    return jnp.where(col <= row, raw, -1e30)


class Attend:
    def __init__(self, qkv, keep, mix, local, mem_out, lse, combined, memory, normal):
        self.qkv, self.keep, self.mix = qkv, keep, mix
        self.local, self.mem_out, self.lse, self.combined = local, mem_out, lse, combined
        self.memory, self.normal = memory, normal
        self.segments = qkv.shape[0] // SEG

    def states(self):
        state = jnp.zeros((DH, DH), f32)
        norm = jnp.zeros((1, DH), f32)
        for n in range(self.segments):
            keep = self.keep[n, 0:1, :]
            state, norm = state * keep, norm * keep
            self.memory[n] = state
            self.normal[n, 0:1, :] = norm
            if n + 1 < self.segments:
                rows = pl.ds(n * SEG, SEG)
                fk = kernel_feature(self.qkv[rows, DH:2 * DH].astype(f32)).astype(bf16)
                state = state + rows_dot(fk, self.qkv[rows, 2 * DH:])
                norm = norm + jnp.sum(fk.astype(f32), axis=0, keepdims=True)

    def block(self, n, i):
        rows = pl.ds(n * SEG + i * ROWS, ROWS)
        seen = pl.ds(n * SEG, (i + 1) * ROWS)
        query = self.qkv[rows, :DH]
        scores = scores_of(query, self.qkv[seen, DH:2 * DH], i * ROWS)
        top = jnp.max(scores, axis=-1, keepdims=True)
        expo = jnp.exp(scores - top)
        total = jnp.sum(expo, axis=-1, keepdims=True)
        probs = (expo * (1.0 / total)).astype(bf16)
        local = jnp.dot(probs, self.qkv[seen, 2 * DH:], preferred_element_type=f32)
        fq = kernel_feature(query.astype(f32)).astype(bf16).astype(f32)
        den = jnp.maximum(jnp.sum(fq * self.normal[n, 0:1, :], axis=-1, keepdims=True), 1.0)
        mem_out = dot_high(fq, self.memory[n]) / den
        mix = self.mix[0:1, :]
        self.local[rows, :] = local
        self.mem_out[rows, :] = mem_out
        self.lse[rows, :] = jnp.broadcast_to(top + jnp.log(total), (ROWS, DH))
        self.combined[rows, :] = (mix * mem_out + (1.0 - mix) * local).astype(bf16)

    def blocks(self):
        return [(n, i) for n in range(self.segments) for i in range(SEG // ROWS)]


class AttendBack:
    def __init__(self, qkv, keep, mix, local, mem_out, lse, memory, normal, upstream, grad,
                 mix_grad, dk, dv, state_grad, norm_grad):
        self.qkv, self.keep, self.mix = qkv, keep, mix
        self.local, self.mem_out, self.lse = local, mem_out, lse
        self.memory, self.normal, self.upstream, self.grad = memory, normal, upstream, grad
        self.mix_grad, self.dk, self.dv = mix_grad, dk, dv
        self.state_grad, self.norm_grad = state_grad, norm_grad
        self.segments = qkv.shape[0] // SEG

    def clear(self):
        self.mix_grad[...] = jnp.zeros_like(self.mix_grad)
        self.dk[...] = jnp.zeros_like(self.dk)
        self.dv[...] = jnp.zeros_like(self.dv)
        self.state_grad[...] = jnp.zeros_like(self.state_grad)
        self.norm_grad[...] = jnp.zeros_like(self.norm_grad)

    def block(self, n, i):
        scale = 1.0 / math.sqrt(DH)
        rows = pl.ds(n * SEG + i * ROWS, ROWS)
        seen = pl.ds(n * SEG, (i + 1) * ROWS)
        query = self.qkv[rows, :DH]
        keys = self.qkv[seen, DH:2 * DH]
        values = self.qkv[seen, 2 * DH:]
        up = self.upstream[rows, :].astype(f32)
        mem_out = self.mem_out[rows, :]
        mix = self.mix[0:1, :]
        mixed = jnp.sum(up * (mem_out - self.local[rows, :]), axis=0, keepdims=True)
        self.mix_grad[0:1, :] += mixed * mix * (1.0 - mix)
        memory_grad = up * mix
        local_grad = (up * (1.0 - mix)).astype(bf16)
        query_f = query.astype(f32)
        fq = kernel_feature(query_f).astype(bf16).astype(f32)
        normal = self.normal[n, 0:1, :]
        raw = jnp.sum(fq * normal, axis=-1, keepdims=True)
        den = jnp.maximum(raw, 1.0)
        numer_grad = memory_grad / den
        den_grad = -jnp.sum(memory_grad * mem_out, axis=-1, keepdims=True) / den
        raw_grad = jnp.where(raw > 1.0, den_grad, 0.0)
        fq_grad = dot_high(numer_grad, self.memory[n], ((1,), (1,))) + raw_grad * normal
        if n > 0:
            self.state_grad[n] += dot_high(fq, numer_grad, ((0,), (0,)))
            self.norm_grad[n, 0:1, :] += jnp.sum(raw_grad * fq, axis=0, keepdims=True)
        scores = scores_of(query, keys, i * ROWS)
        probs = jnp.exp(scores - self.lse[rows, 0:1])
        prob_grad = cols_dot(local_grad, values)
        row_term = jnp.sum(probs * prob_grad, axis=-1, keepdims=True)
        score_grad = (probs * (prob_grad - row_term)).astype(bf16)
        query_grad = jnp.dot(score_grad, keys, preferred_element_type=f32) * scale
        query_grad = query_grad + fq_grad * feature_slope(query_f)
        self.grad[rows, :DH] = query_grad.astype(bf16)
        self.dk[seen, :] += rows_dot(score_grad, query) * scale
        self.dv[seen, :] += rows_dot(probs.astype(bf16), local_grad)

    def states(self):
        state = jnp.zeros((DH, DH), f32)
        norm = jnp.zeros((1, DH), f32)
        for n in reversed(range(self.segments)):
            rows = pl.ds(n * SEG, SEG)
            key = self.qkv[rows, DH:2 * DH].astype(f32)
            key_grad = self.dk[rows, :]
            value_grad = self.dv[rows, :]
            if n + 1 < self.segments:
                fk = kernel_feature(key).astype(bf16).astype(f32)
                value = self.qkv[rows, 2 * DH:].astype(f32)
                fk_grad = dot_high(value, state, ((1,), (1,))) + norm
                key_grad = key_grad + fk_grad * feature_slope(key)
                value_grad = value_grad + dot_high(fk, state)
            self.grad[rows, DH:2 * DH] = key_grad.astype(bf16)
            self.grad[rows, 2 * DH:] = value_grad.astype(bf16)
            if n > 0:
                keep = self.keep[n, 0:1, :]
                state = (state + self.state_grad[n]) * keep
                norm = (norm + self.norm_grad[n, 0:1, :]) * keep

    def blocks(self):
        return [(n, i) for n in range(self.segments) for i in range(SEG // ROWS)]


def attend_kernel(qkv, keep, mix, out_w, cot, gate_up,
                  local, mem_out, lse, combined, memory, normal, mixed_tokens, out_all, cot_all,
                  gate_up_cols, copies, t_s, t_r, *rest):
    sems_o, sems_c, sems_g = halves_of(rest, [11, 7, 5])
    s = Spot()
    mine = pl.ds(pl.multiple_of(s.me * 128, 128), 128)
    own = [
        pltpu.make_async_copy(out_w, out_all.at[mine], copies.at[0]),
        pltpu.make_async_copy(cot, cot_all.at[mine], copies.at[1]),
    ]
    for cp in own:
        cp.start()
    greet(s)
    gather_o = SharedGather(s, out_w, out_all, sems_o)
    gather_c = Gather(s, cot, cot_all, sems_c)
    columns_g = Columns(s, gate_up, gate_up_cols, 2, sems_g)
    gather_o.start()
    gather_c.start()
    columns_g.start(4)
    attend = Attend(qkv, keep, mix, local, mem_out, lse, combined, memory, normal)

    def token_copy(j):
        return send(
            combined.at[pl.ds(j * 128, 128)],
            mixed_tokens.at[:, pl.ds(pl.multiple_of(s.me * DH, DH), DH)],
            t_s.at[j], t_r.at[s.me], j,
        )

    def block(n, i):
        attend.block(n, i)
        for j in range((n * SEG + i * ROWS) // 128, (n * SEG + (i + 1) * ROWS) // 128):
            pl.when(s.me != j)(lambda: token_copy(j).start())

    compute = [attend.states] + [functools.partial(block, n, i) for n, i in attend.blocks()]
    merged(
        gather_o.tasks(),
        gather_c.tasks(),
        columns_g.tasks(),
        compute + nothing(len(compute)),
    )
    mixed_tokens[:, pl.ds(pl.multiple_of(s.me * DH, DH), DH)] = combined[mine, :]
    columns_g.finish()
    for k in range(1, 16):
        src = (s.me + 16 - k) % 16
        b = mixed_tokens.at[:, pl.ds(pl.multiple_of(src * DH, DH), DH)]
        send(b, b, t_s.at[0], t_r.at[src], s.me).wait_recv()
    for j in range(16):
        pl.when(s.me != j)(lambda: token_copy(j).wait_send())
    gather_o.drain()
    gather_c.drain()
    columns_g.drain()
    for cp in own:
        cp.wait()


def attend_forward(qkv, keep, mix, out_weight, cotangent, gate_up, number):
    tokens, width = cotangent.shape
    total = qkv.shape[0]
    segments = total // SEG
    shape = jax.ShapeDtypeStruct
    return communicate(
        attend_kernel, "attend", number, (qkv, keep, mix, out_weight, cotangent, gate_up),
        [vmem()] * 3 + [anywhere()] * 3,
        [
            shape((total, DH), f32), shape((total, DH), f32), shape((total, DH), f32),
            shape((total, DH), bf16), shape((segments, DH, DH), f32), shape((segments, 8, DH), f32),
            shape((tokens, width), bf16),
            shape((total, width), bf16), shape((total, width), bf16),
            shape((width, gate_up.shape[1] // 16), bf16),
        ],
        [vmem()] * 7 + [anywhere()] * 3,
        [dma((2,)), dma((16,)), dma((16,))] + SharedGather.sems() + Gather.sems() + Columns.sems(2),
    )


def feed_kernel(combined, x, gains_all, out_all, cot_all, gate_up_cols, down,
                middle, hidden_all, act, feed_grad, down_v, out_v, cot_v, gate_up_v, hidden, copies,
                *rest):
    sems, sems_d = halves_of(rest, [7, 5])
    s = Spot()
    loads = [
        pltpu.make_async_copy(a, b, copies.at[i])
        for i, (a, b) in enumerate(
            [(out_all, out_v), (gate_up_cols, gate_up_v), (cot_all, cot_v)]
        )
    ]
    for cp in loads:
        cp.start()
    greet(s)
    columns = Columns(s, down, down_v, 1, sems_d)
    columns.start()
    loads[0].wait()
    width = x.shape[1]
    squares = jnp.zeros((x.shape[0], 1), f32)
    for j in range(4):
        w = pl.ds(j * 512, 512)
        got = jnp.dot(combined[...], out_v[:, w], preferred_element_type=f32)
        got = got + x[:, w].astype(f32)
        middle[:, w] = got
        squares = squares + jnp.sum(got * got, axis=-1, keepdims=True)
    factor = lax.rsqrt(squares * (1.0 / width) + epsilon)
    mine = pl.ds(pl.multiple_of(s.me * 128, 128), 128)
    for j in range(16):
        w = pl.ds(j * 128, 128)
        part = (middle[:, w] * factor * gains_all[j, 1:2, :]).astype(bf16)
        hidden[:, w] = part
        hidden_all[mine, w] = part
    gather = Gather(s, hidden, hidden_all, sems)
    gather.start()
    half = act.shape[1]

    def use(j):
        if j == 0:
            for cp in loads[1:]:
                cp.wait()
            columns.finish()
        tok = pl.ds(pl.multiple_of(s.arrival(j) * 512, 512), 512)
        act_grad = jnp.dot(cot_v[tok, :], down_v[...], preferred_element_type=f32)
        gate = jnp.dot(hidden_all[tok, :], gate_up_v[:, :half], preferred_element_type=f32)
        up = jnp.dot(hidden_all[tok, :], gate_up_v[:, half:], preferred_element_type=f32)
        sigma = jax.nn.sigmoid(gate)
        silu = gate * sigma
        act[tok, :] = (silu * up).astype(bf16)
        slope = sigma * (1.0 + gate * (1.0 - sigma))
        feed_grad[tok, :half] = (act_grad * up * slope).astype(bf16)
        feed_grad[tok, half:] = (act_grad * silu).astype(bf16)

    merged(gather.tasks(use), columns.tasks() + nothing(8))
    gather.drain()
    columns.drain()


def feed(combined, x, gains_all, out_all, cot_all, gate_up_cols, down, number):
    tokens, width = x.shape
    total = cot_all.shape[0]
    half = down.shape[1] // 16
    shape = jax.ShapeDtypeStruct
    return communicate(
        feed_kernel, "feed", number,
        (combined, x, gains_all, out_all, cot_all, gate_up_cols, down),
        [vmem()] * 3 + [anywhere()] * 4,
        [
            shape((tokens, width), f32), shape((total, width), bf16),
            shape((total, half), bf16), shape((total, 2 * half), bf16), shape((width, half), bf16),
        ],
        [vmem()] * 5,
        [
            VM(out_all.shape, bf16), VM(cot_all.shape, bf16), VM(gate_up_cols.shape, bf16),
            VM((tokens, width), bf16), dma((3,)),
        ] + Gather.sems() + Columns.sems(1),
    )


def hidden_grad_kernel(feed_grad, gate_up_cols, hidden_all, act, down_cols, out, half, feed_out, *rest):
    sems_w, scratch, scratch_f = halves_of(rest, [5, 11, 11])
    s = Spot()
    greet(s, plane=False)
    weigh = Weigh(s, hidden_all, feed_grad, half, sems_w)
    scatter = Scatter(s, feed_grad, gate_up_cols, out, scratch)
    filler = Scatter(s, act, down_cols, feed_out, scratch_f, FILL[0][0])
    merged(
        scatter.tasks(),
        weigh.products() + nothing(16),
        nothing(2) + filler.tasks(),
        nothing(20) + weigh.folds(),
    )
    scatter.finish()
    filler.finish()
    weigh.drain()


def hidden_grad_of(feed_grad, gate_up_cols, hidden_all, act, down_cols, number):
    shape = jax.ShapeDtypeStruct
    total, cols = feed_grad.shape
    width = gate_up_cols.shape[0]
    fill = FILL[0][1]
    return communicate(
        hidden_grad_kernel, "hidden_grad", number,
        (feed_grad, gate_up_cols, hidden_all, act, down_cols), [vmem()] * 5,
        [
            shape((total // 16, width), f32), shape((16, 64, cols), bf16),
            shape((total // 16, fill), f32),
        ],
        [vmem()] * 3, Weigh.scratch(cols) + Scatter.scratch(width) + Scatter.scratch(fill),
    )


def normed_grad_kernel(grad, in_cols, normed_all, x, gain, act, down_cols, gains, down_half, out_rows,
                       value_grad, gains_out, feed_out, down_rows, down_other, in_mine, in_other,
                       out_other, normed_grad, half, gains_v, got, total, theirs, x_s, x_r, g_s, g_r,
                       *rest):
    sems_d, sems_i, sems_w, scratch, scratch_f = halves_of(rest, [5, 5, 5, 11, 11])
    s = Spot()
    greet(s)
    back_i = Return(s, half, in_mine, 3, sems_i, other=in_other)
    weigh = Weigh(s, normed_all, grad, half, sems_w, back=back_i)
    back_d = Return(s, down_half, down_rows, 1, sems_d, other=down_other)
    scatter = Scatter(s, grad, in_cols, normed_grad, scratch)
    filler = Scatter(s, act, down_cols, feed_out, scratch_f, FILL[2][0])
    over = send_over(out_rows, out_other, x_s.at[0], x_r.at[0], s)
    back_d.start()

    def gain_copy(k):
        to = s.partner(k)
        return send(gains_v.at[to], got.at[s.me], g_s.at[k], g_r.at[s.me], to)

    def epilogue():
        width = x.shape[1]
        values = x[...].astype(f32)
        factor = lax.rsqrt(jnp.mean(values * values, axis=-1, keepdims=True) + epsilon)
        row = jnp.sum(normed_grad[...] * gain[0:1, :] * values, axis=-1, keepdims=True)
        row = row * (1.0 / width) * factor * factor * factor
        for j in range(16):
            w = pl.ds(j * 128, 128)
            v = x[:, w].astype(f32)
            u = normed_grad[:, w]
            value_grad[:, w] = factor * (u * gain[0:1, w]) - v * row
            gains_v[j] = gains[j]
            gains_v[j, 0:1, :] = jnp.sum(u * v * factor, axis=0, keepdims=True)

    merged(
        scatter.tasks(),
        weigh.products() + nothing(24),
        nothing(3) + weigh.folds() + nothing(12),
        nothing(10) + [over.start] + back_d.tasks() + nothing(5),
        nothing(2) + filler.tasks(),
        nothing(16) + back_i.tasks(),
    )
    scatter.finish()
    epilogue()
    for k in range(1, 16):
        gain_copy(k).start()
    filler.finish()
    back_d.finish()
    back_i.finish()
    weigh.drain()
    over.wait()
    for k in range(1, 16):
        src = s.partner(k)
        b = got.at[src]
        send(b, b, g_s.at[k], g_r.at[src], s.me).wait_recv()
    got[s.me] = gains_v[s.me]
    acc = got[0]
    for k in range(1, 16):
        acc = acc + got[k]
    total[...] = acc
    cp = send_over(total, theirs, x_s.at[1], x_r.at[1], s)
    cp.start()
    for k in range(1, 16):
        gain_copy(k).wait_send()
    cp.wait()
    gains_out[...] = total[...] + theirs[...]


def normed_grad_of(grad, in_cols, normed_all, x, gain, act, down_cols, gains, down_half, out_rows, number):
    shape = jax.ShapeDtypeStruct
    total, cols = grad.shape
    tokens, width = x.shape
    fill = FILL[2][1]
    down_rows = shape((64, 16 * down_half.shape[2]), bf16)
    in_rows = shape((64, 16 * cols), bf16)
    return communicate(
        normed_grad_kernel, "normed_grad", number,
        (grad, in_cols, normed_all, x, gain, act, down_cols, gains, down_half, out_rows),
        [vmem()] * 8 + [anywhere()] * 2,
        [
            shape((tokens, width), f32), shape((8, 128), f32), shape((tokens, fill), f32),
            down_rows, down_rows, in_rows, in_rows, shape(out_rows.shape, bf16),
        ],
        [vmem()] * 3 + [anywhere()] * 5,
        [
            VM((tokens, width), f32), VM((16, 64, cols), bf16), VM((16, 8, 128), f32),
            VM((16, 8, 128), f32), VM((8, 128), f32), VM((8, 128), f32),
            dma((2,)), dma((2,)), dma((16,)), dma((16,)),
        ] + Return.sems(1) + Return.sems(3) + Weigh.scratch(cols) + Scatter.scratch(width)
        + Scatter.scratch(fill),
    )


def attend_back_kernel(attended, out_all, qkv, keep, mix, local, mem_out, lse, memory, normal,
                       gate_up_half, cot_all, act, down_cols,
                       attended_all, grad, mix_grad, gate_up_rows, gate_up_other, down_half, feed_out,
                       out_v, cot_v, by_token, upstream, dk, dv, state_grad, norm_grad, copies, h_s, h_r,
                       *rest):
    sems_a, sems_g, sems_w, scratch_f = halves_of(rest, [7, 5, 5, 11])
    s = Spot()
    mine = pl.ds(pl.multiple_of(s.me * 128, 128), 128)
    cot_load = pltpu.make_async_copy(cot_all, cot_v, copies.at[2])
    load = pltpu.make_async_copy(out_all, out_v, copies.at[0])
    load.start()
    own = pltpu.make_async_copy(attended, attended_all.at[mine], copies.at[1])
    own.start()
    cot_load.start()
    greet(s)
    gather = Gather(s, attended, attended_all, sems_a)
    back_g = Return(s, gate_up_half, gate_up_rows, 2, sems_g, other=gate_up_other)
    filler = Scatter(s, act, down_cols, feed_out, scratch_f, FILL[1][0])
    weigh = Weigh(s, cot_v, act, down_half, sems_w)
    attend = AttendBack(qkv, keep, mix, local, mem_out, lse, memory, normal, upstream, grad,
                        mix_grad, dk, dv, state_grad, norm_grad)
    attend.clear()
    gather.start()
    load.wait()

    def head_copy(j):
        return send(by_token.at[:, pl.ds(j * DH, DH)], upstream.at[mine], h_s.at[j], h_r.at[s.me], j)

    for j in range(4):
        w = pl.ds(j * 512, 512)
        by_token[:, w] = cols_dot(attended[...], out_v[w, :]).astype(bf16)
        for h in range(4 * j, 4 * j + 4):
            pl.when(s.me != h)(lambda: head_copy(h).start())
    upstream[mine, :] = by_token[:, pl.ds(pl.multiple_of(s.me * DH, DH), DH)]
    cot_load.wait()
    filler.lag = 8

    def arrive(j):
        b = upstream.at[pl.ds(j * 128, 128)]
        pl.when(s.me != j)(lambda: send(b, b, h_s.at[j], h_r.at[j], s.me).wait_recv())

    def block(n, i):
        for j in range((n * SEG + i * ROWS) // 128, (n * SEG + (i + 1) * ROWS) // 128):
            arrive(j)
        attend.block(n, i)

    compute = [functools.partial(block, n, i) for n, i in attend.blocks()] + [attend.states]
    merged(gather.tasks(), nothing(2) + compute, weigh.products() + nothing(12))
    back_g.start()
    merged(filler.tasks(), back_g.tasks(), weigh.folds())
    filler.finish()
    back_g.finish()
    weigh.drain()
    for j in range(16):
        pl.when(s.me != j)(lambda: head_copy(j).wait_send())
    gather.drain()
    own.wait()


def attend_backward(attended, out_all, qkv, keep, mix, saved, gate_up_half, cot_all, act, down_cols,
                    number):
    tokens, width = attended.shape
    total = qkv.shape[0]
    segments = total // SEG
    shape = jax.ShapeDtypeStruct
    local, mem_out, lse, memory, normal = saved
    rows = shape((64, 16 * gate_up_half.shape[2]), bf16)
    return communicate(
        attend_back_kernel, "attend_back", number,
        (attended, out_all, qkv, keep, mix, local, mem_out, lse, memory, normal,
         gate_up_half, cot_all, act, down_cols),
        [vmem(), anywhere()] + [vmem()] * 8 + [anywhere()] * 2 + [vmem()] * 2,
        [
            shape((total, width), bf16), shape((total, 3 * DH), bf16), shape((8, DH), f32),
            rows, rows, shape((16, 64, act.shape[1]), bf16), shape((tokens, FILL[1][1]), f32),
        ],
        [anywhere(), vmem(), vmem(), anywhere(), anywhere(), vmem(), vmem()],
        [
            VM(out_all.shape, bf16), VM(cot_all.shape, bf16), VM((tokens, width), bf16),
            VM((total, DH), bf16),
            VM((total, DH), f32), VM((total, DH), f32), VM((segments, DH, DH), f32),
            VM((segments, 8, DH), f32), dma((3,)), dma((16,)), dma((16,)),
        ] + Gather.sems() + Return.sems(2) + Weigh.scratch(act.shape[1]) + Scatter.scratch(FILL[1][1]),
    )


def body(
    layer_input,
    first_gain,
    in_weight,
    out_weight,
    mix_gate,
    second_gain,
    gate_up,
    down_weight,
    document_starts,
    cotangent,
):
    tokens, width = layer_input.shape
    total = tokens * H
    segments = total // SEG
    dp = lax.axis_index("dp")

    own_gains = jnp.zeros((8, tokens), f32)
    own_gains = own_gains.at[0].set(first_gain.astype(f32)).at[1].set(second_gain.astype(f32))
    mix = jnp.broadcast_to(jax.nn.sigmoid(mix_gate.astype(f32))[None], (8, DH))
    numbers = jnp.arange(segments)
    fresh = (numbers == 0) | (document_starts[0] > 0)
    keep = jnp.broadcast_to(jnp.where(fresh, 0.0, 1.0)[:, None, None], (segments, 8, DH))

    normed_all, in_cols, gains_all, qkv = project(layer_input, own_gains, in_weight, 0)
    (local, mem_out, lse, combined, memory, normal, mixed_tokens, out_all, cot_all, gate_up_cols,
     ) = attend_forward(qkv, keep, mix, out_weight, cotangent, gate_up, 1)
    middle, hidden_all, act, feed_grad, down_cols = feed(
        mixed_tokens, layer_input, gains_all, out_all, cot_all, gate_up_cols, down_weight, 2
    )

    hidden_grad, gate_up_half, feed_out_0 = hidden_grad_of(
        feed_grad, gate_up_cols, hidden_all, act, down_cols, 3
    )

    first_all = gains_all[:, 0].reshape(width)
    second_all = gains_all[:, 1].reshape(width)
    upstream = cotangent.astype(f32)
    second_factor = lax.rsqrt(jnp.mean(middle * middle, axis=-1, keepdims=True) + epsilon)
    middle_norm_grad, second_local = norm_backward(middle, second_factor, second_all, hidden_grad)
    middle_grad = upstream + middle_norm_grad
    (attended_all, projected_grad, mix_grad, gate_up_rows, gate_up_other, down_half,
     feed_out_1) = attend_backward(
        middle_grad.astype(bf16), out_all, qkv, keep, mix, (local, mem_out, lse, memory, normal),
        gate_up_half, cot_all, act, down_cols, 4,
    )
    out_rows = rows_dot(combined, attended_all).astype(bf16)
    mix_rows = jnp.where((jnp.arange(H) == lax.axis_index(AXIS))[:, None], mix_grad[0:1], 0.0)
    gain_grads = jnp.stack([mix_rows, second_local.reshape(16, 128), mix_rows], axis=1)
    gain_grads = jnp.pad(gain_grads, ((0, 0), (0, 5), (0, 0)))
    (value_grad, gains_out, feed_out_2, down_rows, down_other, in_mine_rows, in_other_rows,
     out_other) = normed_grad_of(
        projected_grad, in_cols, normed_all, layer_input, jnp.broadcast_to(first_all[None], (8, width)),
        act, down_cols, gain_grads, down_half, out_rows, 5,
    )
    input_grad = middle_grad + value_grad
    feed_out = jnp.concatenate([feed_out_0, feed_out_1, feed_out_2], axis=1)
    layer_output = (middle + feed_out).astype(bf16)

    def both_halves(mine, other):
        low = jnp.where(dp == 0, mine, other)
        high = jnp.where(dp == 0, other, mine)
        return jnp.concatenate([low, high]).astype(f32)

    return (
        layer_output,
        input_grad,
        gains_out[0],
        both_halves(in_mine_rows, in_other_rows),
        out_rows.astype(f32) + out_other.astype(f32),
        gains_out[2],
        gains_out[1],
        both_halves(gate_up_rows, gate_up_other),
        both_halves(down_rows, down_other),
    )


def solution(mesh):
    one_group = mesh.shape[AXIS] == H and mesh.shape["dp"] == 2
    return jax.shard_map(
        body if one_group else body_groups,
        mesh=mesh,
        in_specs=(
            P(("dp", "fsdp"), None),
            P("fsdp"),
            P("fsdp", None),
            P("fsdp", None),
            P("fsdp"),
            P("fsdp"),
            P("fsdp", None),
            P("fsdp", None),
            P("dp", None),
            P(("dp", "fsdp"), None),
        ),
        out_specs=(
            P(("dp", "fsdp"), None),
            P(("dp", "fsdp"), None),
            P("fsdp"),
            P("fsdp", None),
            P("fsdp", None),
            P("fsdp"),
            P("fsdp"),
            P("fsdp", None),
            P("fsdp", None),
        ),
        check_vma=False,
    )
```

```python
import functools
import math

import jax
import jax.numpy as jnp
from jax import lax
from jax.experimental import pallas as pl
from jax.experimental.pallas import tpu as pltpu
from jax.sharding import PartitionSpec as P

H = 16
DH = 128
FF = 8192
SEG = 1024

highest = lax.Precision.HIGHEST
epsilon = 1e-06
f32 = jnp.float32
bf16 = jnp.bfloat16
AXIS = "fsdp"


def feature(values):
    return jax.nn.elu(values) + 1.0


def feature_slope(values):
    return jnp.where(values > 0, 1.0, jnp.exp(jnp.minimum(values, 0.0)))


def norm_forward(values, gain):
    factor = lax.rsqrt(jnp.mean(values * values, axis=-1, keepdims=True) + epsilon)
    return (values * factor * gain, factor)


def norm_backward(values, factor, gain, upstream):
    scaled = upstream * gain
    gain_grad = jnp.sum(upstream * values * factor, axis=0)
    value_grad = factor * scaled - values * (factor * factor * factor) * jnp.mean(
        scaled * values, axis=-1, keepdims=True
    )
    return (value_grad, gain_grad)


def dot(left, right, dims):
    return lax.dot_general(left, right, ((dims[0], dims[1]), ((), ())), preferred_element_type=f32)


def rows_dot(left, right):
    return dot(left, right, ((0,), (0,)))


def cols_dot(left, right):
    return dot(left, right, ((1,), (1,)))


class Layout:
    def __init__(self):
        self.count = lax.axis_size(AXIS)
        self.groups = self.count // H
        self.place = lax.axis_index(AXIS)
        self.head = self.place % H
        self.group = self.place // H
        self.inside = None
        self.across = None
        if self.groups > 1:
            self.inside = [[g * H + j for j in range(H)] for g in range(self.groups)]
            self.across = [[g * H + j for g in range(self.groups)] for j in range(H)]

    def gather(self, block):
        return lax.all_gather(block, AXIS, axis=0, tiled=True, axis_index_groups=self.inside)

    def gather_all(self, block):
        return lax.all_gather(block, AXIS, axis=0, tiled=True)

    def scatter_sum(self, whole):
        return lax.psum_scatter(
            whole, AXIS, scatter_dimension=0, tiled=True, axis_index_groups=self.inside
        )

    def columns(self, block, parts):
        rows, width = block.shape
        each = width // (parts * H)
        if self.groups == 1:
            split = block.reshape(rows, parts, H, each)
            out = lax.all_to_all(split, AXIS, 2, 0, tiled=True)
            return out.reshape(rows * self.count, parts * each)
        whole = self.gather_all(block).reshape(rows * self.count, parts, H, each)
        out = lax.dynamic_index_in_dim(whole, self.head, 2, False)
        return out.reshape(rows * self.count, parts * each)

    def own_rows(self, grad, parts):
        rows, width = grad.shape
        each = width // parts
        if self.groups == 1:
            split = grad.astype(bf16).reshape(rows, parts, 1, each)
            out = lax.all_to_all(split, AXIS, 0, 2, tiled=True)
            return out.reshape(rows // self.count, parts * H * each)
        whole = jnp.zeros((rows, parts, H, each), f32)
        whole = lax.dynamic_update_slice_in_dim(
            whole, grad.reshape(rows, parts, 1, each), self.head, 2
        )
        return lax.psum_scatter(
            whole.reshape(rows, parts * H * each), AXIS, scatter_dimension=0, tiled=True
        )

    def to_tokens(self, by_head):
        tokens, each = by_head.shape
        out = lax.all_to_all(
            by_head.reshape(H, tokens // H, each), AXIS, 0, 0, tiled=False,
            axis_index_groups=self.inside,
        )
        return out.transpose(1, 0, 2).reshape(tokens // H, H * each)

    def to_heads(self, by_token):
        tokens, width = by_token.shape
        split = by_token.reshape(tokens, H, width // H).transpose(1, 0, 2)
        out = lax.all_to_all(
            split, AXIS, 0, 0, tiled=False, axis_index_groups=self.inside
        )
        return out.reshape(H * tokens, width // H)


def carry_forward(layout, delta, count, fresh):
    segments = delta.shape[0]

    def walk(state):
        before = []
        for s in range(segments):
            state = jax.tree.map(lambda a: jnp.where(fresh[s], jnp.zeros_like(a), a), state)
            before.append(state)
            state = (state[0] + delta[s], state[1] + count[s])
        return before, state

    state = (jnp.zeros_like(delta[0]), jnp.zeros_like(count[0]))
    if layout.groups > 1:
        _, last = walk(state)
        renewed = jnp.any(fresh).astype(f32)
        every = jax.tree.map(
            lambda a: lax.all_gather(a, AXIS, axis_index_groups=layout.across), last + (renewed,)
        )
        for g in range(layout.groups - 1):
            keep = every[2][g] < 0.5
            after = jax.tree.map(lambda a, e: jnp.where(keep, a, 0.0) + e[g], state, every[:2])
            state = jax.tree.map(lambda a, b: jnp.where(g < layout.group, b, a), state, after)
    before, _ = walk(state)
    return jnp.stack([b[0] for b in before]), jnp.stack([b[1] for b in before])


def carry_backward(layout, state_grad, norm_grad, fresh):
    segments = state_grad.shape[0]

    def walk(state):
        after = [None] * segments
        for s in reversed(range(segments)):
            after[s] = state
            state = (state[0] + state_grad[s], state[1] + norm_grad[s])
            state = jax.tree.map(lambda a: jnp.where(fresh[s], jnp.zeros_like(a), a), state)
        return after, state

    state = (jnp.zeros_like(state_grad[0]), jnp.zeros_like(norm_grad[0]))
    if layout.groups > 1:
        _, first = walk(state)
        renewed = jnp.any(fresh).astype(f32)
        every = jax.tree.map(
            lambda a: lax.all_gather(a, AXIS, axis_index_groups=layout.across), first + (renewed,)
        )
        for g in reversed(range(1, layout.groups)):
            keep = every[2][g] < 0.5
            before = jax.tree.map(lambda a, e: jnp.where(keep, a, 0.0) + e[g], state, every[:2])
            state = jax.tree.map(lambda a, b: jnp.where(g > layout.group, b, a), state, before)
    after, _ = walk(state)
    return jnp.stack([a[0] for a in after]), jnp.stack([a[1] for a in after])


def body_groups(
    layer_input,
    first_gain,
    in_weight,
    out_weight,
    mix_gate,
    second_gain,
    gate_up,
    down_weight,
    document_starts,
    cotangent,
):
    layout = Layout()
    tokens, width = layer_input.shape
    group_tokens = tokens * H
    segments = group_tokens // SEG
    scale = 1.0 / math.sqrt(DH)

    gains = jnp.stack([first_gain, second_gain])
    gains = lax.all_gather(gains, AXIS, axis=1, tiled=True).astype(f32)
    first_all, second_all = gains[0], gains[1]
    if layout.groups == 1:
        mix_own = mix_gate
    else:
        mix_own = lax.dynamic_slice_in_dim(layout.gather_all(mix_gate), layout.head * DH, DH)
    mix = jax.nn.sigmoid(mix_own.astype(f32))[None]

    inputs = layer_input.astype(f32)
    normed, first_factor = norm_forward(inputs, first_all)
    normed_all = layout.gather(normed.astype(bf16))
    in_cols = layout.columns(in_weight, 3)
    out_all = layout.gather_all(out_weight)
    cot_all = layout.gather(cotangent)
    gate_up_cols = layout.columns(gate_up, 2)
    down_cols = layout.columns(down_weight, 1)

    projected = jnp.dot(normed_all, in_cols, preferred_element_type=f32).astype(bf16)
    by_segment = projected.reshape(segments, SEG, 3, DH)
    query, key, value = by_segment[:, :, 0], by_segment[:, :, 1], by_segment[:, :, 2]
    index = jnp.arange(SEG, dtype=jnp.int32)
    allowed = index[None, :] <= index[:, None]

    def attention_scores():
        raw = jnp.einsum("sqc,skc->sqk", query, key, preferred_element_type=f32) * scale
        return jnp.where(allowed[None], raw, -1e30)

    scores = attention_scores()
    top = jnp.max(scores, axis=-1, keepdims=True)
    expo = jnp.exp(scores - top)
    total = jnp.sum(expo, axis=-1, keepdims=True)
    log_total = top + jnp.log(total)
    probs_low = (expo / total).astype(bf16)
    local_out = jnp.einsum("sqk,skc->sqc", probs_low, value, preferred_element_type=f32)

    query_f, key_f, value_f = query.astype(f32), key.astype(f32), value.astype(f32)
    query_feature = feature(query_f).astype(bf16)
    key_feature = feature(key_f).astype(bf16)
    delta = jnp.einsum("slc,sla->sca", key_feature, value, preferred_element_type=f32)
    count = jnp.sum(key_feature.astype(f32), axis=1)
    numbers = layout.group * segments + jnp.arange(segments)
    fresh = (numbers == 0) | (
        lax.dynamic_slice_in_dim(document_starts[0], layout.group * segments, segments) > 0
    )
    memory, normal = carry_forward(layout, delta, count, fresh)
    query_feature_f = query_feature.astype(f32)
    numerator = jnp.einsum("sie,sej->sij", query_feature_f, memory, precision=highest)
    raw_denom = jnp.einsum("sik,sk->si", query_feature_f, normal, precision=highest)[..., None]
    denom = jnp.maximum(raw_denom, 1.0)
    memory_out = numerator / denom
    combined = mix * memory_out + (1.0 - mix) * local_out
    combined_head = combined.reshape(group_tokens, DH).astype(bf16)
    combined_low = layout.to_tokens(combined_head)
    attended = jnp.dot(combined_low, out_all, preferred_element_type=f32)
    middle = inputs + attended

    hidden, second_factor = norm_forward(middle, second_all)
    hidden_all = layout.gather(hidden.astype(bf16))
    act_grad = jnp.dot(cot_all, down_cols, preferred_element_type=f32)
    both = jnp.dot(hidden_all, gate_up_cols, preferred_element_type=f32)
    half = both.shape[1] // 2
    gate_part, up_part = both[:, :half], both[:, half:]
    sigma = jax.nn.sigmoid(gate_part)
    silu = gate_part * sigma
    activated = (silu * up_part).astype(bf16)
    silu_slope = sigma * (1.0 + gate_part * (1.0 - sigma))
    feed_grad = jnp.concatenate(
        [act_grad * up_part * silu_slope, act_grad * silu], axis=1
    ).astype(bf16)
    feed_out = layout.scatter_sum(cols_dot(activated, down_cols).astype(bf16))
    hidden_grad = layout.scatter_sum(cols_dot(feed_grad, gate_up_cols).astype(bf16))
    layer_output = (middle + feed_out.astype(f32)).astype(bf16)
    gate_up_part = layout.own_rows(rows_dot(hidden_all, feed_grad), 2)
    down_part = layout.own_rows(rows_dot(cot_all, activated), 1)

    upstream = cotangent.astype(f32)
    middle_norm_grad, second_local = norm_backward(
        middle, second_factor, second_all, hidden_grad.astype(f32)
    )
    middle_grad = upstream + middle_norm_grad
    attended_grad = middle_grad.astype(bf16)
    attended_grad_all = layout.gather(attended_grad)
    combined_grad = layout.to_heads(cols_dot(attended_grad, out_all).astype(bf16))
    combined_grad = combined_grad.astype(f32).reshape(segments, SEG, DH)
    out_rows_grad = rows_dot(combined_head, attended_grad_all)
    if layout.groups == 1:
        out_part = out_rows_grad
    else:
        whole = jnp.zeros((H * DH, width), f32)
        whole = lax.dynamic_update_slice_in_dim(whole, out_rows_grad, layout.head * DH, 0)
        out_part = lax.psum_scatter(whole, AXIS, scatter_dimension=0, tiled=True)
    mix_local = jnp.sum(combined_grad * (memory_out - local_out), axis=(0, 1)) * (
        mix * (1.0 - mix)
    ).reshape(DH)

    memory_grad = combined_grad * mix
    local_grad = (combined_grad * (1.0 - mix)).astype(bf16)
    numer_grad = memory_grad / denom
    denom_grad = -jnp.sum(memory_grad * memory_out, axis=-1, keepdims=True) / denom
    raw_grad = jnp.where(raw_denom > 1.0, denom_grad, 0.0)
    query_feature_grad = (
        jnp.einsum("sij,sej->sie", numer_grad, memory, precision=highest)
        + raw_grad * normal[:, None]
    )
    state_grad = jnp.einsum("sie,sij->sej", query_feature_f, numer_grad, precision=highest)
    norm_grad = jnp.sum(raw_grad * query_feature_f, axis=1)
    delta_grad, count_grad = carry_backward(layout, state_grad, norm_grad, fresh)
    key_feature_grad = (
        jnp.einsum("sij,sej->sie", value_f, delta_grad, precision=highest) + count_grad[:, None]
    )
    value_memory_grad = jnp.einsum(
        "sie,sej->sij", key_feature.astype(f32), delta_grad, precision=highest
    )
    query_memory_grad = query_feature_grad * feature_slope(query_f)
    key_memory_grad = key_feature_grad * feature_slope(key_f)

    probs = jnp.exp(attention_scores() - log_total)
    prob_grad = jnp.einsum("sqc,skc->sqk", local_grad, value, preferred_element_type=f32)
    row_term = jnp.sum(probs * prob_grad, axis=-1, keepdims=True)
    score_grad = (probs * (prob_grad - row_term)).astype(bf16)
    query_grad = query_memory_grad + scale * jnp.einsum(
        "sqk,skc->sqc", score_grad, key, preferred_element_type=f32
    )
    key_grad = key_memory_grad + scale * jnp.einsum(
        "sqk,sqc->skc", score_grad, query, preferred_element_type=f32
    )
    value_grad = value_memory_grad + jnp.einsum(
        "sqk,sqc->skc", probs.astype(bf16), local_grad, preferred_element_type=f32
    )
    projected_grad = (
        jnp.stack([query_grad, key_grad, value_grad], axis=2)
        .reshape(group_tokens, 3 * DH)
        .astype(bf16)
    )
    normed_grad = layout.scatter_sum(cols_dot(projected_grad, in_cols).astype(bf16))
    in_part = layout.own_rows(rows_dot(normed_all, projected_grad), 3)
    input_norm_grad, first_local = norm_backward(
        inputs, first_factor, first_all, normed_grad.astype(f32)
    )
    input_grad = middle_grad + input_norm_grad

    gains_part = lax.psum_scatter(
        jnp.stack([first_local, second_local]), AXIS, scatter_dimension=1, tiled=True
    )
    if layout.groups == 1:
        mix_part = mix_local
    else:
        whole = jnp.zeros((H * DH,), f32)
        whole = lax.dynamic_update_slice_in_dim(whole, mix_local, layout.head * DH, 0)
        mix_part = lax.psum_scatter(whole, AXIS, scatter_dimension=0, tiled=True)

    def over_sequences(part):
        return lax.psum(part.astype(bf16), "dp").astype(f32)

    small = over_sequences(jnp.concatenate([gains_part, mix_part[None]]))
    return (
        layer_output,
        input_grad,
        small[0],
        over_sequences(in_part),
        over_sequences(out_part),
        small[2],
        small[1],
        over_sequences(gate_up_part),
        over_sequences(down_part),
    )


MESH = pl.DeviceIdType.MESH
LIMIT = 60 * 2**20
FILL = ((0, 512), (512, 1024), (1536, 512))
ROWS = 256
dma = pltpu.SemaphoreType.DMA
VM = pltpu.VMEM


def vmem():
    return pl.BlockSpec(memory_space=pltpu.VMEM)


def anywhere():
    return pl.BlockSpec(memory_space=pl.ANY)


class Spot:
    def __init__(self):
        self.dp = lax.axis_index("dp")
        self.me = lax.axis_index(AXIS)
        self.z = self.me // 4
        self.y = (self.me // 2) % 2
        self.c = self.me % 2

    def at(self, z, y, c):
        return z * 4 + y * 2 + c

    def partner(self, k):
        out = self.me
        for bit in (1, 2, 4, 8):
            if k & bit:
                out = out + bit - 2 * bit * ((self.me // bit) % 2)
        return out

    def arrival(self, j):
        if j == 0:
            return self.z
        ends = jnp.where(self.z == 0, j, 3 - j)
        middle = {1: (0, 3), 2: (2, 1), 3: (3, 0)}[j]
        inner = jnp.where(self.z == 1, middle[0], middle[1])
        return jnp.where((self.z == 0) | (self.z == 3), ends, inner)


def greet(s, plane=True, other=True):
    ids = []
    if plane:
        ids += [{AXIS: (s.me + k) % 16} for k in range(1, 16)]
    else:
        ids += [{AXIS: s.at((s.z + k) % 4, s.y, s.c)} for k in (1, 2, 3)]
        ids += [{AXIS: s.at(s.z, 1 - s.y, s.c)}, {AXIS: s.at(s.z, s.y, 1 - s.c)}]
    if other:
        ids += [{"dp": 1 - s.dp}]
    barrier = pltpu.get_barrier_semaphore()
    for d in ids:
        pl.semaphore_signal(barrier, inc=1, device_id=d, device_id_type=MESH)
    pl.semaphore_wait(barrier, len(ids))


def send(src, dst, ssem, rsem, to):
    return pltpu.make_async_remote_copy(
        src_ref=src, dst_ref=dst, send_sem=ssem, recv_sem=rsem,
        device_id={AXIS: to}, device_id_type=MESH,
    )


def send_over(src, dst, ssem, rsem, s):
    return pltpu.make_async_remote_copy(
        src_ref=src, dst_ref=dst, send_sem=ssem, recv_sem=rsem,
        device_id={"dp": 1 - s.dp}, device_id_type=MESH,
    )


def merged(*lists):
    keyed = []
    for n, tasks in enumerate(lists):
        keyed += [((i + 0.5) / len(tasks), n, i, t) for i, t in enumerate(tasks)]
    for _, _, _, t in sorted(keyed, key=lambda e: e[:3]):
        t()


class Gather:
    chunks = 4

    @classmethod
    def sems(cls):
        return [dma((cls.chunks, 4))] * 5 + [dma((cls.chunks, 8))] * 2

    def __init__(self, s, src, dst, sems):
        self.s, self.src, self.dst = s, src, dst
        self.zr, self.zu, self.zd, self.ys, self.yr, self.ss, self.sr = sems[:7]
        self.rows = 128 // self.chunks
        self.skip = 0

    def block(self, ch, z, y, c):
        start = self.s.at(z, y, c) * 128 + self.skip + ch * self.rows
        return self.dst.at[pl.ds(pl.multiple_of(start, self.rows), self.rows)]

    def own(self, ch):
        start = pl.multiple_of(self.skip + ch * self.rows, self.rows)
        return self.src.at[pl.ds(start, self.rows)]

    def zcopy(self, ch, zo, up, own=False):
        s = self.s
        dst = self.block(ch, zo, s.y, s.c)
        to = s.at(s.z + 1 if up else s.z - 1, s.y, s.c)
        return send(
            self.own(ch) if own else dst, dst,
            (self.zu if up else self.zd).at[ch, zo], self.zr.at[ch, zo], to,
        )

    def ycopy(self, ch, zo, own=False):
        s = self.s
        dst = self.block(ch, zo, s.y, s.c)
        src = self.own(ch) if own else dst
        return send(src, dst, self.ys.at[ch, zo], self.yr.at[ch, zo], s.at(s.z, 1 - s.y, s.c))

    def scopy(self, ch, zo, yo, own=False):
        s = self.s
        dst = self.block(ch, zo, yo, s.c)
        n = zo * 2 + yo
        src = self.own(ch) if own else dst
        return send(src, dst, self.ss.at[ch, n], self.sr.at[ch, n], s.at(s.z, s.y, 1 - s.c))

    def start(self):
        s = self.s
        for ch in range(self.chunks):
            pl.when(s.z < 3)(lambda: self.zcopy(ch, s.z, True, True).start())
            pl.when(s.z > 0)(lambda: self.zcopy(ch, s.z, False, True).start())
            self.ycopy(ch, s.z, True).start()
            self.scopy(ch, s.z, s.y, True).start()

    def passed_on(self, ch, zo, yo):
        self.scopy(ch, zo, yo).start()

    def z_arrive(self, ch, j):
        s = self.s
        zo = s.arrival(j)
        self.zcopy(ch, zo, True).wait_recv()
        pl.when((zo < s.z) & (s.z < 3))(lambda: self.zcopy(ch, zo, True).start())
        pl.when((zo > s.z) & (s.z > 0))(lambda: self.zcopy(ch, zo, False).start())
        self.ycopy(ch, zo).start()
        self.passed_on(ch, zo, s.y)

    def y_arrive(self, ch, j):
        s = self.s
        zo = s.arrival(j)
        b = self.block(ch, zo, 1 - s.y, s.c)
        send(b, b, self.ys.at[ch, zo], self.yr.at[ch, zo], s.me).wait_recv()
        self.passed_on(ch, zo, 1 - s.y)

    def s_arrive(self, j):
        s = self.s
        zo = s.arrival(j)
        for ch in range(self.chunks):
            for yo in range(2):
                n = zo * 2 + yo
                b = self.block(ch, zo, yo, 1 - s.c)
                send(b, b, self.ss.at[ch, n], self.sr.at[ch, n], s.me).wait_recv()

    def tasks(self, use=None):
        out = []
        for step in range(1, 5):
            for ch in range(self.chunks):
                if step < 4:
                    out.append(functools.partial(self.z_arrive, ch, step))
                out.append(functools.partial(self.y_arrive, ch, step - 1))
                if step == 4 and ch < 3 and use is not None:
                    out.append(functools.partial(use, ch))
            out.append(functools.partial(self.s_arrive, step - 1))
        if use is not None:
            out.append(functools.partial(use, 3))
        return out

    def drain(self):
        s = self.s
        for ch in range(self.chunks):
            for zo in range(4):
                pl.when((s.z < 3) & (zo <= s.z))(lambda: self.zcopy(ch, zo, True).wait_send())
                pl.when((s.z > 0) & (zo >= s.z))(lambda: self.zcopy(ch, zo, False).wait_send())
                self.ycopy(ch, zo).wait_send()
                for yo in range(2):
                    self.scopy(ch, zo, yo).wait_send()


class SharedGather(Gather):
    chunks = 2

    @classmethod
    def sems(cls):
        return Gather.sems.__func__(cls) + [dma((cls.chunks, 8))] * 4

    def __init__(self, s, src, dst, sems):
        super().__init__(s, src, dst, sems)
        self.xs, self.xr, self.ts, self.tr = sems[7:]
        self.rows = 64 // self.chunks
        self.skip = s.dp * 64

    def other(self, ch, z, y, c):
        start = self.s.at(z, y, c) * 128 + (1 - self.s.dp) * 64 + ch * self.rows
        return self.dst.at[pl.ds(pl.multiple_of(start, self.rows), self.rows)]

    def xcopy(self, ch, zo, yo):
        s = self.s
        b = self.block(ch, zo, yo, s.c)
        n = zo * 2 + yo
        return send_over(b, b, self.xs.at[ch, n], self.xr.at[ch, n], s)

    def tcopy(self, ch, zo, yo, own=False):
        s = self.s
        b = self.other(ch, zo, yo, s.c)
        n = zo * 2 + yo
        src = b
        if own:
            start = pl.multiple_of((1 - s.dp) * 64 + ch * self.rows, self.rows)
            src = self.src.at[pl.ds(start, self.rows)]
        return send(src, b, self.ts.at[ch, n], self.tr.at[ch, n], s.at(s.z, s.y, 1 - s.c))

    def start(self):
        super().start()
        for ch in range(self.chunks):
            self.tcopy(ch, self.s.z, self.s.y, True).start()

    def passed_on(self, ch, zo, yo):
        self.xcopy(ch, zo, yo).start()
        self.scopy(ch, zo, yo).start()

    def x_arrive(self, j, yo):
        s = self.s
        zo = s.arrival(j)
        row = s.y if yo == 0 else 1 - s.y
        for ch in range(self.chunks):
            b = self.other(ch, zo, row, s.c)
            n = zo * 2 + row
            send_over(b, b, self.xs.at[ch, n], self.xr.at[ch, n], s).wait_recv()
            self.tcopy(ch, zo, row).start()

    def tasks(self):
        out = super().tasks()
        for j in range(4):
            for yo in range(2):
                if j + yo > 0:
                    out.append(functools.partial(self.x_arrive, j, yo))
        return out

    def finish(self):
        s = self.s
        for ch in range(self.chunks):
            for n in range(8):
                b = self.other(ch, n // 2, n % 2, 1 - s.c)
                send(b, b, self.ts.at[ch, n], self.tr.at[ch, n], s.me).wait_recv()

    def drain(self):
        s = self.s
        super().drain()
        for ch in range(self.chunks):
            for zo in range(4):
                for yo in range(2):
                    self.tcopy(ch, zo, yo).wait_send()
                    far = (s.z != zo) | (s.y != yo)
                    pl.when(far)(lambda: self.xcopy(ch, zo, yo).wait_send())


class Columns:
    @staticmethod
    def sems(parts):
        return [dma((16, parts)), dma((16, parts)), dma((16,)), dma((16,)), dma((parts,))]

    def __init__(self, s, w, dst, parts, sems):
        self.s, self.w, self.dst, self.parts = s, w, dst, parts
        self.e = dst.shape[1] // parts
        self.ps, self.pr, self.xs, self.xr, self.own = sems

    def rows(self, src, half):
        return pl.ds(pl.multiple_of(src * 128 + half * 64, 64), 64)

    def cols(self, p, h):
        return pl.ds(pl.multiple_of(p * 16 * self.e + h * self.e, 128), self.e)

    def copy(self, k, p):
        s = self.s
        to = s.partner(k)
        half = pl.ds(pl.multiple_of(s.dp * 64, 64), 64)
        return send(
            self.w.at[half, self.cols(p, to)],
            self.dst.at[self.rows(s.me, s.dp), pl.ds(p * self.e, self.e)],
            self.ps.at[k, p], self.pr.at[s.me, p], to,
        )

    def local(self, p):
        s = self.s
        return pltpu.make_async_copy(
            self.w.at[:, self.cols(p, s.me)],
            self.dst.at[pl.ds(pl.multiple_of(s.me * 128, 128), 128), pl.ds(p * self.e, self.e)],
            self.own.at[p],
        )

    def begin(self, k):
        for p in range(self.parts):
            (self.copy(k, p) if k else self.local(p)).start()

    def start(self, ahead=16):
        self.ahead = ahead
        for k in range(ahead):
            self.begin(k)

    def over(self, src):
        s = self.s
        b = self.dst.at[self.rows(src, s.dp)]
        return send_over(b, b, self.xs.at[src], self.xr.at[src], s)

    def arrive(self, k):
        s = self.s
        if k + self.ahead - 1 < 16:
            self.begin(k + self.ahead - 1)
        src = s.partner(k)
        for p in range(self.parts):
            b = self.dst.at[self.rows(src, s.dp), pl.ds(p * self.e, self.e)]
            send(b, b, self.ps.at[k, p], self.pr.at[src, p], s.me).wait_recv()
        self.over(src).start()

    def tasks(self):
        return [functools.partial(self.arrive, k) for k in range(1, 16)]

    def finish(self):
        s = self.s
        for k in range(1, 16):
            src = s.partner(k)
            b = self.dst.at[self.rows(src, 1 - s.dp)]
            send_over(b, b, self.xs.at[src], self.xr.at[src], s).wait_recv()
        for p in range(self.parts):
            self.local(p).wait()

    def drain(self):
        s = self.s
        for k in range(1, 16):
            for p in range(self.parts):
                self.copy(k, p).wait_send()
            self.over(s.partner(k)).wait_send()


class Return:
    @staticmethod
    def sems(parts):
        return [dma((16, parts))] * 4 + [dma((parts,))]

    ahead = 16

    def __init__(self, s, src, dst, parts, sems, other=None):
        self.s, self.src, self.dst, self.parts, self.other = s, src, dst, parts, other
        self.e = src.shape[2] // parts
        self.ps, self.pr, self.xs, self.xr, self.own = sems

    def place(self, ref, p, h):
        return ref.at[:, pl.ds(pl.multiple_of(p * 16 * self.e + h * self.e, 128), self.e)]

    def copy(self, k, p):
        s = self.s
        to = s.partner(k)
        return send(
            self.src.at[to, :, pl.ds(p * self.e, self.e)], self.place(self.dst, p, s.me),
            self.ps.at[k, p], self.pr.at[s.me, p], to,
        )

    def local(self, p):
        s = self.s
        return pltpu.make_async_copy(
            self.src.at[s.me, :, pl.ds(p * self.e, self.e)], self.place(self.dst, p, s.me),
            self.own.at[p],
        )

    def begin(self, k):
        for p in range(self.parts):
            if k:
                self.copy(k, p).start()
                continue
            self.local(p).start()
            if self.other is not None:
                self.over(self.s.me, p, own=True).start()

    def start(self, ahead=16):
        self.ahead = ahead
        for k in range(ahead):
            self.begin(k)

    def over(self, h, p, own=False):
        s = self.s
        src = self.src.at[s.me, :, pl.ds(p * self.e, self.e)] if own else self.place(self.dst, p, h)
        return send_over(src, self.place(self.other, p, h), self.xs.at[h, p], self.xr.at[h, p], s)

    def arrive(self, k):
        s = self.s
        if k + self.ahead - 1 < 16:
            self.begin(k + self.ahead - 1)
        h = s.partner(k)
        for p in range(self.parts):
            b = self.place(self.dst, p, h)
            send(b, b, self.ps.at[k, p], self.pr.at[h, p], s.me).wait_recv()
            if self.other is not None:
                self.over(h, p).start()

    def tasks(self):
        return [functools.partial(self.arrive, k) for k in range(1, 16)]

    def finish(self):
        s = self.s
        for p in range(self.parts):
            self.local(p).wait()
        if self.other is not None:
            for k in range(16):
                h = s.partner(k)
                for p in range(self.parts):
                    b = self.place(self.other, p, h)
                    send_over(b, b, self.xs.at[h, p], self.xr.at[h, p], s).wait_recv()
        for k in range(1, 16):
            for p in range(self.parts):
                self.copy(k, p).wait_send()
        if self.other is not None:
            for k in range(16):
                for p in range(self.parts):
                    self.over(s.partner(k), p).wait_send()


class Scatter:
    lag = 3

    @staticmethod
    def scratch(width):
        q = width // 512
        return [
            VM((4, 2, 256, width), bf16), VM((4, 2, 128, width), bf16), VM((4, 2, 128, width), bf16),
            VM((4, 128, width), bf16), VM((5, 128, width), bf16),
            dma((4, q, 2)), dma((4, q, 2)), dma((4, q)), dma((4, q)), dma((4, q)), dma((5, q)),
        ]

    def __init__(self, s, left, right, out, scratch, first=0):
        self.s, self.left, self.right, self.out, self.first = s, left, right, out, first
        self.part, self.sib, self.mid, self.got_y, self.got_z = scratch[:5]
        self.ss, self.sr, self.ys, self.yr, self.zs, self.zr = scratch[5:]
        self.cols = 512
        self.pieces = out.shape[1] // 512
        self.order = [s.arrival(j) for j in (3, 2, 1, 0)]

    def w(self, h):
        return pl.ds(h * self.cols, self.cols)

    def compute(self, k, h, yd, slot):
        tok = pl.multiple_of((self.order[k] * 2 + yd) * 256, 256)
        p = cols_dot(self.left[pl.ds(tok, 256), :], self.right[pl.ds(self.first + h * self.cols, self.cols), :])
        self.part[k, slot, :, self.w(h)] = p.astype(bf16)

    def sib_copy(self, k, h, slot):
        s = self.s
        src = self.part.at[k, slot, pl.ds(pl.multiple_of((1 - s.c) * 128, 128), 128), self.w(h)]
        return send(
            src, self.sib.at[k, slot, :, self.w(h)],
            self.ss.at[k, h, slot], self.sr.at[k, h, slot], s.at(s.z, s.y, 1 - s.c),
        )

    def y_copy(self, k, h):
        s = self.s
        return send(
            self.mid.at[k, 0, :, self.w(h)], self.got_y.at[k, :, self.w(h)],
            self.ys.at[k, h], self.yr.at[k, h], s.at(s.z, 1 - s.y, s.c),
        )

    def z_copy(self, k, h):
        s = self.s
        to = self.order[k]
        up = to > s.z
        hop = jnp.where(up, s.z + 1, s.z - 1)
        slot = jnp.where(up | (hop != to), to, 4)
        return send(
            self.mid.at[k, 1, :, self.w(h)], self.got_z.at[slot, :, self.w(h)],
            self.zs.at[k, h], self.zr.at[slot, h], s.at(hop, s.y, s.c),
        )

    def z_wait(self, slot, h):
        b = self.got_z.at[slot, :, self.w(h)]
        send(b, b, self.zs.at[0, h], self.zr.at[slot, h], self.s.me).wait_recv()

    def fold(self, k, h, slot):
        s = self.s
        self.sib_copy(k, h, slot).wait_recv()
        own = self.part[k, slot, pl.ds(pl.multiple_of(s.c * 128, 128), 128), self.w(h)]
        total = own.astype(f32) + self.sib[k, slot, :, self.w(h)].astype(f32)
        self.mid[k, slot, :, self.w(h)] = total.astype(bf16)

    def after_y(self, k, h):
        s = self.s
        w = self.w(h)
        self.y_copy(k, h).wait_recv()
        total = self.mid[k, 1, :, w].astype(f32) + self.got_y[k, :, w].astype(f32)
        if k == 3:
            self.out[:, w] = total
            return
        to = self.order[k]
        first = jnp.where(to > s.z, s.z == 0, s.z == 3)

        @pl.when(first)
        def _():
            self.mid[k, 1, :, w] = total.astype(bf16)

        @pl.when(jnp.logical_not(first))
        def _():
            self.z_wait(to, h)
            self.mid[k, 1, :, w] = (total + self.got_z[to, :, w].astype(f32)).astype(bf16)

        self.z_copy(k, h).start()

    def tasks(self):
        steps = [(k, h) for k in range(4) for h in range(self.pieces)]
        s = self.s

        def step(i):
            k, h = steps[i]
            self.compute(k, h, 1 - s.y, 0)
            self.sib_copy(k, h, 0).start()
            self.compute(k, h, s.y, 1)
            self.sib_copy(k, h, 1).start()
            self.fold(k, h, 0)
            self.y_copy(k, h).start()
            self.fold(k, h, 1)

        out = []
        for i in range(len(steps) + self.lag):
            if i < len(steps):
                out.append(functools.partial(step, i))
            if i >= self.lag:
                out.append(functools.partial(self.after_y, *steps[i - self.lag]))
        return out

    def finish(self):
        s = self.s
        for h in range(self.pieces):
            w = self.w(h)

            @pl.when(s.z > 0)
            def _():
                self.z_wait(s.z, h)
                self.out[:, w] += self.got_z[s.z, :, w].astype(f32)

            @pl.when(s.z < 3)
            def _():
                self.z_wait(4, h)
                self.out[:, w] += self.got_z[4, :, w].astype(f32)

        for k in range(4):
            for h in range(self.pieces):
                self.sib_copy(k, h, 0).wait_send()
                self.sib_copy(k, h, 1).wait_send()
                self.y_copy(k, h).wait_send()
                if k < 3:
                    self.z_copy(k, h).wait_send()


class Weigh:
    steps = 8

    @classmethod
    def scratch(cls, cols):
        return [
            VM((16, 64, cols), f32), VM((16, 64, cols), bf16), VM((16, 64, cols), bf16),
            dma((cls.steps,)), dma((cls.steps,)),
        ]

    def __init__(self, s, left, right, half, scratch, back=None):
        self.s, self.left, self.right, self.half, self.back = s, left, right, half, back
        self.mine, self.sent, self.got, self.xs, self.xr = scratch

    def at(self, n):
        return self.s.partner(2 * n) // 2

    def copy(self, n):
        i = self.at(n)
        w = pl.ds(2 * i, 2)
        return send_over(self.sent.at[w], self.got.at[w], self.xs.at[i], self.xr.at[i], self.s)

    def compute(self, n):
        i = self.at(n)
        low = self.s.dp == 0
        cols = pl.ds(pl.multiple_of(i * 256, 256), 256)
        got = rows_dot(self.left[:, cols], self.right[...])
        for m in range(2):
            a, b = got[m * 128:m * 128 + 64], got[m * 128 + 64:m * 128 + 128]
            self.mine[2 * i + m] = jnp.where(low, a, b)
            self.sent[2 * i + m] = jnp.where(low, b, a).astype(bf16)
        self.copy(n).start()

    def fold(self, n):
        self.copy(n).wait_recv()
        w = pl.ds(2 * self.at(n), 2)
        self.half[w] = (self.mine[w] + self.got[w].astype(f32)).astype(bf16)
        if self.back is not None:
            self.back.begin(2 * n)
            self.back.begin(2 * n + 1)

    def products(self):
        return [functools.partial(self.compute, i) for i in range(self.steps)]

    def folds(self):
        return [functools.partial(self.fold, i) for i in range(self.steps)]

    def drain(self):
        for i in range(self.steps):
            self.copy(i).wait_send()


def nothing(n):
    return [lambda: None] * n


def halves_of(refs, counts):
    out, at = [], 0
    for n in counts:
        out.append(refs[at:at + n])
        at += n
    return out


def communicate(kernel, name, number, ins, in_specs, outs, out_specs, scratch, flops=0):
    return pl.pallas_call(
        kernel, out_shape=outs, in_specs=in_specs, out_specs=out_specs, scratch_shapes=scratch,
        compiler_params=pltpu.CompilerParams(
            collective_id=number, has_side_effects=True, vmem_limit_bytes=LIMIT
        ),
        cost_estimate=pl.CostEstimate(flops=flops, bytes_accessed=2**24, transcendentals=0),
        name=name,
    )(*ins)


def project_kernel(x, gains, in_w, normed_all, in_cols, gains_all, projected, x_all, normed, row,
                   copies, g_s, g_r, *rest):
    gather_sems, col_sems = halves_of(rest, [7, 5])
    s = Spot()
    greet(s)

    def gain_copy(k):
        return send(gains, gains_all.at[s.me], g_s.at[k], g_r.at[s.me], s.partner(k))

    gather = Gather(s, x, x_all, gather_sems)
    gather.start()
    for k in range(1, 16):
        gain_copy(k).start()
    columns = Columns(s, in_w, in_cols, 3, col_sems)
    columns.start()
    gains_all[s.me] = gains[...]
    x_all[pl.ds(pl.multiple_of(s.me * 128, 128), 128), :] = x[...]

    def gain_row():
        for k in range(1, 16):
            src = s.partner(k)
            b = gains_all.at[src]
            send(b, b, g_s.at[k], g_r.at[src], s.me).wait_recv()
        for j in range(16):
            row[0:1, pl.ds(j * 128, 128)] = gains_all[j, 0:1, :]

    def out_copy(j):
        tok = pl.ds(pl.multiple_of(s.arrival(j) * 512, 512), 512)
        return pltpu.make_async_copy(normed.at[tok], normed_all.at[tok], copies.at[j])

    def use(j):
        if j == 0:
            columns.finish()
            gain_row()
        for n in range(4):
            rows = pl.ds(pl.multiple_of(s.arrival(j) * 512 + n * 128, 128), 128)
            values = x_all[rows, :].astype(f32)
            factor = lax.rsqrt(jnp.mean(values * values, axis=-1, keepdims=True) + epsilon)
            normed[rows, :] = (values * factor * row[0:1, :]).astype(bf16)
        out_copy(j).start()
        tok = pl.ds(pl.multiple_of(s.arrival(j) * 512, 512), 512)
        out = jnp.dot(normed[tok, :], in_cols[...], preferred_element_type=f32)
        projected[tok, :] = out.astype(bf16)

    merged(gather.tasks(use), nothing(2) + columns.tasks() + nothing(8))
    gather.drain()
    columns.drain()
    for k in range(1, 16):
        gain_copy(k).wait_send()
    for j in range(4):
        out_copy(j).wait()


def project(x, gains, in_weight, number):
    tokens, width = x.shape
    return communicate(
        project_kernel, "project", number, (x, gains, in_weight), [vmem(), vmem(), anywhere()],
        [
            jax.ShapeDtypeStruct((16 * tokens, width), bf16),
            jax.ShapeDtypeStruct((width, 3 * DH), bf16),
            jax.ShapeDtypeStruct((16, 8, 128), f32),
            jax.ShapeDtypeStruct((16 * tokens, 3 * DH), bf16),
        ],
        [anywhere(), vmem(), vmem(), vmem()],
        [
            VM((16 * tokens, width), bf16), VM((16 * tokens, width), bf16), VM((8, width), f32),
            dma((4,)), dma((16,)), dma((16,)),
        ] + Gather.sems() + Columns.sems(3),
    )


def kernel_feature(t):
    return jnp.where(t > 0, t + 1.0, jnp.exp(jnp.minimum(t, 0.0)))


def dot_high(left, right, dims=((1,), (0,))):
    return lax.dot_general(
        left, right, (dims, ((), ())), preferred_element_type=f32, precision=highest
    )


def scores_of(query, keys, first):
    raw = cols_dot(query, keys) * (1.0 / math.sqrt(DH))
    row = lax.broadcasted_iota(jnp.int32, raw.shape, 0) + first
    col = lax.broadcasted_iota(jnp.int32, raw.shape, 1)
    return jnp.where(col <= row, raw, -1e30)


class Attend:
    def __init__(self, qkv, keep, mix, local, mem_out, lse, combined, memory, normal):
        self.qkv, self.keep, self.mix = qkv, keep, mix
        self.local, self.mem_out, self.lse, self.combined = local, mem_out, lse, combined
        self.memory, self.normal = memory, normal
        self.segments = qkv.shape[0] // SEG

    def states(self):
        state = jnp.zeros((DH, DH), f32)
        norm = jnp.zeros((1, DH), f32)
        for n in range(self.segments):
            keep = self.keep[n, 0:1, :]
            state, norm = state * keep, norm * keep
            self.memory[n] = state
            self.normal[n, 0:1, :] = norm
            if n + 1 < self.segments:
                rows = pl.ds(n * SEG, SEG)
                fk = kernel_feature(self.qkv[rows, DH:2 * DH].astype(f32)).astype(bf16)
                state = state + rows_dot(fk, self.qkv[rows, 2 * DH:])
                norm = norm + jnp.sum(fk.astype(f32), axis=0, keepdims=True)

    def block(self, n, i):
        rows = pl.ds(n * SEG + i * ROWS, ROWS)
        seen = pl.ds(n * SEG, (i + 1) * ROWS)
        query = self.qkv[rows, :DH]
        scores = scores_of(query, self.qkv[seen, DH:2 * DH], i * ROWS)
        top = jnp.max(scores, axis=-1, keepdims=True)
        expo = jnp.exp(scores - top)
        total = jnp.sum(expo, axis=-1, keepdims=True)
        probs = (expo * (1.0 / total)).astype(bf16)
        local = jnp.dot(probs, self.qkv[seen, 2 * DH:], preferred_element_type=f32)
        fq = kernel_feature(query.astype(f32)).astype(bf16).astype(f32)
        den = jnp.maximum(jnp.sum(fq * self.normal[n, 0:1, :], axis=-1, keepdims=True), 1.0)
        mem_out = dot_high(fq, self.memory[n]) / den
        mix = self.mix[0:1, :]
        self.local[rows, :] = local
        self.mem_out[rows, :] = mem_out
        self.lse[rows, :] = jnp.broadcast_to(top + jnp.log(total), (ROWS, DH))
        self.combined[rows, :] = (mix * mem_out + (1.0 - mix) * local).astype(bf16)

    def blocks(self):
        return [(n, i) for n in range(self.segments) for i in range(SEG // ROWS)]


class AttendBack:
    def __init__(self, qkv, keep, mix, local, mem_out, lse, memory, normal, upstream, grad,
                 mix_grad, dk, dv, state_grad, norm_grad):
        self.qkv, self.keep, self.mix = qkv, keep, mix
        self.local, self.mem_out, self.lse = local, mem_out, lse
        self.memory, self.normal, self.upstream, self.grad = memory, normal, upstream, grad
        self.mix_grad, self.dk, self.dv = mix_grad, dk, dv
        self.state_grad, self.norm_grad = state_grad, norm_grad
        self.segments = qkv.shape[0] // SEG

    def clear(self):
        self.mix_grad[...] = jnp.zeros_like(self.mix_grad)
        self.dk[...] = jnp.zeros_like(self.dk)
        self.dv[...] = jnp.zeros_like(self.dv)
        self.state_grad[...] = jnp.zeros_like(self.state_grad)
        self.norm_grad[...] = jnp.zeros_like(self.norm_grad)

    def block(self, n, i):
        scale = 1.0 / math.sqrt(DH)
        rows = pl.ds(n * SEG + i * ROWS, ROWS)
        seen = pl.ds(n * SEG, (i + 1) * ROWS)
        query = self.qkv[rows, :DH]
        keys = self.qkv[seen, DH:2 * DH]
        values = self.qkv[seen, 2 * DH:]
        up = self.upstream[rows, :].astype(f32)
        mem_out = self.mem_out[rows, :]
        mix = self.mix[0:1, :]
        mixed = jnp.sum(up * (mem_out - self.local[rows, :]), axis=0, keepdims=True)
        self.mix_grad[0:1, :] += mixed * mix * (1.0 - mix)
        memory_grad = up * mix
        local_grad = (up * (1.0 - mix)).astype(bf16)
        query_f = query.astype(f32)
        fq = kernel_feature(query_f).astype(bf16).astype(f32)
        normal = self.normal[n, 0:1, :]
        raw = jnp.sum(fq * normal, axis=-1, keepdims=True)
        den = jnp.maximum(raw, 1.0)
        numer_grad = memory_grad / den
        den_grad = -jnp.sum(memory_grad * mem_out, axis=-1, keepdims=True) / den
        raw_grad = jnp.where(raw > 1.0, den_grad, 0.0)
        fq_grad = dot_high(numer_grad, self.memory[n], ((1,), (1,))) + raw_grad * normal
        if n > 0:
            self.state_grad[n] += dot_high(fq, numer_grad, ((0,), (0,)))
            self.norm_grad[n, 0:1, :] += jnp.sum(raw_grad * fq, axis=0, keepdims=True)
        scores = scores_of(query, keys, i * ROWS)
        probs = jnp.exp(scores - self.lse[rows, 0:1])
        prob_grad = cols_dot(local_grad, values)
        row_term = jnp.sum(probs * prob_grad, axis=-1, keepdims=True)
        score_grad = (probs * (prob_grad - row_term)).astype(bf16)
        query_grad = jnp.dot(score_grad, keys, preferred_element_type=f32) * scale
        query_grad = query_grad + fq_grad * feature_slope(query_f)
        self.grad[rows, :DH] = query_grad.astype(bf16)
        self.dk[seen, :] += rows_dot(score_grad, query) * scale
        self.dv[seen, :] += rows_dot(probs.astype(bf16), local_grad)

    def states(self):
        state = jnp.zeros((DH, DH), f32)
        norm = jnp.zeros((1, DH), f32)
        for n in reversed(range(self.segments)):
            rows = pl.ds(n * SEG, SEG)
            key = self.qkv[rows, DH:2 * DH].astype(f32)
            key_grad = self.dk[rows, :]
            value_grad = self.dv[rows, :]
            if n + 1 < self.segments:
                fk = kernel_feature(key).astype(bf16).astype(f32)
                value = self.qkv[rows, 2 * DH:].astype(f32)
                fk_grad = dot_high(value, state, ((1,), (1,))) + norm
                key_grad = key_grad + fk_grad * feature_slope(key)
                value_grad = value_grad + dot_high(fk, state)
            self.grad[rows, DH:2 * DH] = key_grad.astype(bf16)
            self.grad[rows, 2 * DH:] = value_grad.astype(bf16)
            if n > 0:
                keep = self.keep[n, 0:1, :]
                state = (state + self.state_grad[n]) * keep
                norm = (norm + self.norm_grad[n, 0:1, :]) * keep

    def blocks(self):
        return [(n, i) for n in range(self.segments) for i in range(SEG // ROWS)]


def attend_kernel(qkv, keep, mix, x, gains_all, out_w, cot, gate_up,
                  local, mem_out, lse, combined, memory, normal, middle, hidden, out_all, cot_all,
                  gate_up_cols, mixed_tokens, copies, t_s, t_r, *rest):
    sems_o, sems_c, sems_g = halves_of(rest, [11, 7, 5])
    s = Spot()
    mine = pl.ds(pl.multiple_of(s.me * 128, 128), 128)
    own = [
        pltpu.make_async_copy(out_w, out_all.at[mine], copies.at[0]),
        pltpu.make_async_copy(cot, cot_all.at[mine], copies.at[1]),
    ]
    for cp in own:
        cp.start()
    greet(s)
    gather_o = SharedGather(s, out_w, out_all, sems_o)
    gather_c = Gather(s, cot, cot_all, sems_c)
    columns_g = Columns(s, gate_up, gate_up_cols, 2, sems_g)
    gather_o.start()
    gather_c.start()
    columns_g.start(4)
    attend = Attend(qkv, keep, mix, local, mem_out, lse, combined, memory, normal)

    def token_copy(j):
        return send(
            combined.at[pl.ds(j * 128, 128)],
            mixed_tokens.at[:, pl.ds(pl.multiple_of(s.me * DH, DH), DH)],
            t_s.at[j], t_r.at[s.me], j,
        )

    def block(n, i):
        attend.block(n, i)
        for j in range((n * SEG + i * ROWS) // 128, (n * SEG + (i + 1) * ROWS) // 128):
            pl.when(s.me != j)(lambda: token_copy(j).start())

    compute = [attend.states] + [functools.partial(block, n, i) for n, i in attend.blocks()]

    def tokens():
        own[0].wait()
        gather_o.finish()
        mixed_tokens[:, pl.ds(pl.multiple_of(s.me * DH, DH), DH)] = combined[mine, :]
        for k in range(1, 16):
            src = s.partner(k)
            b = mixed_tokens.at[:, pl.ds(pl.multiple_of(src * DH, DH), DH)]
            send(b, b, t_s.at[0], t_r.at[src], s.me).wait_recv()

    def output(j):
        w = pl.ds(j * 512, 512)
        got = jnp.dot(mixed_tokens[...], out_all[:, w], preferred_element_type=f32)
        middle[:, w] = got + x[:, w].astype(f32)

    def norm():
        values = middle[...]
        factor = lax.rsqrt(jnp.mean(values * values, axis=-1, keepdims=True) + epsilon)
        for j in range(16):
            w = pl.ds(j * 128, 128)
            hidden[:, w] = (middle[:, w] * factor * gains_all[j, 1:2, :]).astype(bf16)

    after = [tokens] + [functools.partial(output, j) for j in range(4)] + [norm]
    merged(
        gather_o.tasks(),
        gather_c.tasks(),
        columns_g.tasks(),
        compute + nothing(len(compute)),
    )
    merged(after)
    columns_g.finish()
    for j in range(16):
        pl.when(s.me != j)(lambda: token_copy(j).wait_send())
    gather_o.drain()
    gather_c.drain()
    columns_g.drain()
    own[1].wait()


def attend_forward(qkv, keep, mix, x, gains_all, out_weight, cotangent, gate_up, number):
    tokens, width = cotangent.shape
    total = qkv.shape[0]
    segments = total // SEG
    shape = jax.ShapeDtypeStruct
    return communicate(
        attend_kernel, "attend", number,
        (qkv, keep, mix, x, gains_all, out_weight, cotangent, gate_up), [vmem()] * 5 + [anywhere()] * 3,
        [
            shape((total, DH), f32), shape((total, DH), f32), shape((total, DH), f32),
            shape((total, DH), bf16), shape((segments, DH, DH), f32), shape((segments, 8, DH), f32),
            shape((tokens, width), f32), shape((tokens, width), bf16),
            shape((total, width), bf16), shape((total, width), bf16),
            shape((width, gate_up.shape[1] // 16), bf16),
        ],
        [vmem()] * 9 + [anywhere()] * 2,
        [VM((tokens, width), bf16), dma((2,)), dma((16,)), dma((16,))] + SharedGather.sems() + Gather.sems() + Columns.sems(2),
    )


def feed_kernel(hidden, cot_all, gate_up_cols, down,
                hidden_all, act, feed_grad, down_cols,
                hidden_v, act_v, grad_v, down_v, cot_v, gate_up_v, copies, outs, *rest):
    sems, sems_d = halves_of(rest, [7, 5])
    s = Spot()
    loads = [
        pltpu.make_async_copy(a, b, copies.at[i])
        for i, (a, b) in enumerate([(gate_up_cols, gate_up_v), (cot_all, cot_v)])
    ]
    for cp in loads:
        cp.start()
    greet(s)
    gather = Gather(s, hidden, hidden_v, sems)
    gather.start()
    columns = Columns(s, down, down_v, 1, sems_d)
    columns.start()
    hidden_v[pl.ds(pl.multiple_of(s.me * 128, 128), 128), :] = hidden[...]
    half = act.shape[1]

    def out_copies(j):
        tok = pl.ds(pl.multiple_of(s.arrival(j) * 512, 512), 512)
        pairs = [(hidden_v, hidden_all), (act_v, act), (grad_v, feed_grad)]
        return [
            pltpu.make_async_copy(a.at[tok], b.at[tok], outs.at[j, i]) for i, (a, b) in enumerate(pairs)
        ]

    out_down = pltpu.make_async_copy(down_v, down_cols, outs.at[4, 0])

    def use(j):
        if j == 0:
            for cp in loads:
                cp.wait()
            columns.finish()
            out_down.start()
        tok = pl.ds(pl.multiple_of(s.arrival(j) * 512, 512), 512)
        act_grad = jnp.dot(cot_v[tok, :], down_v[...], preferred_element_type=f32)
        gate = jnp.dot(hidden_v[tok, :], gate_up_v[:, :half], preferred_element_type=f32)
        up = jnp.dot(hidden_v[tok, :], gate_up_v[:, half:], preferred_element_type=f32)
        sigma = jax.nn.sigmoid(gate)
        silu = gate * sigma
        act_v[tok, :] = (silu * up).astype(bf16)
        slope = sigma * (1.0 + gate * (1.0 - sigma))
        grad_v[tok, :half] = (act_grad * up * slope).astype(bf16)
        grad_v[tok, half:] = (act_grad * silu).astype(bf16)
        for cp in out_copies(j):
            cp.start()

    merged(gather.tasks(use), nothing(2) + columns.tasks() + nothing(8))
    gather.drain()
    columns.drain()
    out_down.wait()
    for j in range(4):
        for cp in out_copies(j):
            cp.wait()


def feed(hidden, cot_all, gate_up_cols, down, number):
    total, width = cot_all.shape
    half = down.shape[1] // 16
    shape = jax.ShapeDtypeStruct
    return communicate(
        feed_kernel, "feed", number, (hidden, cot_all, gate_up_cols, down),
        [vmem()] + [anywhere()] * 3,
        [
            shape((total, width), bf16), shape((total, half), bf16), shape((total, 2 * half), bf16),
            shape((width, half), bf16),
        ],
        [anywhere()] * 4,
        [
            VM((total, width), bf16), VM((total, half), bf16), VM((total, 2 * half), bf16),
            VM((width, half), bf16), VM((total, width), bf16), VM(gate_up_cols.shape, bf16),
            dma((2,)), dma((5, 3)),
        ] + Gather.sems() + Columns.sems(1),
    )


def loaded(pairs, sems):
    copies = [pltpu.make_async_copy(a, b, sems.at[i]) for i, (a, b) in enumerate(pairs)]
    for cp in copies:
        cp.start()
    return [cp.wait for cp in copies]


def hidden_grad_kernel(feed_grad, gate_up_cols, hidden_all, act, down_cols, out, half, feed_out,
                       hidden_v, act_v, down_v, copies, *rest):
    sems_w, scratch, scratch_f = halves_of(rest, [5, 11, 11])
    s = Spot()
    loads = loaded([(hidden_all, hidden_v), (act, act_v), (down_cols, down_v)], copies)
    greet(s, plane=False)
    weigh = Weigh(s, hidden_v, feed_grad, half, sems_w)
    scatter = Scatter(s, feed_grad, gate_up_cols, out, scratch)
    filler = Scatter(s, act_v, down_v, feed_out, scratch_f, FILL[0][0])
    merged(
        scatter.tasks(),
        loads + weigh.products() + nothing(16),
        nothing(4) + filler.tasks(),
        nothing(20) + weigh.folds(),
    )
    scatter.finish()
    filler.finish()
    weigh.drain()


def hidden_grad_of(feed_grad, gate_up_cols, hidden_all, act, down_cols, number):
    shape = jax.ShapeDtypeStruct
    total, cols = feed_grad.shape
    width = gate_up_cols.shape[0]
    fill = FILL[0][1]
    return communicate(
        hidden_grad_kernel, "hidden_grad", number,
        (feed_grad, gate_up_cols, hidden_all, act, down_cols), [vmem()] * 2 + [anywhere()] * 3,
        [
            shape((total // 16, width), f32), shape((16, 64, cols), bf16),
            shape((total // 16, fill), f32),
        ],
        [vmem()] * 3,
        [VM(hidden_all.shape, bf16), VM(act.shape, bf16), VM(down_cols.shape, bf16), dma((3,))]
        + Weigh.scratch(cols) + Scatter.scratch(width) + Scatter.scratch(fill),
    )


def normed_grad_kernel(grad, in_cols, normed_all, x, gain, act, down_cols, gains, down_half, out_rows,
                       value_grad, gains_out, feed_out, down_rows, down_other, in_mine, in_other,
                       out_other, normed_grad, half, gains_v, got, total, theirs, normed_v, act_v, down_v,
                       copies, x_s, x_r, g_s, g_r,
                       *rest):
    sems_d, sems_i, sems_w, scratch, scratch_f = halves_of(rest, [5, 5, 5, 11, 11])
    s = Spot()
    loads = loaded([(normed_all, normed_v), (act, act_v), (down_cols, down_v)], copies)
    greet(s)
    back_i = Return(s, half, in_mine, 3, sems_i, other=in_other)
    weigh = Weigh(s, normed_v, grad, half, sems_w, back=back_i)
    back_d = Return(s, down_half, down_rows, 1, sems_d, other=down_other)
    scatter = Scatter(s, grad, in_cols, normed_grad, scratch)
    filler = Scatter(s, act_v, down_v, feed_out, scratch_f, FILL[2][0])
    over = send_over(out_rows, out_other, x_s.at[0], x_r.at[0], s)
    back_d.start()

    def gain_copy(k):
        to = s.partner(k)
        return send(gains_v.at[to], got.at[s.me], g_s.at[k], g_r.at[s.me], to)

    def epilogue():
        width = x.shape[1]
        values = x[...].astype(f32)
        factor = lax.rsqrt(jnp.mean(values * values, axis=-1, keepdims=True) + epsilon)
        row = jnp.sum(normed_grad[...] * gain[0:1, :] * values, axis=-1, keepdims=True)
        row = row * (1.0 / width) * factor * factor * factor
        for j in range(16):
            w = pl.ds(j * 128, 128)
            v = x[:, w].astype(f32)
            u = normed_grad[:, w]
            value_grad[:, w] = factor * (u * gain[0:1, w]) - v * row
            gains_v[j] = gains[j]
            gains_v[j, 0:1, :] = jnp.sum(u * v * factor, axis=0, keepdims=True)

    merged(
        scatter.tasks(),
        loads + weigh.products() + nothing(24),
        nothing(5) + weigh.folds() + nothing(12),
        nothing(10) + [over.start] + back_d.tasks() + nothing(5),
        nothing(4) + filler.tasks(),
        nothing(16) + back_i.tasks(),
    )
    scatter.finish()
    epilogue()
    for k in range(1, 16):
        gain_copy(k).start()
    filler.finish()
    back_d.finish()
    back_i.finish()
    weigh.drain()
    over.wait()
    for k in range(1, 16):
        src = s.partner(k)
        b = got.at[src]
        send(b, b, g_s.at[k], g_r.at[src], s.me).wait_recv()
    got[s.me] = gains_v[s.me]
    acc = got[0]
    for k in range(1, 16):
        acc = acc + got[k]
    total[...] = acc
    cp = send_over(total, theirs, x_s.at[1], x_r.at[1], s)
    cp.start()
    for k in range(1, 16):
        gain_copy(k).wait_send()
    cp.wait()
    gains_out[...] = total[...] + theirs[...]


def normed_grad_of(grad, in_cols, normed_all, x, gain, act, down_cols, gains, down_half, out_rows, number):
    shape = jax.ShapeDtypeStruct
    total, cols = grad.shape
    tokens, width = x.shape
    fill = FILL[2][1]
    down_rows = shape((64, 16 * down_half.shape[2]), bf16)
    in_rows = shape((64, 16 * cols), bf16)
    return communicate(
        normed_grad_kernel, "normed_grad", number,
        (grad, in_cols, normed_all, x, gain, act, down_cols, gains, down_half, out_rows),
        [vmem()] * 2 + [anywhere()] + [vmem()] * 2 + [anywhere()] * 2 + [vmem()] + [anywhere()] * 2,
        [
            shape((tokens, width), f32), shape((8, 128), f32), shape((tokens, fill), f32),
            down_rows, down_rows, in_rows, in_rows, shape(out_rows.shape, bf16),
        ],
        [vmem()] * 3 + [anywhere()] * 5,
        [
            VM((tokens, width), f32), VM((16, 64, cols), bf16), VM((16, 8, 128), f32),
            VM((16, 8, 128), f32), VM((8, 128), f32), VM((8, 128), f32),
            VM(normed_all.shape, bf16), VM(act.shape, bf16), VM(down_cols.shape, bf16), dma((3,)),
            dma((2,)), dma((2,)), dma((16,)), dma((16,)),
        ] + Return.sems(1) + Return.sems(3) + Weigh.scratch(cols) + Scatter.scratch(width)
        + Scatter.scratch(fill),
    )


def attend_back_kernel(attended, out_all, qkv, keep, mix, local, mem_out, lse, memory, normal,
                       gate_up_half, cot_all, act, down_cols,
                       attended_all, grad, mix_grad, gate_up_rows, gate_up_other, down_half, feed_out,
                       out_v, cot_v, by_token, upstream, dk, dv, state_grad, norm_grad, copies, h_s, h_r,
                       *rest):
    sems_a, sems_g, sems_w, scratch_f = halves_of(rest, [7, 5, 5, 11])
    s = Spot()
    mine = pl.ds(pl.multiple_of(s.me * 128, 128), 128)
    cot_load = pltpu.make_async_copy(cot_all, cot_v, copies.at[2])
    load = pltpu.make_async_copy(out_all, out_v, copies.at[0])
    load.start()
    own = pltpu.make_async_copy(attended, attended_all.at[mine], copies.at[1])
    own.start()
    cot_load.start()
    greet(s)
    gather = Gather(s, attended, attended_all, sems_a)
    back_g = Return(s, gate_up_half, gate_up_rows, 2, sems_g, other=gate_up_other)
    filler = Scatter(s, act, down_cols, feed_out, scratch_f, FILL[1][0])
    weigh = Weigh(s, cot_v, act, down_half, sems_w)
    attend = AttendBack(qkv, keep, mix, local, mem_out, lse, memory, normal, upstream, grad,
                        mix_grad, dk, dv, state_grad, norm_grad)
    attend.clear()
    gather.start()
    load.wait()

    def head_copy(j):
        return send(by_token.at[:, pl.ds(j * DH, DH)], upstream.at[mine], h_s.at[j], h_r.at[s.me], j)

    for j in range(4):
        w = pl.ds(j * 512, 512)
        by_token[:, w] = cols_dot(attended[...], out_v[w, :]).astype(bf16)
        for h in range(4 * j, 4 * j + 4):
            pl.when(s.me != h)(lambda: head_copy(h).start())
    upstream[mine, :] = by_token[:, pl.ds(pl.multiple_of(s.me * DH, DH), DH)]
    cot_load.wait()
    filler.lag = 8

    def arrive(j):
        b = upstream.at[pl.ds(j * 128, 128)]
        pl.when(s.me != j)(lambda: send(b, b, h_s.at[j], h_r.at[j], s.me).wait_recv())

    def block(n, i):
        for j in range((n * SEG + i * ROWS) // 128, (n * SEG + (i + 1) * ROWS) // 128):
            arrive(j)
        attend.block(n, i)

    compute = [functools.partial(block, n, i) for n, i in attend.blocks()] + [attend.states]
    merged(gather.tasks(), nothing(2) + compute, weigh.products() + nothing(12))
    back_g.start()
    merged(filler.tasks(), back_g.tasks(), weigh.folds())
    filler.finish()
    back_g.finish()
    weigh.drain()
    for j in range(16):
        pl.when(s.me != j)(lambda: head_copy(j).wait_send())
    gather.drain()
    own.wait()


def attend_backward(attended, out_all, qkv, keep, mix, saved, gate_up_half, cot_all, act, down_cols,
                    number):
    tokens, width = attended.shape
    total = qkv.shape[0]
    segments = total // SEG
    shape = jax.ShapeDtypeStruct
    local, mem_out, lse, memory, normal = saved
    rows = shape((64, 16 * gate_up_half.shape[2]), bf16)
    return communicate(
        attend_back_kernel, "attend_back", number,
        (attended, out_all, qkv, keep, mix, local, mem_out, lse, memory, normal,
         gate_up_half, cot_all, act, down_cols),
        [vmem(), anywhere()] + [vmem()] * 8 + [anywhere()] * 2 + [vmem()] * 2,
        [
            shape((total, width), bf16), shape((total, 3 * DH), bf16), shape((8, DH), f32),
            rows, rows, shape((16, 64, act.shape[1]), bf16), shape((tokens, FILL[1][1]), f32),
        ],
        [anywhere(), vmem(), vmem(), anywhere(), anywhere(), vmem(), vmem()],
        [
            VM(out_all.shape, bf16), VM(cot_all.shape, bf16), VM((tokens, width), bf16),
            VM((total, DH), bf16),
            VM((total, DH), f32), VM((total, DH), f32), VM((segments, DH, DH), f32),
            VM((segments, 8, DH), f32), dma((3,)), dma((16,)), dma((16,)),
        ] + Gather.sems() + Return.sems(2) + Weigh.scratch(act.shape[1]) + Scatter.scratch(FILL[1][1]),
    )


def body(
    layer_input,
    first_gain,
    in_weight,
    out_weight,
    mix_gate,
    second_gain,
    gate_up,
    down_weight,
    document_starts,
    cotangent,
):
    tokens, width = layer_input.shape
    total = tokens * H
    segments = total // SEG
    dp = lax.axis_index("dp")

    own_gains = jnp.zeros((8, tokens), f32)
    own_gains = own_gains.at[0].set(first_gain.astype(f32)).at[1].set(second_gain.astype(f32))
    mix = jnp.broadcast_to(jax.nn.sigmoid(mix_gate.astype(f32))[None], (8, DH))
    numbers = jnp.arange(segments)
    fresh = (numbers == 0) | (document_starts[0] > 0)
    keep = jnp.broadcast_to(jnp.where(fresh, 0.0, 1.0)[:, None, None], (segments, 8, DH))

    normed_all, in_cols, gains_all, qkv = project(layer_input, own_gains, in_weight, 0)
    (local, mem_out, lse, combined, memory, normal, middle, hidden, out_all, cot_all,
     gate_up_cols) = attend_forward(
        qkv, keep, mix, layer_input, gains_all, out_weight, cotangent, gate_up, 1
    )
    hidden_all, act, feed_grad, down_cols = feed(hidden, cot_all, gate_up_cols, down_weight, 2)

    hidden_grad, gate_up_half, feed_out_0 = hidden_grad_of(
        feed_grad, gate_up_cols, hidden_all, act, down_cols, 3
    )

    first_all = gains_all[:, 0].reshape(width)
    second_all = gains_all[:, 1].reshape(width)
    upstream = cotangent.astype(f32)
    second_factor = lax.rsqrt(jnp.mean(middle * middle, axis=-1, keepdims=True) + epsilon)
    middle_norm_grad, second_local = norm_backward(middle, second_factor, second_all, hidden_grad)
    middle_grad = upstream + middle_norm_grad
    (attended_all, projected_grad, mix_grad, gate_up_rows, gate_up_other, down_half,
     feed_out_1) = attend_backward(
        middle_grad.astype(bf16), out_all, qkv, keep, mix, (local, mem_out, lse, memory, normal),
        gate_up_half, cot_all, act, down_cols, 4,
    )
    out_rows = rows_dot(combined, attended_all).astype(bf16)
    mix_rows = jnp.where((jnp.arange(H) == lax.axis_index(AXIS))[:, None], mix_grad[0:1], 0.0)
    gain_grads = jnp.stack([mix_rows, second_local.reshape(16, 128), mix_rows], axis=1)
    gain_grads = jnp.pad(gain_grads, ((0, 0), (0, 5), (0, 0)))
    (value_grad, gains_out, feed_out_2, down_rows, down_other, in_mine_rows, in_other_rows,
     out_other) = normed_grad_of(
        projected_grad, in_cols, normed_all, layer_input, jnp.broadcast_to(first_all[None], (8, width)),
        act, down_cols, gain_grads, down_half, out_rows, 5,
    )
    input_grad = middle_grad + value_grad
    feed_out = jnp.concatenate([feed_out_0, feed_out_1, feed_out_2], axis=1)
    layer_output = (middle + feed_out).astype(bf16)

    def both_halves(mine, other):
        low = jnp.where(dp == 0, mine, other)
        high = jnp.where(dp == 0, other, mine)
        return jnp.concatenate([low, high]).astype(f32)

    return (
        layer_output,
        input_grad,
        gains_out[0],
        both_halves(in_mine_rows, in_other_rows),
        out_rows.astype(f32) + out_other.astype(f32),
        gains_out[2],
        gains_out[1],
        both_halves(gate_up_rows, gate_up_other),
        both_halves(down_rows, down_other),
    )


def solution(mesh):
    one_group = mesh.shape[AXIS] == H and mesh.shape["dp"] == 2
    return jax.shard_map(
        body if one_group else body_groups,
        mesh=mesh,
        in_specs=(
            P(("dp", "fsdp"), None),
            P("fsdp"),
            P("fsdp", None),
            P("fsdp", None),
            P("fsdp"),
            P("fsdp"),
            P("fsdp", None),
            P("fsdp", None),
            P("dp", None),
            P(("dp", "fsdp"), None),
        ),
        out_specs=(
            P(("dp", "fsdp"), None),
            P(("dp", "fsdp"), None),
            P("fsdp"),
            P("fsdp", None),
            P("fsdp", None),
            P("fsdp"),
            P("fsdp"),
            P("fsdp", None),
            P("fsdp", None),
        ),
        check_vma=False,
    )
```

```python
import functools
import math

import jax
import jax.numpy as jnp
from jax import lax
from jax.experimental import pallas as pl
from jax.experimental.pallas import tpu as pltpu
from jax.sharding import PartitionSpec as P

H = 16
DH = 128
FF = 8192
SEG = 1024

highest = lax.Precision.HIGHEST
epsilon = 1e-06
f32 = jnp.float32
bf16 = jnp.bfloat16
AXIS = "fsdp"


def feature(values):
    return jax.nn.elu(values) + 1.0


def feature_slope(values):
    return jnp.where(values > 0, 1.0, jnp.exp(jnp.minimum(values, 0.0)))


def norm_forward(values, gain):
    factor = lax.rsqrt(jnp.mean(values * values, axis=-1, keepdims=True) + epsilon)
    return (values * factor * gain, factor)


def norm_backward(values, factor, gain, upstream):
    scaled = upstream * gain
    gain_grad = jnp.sum(upstream * values * factor, axis=0)
    value_grad = factor * scaled - values * (factor * factor * factor) * jnp.mean(
        scaled * values, axis=-1, keepdims=True
    )
    return (value_grad, gain_grad)


def dot(left, right, dims):
    return lax.dot_general(left, right, ((dims[0], dims[1]), ((), ())), preferred_element_type=f32)


def rows_dot(left, right):
    return dot(left, right, ((0,), (0,)))


def cols_dot(left, right):
    return dot(left, right, ((1,), (1,)))


class Layout:
    def __init__(self):
        self.count = lax.axis_size(AXIS)
        self.groups = self.count // H
        self.place = lax.axis_index(AXIS)
        self.head = self.place % H
        self.group = self.place // H
        self.inside = None
        self.across = None
        if self.groups > 1:
            self.inside = [[g * H + j for j in range(H)] for g in range(self.groups)]
            self.across = [[g * H + j for g in range(self.groups)] for j in range(H)]

    def gather(self, block):
        return lax.all_gather(block, AXIS, axis=0, tiled=True, axis_index_groups=self.inside)

    def gather_all(self, block):
        return lax.all_gather(block, AXIS, axis=0, tiled=True)

    def scatter_sum(self, whole):
        return lax.psum_scatter(
            whole, AXIS, scatter_dimension=0, tiled=True, axis_index_groups=self.inside
        )

    def columns(self, block, parts):
        rows, width = block.shape
        each = width // (parts * H)
        if self.groups == 1:
            split = block.reshape(rows, parts, H, each)
            out = lax.all_to_all(split, AXIS, 2, 0, tiled=True)
            return out.reshape(rows * self.count, parts * each)
        whole = self.gather_all(block).reshape(rows * self.count, parts, H, each)
        out = lax.dynamic_index_in_dim(whole, self.head, 2, False)
        return out.reshape(rows * self.count, parts * each)

    def own_rows(self, grad, parts):
        rows, width = grad.shape
        each = width // parts
        if self.groups == 1:
            split = grad.astype(bf16).reshape(rows, parts, 1, each)
            out = lax.all_to_all(split, AXIS, 0, 2, tiled=True)
            return out.reshape(rows // self.count, parts * H * each)
        whole = jnp.zeros((rows, parts, H, each), f32)
        whole = lax.dynamic_update_slice_in_dim(
            whole, grad.reshape(rows, parts, 1, each), self.head, 2
        )
        return lax.psum_scatter(
            whole.reshape(rows, parts * H * each), AXIS, scatter_dimension=0, tiled=True
        )

    def to_tokens(self, by_head):
        tokens, each = by_head.shape
        out = lax.all_to_all(
            by_head.reshape(H, tokens // H, each), AXIS, 0, 0, tiled=False,
            axis_index_groups=self.inside,
        )
        return out.transpose(1, 0, 2).reshape(tokens // H, H * each)

    def to_heads(self, by_token):
        tokens, width = by_token.shape
        split = by_token.reshape(tokens, H, width // H).transpose(1, 0, 2)
        out = lax.all_to_all(
            split, AXIS, 0, 0, tiled=False, axis_index_groups=self.inside
        )
        return out.reshape(H * tokens, width // H)


def carry_forward(layout, delta, count, fresh):
    segments = delta.shape[0]

    def walk(state):
        before = []
        for s in range(segments):
            state = jax.tree.map(lambda a: jnp.where(fresh[s], jnp.zeros_like(a), a), state)
            before.append(state)
            state = (state[0] + delta[s], state[1] + count[s])
        return before, state

    state = (jnp.zeros_like(delta[0]), jnp.zeros_like(count[0]))
    if layout.groups > 1:
        _, last = walk(state)
        renewed = jnp.any(fresh).astype(f32)
        every = jax.tree.map(
            lambda a: lax.all_gather(a, AXIS, axis_index_groups=layout.across), last + (renewed,)
        )
        for g in range(layout.groups - 1):
            keep = every[2][g] < 0.5
            after = jax.tree.map(lambda a, e: jnp.where(keep, a, 0.0) + e[g], state, every[:2])
            state = jax.tree.map(lambda a, b: jnp.where(g < layout.group, b, a), state, after)
    before, _ = walk(state)
    return jnp.stack([b[0] for b in before]), jnp.stack([b[1] for b in before])


def carry_backward(layout, state_grad, norm_grad, fresh):
    segments = state_grad.shape[0]

    def walk(state):
        after = [None] * segments
        for s in reversed(range(segments)):
            after[s] = state
            state = (state[0] + state_grad[s], state[1] + norm_grad[s])
            state = jax.tree.map(lambda a: jnp.where(fresh[s], jnp.zeros_like(a), a), state)
        return after, state

    state = (jnp.zeros_like(state_grad[0]), jnp.zeros_like(norm_grad[0]))
    if layout.groups > 1:
        _, first = walk(state)
        renewed = jnp.any(fresh).astype(f32)
        every = jax.tree.map(
            lambda a: lax.all_gather(a, AXIS, axis_index_groups=layout.across), first + (renewed,)
        )
        for g in reversed(range(1, layout.groups)):
            keep = every[2][g] < 0.5
            before = jax.tree.map(lambda a, e: jnp.where(keep, a, 0.0) + e[g], state, every[:2])
            state = jax.tree.map(lambda a, b: jnp.where(g > layout.group, b, a), state, before)
    after, _ = walk(state)
    return jnp.stack([a[0] for a in after]), jnp.stack([a[1] for a in after])


def body_groups(
    layer_input,
    first_gain,
    in_weight,
    out_weight,
    mix_gate,
    second_gain,
    gate_up,
    down_weight,
    document_starts,
    cotangent,
):
    layout = Layout()
    tokens, width = layer_input.shape
    group_tokens = tokens * H
    segments = group_tokens // SEG
    scale = 1.0 / math.sqrt(DH)

    gains = jnp.stack([first_gain, second_gain])
    gains = lax.all_gather(gains, AXIS, axis=1, tiled=True).astype(f32)
    first_all, second_all = gains[0], gains[1]
    if layout.groups == 1:
        mix_own = mix_gate
    else:
        mix_own = lax.dynamic_slice_in_dim(layout.gather_all(mix_gate), layout.head * DH, DH)
    mix = jax.nn.sigmoid(mix_own.astype(f32))[None]

    inputs = layer_input.astype(f32)
    normed, first_factor = norm_forward(inputs, first_all)
    normed_all = layout.gather(normed.astype(bf16))
    in_cols = layout.columns(in_weight, 3)
    out_all = layout.gather_all(out_weight)
    cot_all = layout.gather(cotangent)
    gate_up_cols = layout.columns(gate_up, 2)
    down_cols = layout.columns(down_weight, 1)

    projected = jnp.dot(normed_all, in_cols, preferred_element_type=f32).astype(bf16)
    by_segment = projected.reshape(segments, SEG, 3, DH)
    query, key, value = by_segment[:, :, 0], by_segment[:, :, 1], by_segment[:, :, 2]
    index = jnp.arange(SEG, dtype=jnp.int32)
    allowed = index[None, :] <= index[:, None]

    def attention_scores():
        raw = jnp.einsum("sqc,skc->sqk", query, key, preferred_element_type=f32) * scale
        return jnp.where(allowed[None], raw, -1e30)

    scores = attention_scores()
    top = jnp.max(scores, axis=-1, keepdims=True)
    expo = jnp.exp(scores - top)
    total = jnp.sum(expo, axis=-1, keepdims=True)
    log_total = top + jnp.log(total)
    probs_low = (expo / total).astype(bf16)
    local_out = jnp.einsum("sqk,skc->sqc", probs_low, value, preferred_element_type=f32)

    query_f, key_f, value_f = query.astype(f32), key.astype(f32), value.astype(f32)
    query_feature = feature(query_f).astype(bf16)
    key_feature = feature(key_f).astype(bf16)
    delta = jnp.einsum("slc,sla->sca", key_feature, value, preferred_element_type=f32)
    count = jnp.sum(key_feature.astype(f32), axis=1)
    numbers = layout.group * segments + jnp.arange(segments)
    fresh = (numbers == 0) | (
        lax.dynamic_slice_in_dim(document_starts[0], layout.group * segments, segments) > 0
    )
    memory, normal = carry_forward(layout, delta, count, fresh)
    query_feature_f = query_feature.astype(f32)
    numerator = jnp.einsum("sie,sej->sij", query_feature_f, memory, precision=highest)
    raw_denom = jnp.einsum("sik,sk->si", query_feature_f, normal, precision=highest)[..., None]
    denom = jnp.maximum(raw_denom, 1.0)
    memory_out = numerator / denom
    combined = mix * memory_out + (1.0 - mix) * local_out
    combined_head = combined.reshape(group_tokens, DH).astype(bf16)
    combined_low = layout.to_tokens(combined_head)
    attended = jnp.dot(combined_low, out_all, preferred_element_type=f32)
    middle = inputs + attended

    hidden, second_factor = norm_forward(middle, second_all)
    hidden_all = layout.gather(hidden.astype(bf16))
    act_grad = jnp.dot(cot_all, down_cols, preferred_element_type=f32)
    both = jnp.dot(hidden_all, gate_up_cols, preferred_element_type=f32)
    half = both.shape[1] // 2
    gate_part, up_part = both[:, :half], both[:, half:]
    sigma = jax.nn.sigmoid(gate_part)
    silu = gate_part * sigma
    activated = (silu * up_part).astype(bf16)
    silu_slope = sigma * (1.0 + gate_part * (1.0 - sigma))
    feed_grad = jnp.concatenate(
        [act_grad * up_part * silu_slope, act_grad * silu], axis=1
    ).astype(bf16)
    feed_out = layout.scatter_sum(cols_dot(activated, down_cols).astype(bf16))
    hidden_grad = layout.scatter_sum(cols_dot(feed_grad, gate_up_cols).astype(bf16))
    layer_output = (middle + feed_out.astype(f32)).astype(bf16)
    gate_up_part = layout.own_rows(rows_dot(hidden_all, feed_grad), 2)
    down_part = layout.own_rows(rows_dot(cot_all, activated), 1)

    upstream = cotangent.astype(f32)
    middle_norm_grad, second_local = norm_backward(
        middle, second_factor, second_all, hidden_grad.astype(f32)
    )
    middle_grad = upstream + middle_norm_grad
    attended_grad = middle_grad.astype(bf16)
    attended_grad_all = layout.gather(attended_grad)
    combined_grad = layout.to_heads(cols_dot(attended_grad, out_all).astype(bf16))
    combined_grad = combined_grad.astype(f32).reshape(segments, SEG, DH)
    out_rows_grad = rows_dot(combined_head, attended_grad_all)
    if layout.groups == 1:
        out_part = out_rows_grad
    else:
        whole = jnp.zeros((H * DH, width), f32)
        whole = lax.dynamic_update_slice_in_dim(whole, out_rows_grad, layout.head * DH, 0)
        out_part = lax.psum_scatter(whole, AXIS, scatter_dimension=0, tiled=True)
    mix_local = jnp.sum(combined_grad * (memory_out - local_out), axis=(0, 1)) * (
        mix * (1.0 - mix)
    ).reshape(DH)

    memory_grad = combined_grad * mix
    local_grad = (combined_grad * (1.0 - mix)).astype(bf16)
    numer_grad = memory_grad / denom
    denom_grad = -jnp.sum(memory_grad * memory_out, axis=-1, keepdims=True) / denom
    raw_grad = jnp.where(raw_denom > 1.0, denom_grad, 0.0)
    query_feature_grad = (
        jnp.einsum("sij,sej->sie", numer_grad, memory, precision=highest)
        + raw_grad * normal[:, None]
    )
    state_grad = jnp.einsum("sie,sij->sej", query_feature_f, numer_grad, precision=highest)
    norm_grad = jnp.sum(raw_grad * query_feature_f, axis=1)
    delta_grad, count_grad = carry_backward(layout, state_grad, norm_grad, fresh)
    key_feature_grad = (
        jnp.einsum("sij,sej->sie", value_f, delta_grad, precision=highest) + count_grad[:, None]
    )
    value_memory_grad = jnp.einsum(
        "sie,sej->sij", key_feature.astype(f32), delta_grad, precision=highest
    )
    query_memory_grad = query_feature_grad * feature_slope(query_f)
    key_memory_grad = key_feature_grad * feature_slope(key_f)

    probs = jnp.exp(attention_scores() - log_total)
    prob_grad = jnp.einsum("sqc,skc->sqk", local_grad, value, preferred_element_type=f32)
    row_term = jnp.sum(probs * prob_grad, axis=-1, keepdims=True)
    score_grad = (probs * (prob_grad - row_term)).astype(bf16)
    query_grad = query_memory_grad + scale * jnp.einsum(
        "sqk,skc->sqc", score_grad, key, preferred_element_type=f32
    )
    key_grad = key_memory_grad + scale * jnp.einsum(
        "sqk,sqc->skc", score_grad, query, preferred_element_type=f32
    )
    value_grad = value_memory_grad + jnp.einsum(
        "sqk,sqc->skc", probs.astype(bf16), local_grad, preferred_element_type=f32
    )
    projected_grad = (
        jnp.stack([query_grad, key_grad, value_grad], axis=2)
        .reshape(group_tokens, 3 * DH)
        .astype(bf16)
    )
    normed_grad = layout.scatter_sum(cols_dot(projected_grad, in_cols).astype(bf16))
    in_part = layout.own_rows(rows_dot(normed_all, projected_grad), 3)
    input_norm_grad, first_local = norm_backward(
        inputs, first_factor, first_all, normed_grad.astype(f32)
    )
    input_grad = middle_grad + input_norm_grad

    gains_part = lax.psum_scatter(
        jnp.stack([first_local, second_local]), AXIS, scatter_dimension=1, tiled=True
    )
    if layout.groups == 1:
        mix_part = mix_local
    else:
        whole = jnp.zeros((H * DH,), f32)
        whole = lax.dynamic_update_slice_in_dim(whole, mix_local, layout.head * DH, 0)
        mix_part = lax.psum_scatter(whole, AXIS, scatter_dimension=0, tiled=True)

    def over_sequences(part):
        return lax.psum(part.astype(bf16), "dp").astype(f32)

    small = over_sequences(jnp.concatenate([gains_part, mix_part[None]]))
    return (
        layer_output,
        input_grad,
        small[0],
        over_sequences(in_part),
        over_sequences(out_part),
        small[2],
        small[1],
        over_sequences(gate_up_part),
        over_sequences(down_part),
    )


MESH = pl.DeviceIdType.MESH
LIMIT = 60 * 2**20
FILL = ((0, 512), (512, 1024), (1536, 512))
ROWS = 256
dma = pltpu.SemaphoreType.DMA
VM = pltpu.VMEM


def vmem():
    return pl.BlockSpec(memory_space=pltpu.VMEM)


def anywhere():
    return pl.BlockSpec(memory_space=pl.ANY)


class Spot:
    def __init__(self):
        self.dp = lax.axis_index("dp")
        self.me = lax.axis_index(AXIS)
        self.z = self.me // 4
        self.y = (self.me // 2) % 2
        self.c = self.me % 2

    def at(self, z, y, c):
        return z * 4 + y * 2 + c

    def partner(self, k):
        out = self.me
        for bit in (1, 2, 4, 8):
            if k & bit:
                out = out + bit - 2 * bit * ((self.me // bit) % 2)
        return out

    def arrival(self, j):
        if j == 0:
            return self.z
        ends = jnp.where(self.z == 0, j, 3 - j)
        middle = {1: (0, 3), 2: (2, 1), 3: (3, 0)}[j]
        inner = jnp.where(self.z == 1, middle[0], middle[1])
        return jnp.where((self.z == 0) | (self.z == 3), ends, inner)


def greet(s, plane=True, other=True):
    ids = []
    if plane:
        ids += [{AXIS: (s.me + k) % 16} for k in range(1, 16)]
    else:
        ids += [{AXIS: s.at((s.z + k) % 4, s.y, s.c)} for k in (1, 2, 3)]
        ids += [{AXIS: s.at(s.z, 1 - s.y, s.c)}, {AXIS: s.at(s.z, s.y, 1 - s.c)}]
    if other:
        ids += [{"dp": 1 - s.dp}]
    barrier = pltpu.get_barrier_semaphore()
    for d in ids:
        pl.semaphore_signal(barrier, inc=1, device_id=d, device_id_type=MESH)
    pl.semaphore_wait(barrier, len(ids))


def send(src, dst, ssem, rsem, to):
    return pltpu.make_async_remote_copy(
        src_ref=src, dst_ref=dst, send_sem=ssem, recv_sem=rsem,
        device_id={AXIS: to}, device_id_type=MESH,
    )


def send_over(src, dst, ssem, rsem, s):
    return pltpu.make_async_remote_copy(
        src_ref=src, dst_ref=dst, send_sem=ssem, recv_sem=rsem,
        device_id={"dp": 1 - s.dp}, device_id_type=MESH,
    )


def merged(*lists):
    keyed = []
    for n, tasks in enumerate(lists):
        keyed += [((i + 0.5) / len(tasks), n, i, t) for i, t in enumerate(tasks)]
    for _, _, _, t in sorted(keyed, key=lambda e: e[:3]):
        t()


class Gather:
    chunks = 4

    @classmethod
    def sems(cls):
        return [dma((cls.chunks, 4))] * 5 + [dma((cls.chunks, 8))] * 2

    def __init__(self, s, src, dst, sems):
        self.s, self.src, self.dst = s, src, dst
        self.zr, self.zu, self.zd, self.ys, self.yr, self.ss, self.sr = sems[:7]
        self.rows = 128 // self.chunks
        self.skip = 0

    def block(self, ch, z, y, c):
        start = self.s.at(z, y, c) * 128 + self.skip + ch * self.rows
        return self.dst.at[pl.ds(pl.multiple_of(start, self.rows), self.rows)]

    def own(self, ch):
        start = pl.multiple_of(self.skip + ch * self.rows, self.rows)
        return self.src.at[pl.ds(start, self.rows)]

    def zcopy(self, ch, zo, up, own=False):
        s = self.s
        dst = self.block(ch, zo, s.y, s.c)
        to = s.at(s.z + 1 if up else s.z - 1, s.y, s.c)
        return send(
            self.own(ch) if own else dst, dst,
            (self.zu if up else self.zd).at[ch, zo], self.zr.at[ch, zo], to,
        )

    def ycopy(self, ch, zo, own=False):
        s = self.s
        dst = self.block(ch, zo, s.y, s.c)
        src = self.own(ch) if own else dst
        return send(src, dst, self.ys.at[ch, zo], self.yr.at[ch, zo], s.at(s.z, 1 - s.y, s.c))

    def scopy(self, ch, zo, yo, own=False):
        s = self.s
        dst = self.block(ch, zo, yo, s.c)
        n = zo * 2 + yo
        src = self.own(ch) if own else dst
        return send(src, dst, self.ss.at[ch, n], self.sr.at[ch, n], s.at(s.z, s.y, 1 - s.c))

    def start(self):
        s = self.s
        for ch in range(self.chunks):
            pl.when(s.z < 3)(lambda: self.zcopy(ch, s.z, True, True).start())
            pl.when(s.z > 0)(lambda: self.zcopy(ch, s.z, False, True).start())
            self.ycopy(ch, s.z, True).start()
            self.scopy(ch, s.z, s.y, True).start()

    def passed_on(self, ch, zo, yo):
        self.scopy(ch, zo, yo).start()

    def z_arrive(self, ch, j):
        s = self.s
        zo = s.arrival(j)
        self.zcopy(ch, zo, True).wait_recv()
        pl.when((zo < s.z) & (s.z < 3))(lambda: self.zcopy(ch, zo, True).start())
        pl.when((zo > s.z) & (s.z > 0))(lambda: self.zcopy(ch, zo, False).start())
        self.ycopy(ch, zo).start()
        self.passed_on(ch, zo, s.y)

    def y_arrive(self, ch, j):
        s = self.s
        zo = s.arrival(j)
        b = self.block(ch, zo, 1 - s.y, s.c)
        send(b, b, self.ys.at[ch, zo], self.yr.at[ch, zo], s.me).wait_recv()
        self.passed_on(ch, zo, 1 - s.y)

    def s_arrive(self, j):
        s = self.s
        zo = s.arrival(j)
        for ch in range(self.chunks):
            for yo in range(2):
                n = zo * 2 + yo
                b = self.block(ch, zo, yo, 1 - s.c)
                send(b, b, self.ss.at[ch, n], self.sr.at[ch, n], s.me).wait_recv()

    def tasks(self, use=None):
        out = []
        for step in range(1, 5):
            for ch in range(self.chunks):
                if step < 4:
                    out.append(functools.partial(self.z_arrive, ch, step))
                out.append(functools.partial(self.y_arrive, ch, step - 1))
                if step == 4 and ch < 3 and use is not None:
                    out.append(functools.partial(use, ch))
            out.append(functools.partial(self.s_arrive, step - 1))
        if use is not None:
            out.append(functools.partial(use, 3))
        return out

    def drain(self):
        s = self.s
        for ch in range(self.chunks):
            for zo in range(4):
                pl.when((s.z < 3) & (zo <= s.z))(lambda: self.zcopy(ch, zo, True).wait_send())
                pl.when((s.z > 0) & (zo >= s.z))(lambda: self.zcopy(ch, zo, False).wait_send())
                self.ycopy(ch, zo).wait_send()
                for yo in range(2):
                    self.scopy(ch, zo, yo).wait_send()


class SharedGather(Gather):
    chunks = 2

    @classmethod
    def sems(cls):
        return Gather.sems.__func__(cls) + [dma((cls.chunks, 8))] * 4

    def __init__(self, s, src, dst, sems):
        super().__init__(s, src, dst, sems)
        self.xs, self.xr, self.ts, self.tr = sems[7:]
        self.rows = 64 // self.chunks
        self.skip = s.dp * 64

    def other(self, ch, z, y, c):
        start = self.s.at(z, y, c) * 128 + (1 - self.s.dp) * 64 + ch * self.rows
        return self.dst.at[pl.ds(pl.multiple_of(start, self.rows), self.rows)]

    def xcopy(self, ch, zo, yo):
        s = self.s
        b = self.block(ch, zo, yo, s.c)
        n = zo * 2 + yo
        return send_over(b, b, self.xs.at[ch, n], self.xr.at[ch, n], s)

    def tcopy(self, ch, zo, yo, own=False):
        s = self.s
        b = self.other(ch, zo, yo, s.c)
        n = zo * 2 + yo
        src = b
        if own:
            start = pl.multiple_of((1 - s.dp) * 64 + ch * self.rows, self.rows)
            src = self.src.at[pl.ds(start, self.rows)]
        return send(src, b, self.ts.at[ch, n], self.tr.at[ch, n], s.at(s.z, s.y, 1 - s.c))

    def start(self):
        super().start()
        for ch in range(self.chunks):
            self.tcopy(ch, self.s.z, self.s.y, True).start()

    def passed_on(self, ch, zo, yo):
        self.xcopy(ch, zo, yo).start()
        self.scopy(ch, zo, yo).start()

    def x_arrive(self, j, yo):
        s = self.s
        zo = s.arrival(j)
        row = s.y if yo == 0 else 1 - s.y
        for ch in range(self.chunks):
            b = self.other(ch, zo, row, s.c)
            n = zo * 2 + row
            send_over(b, b, self.xs.at[ch, n], self.xr.at[ch, n], s).wait_recv()
            self.tcopy(ch, zo, row).start()

    def tasks(self):
        out = super().tasks()
        for j in range(4):
            for yo in range(2):
                if j + yo > 0:
                    out.append(functools.partial(self.x_arrive, j, yo))
        return out

    def finish(self):
        s = self.s
        for ch in range(self.chunks):
            for n in range(8):
                b = self.other(ch, n // 2, n % 2, 1 - s.c)
                send(b, b, self.ts.at[ch, n], self.tr.at[ch, n], s.me).wait_recv()

    def drain(self):
        s = self.s
        super().drain()
        for ch in range(self.chunks):
            for zo in range(4):
                for yo in range(2):
                    self.tcopy(ch, zo, yo).wait_send()
                    far = (s.z != zo) | (s.y != yo)
                    pl.when(far)(lambda: self.xcopy(ch, zo, yo).wait_send())


class Columns:
    @staticmethod
    def sems(parts):
        return [dma((16, parts)), dma((16, parts)), dma((16,)), dma((16,)), dma((parts,))]

    def __init__(self, s, w, dst, parts, sems):
        self.s, self.w, self.dst, self.parts = s, w, dst, parts
        self.e = dst.shape[1] // parts
        self.ps, self.pr, self.xs, self.xr, self.own = sems

    def rows(self, src, half):
        return pl.ds(pl.multiple_of(src * 128 + half * 64, 64), 64)

    def cols(self, p, h):
        return pl.ds(pl.multiple_of(p * 16 * self.e + h * self.e, 128), self.e)

    def copy(self, k, p):
        s = self.s
        to = s.partner(k)
        half = pl.ds(pl.multiple_of(s.dp * 64, 64), 64)
        return send(
            self.w.at[half, self.cols(p, to)],
            self.dst.at[self.rows(s.me, s.dp), pl.ds(p * self.e, self.e)],
            self.ps.at[k, p], self.pr.at[s.me, p], to,
        )

    def local(self, p):
        s = self.s
        return pltpu.make_async_copy(
            self.w.at[:, self.cols(p, s.me)],
            self.dst.at[pl.ds(pl.multiple_of(s.me * 128, 128), 128), pl.ds(p * self.e, self.e)],
            self.own.at[p],
        )

    def begin(self, k):
        for p in range(self.parts):
            (self.copy(k, p) if k else self.local(p)).start()

    def start(self, ahead=16):
        self.ahead = ahead
        for k in range(ahead):
            self.begin(k)

    def over(self, src):
        s = self.s
        b = self.dst.at[self.rows(src, s.dp)]
        return send_over(b, b, self.xs.at[src], self.xr.at[src], s)

    def arrive(self, k):
        s = self.s
        if k + self.ahead - 1 < 16:
            self.begin(k + self.ahead - 1)
        src = s.partner(k)
        for p in range(self.parts):
            b = self.dst.at[self.rows(src, s.dp), pl.ds(p * self.e, self.e)]
            send(b, b, self.ps.at[k, p], self.pr.at[src, p], s.me).wait_recv()
        self.over(src).start()

    def tasks(self):
        return [functools.partial(self.arrive, k) for k in range(1, 16)]

    def finish(self):
        s = self.s
        for k in range(1, 16):
            src = s.partner(k)
            b = self.dst.at[self.rows(src, 1 - s.dp)]
            send_over(b, b, self.xs.at[src], self.xr.at[src], s).wait_recv()
        for p in range(self.parts):
            self.local(p).wait()

    def drain(self):
        s = self.s
        for k in range(1, 16):
            for p in range(self.parts):
                self.copy(k, p).wait_send()
            self.over(s.partner(k)).wait_send()


class Return:
    @staticmethod
    def sems(parts):
        return [dma((16, parts))] * 4 + [dma((parts,))]

    ahead = 16

    def __init__(self, s, src, dst, parts, sems, other=None):
        self.s, self.src, self.dst, self.parts, self.other = s, src, dst, parts, other
        self.e = src.shape[2] // parts
        self.ps, self.pr, self.xs, self.xr, self.own = sems

    def place(self, ref, p, h):
        return ref.at[:, pl.ds(pl.multiple_of(p * 16 * self.e + h * self.e, 128), self.e)]

    def copy(self, k, p):
        s = self.s
        to = s.partner(k)
        return send(
            self.src.at[to, :, pl.ds(p * self.e, self.e)], self.place(self.dst, p, s.me),
            self.ps.at[k, p], self.pr.at[s.me, p], to,
        )

    def local(self, p):
        s = self.s
        return pltpu.make_async_copy(
            self.src.at[s.me, :, pl.ds(p * self.e, self.e)], self.place(self.dst, p, s.me),
            self.own.at[p],
        )

    def begin(self, k):
        for p in range(self.parts):
            if k:
                self.copy(k, p).start()
                continue
            self.local(p).start()
            if self.other is not None:
                self.over(self.s.me, p, own=True).start()

    def start(self, ahead=16):
        self.ahead = ahead
        for k in range(ahead):
            self.begin(k)

    def over(self, h, p, own=False):
        s = self.s
        src = self.src.at[s.me, :, pl.ds(p * self.e, self.e)] if own else self.place(self.dst, p, h)
        return send_over(src, self.place(self.other, p, h), self.xs.at[h, p], self.xr.at[h, p], s)

    def arrive(self, k):
        s = self.s
        if k + self.ahead - 1 < 16:
            self.begin(k + self.ahead - 1)
        h = s.partner(k)
        for p in range(self.parts):
            b = self.place(self.dst, p, h)
            send(b, b, self.ps.at[k, p], self.pr.at[h, p], s.me).wait_recv()
            if self.other is not None:
                self.over(h, p).start()

    def tasks(self):
        return [functools.partial(self.arrive, k) for k in range(1, 16)]

    def finish(self):
        s = self.s
        for p in range(self.parts):
            self.local(p).wait()
        if self.other is not None:
            for k in range(16):
                h = s.partner(k)
                for p in range(self.parts):
                    b = self.place(self.other, p, h)
                    send_over(b, b, self.xs.at[h, p], self.xr.at[h, p], s).wait_recv()
        for k in range(1, 16):
            for p in range(self.parts):
                self.copy(k, p).wait_send()
        if self.other is not None:
            for k in range(16):
                for p in range(self.parts):
                    self.over(s.partner(k), p).wait_send()


class Scatter:
    lag = 3

    @staticmethod
    def scratch(width):
        q = width // 512
        return [
            VM((4, 2, 256, width), bf16), VM((4, 2, 128, width), bf16), VM((4, 2, 128, width), bf16),
            VM((4, 128, width), bf16), VM((5, 128, width), bf16),
            dma((4, q, 2)), dma((4, q, 2)), dma((4, q)), dma((4, q)), dma((4, q)), dma((5, q)),
        ]

    def __init__(self, s, left, right, out, scratch, first=0):
        self.s, self.left, self.right, self.out, self.first = s, left, right, out, first
        self.part, self.sib, self.mid, self.got_y, self.got_z = scratch[:5]
        self.ss, self.sr, self.ys, self.yr, self.zs, self.zr = scratch[5:]
        self.cols = 512
        self.pieces = out.shape[1] // 512
        self.order = [s.arrival(j) for j in (3, 2, 1, 0)]

    def w(self, h):
        return pl.ds(h * self.cols, self.cols)

    def compute(self, k, h, yd, slot):
        tok = pl.multiple_of((self.order[k] * 2 + yd) * 256, 256)
        p = cols_dot(self.left[pl.ds(tok, 256), :], self.right[pl.ds(self.first + h * self.cols, self.cols), :])
        self.part[k, slot, :, self.w(h)] = p.astype(bf16)

    def sib_copy(self, k, h, slot):
        s = self.s
        src = self.part.at[k, slot, pl.ds(pl.multiple_of((1 - s.c) * 128, 128), 128), self.w(h)]
        return send(
            src, self.sib.at[k, slot, :, self.w(h)],
            self.ss.at[k, h, slot], self.sr.at[k, h, slot], s.at(s.z, s.y, 1 - s.c),
        )

    def y_copy(self, k, h):
        s = self.s
        return send(
            self.mid.at[k, 0, :, self.w(h)], self.got_y.at[k, :, self.w(h)],
            self.ys.at[k, h], self.yr.at[k, h], s.at(s.z, 1 - s.y, s.c),
        )

    def z_copy(self, k, h):
        s = self.s
        to = self.order[k]
        up = to > s.z
        hop = jnp.where(up, s.z + 1, s.z - 1)
        slot = jnp.where(up | (hop != to), to, 4)
        return send(
            self.mid.at[k, 1, :, self.w(h)], self.got_z.at[slot, :, self.w(h)],
            self.zs.at[k, h], self.zr.at[slot, h], s.at(hop, s.y, s.c),
        )

    def z_wait(self, slot, h):
        b = self.got_z.at[slot, :, self.w(h)]
        send(b, b, self.zs.at[0, h], self.zr.at[slot, h], self.s.me).wait_recv()

    def fold(self, k, h, slot):
        s = self.s
        self.sib_copy(k, h, slot).wait_recv()
        own = self.part[k, slot, pl.ds(pl.multiple_of(s.c * 128, 128), 128), self.w(h)]
        total = own.astype(f32) + self.sib[k, slot, :, self.w(h)].astype(f32)
        self.mid[k, slot, :, self.w(h)] = total.astype(bf16)

    def after_y(self, k, h):
        s = self.s
        w = self.w(h)
        self.y_copy(k, h).wait_recv()
        total = self.mid[k, 1, :, w].astype(f32) + self.got_y[k, :, w].astype(f32)
        if k == 3:
            self.out[:, w] = total
            return
        to = self.order[k]
        first = jnp.where(to > s.z, s.z == 0, s.z == 3)

        @pl.when(first)
        def _():
            self.mid[k, 1, :, w] = total.astype(bf16)

        @pl.when(jnp.logical_not(first))
        def _():
            self.z_wait(to, h)
            self.mid[k, 1, :, w] = (total + self.got_z[to, :, w].astype(f32)).astype(bf16)

        self.z_copy(k, h).start()

    def tasks(self):
        steps = [(k, h) for k in range(4) for h in range(self.pieces)]
        s = self.s

        def step(i):
            k, h = steps[i]
            self.compute(k, h, 1 - s.y, 0)
            self.sib_copy(k, h, 0).start()
            self.compute(k, h, s.y, 1)
            self.sib_copy(k, h, 1).start()
            self.fold(k, h, 0)
            self.y_copy(k, h).start()
            self.fold(k, h, 1)

        out = []
        for i in range(len(steps) + self.lag):
            if i < len(steps):
                out.append(functools.partial(step, i))
            if i >= self.lag:
                out.append(functools.partial(self.after_y, *steps[i - self.lag]))
        return out

    def finish(self):
        s = self.s
        for h in range(self.pieces):
            w = self.w(h)

            @pl.when(s.z > 0)
            def _():
                self.z_wait(s.z, h)
                self.out[:, w] += self.got_z[s.z, :, w].astype(f32)

            @pl.when(s.z < 3)
            def _():
                self.z_wait(4, h)
                self.out[:, w] += self.got_z[4, :, w].astype(f32)

        for k in range(4):
            for h in range(self.pieces):
                self.sib_copy(k, h, 0).wait_send()
                self.sib_copy(k, h, 1).wait_send()
                self.y_copy(k, h).wait_send()
                if k < 3:
                    self.z_copy(k, h).wait_send()


class Weigh:
    steps = 8

    @classmethod
    def scratch(cls, cols):
        return [
            VM((16, 64, cols), f32), VM((16, 64, cols), bf16), VM((16, 64, cols), bf16),
            dma((cls.steps,)), dma((cls.steps,)),
        ]

    def __init__(self, s, left, right, half, scratch, back=None):
        self.s, self.left, self.right, self.half, self.back = s, left, right, half, back
        self.mine, self.sent, self.got, self.xs, self.xr = scratch

    def at(self, n):
        return self.s.partner(2 * n) // 2

    def copy(self, n):
        i = self.at(n)
        w = pl.ds(2 * i, 2)
        return send_over(self.sent.at[w], self.got.at[w], self.xs.at[i], self.xr.at[i], self.s)

    def compute(self, n):
        i = self.at(n)
        low = self.s.dp == 0
        cols = pl.ds(pl.multiple_of(i * 256, 256), 256)
        got = rows_dot(self.left[:, cols], self.right[...])
        for m in range(2):
            a, b = got[m * 128:m * 128 + 64], got[m * 128 + 64:m * 128 + 128]
            self.mine[2 * i + m] = jnp.where(low, a, b)
            self.sent[2 * i + m] = jnp.where(low, b, a).astype(bf16)
        self.copy(n).start()

    def fold(self, n):
        self.copy(n).wait_recv()
        w = pl.ds(2 * self.at(n), 2)
        self.half[w] = (self.mine[w] + self.got[w].astype(f32)).astype(bf16)
        if self.back is not None:
            self.back.begin(2 * n)
            self.back.begin(2 * n + 1)

    def products(self):
        return [functools.partial(self.compute, i) for i in range(self.steps)]

    def folds(self):
        return [functools.partial(self.fold, i) for i in range(self.steps)]

    def drain(self):
        for i in range(self.steps):
            self.copy(i).wait_send()


def nothing(n):
    return [lambda: None] * n


def halves_of(refs, counts):
    out, at = [], 0
    for n in counts:
        out.append(refs[at:at + n])
        at += n
    return out


def communicate(kernel, name, number, ins, in_specs, outs, out_specs, scratch, flops=0):
    return pl.pallas_call(
        kernel, out_shape=outs, in_specs=in_specs, out_specs=out_specs, scratch_shapes=scratch,
        compiler_params=pltpu.CompilerParams(
            collective_id=number, has_side_effects=True, vmem_limit_bytes=LIMIT
        ),
        cost_estimate=pl.CostEstimate(flops=flops, bytes_accessed=2**24, transcendentals=0),
        name=name,
    )(*ins)


def project_kernel(x, gains, in_w, normed_all, in_cols, gains_all, projected, x_all, normed, row,
                   copies, g_s, g_r, *rest):
    gather_sems, col_sems = halves_of(rest, [7, 5])
    s = Spot()
    greet(s)

    def gain_copy(k):
        return send(gains, gains_all.at[s.me], g_s.at[k], g_r.at[s.me], s.partner(k))

    gather = Gather(s, x, x_all, gather_sems)
    gather.start()
    for k in range(1, 16):
        gain_copy(k).start()
    columns = Columns(s, in_w, in_cols, 3, col_sems)
    columns.start()
    gains_all[s.me] = gains[...]
    x_all[pl.ds(pl.multiple_of(s.me * 128, 128), 128), :] = x[...]

    def gain_row():
        for k in range(1, 16):
            src = s.partner(k)
            b = gains_all.at[src]
            send(b, b, g_s.at[k], g_r.at[src], s.me).wait_recv()
        for j in range(16):
            row[0:1, pl.ds(j * 128, 128)] = gains_all[j, 0:1, :]

    def out_copy(j):
        tok = pl.ds(pl.multiple_of(s.arrival(j) * 512, 512), 512)
        return pltpu.make_async_copy(normed.at[tok], normed_all.at[tok], copies.at[j])

    def use(j):
        if j == 0:
            columns.finish()
            gain_row()
        for n in range(4):
            rows = pl.ds(pl.multiple_of(s.arrival(j) * 512 + n * 128, 128), 128)
            values = x_all[rows, :].astype(f32)
            factor = lax.rsqrt(jnp.mean(values * values, axis=-1, keepdims=True) + epsilon)
            normed[rows, :] = (values * factor * row[0:1, :]).astype(bf16)
        out_copy(j).start()
        tok = pl.ds(pl.multiple_of(s.arrival(j) * 512, 512), 512)
        out = jnp.dot(normed[tok, :], in_cols[...], preferred_element_type=f32)
        projected[tok, :] = out.astype(bf16)

    merged(gather.tasks(use), nothing(2) + columns.tasks() + nothing(8))
    gather.drain()
    columns.drain()
    for k in range(1, 16):
        gain_copy(k).wait_send()
    for j in range(4):
        out_copy(j).wait()


def project(x, gains, in_weight, number):
    tokens, width = x.shape
    return communicate(
        project_kernel, "project", number, (x, gains, in_weight), [vmem(), vmem(), anywhere()],
        [
            jax.ShapeDtypeStruct((16 * tokens, width), bf16),
            jax.ShapeDtypeStruct((width, 3 * DH), bf16),
            jax.ShapeDtypeStruct((16, 8, 128), f32),
            jax.ShapeDtypeStruct((16 * tokens, 3 * DH), bf16),
        ],
        [anywhere(), vmem(), vmem(), vmem()],
        [
            VM((16 * tokens, width), bf16), VM((16 * tokens, width), bf16), VM((8, width), f32),
            dma((4,)), dma((16,)), dma((16,)),
        ] + Gather.sems() + Columns.sems(3),
    )


def kernel_feature(t):
    return jnp.where(t > 0, t + 1.0, jnp.exp(jnp.minimum(t, 0.0)))


def dot_high(left, right, dims=((1,), (0,))):
    return lax.dot_general(
        left, right, (dims, ((), ())), preferred_element_type=f32, precision=highest
    )


def scores_of(query, keys, first):
    raw = cols_dot(query, keys) * (1.0 / math.sqrt(DH))
    row = lax.broadcasted_iota(jnp.int32, raw.shape, 0) + first
    col = lax.broadcasted_iota(jnp.int32, raw.shape, 1)
    return jnp.where(col <= row, raw, -1e30)


class Attend:
    def __init__(self, qkv, keep, mix, local, mem_out, lse, combined, memory, normal):
        self.qkv, self.keep, self.mix = qkv, keep, mix
        self.local, self.mem_out, self.lse, self.combined = local, mem_out, lse, combined
        self.memory, self.normal = memory, normal
        self.segments = qkv.shape[0] // SEG

    def states(self):
        state = jnp.zeros((DH, DH), f32)
        norm = jnp.zeros((1, DH), f32)
        for n in range(self.segments):
            keep = self.keep[n, 0:1, :]
            state, norm = state * keep, norm * keep
            self.memory[n] = state
            self.normal[n, 0:1, :] = norm
            if n + 1 < self.segments:
                rows = pl.ds(n * SEG, SEG)
                fk = kernel_feature(self.qkv[rows, DH:2 * DH].astype(f32)).astype(bf16)
                state = state + rows_dot(fk, self.qkv[rows, 2 * DH:])
                norm = norm + jnp.sum(fk.astype(f32), axis=0, keepdims=True)

    def block(self, n, i):
        rows = pl.ds(n * SEG + i * ROWS, ROWS)
        seen = pl.ds(n * SEG, (i + 1) * ROWS)
        query = self.qkv[rows, :DH]
        scores = scores_of(query, self.qkv[seen, DH:2 * DH], i * ROWS)
        top = jnp.max(scores, axis=-1, keepdims=True)
        expo = jnp.exp(scores - top)
        total = jnp.sum(expo, axis=-1, keepdims=True)
        probs = (expo * (1.0 / total)).astype(bf16)
        local = jnp.dot(probs, self.qkv[seen, 2 * DH:], preferred_element_type=f32)
        fq = kernel_feature(query.astype(f32)).astype(bf16).astype(f32)
        den = jnp.maximum(jnp.sum(fq * self.normal[n, 0:1, :], axis=-1, keepdims=True), 1.0)
        mem_out = dot_high(fq, self.memory[n]) / den
        mix = self.mix[0:1, :]
        self.local[rows, :] = local
        self.mem_out[rows, :] = mem_out
        self.lse[rows, :] = jnp.broadcast_to(top + jnp.log(total), (ROWS, DH))
        self.combined[rows, :] = (mix * mem_out + (1.0 - mix) * local).astype(bf16)

    def blocks(self):
        return [(n, i) for n in range(self.segments) for i in range(SEG // ROWS)]


class AttendBack:
    def __init__(self, qkv, keep, mix, local, mem_out, lse, memory, normal, upstream, grad,
                 mix_grad, dk, dv, state_grad, norm_grad):
        self.qkv, self.keep, self.mix = qkv, keep, mix
        self.local, self.mem_out, self.lse = local, mem_out, lse
        self.memory, self.normal, self.upstream, self.grad = memory, normal, upstream, grad
        self.mix_grad, self.dk, self.dv = mix_grad, dk, dv
        self.state_grad, self.norm_grad = state_grad, norm_grad
        self.segments = qkv.shape[0] // SEG

    def clear(self):
        self.mix_grad[...] = jnp.zeros_like(self.mix_grad)
        self.dk[...] = jnp.zeros_like(self.dk)
        self.dv[...] = jnp.zeros_like(self.dv)
        self.state_grad[...] = jnp.zeros_like(self.state_grad)
        self.norm_grad[...] = jnp.zeros_like(self.norm_grad)

    def block(self, n, i):
        scale = 1.0 / math.sqrt(DH)
        rows = pl.ds(n * SEG + i * ROWS, ROWS)
        seen = pl.ds(n * SEG, (i + 1) * ROWS)
        query = self.qkv[rows, :DH]
        keys = self.qkv[seen, DH:2 * DH]
        values = self.qkv[seen, 2 * DH:]
        up = self.upstream[rows, :].astype(f32)
        mem_out = self.mem_out[rows, :]
        mix = self.mix[0:1, :]
        mixed = jnp.sum(up * (mem_out - self.local[rows, :]), axis=0, keepdims=True)
        self.mix_grad[0:1, :] += mixed * mix * (1.0 - mix)
        memory_grad = up * mix
        local_grad = (up * (1.0 - mix)).astype(bf16)
        query_f = query.astype(f32)
        fq = kernel_feature(query_f).astype(bf16).astype(f32)
        normal = self.normal[n, 0:1, :]
        raw = jnp.sum(fq * normal, axis=-1, keepdims=True)
        den = jnp.maximum(raw, 1.0)
        numer_grad = memory_grad / den
        den_grad = -jnp.sum(memory_grad * mem_out, axis=-1, keepdims=True) / den
        raw_grad = jnp.where(raw > 1.0, den_grad, 0.0)
        fq_grad = dot_high(numer_grad, self.memory[n], ((1,), (1,))) + raw_grad * normal
        if n > 0:
            self.state_grad[n] += dot_high(fq, numer_grad, ((0,), (0,)))
            self.norm_grad[n, 0:1, :] += jnp.sum(raw_grad * fq, axis=0, keepdims=True)
        scores = scores_of(query, keys, i * ROWS)
        probs = jnp.exp(scores - self.lse[rows, 0:1])
        prob_grad = cols_dot(local_grad, values)
        row_term = jnp.sum(probs * prob_grad, axis=-1, keepdims=True)
        score_grad = (probs * (prob_grad - row_term)).astype(bf16)
        query_grad = jnp.dot(score_grad, keys, preferred_element_type=f32) * scale
        query_grad = query_grad + fq_grad * feature_slope(query_f)
        self.grad[rows, :DH] = query_grad.astype(bf16)
        self.dk[seen, :] += rows_dot(score_grad, query) * scale
        self.dv[seen, :] += rows_dot(probs.astype(bf16), local_grad)

    def states(self):
        state = jnp.zeros((DH, DH), f32)
        norm = jnp.zeros((1, DH), f32)
        for n in reversed(range(self.segments)):
            rows = pl.ds(n * SEG, SEG)
            key = self.qkv[rows, DH:2 * DH].astype(f32)
            key_grad = self.dk[rows, :]
            value_grad = self.dv[rows, :]
            if n + 1 < self.segments:
                fk = kernel_feature(key).astype(bf16).astype(f32)
                value = self.qkv[rows, 2 * DH:].astype(f32)
                fk_grad = dot_high(value, state, ((1,), (1,))) + norm
                key_grad = key_grad + fk_grad * feature_slope(key)
                value_grad = value_grad + dot_high(fk, state)
            self.grad[rows, DH:2 * DH] = key_grad.astype(bf16)
            self.grad[rows, 2 * DH:] = value_grad.astype(bf16)
            if n > 0:
                keep = self.keep[n, 0:1, :]
                state = (state + self.state_grad[n]) * keep
                norm = (norm + self.norm_grad[n, 0:1, :]) * keep

    def blocks(self):
        return [(n, i) for n in range(self.segments) for i in range(SEG // ROWS)]


def forward_kernel(qkv, keep, mix, x, gains_all, out_w, cot, gate_up, down,
                   local, mem_out, lse, combined, memory, normal, middle, out_all, cot_all,
                   gate_up_cols, down_cols, hidden_all, act, feed_grad,
                   mixed_tokens, hidden, out_v, cot_v, gate_up_v, down_v, hidden_v, act_v, grad_v,
                   copies, outs, t_s, t_r, *rest):
    sems_o, sems_c, sems_g, sems_d, sems_h = halves_of(rest, [11, 7, 5, 5, 7])
    s = Spot()
    mine = pl.ds(pl.multiple_of(s.me * 128, 128), 128)
    own = [
        pltpu.make_async_copy(out_w, out_v.at[mine], copies.at[0]),
        pltpu.make_async_copy(cot, cot_v.at[mine], copies.at[1]),
    ]
    for cp in own:
        cp.start()
    greet(s)
    gather_o = SharedGather(s, out_w, out_v, sems_o)
    gather_c = Gather(s, cot, cot_v, sems_c)
    gather_h = Gather(s, hidden, hidden_v, sems_h)
    columns_g = Columns(s, gate_up, gate_up_v, 2, sems_g)
    columns_d = Columns(s, down, down_v, 1, sems_d)
    gather_o.start()
    gather_c.start()
    columns_g.start(4)
    attend = Attend(qkv, keep, mix, local, mem_out, lse, combined, memory, normal)

    def token_copy(j):
        return send(
            combined.at[pl.ds(j * 128, 128)],
            mixed_tokens.at[:, pl.ds(pl.multiple_of(s.me * DH, DH), DH)],
            t_s.at[j], t_r.at[s.me], j,
        )

    def block(n, i):
        attend.block(n, i)
        for j in range((n * SEG + i * ROWS) // 128, (n * SEG + (i + 1) * ROWS) // 128):
            pl.when(s.me != j)(lambda: token_copy(j).start())

    compute = [attend.states] + [functools.partial(block, n, i) for n, i in attend.blocks()]
    wholes = [
        pltpu.make_async_copy(a, b, outs.at[4, i])
        for i, (a, b) in enumerate(
            [(out_v, out_all), (cot_v, cot_all), (gate_up_v, gate_up_cols), (down_v, down_cols)]
        )
    ]

    def tokens():
        own[0].wait()
        gather_o.finish()
        mixed_tokens[:, pl.ds(pl.multiple_of(s.me * DH, DH), DH)] = combined[mine, :]
        for k in range(1, 16):
            src = s.partner(k)
            b = mixed_tokens.at[:, pl.ds(pl.multiple_of(src * DH, DH), DH)]
            send(b, b, t_s.at[0], t_r.at[src], s.me).wait_recv()

    def output(j):
        w = pl.ds(j * 512, 512)
        got = jnp.dot(mixed_tokens[...], out_v[:, w], preferred_element_type=f32)
        middle[:, w] = got + x[:, w].astype(f32)

    def norm():
        values = middle[...]
        factor = lax.rsqrt(jnp.mean(values * values, axis=-1, keepdims=True) + epsilon)
        for j in range(16):
            w = pl.ds(j * 128, 128)
            part = (middle[:, w] * factor * gains_all[j, 1:2, :]).astype(bf16)
            hidden[:, w] = part
            hidden_v[mine, w] = part
        gather_h.start()
        wholes[0].start()

    half = act.shape[1]

    def out_copies(j):
        tok = pl.ds(pl.multiple_of(s.arrival(j) * 512, 512), 512)
        pairs = [(hidden_v, hidden_all), (act_v, act), (grad_v, feed_grad)]
        return [
            pltpu.make_async_copy(a.at[tok], b.at[tok], outs.at[j, i]) for i, (a, b) in enumerate(pairs)
        ]

    def use(j):
        if j == 0:
            own[1].wait()
            columns_g.finish()
            columns_d.finish()
            for cp in wholes[1:]:
                cp.start()
        tok = pl.ds(pl.multiple_of(s.arrival(j) * 512, 512), 512)
        act_grad = jnp.dot(cot_v[tok, :], down_v[...], preferred_element_type=f32)
        gate = jnp.dot(hidden_v[tok, :], gate_up_v[:, :half], preferred_element_type=f32)
        up = jnp.dot(hidden_v[tok, :], gate_up_v[:, half:], preferred_element_type=f32)
        sigma = jax.nn.sigmoid(gate)
        silu = gate * sigma
        act_v[tok, :] = (silu * up).astype(bf16)
        slope = sigma * (1.0 + gate * (1.0 - sigma))
        grad_v[tok, :half] = (act_grad * up * slope).astype(bf16)
        grad_v[tok, half:] = (act_grad * silu).astype(bf16)
        for cp in out_copies(j):
            cp.start()

    after = [tokens] + [functools.partial(output, j) for j in range(4)] + [norm]
    c_tasks = gather_c.tasks()
    early = len(c_tasks) * 4 // 5
    merged(gather_o.tasks(), c_tasks[:early], columns_g.tasks(), compute + nothing(len(compute)))
    merged(after, [functools.partial(columns_d.start, 4)])
    merged(
        gather_h.tasks(use),
        c_tasks[early:] + nothing(12),
        nothing(2) + columns_d.tasks() + nothing(8),
    )
    for j in range(16):
        pl.when(s.me != j)(lambda: token_copy(j).wait_send())
    for part in (gather_o, gather_c, gather_h, columns_g, columns_d):
        part.drain()
    for cp in wholes:
        cp.wait()
    for j in range(4):
        for cp in out_copies(j):
            cp.wait()


def forward_of(qkv, keep, mix, x, gains_all, out_weight, cotangent, gate_up, down, number):
    tokens, width = x.shape
    total = qkv.shape[0]
    segments = total // SEG
    half = down.shape[1] // 16
    shape = jax.ShapeDtypeStruct
    rows, cols, fine = (total, width), (width, 2 * half), (total, half)
    return communicate(
        forward_kernel, "forward", number,
        (qkv, keep, mix, x, gains_all, out_weight, cotangent, gate_up, down),
        [vmem()] * 5 + [anywhere()] * 4,
        [
            shape((total, DH), f32), shape((total, DH), f32), shape((total, DH), f32),
            shape((total, DH), bf16), shape((segments, DH, DH), f32), shape((segments, 8, DH), f32),
            shape((tokens, width), f32),
            shape((width, width), bf16), shape(rows, bf16), shape(cols, bf16), shape((width, half), bf16),
            shape(rows, bf16), shape(fine, bf16), shape((total, 2 * half), bf16),
        ],
        [vmem()] * 7 + [anywhere()] * 7,
        [
            VM((tokens, width), bf16), VM((tokens, width), bf16), VM((width, width), bf16),
            VM(rows, bf16), VM(cols, bf16), VM((width, half), bf16), VM(rows, bf16), VM(fine, bf16),
            VM((total, 2 * half), bf16), dma((2,)), dma((5, 4)), dma((16,)), dma((16,)),
        ] + SharedGather.sems() + Gather.sems() + Columns.sems(2) + Columns.sems(1) + Gather.sems(),
    )


def loaded(pairs, sems):
    copies = [pltpu.make_async_copy(a, b, sems.at[i]) for i, (a, b) in enumerate(pairs)]
    for cp in copies:
        cp.start()
    return [cp.wait for cp in copies]


def hidden_grad_kernel(feed_grad, gate_up_cols, hidden_all, act, down_cols, out, half, feed_out,
                       hidden_v, act_v, down_v, copies, *rest):
    sems_w, scratch, scratch_f = halves_of(rest, [5, 11, 11])
    s = Spot()
    loads = loaded([(hidden_all, hidden_v), (act, act_v), (down_cols, down_v)], copies)
    greet(s, plane=False)
    weigh = Weigh(s, hidden_v, feed_grad, half, sems_w)
    scatter = Scatter(s, feed_grad, gate_up_cols, out, scratch)
    filler = Scatter(s, act_v, down_v, feed_out, scratch_f, FILL[0][0])
    merged(
        scatter.tasks(),
        loads + weigh.products() + nothing(16),
        nothing(4) + filler.tasks(),
        nothing(20) + weigh.folds(),
    )
    scatter.finish()
    filler.finish()
    weigh.drain()


def hidden_grad_of(feed_grad, gate_up_cols, hidden_all, act, down_cols, number):
    shape = jax.ShapeDtypeStruct
    total, cols = feed_grad.shape
    width = gate_up_cols.shape[0]
    fill = FILL[0][1]
    return communicate(
        hidden_grad_kernel, "hidden_grad", number,
        (feed_grad, gate_up_cols, hidden_all, act, down_cols), [vmem()] * 2 + [anywhere()] * 3,
        [
            shape((total // 16, width), f32), shape((16, 64, cols), bf16),
            shape((total // 16, fill), f32),
        ],
        [vmem()] * 3,
        [VM(hidden_all.shape, bf16), VM(act.shape, bf16), VM(down_cols.shape, bf16), dma((3,))]
        + Weigh.scratch(cols) + Scatter.scratch(width) + Scatter.scratch(fill),
    )


def normed_grad_kernel(grad, in_cols, normed_all, x, gain, act, down_cols, gains, down_half, combined,
                       attended_all,
                       value_grad, gains_out, feed_out, out_rows, down_rows, down_other, in_mine,
                       in_other, out_other, attended_v, normed_grad, half, gains_v, got, total, theirs, normed_v, act_v, down_v,
                       copies, x_s, x_r, g_s, g_r,
                       *rest):
    sems_d, sems_i, sems_w, scratch, scratch_f = halves_of(rest, [5, 5, 5, 11, 11])
    s = Spot()
    loads = loaded(
        [(normed_all, normed_v), (act, act_v), (down_cols, down_v), (attended_all, attended_v)], copies
    )
    greet(s)
    back_i = Return(s, half, in_mine, 3, sems_i, other=in_other)
    weigh = Weigh(s, normed_v, grad, half, sems_w, back=back_i)
    back_d = Return(s, down_half, down_rows, 1, sems_d, other=down_other)
    scatter = Scatter(s, grad, in_cols, normed_grad, scratch)
    filler = Scatter(s, act_v, down_v, feed_out, scratch_f, FILL[2][0])
    over = send_over(out_rows, out_other, x_s.at[0], x_r.at[0], s)
    back_d.start()

    def out_product(j):
        w = pl.ds(j * 512, 512)
        out_rows[:, w] = rows_dot(combined[...], attended_v[:, w]).astype(bf16)

    products = [functools.partial(out_product, j) for j in range(4)]

    def gain_copy(k):
        to = s.partner(k)
        return send(gains_v.at[to], got.at[s.me], g_s.at[k], g_r.at[s.me], to)

    def epilogue():
        width = x.shape[1]
        values = x[...].astype(f32)
        factor = lax.rsqrt(jnp.mean(values * values, axis=-1, keepdims=True) + epsilon)
        row = jnp.sum(normed_grad[...] * gain[0:1, :] * values, axis=-1, keepdims=True)
        row = row * (1.0 / width) * factor * factor * factor
        for j in range(16):
            w = pl.ds(j * 128, 128)
            v = x[:, w].astype(f32)
            u = normed_grad[:, w]
            value_grad[:, w] = factor * (u * gain[0:1, w]) - v * row
            gains_v[j] = gains[j]
            gains_v[j, 0:1, :] = jnp.sum(u * v * factor, axis=0, keepdims=True)

    merged(
        scatter.tasks(),
        loads[:3] + weigh.products() + nothing(24),
        nothing(5) + weigh.folds() + nothing(12),
        nothing(4) + loads[3:] + products + [over.start] + back_d.tasks() + nothing(5),
        nothing(4) + filler.tasks(),
        nothing(16) + back_i.tasks(),
    )
    scatter.finish()
    epilogue()
    for k in range(1, 16):
        gain_copy(k).start()
    filler.finish()
    back_d.finish()
    back_i.finish()
    weigh.drain()
    over.wait()
    for k in range(1, 16):
        src = s.partner(k)
        b = got.at[src]
        send(b, b, g_s.at[k], g_r.at[src], s.me).wait_recv()
    got[s.me] = gains_v[s.me]
    acc = got[0]
    for k in range(1, 16):
        acc = acc + got[k]
    total[...] = acc
    cp = send_over(total, theirs, x_s.at[1], x_r.at[1], s)
    cp.start()
    for k in range(1, 16):
        gain_copy(k).wait_send()
    cp.wait()
    gains_out[...] = total[...] + theirs[...]


def normed_grad_of(grad, in_cols, normed_all, x, gain, act, down_cols, gains, down_half, combined,
                   attended_all, number):
    shape = jax.ShapeDtypeStruct
    total, cols = grad.shape
    tokens, width = x.shape
    fill = FILL[2][1]
    down_rows = shape((64, 16 * down_half.shape[2]), bf16)
    in_rows = shape((64, 16 * cols), bf16)
    return communicate(
        normed_grad_kernel, "normed_grad", number,
        (grad, in_cols, normed_all, x, gain, act, down_cols, gains, down_half, combined, attended_all),
        [vmem()] * 2 + [anywhere()] + [vmem()] * 2 + [anywhere()] * 2 + [vmem(), anywhere(), vmem(), anywhere()],
        [
            shape((tokens, width), f32), shape((8, 128), f32), shape((tokens, fill), f32),
            shape((DH, width), bf16), down_rows, down_rows, in_rows, in_rows, shape((DH, width), bf16),
        ],
        [vmem()] * 4 + [anywhere()] * 5,
        [
            VM(attended_all.shape, bf16),
            VM((tokens, width), f32), VM((16, 64, cols), bf16), VM((16, 8, 128), f32),
            VM((16, 8, 128), f32), VM((8, 128), f32), VM((8, 128), f32),
            VM(normed_all.shape, bf16), VM(act.shape, bf16), VM(down_cols.shape, bf16), dma((4,)),
            dma((2,)), dma((2,)), dma((16,)), dma((16,)),
        ] + Return.sems(1) + Return.sems(3) + Weigh.scratch(cols) + Scatter.scratch(width)
        + Scatter.scratch(fill),
    )


def attend_back_kernel(attended, out_all, qkv, keep, mix, local, mem_out, lse, memory, normal,
                       gate_up_half, cot_all, act, down_cols,
                       attended_all, grad, mix_grad, gate_up_rows, gate_up_other, down_half, feed_out,
                       out_v, cot_v, by_token, upstream, dk, dv, state_grad, norm_grad, copies, h_s, h_r,
                       *rest):
    sems_a, sems_g, sems_w, scratch_f = halves_of(rest, [7, 5, 5, 11])
    s = Spot()
    mine = pl.ds(pl.multiple_of(s.me * 128, 128), 128)
    cot_load = pltpu.make_async_copy(cot_all, cot_v, copies.at[2])
    load = pltpu.make_async_copy(out_all, out_v, copies.at[0])
    load.start()
    own = pltpu.make_async_copy(attended, attended_all.at[mine], copies.at[1])
    own.start()
    cot_load.start()
    greet(s)
    gather = Gather(s, attended, attended_all, sems_a)
    back_g = Return(s, gate_up_half, gate_up_rows, 2, sems_g, other=gate_up_other)
    filler = Scatter(s, act, down_cols, feed_out, scratch_f, FILL[1][0])
    weigh = Weigh(s, cot_v, act, down_half, sems_w)
    attend = AttendBack(qkv, keep, mix, local, mem_out, lse, memory, normal, upstream, grad,
                        mix_grad, dk, dv, state_grad, norm_grad)
    attend.clear()
    gather.start()
    load.wait()

    def head_copy(j):
        return send(by_token.at[:, pl.ds(j * DH, DH)], upstream.at[mine], h_s.at[j], h_r.at[s.me], j)

    for j in range(4):
        w = pl.ds(j * 512, 512)
        by_token[:, w] = cols_dot(attended[...], out_v[w, :]).astype(bf16)
        for h in range(4 * j, 4 * j + 4):
            pl.when(s.me != h)(lambda: head_copy(h).start())
    upstream[mine, :] = by_token[:, pl.ds(pl.multiple_of(s.me * DH, DH), DH)]
    cot_load.wait()
    filler.lag = 8

    def arrive(j):
        b = upstream.at[pl.ds(j * 128, 128)]
        pl.when(s.me != j)(lambda: send(b, b, h_s.at[j], h_r.at[j], s.me).wait_recv())

    def block(n, i):
        for j in range((n * SEG + i * ROWS) // 128, (n * SEG + (i + 1) * ROWS) // 128):
            arrive(j)
        attend.block(n, i)

    compute = [functools.partial(block, n, i) for n, i in attend.blocks()] + [attend.states]
    merged(gather.tasks(), nothing(2) + compute, weigh.products() + nothing(12))
    back_g.start()
    merged(filler.tasks(), back_g.tasks(), weigh.folds())
    filler.finish()
    back_g.finish()
    weigh.drain()
    for j in range(16):
        pl.when(s.me != j)(lambda: head_copy(j).wait_send())
    gather.drain()
    own.wait()


def attend_backward(attended, out_all, qkv, keep, mix, saved, gate_up_half, cot_all, act, down_cols,
                    number):
    tokens, width = attended.shape
    total = qkv.shape[0]
    segments = total // SEG
    shape = jax.ShapeDtypeStruct
    local, mem_out, lse, memory, normal = saved
    rows = shape((64, 16 * gate_up_half.shape[2]), bf16)
    return communicate(
        attend_back_kernel, "attend_back", number,
        (attended, out_all, qkv, keep, mix, local, mem_out, lse, memory, normal,
         gate_up_half, cot_all, act, down_cols),
        [vmem(), anywhere()] + [vmem()] * 8 + [anywhere()] * 2 + [vmem()] * 2,
        [
            shape((total, width), bf16), shape((total, 3 * DH), bf16), shape((8, DH), f32),
            rows, rows, shape((16, 64, act.shape[1]), bf16), shape((tokens, FILL[1][1]), f32),
        ],
        [anywhere(), vmem(), vmem(), anywhere(), anywhere(), vmem(), vmem()],
        [
            VM(out_all.shape, bf16), VM(cot_all.shape, bf16), VM((tokens, width), bf16),
            VM((total, DH), bf16),
            VM((total, DH), f32), VM((total, DH), f32), VM((segments, DH, DH), f32),
            VM((segments, 8, DH), f32), dma((3,)), dma((16,)), dma((16,)),
        ] + Gather.sems() + Return.sems(2) + Weigh.scratch(act.shape[1]) + Scatter.scratch(FILL[1][1]),
    )


def body(
    layer_input,
    first_gain,
    in_weight,
    out_weight,
    mix_gate,
    second_gain,
    gate_up,
    down_weight,
    document_starts,
    cotangent,
):
    tokens, width = layer_input.shape
    total = tokens * H
    segments = total // SEG
    dp = lax.axis_index("dp")

    own_gains = jnp.zeros((8, tokens), f32)
    own_gains = own_gains.at[0].set(first_gain.astype(f32)).at[1].set(second_gain.astype(f32))
    mix = jnp.broadcast_to(jax.nn.sigmoid(mix_gate.astype(f32))[None], (8, DH))
    numbers = jnp.arange(segments)
    fresh = (numbers == 0) | (document_starts[0] > 0)
    keep = jnp.broadcast_to(jnp.where(fresh, 0.0, 1.0)[:, None, None], (segments, 8, DH))

    normed_all, in_cols, gains_all, qkv = project(layer_input, own_gains, in_weight, 0)
    (local, mem_out, lse, combined, memory, normal, middle, out_all, cot_all, gate_up_cols, down_cols,
     hidden_all, act, feed_grad) = forward_of(
        qkv, keep, mix, layer_input, gains_all, out_weight, cotangent, gate_up, down_weight, 1
    )
    hidden_grad, gate_up_half, feed_out_0 = hidden_grad_of(
        feed_grad, gate_up_cols, hidden_all, act, down_cols, 3
    )

    first_all = gains_all[:, 0].reshape(width)
    second_all = gains_all[:, 1].reshape(width)
    upstream = cotangent.astype(f32)
    second_factor = lax.rsqrt(jnp.mean(middle * middle, axis=-1, keepdims=True) + epsilon)
    middle_norm_grad, second_local = norm_backward(middle, second_factor, second_all, hidden_grad)
    middle_grad = upstream + middle_norm_grad
    (attended_all, projected_grad, mix_grad, gate_up_rows, gate_up_other, down_half,
     feed_out_1) = attend_backward(
        middle_grad.astype(bf16), out_all, qkv, keep, mix, (local, mem_out, lse, memory, normal),
        gate_up_half, cot_all, act, down_cols, 4,
    )
    mix_rows = jnp.where((jnp.arange(H) == lax.axis_index(AXIS))[:, None], mix_grad[0:1], 0.0)
    gain_grads = jnp.stack([mix_rows, second_local.reshape(16, 128), mix_rows], axis=1)
    gain_grads = jnp.pad(gain_grads, ((0, 0), (0, 5), (0, 0)))
    (value_grad, gains_out, feed_out_2, out_rows, down_rows, down_other, in_mine_rows, in_other_rows,
     out_other) = normed_grad_of(
        projected_grad, in_cols, normed_all, layer_input, jnp.broadcast_to(first_all[None], (8, width)),
        act, down_cols, gain_grads, down_half, combined, attended_all, 5,
    )
    input_grad = middle_grad + value_grad
    feed_out = jnp.concatenate([feed_out_0, feed_out_1, feed_out_2], axis=1)
    layer_output = (middle + feed_out).astype(bf16)

    def both_halves(mine, other):
        low = jnp.where(dp == 0, mine, other)
        high = jnp.where(dp == 0, other, mine)
        return jnp.concatenate([low, high]).astype(f32)

    return (
        layer_output,
        input_grad,
        gains_out[0],
        both_halves(in_mine_rows, in_other_rows),
        out_rows.astype(f32) + out_other.astype(f32),
        gains_out[2],
        gains_out[1],
        both_halves(gate_up_rows, gate_up_other),
        both_halves(down_rows, down_other),
    )


def solution(mesh):
    one_group = mesh.shape[AXIS] == H and mesh.shape["dp"] == 2
    return jax.shard_map(
        body if one_group else body_groups,
        mesh=mesh,
        in_specs=(
            P(("dp", "fsdp"), None),
            P("fsdp"),
            P("fsdp", None),
            P("fsdp", None),
            P("fsdp"),
            P("fsdp"),
            P("fsdp", None),
            P("fsdp", None),
            P("dp", None),
            P(("dp", "fsdp"), None),
        ),
        out_specs=(
            P(("dp", "fsdp"), None),
            P(("dp", "fsdp"), None),
            P("fsdp"),
            P("fsdp", None),
            P("fsdp", None),
            P("fsdp"),
            P("fsdp"),
            P("fsdp", None),
            P("fsdp", None),
        ),
        check_vma=False,
    )
```

```python
import functools
import math

import jax
import jax.numpy as jnp
from jax import lax
from jax.experimental import pallas as pl
from jax.experimental.pallas import tpu as pltpu
from jax.sharding import PartitionSpec as P

H = 16
DH = 128
FF = 8192
SEG = 1024

highest = lax.Precision.HIGHEST
epsilon = 1e-06
f32 = jnp.float32
bf16 = jnp.bfloat16
AXIS = "fsdp"


def feature(values):
    return jax.nn.elu(values) + 1.0


def feature_slope(values):
    return jnp.where(values > 0, 1.0, jnp.exp(jnp.minimum(values, 0.0)))


def norm_forward(values, gain):
    factor = lax.rsqrt(jnp.mean(values * values, axis=-1, keepdims=True) + epsilon)
    return (values * factor * gain, factor)


def norm_backward(values, factor, gain, upstream):
    scaled = upstream * gain
    gain_grad = jnp.sum(upstream * values * factor, axis=0)
    value_grad = factor * scaled - values * (factor * factor * factor) * jnp.mean(
        scaled * values, axis=-1, keepdims=True
    )
    return (value_grad, gain_grad)


def dot(left, right, dims):
    return lax.dot_general(left, right, ((dims[0], dims[1]), ((), ())), preferred_element_type=f32)


def rows_dot(left, right):
    return dot(left, right, ((0,), (0,)))


def cols_dot(left, right):
    return dot(left, right, ((1,), (1,)))


class Layout:
    def __init__(self):
        self.count = lax.axis_size(AXIS)
        self.groups = self.count // H
        self.place = lax.axis_index(AXIS)
        self.head = self.place % H
        self.group = self.place // H
        self.inside = None
        self.across = None
        if self.groups > 1:
            self.inside = [[g * H + j for j in range(H)] for g in range(self.groups)]
            self.across = [[g * H + j for g in range(self.groups)] for j in range(H)]

    def gather(self, block):
        return lax.all_gather(block, AXIS, axis=0, tiled=True, axis_index_groups=self.inside)

    def gather_all(self, block):
        return lax.all_gather(block, AXIS, axis=0, tiled=True)

    def scatter_sum(self, whole):
        return lax.psum_scatter(
            whole, AXIS, scatter_dimension=0, tiled=True, axis_index_groups=self.inside
        )

    def columns(self, block, parts):
        rows, width = block.shape
        each = width // (parts * H)
        if self.groups == 1:
            split = block.reshape(rows, parts, H, each)
            out = lax.all_to_all(split, AXIS, 2, 0, tiled=True)
            return out.reshape(rows * self.count, parts * each)
        whole = self.gather_all(block).reshape(rows * self.count, parts, H, each)
        out = lax.dynamic_index_in_dim(whole, self.head, 2, False)
        return out.reshape(rows * self.count, parts * each)

    def own_rows(self, grad, parts):
        rows, width = grad.shape
        each = width // parts
        if self.groups == 1:
            split = grad.astype(bf16).reshape(rows, parts, 1, each)
            out = lax.all_to_all(split, AXIS, 0, 2, tiled=True)
            return out.reshape(rows // self.count, parts * H * each)
        whole = jnp.zeros((rows, parts, H, each), f32)
        whole = lax.dynamic_update_slice_in_dim(
            whole, grad.reshape(rows, parts, 1, each), self.head, 2
        )
        return lax.psum_scatter(
            whole.reshape(rows, parts * H * each), AXIS, scatter_dimension=0, tiled=True
        )

    def to_tokens(self, by_head):
        tokens, each = by_head.shape
        out = lax.all_to_all(
            by_head.reshape(H, tokens // H, each), AXIS, 0, 0, tiled=False,
            axis_index_groups=self.inside,
        )
        return out.transpose(1, 0, 2).reshape(tokens // H, H * each)

    def to_heads(self, by_token):
        tokens, width = by_token.shape
        split = by_token.reshape(tokens, H, width // H).transpose(1, 0, 2)
        out = lax.all_to_all(
            split, AXIS, 0, 0, tiled=False, axis_index_groups=self.inside
        )
        return out.reshape(H * tokens, width // H)


def carry_forward(layout, delta, count, fresh):
    segments = delta.shape[0]

    def walk(state):
        before = []
        for s in range(segments):
            state = jax.tree.map(lambda a: jnp.where(fresh[s], jnp.zeros_like(a), a), state)
            before.append(state)
            state = (state[0] + delta[s], state[1] + count[s])
        return before, state

    state = (jnp.zeros_like(delta[0]), jnp.zeros_like(count[0]))
    if layout.groups > 1:
        _, last = walk(state)
        renewed = jnp.any(fresh).astype(f32)
        every = jax.tree.map(
            lambda a: lax.all_gather(a, AXIS, axis_index_groups=layout.across), last + (renewed,)
        )
        for g in range(layout.groups - 1):
            keep = every[2][g] < 0.5
            after = jax.tree.map(lambda a, e: jnp.where(keep, a, 0.0) + e[g], state, every[:2])
            state = jax.tree.map(lambda a, b: jnp.where(g < layout.group, b, a), state, after)
    before, _ = walk(state)
    return jnp.stack([b[0] for b in before]), jnp.stack([b[1] for b in before])


def carry_backward(layout, state_grad, norm_grad, fresh):
    segments = state_grad.shape[0]

    def walk(state):
        after = [None] * segments
        for s in reversed(range(segments)):
            after[s] = state
            state = (state[0] + state_grad[s], state[1] + norm_grad[s])
            state = jax.tree.map(lambda a: jnp.where(fresh[s], jnp.zeros_like(a), a), state)
        return after, state

    state = (jnp.zeros_like(state_grad[0]), jnp.zeros_like(norm_grad[0]))
    if layout.groups > 1:
        _, first = walk(state)
        renewed = jnp.any(fresh).astype(f32)
        every = jax.tree.map(
            lambda a: lax.all_gather(a, AXIS, axis_index_groups=layout.across), first + (renewed,)
        )
        for g in reversed(range(1, layout.groups)):
            keep = every[2][g] < 0.5
            before = jax.tree.map(lambda a, e: jnp.where(keep, a, 0.0) + e[g], state, every[:2])
            state = jax.tree.map(lambda a, b: jnp.where(g > layout.group, b, a), state, before)
    after, _ = walk(state)
    return jnp.stack([a[0] for a in after]), jnp.stack([a[1] for a in after])


def body_groups(
    layer_input,
    first_gain,
    in_weight,
    out_weight,
    mix_gate,
    second_gain,
    gate_up,
    down_weight,
    document_starts,
    cotangent,
):
    layout = Layout()
    tokens, width = layer_input.shape
    group_tokens = tokens * H
    segments = group_tokens // SEG
    scale = 1.0 / math.sqrt(DH)

    gains = jnp.stack([first_gain, second_gain])
    gains = lax.all_gather(gains, AXIS, axis=1, tiled=True).astype(f32)
    first_all, second_all = gains[0], gains[1]
    if layout.groups == 1:
        mix_own = mix_gate
    else:
        mix_own = lax.dynamic_slice_in_dim(layout.gather_all(mix_gate), layout.head * DH, DH)
    mix = jax.nn.sigmoid(mix_own.astype(f32))[None]

    inputs = layer_input.astype(f32)
    normed, first_factor = norm_forward(inputs, first_all)
    normed_all = layout.gather(normed.astype(bf16))
    in_cols = layout.columns(in_weight, 3)
    out_all = layout.gather_all(out_weight)
    cot_all = layout.gather(cotangent)
    gate_up_cols = layout.columns(gate_up, 2)
    down_cols = layout.columns(down_weight, 1)

    projected = jnp.dot(normed_all, in_cols, preferred_element_type=f32).astype(bf16)
    by_segment = projected.reshape(segments, SEG, 3, DH)
    query, key, value = by_segment[:, :, 0], by_segment[:, :, 1], by_segment[:, :, 2]
    index = jnp.arange(SEG, dtype=jnp.int32)
    allowed = index[None, :] <= index[:, None]

    def attention_scores():
        raw = jnp.einsum("sqc,skc->sqk", query, key, preferred_element_type=f32) * scale
        return jnp.where(allowed[None], raw, -1e30)

    scores = attention_scores()
    top = jnp.max(scores, axis=-1, keepdims=True)
    expo = jnp.exp(scores - top)
    total = jnp.sum(expo, axis=-1, keepdims=True)
    log_total = top + jnp.log(total)
    probs_low = (expo / total).astype(bf16)
    local_out = jnp.einsum("sqk,skc->sqc", probs_low, value, preferred_element_type=f32)

    query_f, key_f, value_f = query.astype(f32), key.astype(f32), value.astype(f32)
    query_feature = feature(query_f).astype(bf16)
    key_feature = feature(key_f).astype(bf16)
    delta = jnp.einsum("slc,sla->sca", key_feature, value, preferred_element_type=f32)
    count = jnp.sum(key_feature.astype(f32), axis=1)
    numbers = layout.group * segments + jnp.arange(segments)
    fresh = (numbers == 0) | (
        lax.dynamic_slice_in_dim(document_starts[0], layout.group * segments, segments) > 0
    )
    memory, normal = carry_forward(layout, delta, count, fresh)
    query_feature_f = query_feature.astype(f32)
    numerator = jnp.einsum("sie,sej->sij", query_feature_f, memory, precision=highest)
    raw_denom = jnp.einsum("sik,sk->si", query_feature_f, normal, precision=highest)[..., None]
    denom = jnp.maximum(raw_denom, 1.0)
    memory_out = numerator / denom
    combined = mix * memory_out + (1.0 - mix) * local_out
    combined_head = combined.reshape(group_tokens, DH).astype(bf16)
    combined_low = layout.to_tokens(combined_head)
    attended = jnp.dot(combined_low, out_all, preferred_element_type=f32)
    middle = inputs + attended

    hidden, second_factor = norm_forward(middle, second_all)
    hidden_all = layout.gather(hidden.astype(bf16))
    act_grad = jnp.dot(cot_all, down_cols, preferred_element_type=f32)
    both = jnp.dot(hidden_all, gate_up_cols, preferred_element_type=f32)
    half = both.shape[1] // 2
    gate_part, up_part = both[:, :half], both[:, half:]
    sigma = jax.nn.sigmoid(gate_part)
    silu = gate_part * sigma
    activated = (silu * up_part).astype(bf16)
    silu_slope = sigma * (1.0 + gate_part * (1.0 - sigma))
    feed_grad = jnp.concatenate(
        [act_grad * up_part * silu_slope, act_grad * silu], axis=1
    ).astype(bf16)
    feed_out = layout.scatter_sum(cols_dot(activated, down_cols).astype(bf16))
    hidden_grad = layout.scatter_sum(cols_dot(feed_grad, gate_up_cols).astype(bf16))
    layer_output = (middle + feed_out.astype(f32)).astype(bf16)
    gate_up_part = layout.own_rows(rows_dot(hidden_all, feed_grad), 2)
    down_part = layout.own_rows(rows_dot(cot_all, activated), 1)

    upstream = cotangent.astype(f32)
    middle_norm_grad, second_local = norm_backward(
        middle, second_factor, second_all, hidden_grad.astype(f32)
    )
    middle_grad = upstream + middle_norm_grad
    attended_grad = middle_grad.astype(bf16)
    attended_grad_all = layout.gather(attended_grad)
    combined_grad = layout.to_heads(cols_dot(attended_grad, out_all).astype(bf16))
    combined_grad = combined_grad.astype(f32).reshape(segments, SEG, DH)
    out_rows_grad = rows_dot(combined_head, attended_grad_all)
    if layout.groups == 1:
        out_part = out_rows_grad
    else:
        whole = jnp.zeros((H * DH, width), f32)
        whole = lax.dynamic_update_slice_in_dim(whole, out_rows_grad, layout.head * DH, 0)
        out_part = lax.psum_scatter(whole, AXIS, scatter_dimension=0, tiled=True)
    mix_local = jnp.sum(combined_grad * (memory_out - local_out), axis=(0, 1)) * (
        mix * (1.0 - mix)
    ).reshape(DH)

    memory_grad = combined_grad * mix
    local_grad = (combined_grad * (1.0 - mix)).astype(bf16)
    numer_grad = memory_grad / denom
    denom_grad = -jnp.sum(memory_grad * memory_out, axis=-1, keepdims=True) / denom
    raw_grad = jnp.where(raw_denom > 1.0, denom_grad, 0.0)
    query_feature_grad = (
        jnp.einsum("sij,sej->sie", numer_grad, memory, precision=highest)
        + raw_grad * normal[:, None]
    )
    state_grad = jnp.einsum("sie,sij->sej", query_feature_f, numer_grad, precision=highest)
    norm_grad = jnp.sum(raw_grad * query_feature_f, axis=1)
    delta_grad, count_grad = carry_backward(layout, state_grad, norm_grad, fresh)
    key_feature_grad = (
        jnp.einsum("sij,sej->sie", value_f, delta_grad, precision=highest) + count_grad[:, None]
    )
    value_memory_grad = jnp.einsum(
        "sie,sej->sij", key_feature.astype(f32), delta_grad, precision=highest
    )
    query_memory_grad = query_feature_grad * feature_slope(query_f)
    key_memory_grad = key_feature_grad * feature_slope(key_f)

    probs = jnp.exp(attention_scores() - log_total)
    prob_grad = jnp.einsum("sqc,skc->sqk", local_grad, value, preferred_element_type=f32)
    row_term = jnp.sum(probs * prob_grad, axis=-1, keepdims=True)
    score_grad = (probs * (prob_grad - row_term)).astype(bf16)
    query_grad = query_memory_grad + scale * jnp.einsum(
        "sqk,skc->sqc", score_grad, key, preferred_element_type=f32
    )
    key_grad = key_memory_grad + scale * jnp.einsum(
        "sqk,sqc->skc", score_grad, query, preferred_element_type=f32
    )
    value_grad = value_memory_grad + jnp.einsum(
        "sqk,sqc->skc", probs.astype(bf16), local_grad, preferred_element_type=f32
    )
    projected_grad = (
        jnp.stack([query_grad, key_grad, value_grad], axis=2)
        .reshape(group_tokens, 3 * DH)
        .astype(bf16)
    )
    normed_grad = layout.scatter_sum(cols_dot(projected_grad, in_cols).astype(bf16))
    in_part = layout.own_rows(rows_dot(normed_all, projected_grad), 3)
    input_norm_grad, first_local = norm_backward(
        inputs, first_factor, first_all, normed_grad.astype(f32)
    )
    input_grad = middle_grad + input_norm_grad

    gains_part = lax.psum_scatter(
        jnp.stack([first_local, second_local]), AXIS, scatter_dimension=1, tiled=True
    )
    if layout.groups == 1:
        mix_part = mix_local
    else:
        whole = jnp.zeros((H * DH,), f32)
        whole = lax.dynamic_update_slice_in_dim(whole, mix_local, layout.head * DH, 0)
        mix_part = lax.psum_scatter(whole, AXIS, scatter_dimension=0, tiled=True)

    def over_sequences(part):
        return lax.psum(part.astype(bf16), "dp").astype(f32)

    small = over_sequences(jnp.concatenate([gains_part, mix_part[None]]))
    return (
        layer_output,
        input_grad,
        small[0],
        over_sequences(in_part),
        over_sequences(out_part),
        small[2],
        small[1],
        over_sequences(gate_up_part),
        over_sequences(down_part),
    )


MESH = pl.DeviceIdType.MESH
LIMIT = 60 * 2**20
FILL = ((0, 512), (512, 1024), (1536, 512))
ROWS = 256
dma = pltpu.SemaphoreType.DMA
VM = pltpu.VMEM


def vmem():
    return pl.BlockSpec(memory_space=pltpu.VMEM)


def anywhere():
    return pl.BlockSpec(memory_space=pl.ANY)


class Spot:
    def __init__(self):
        self.dp = lax.axis_index("dp")
        self.me = lax.axis_index(AXIS)
        self.z = self.me // 4
        self.y = (self.me // 2) % 2
        self.c = self.me % 2

    def at(self, z, y, c):
        return z * 4 + y * 2 + c

    def partner(self, k):
        out = self.me
        for bit in (1, 2, 4, 8):
            if k & bit:
                out = out + bit - 2 * bit * ((self.me // bit) % 2)
        return out

    def arrival(self, j):
        if j == 0:
            return self.z
        ends = jnp.where(self.z == 0, j, 3 - j)
        middle = {1: (0, 3), 2: (2, 1), 3: (3, 0)}[j]
        inner = jnp.where(self.z == 1, middle[0], middle[1])
        return jnp.where((self.z == 0) | (self.z == 3), ends, inner)


def greet(s, plane=True, other=True):
    ids = []
    if plane:
        ids += [{AXIS: (s.me + k) % 16} for k in range(1, 16)]
    else:
        ids += [{AXIS: s.at((s.z + k) % 4, s.y, s.c)} for k in (1, 2, 3)]
        ids += [{AXIS: s.at(s.z, 1 - s.y, s.c)}, {AXIS: s.at(s.z, s.y, 1 - s.c)}]
    if other:
        ids += [{"dp": 1 - s.dp}]
    barrier = pltpu.get_barrier_semaphore()
    for d in ids:
        pl.semaphore_signal(barrier, inc=1, device_id=d, device_id_type=MESH)
    pl.semaphore_wait(barrier, len(ids))


def send(src, dst, ssem, rsem, to):
    return pltpu.make_async_remote_copy(
        src_ref=src, dst_ref=dst, send_sem=ssem, recv_sem=rsem,
        device_id={AXIS: to}, device_id_type=MESH,
    )


def send_over(src, dst, ssem, rsem, s):
    return pltpu.make_async_remote_copy(
        src_ref=src, dst_ref=dst, send_sem=ssem, recv_sem=rsem,
        device_id={"dp": 1 - s.dp}, device_id_type=MESH,
    )


def merged(*lists):
    keyed = []
    for n, tasks in enumerate(lists):
        keyed += [((i + 0.5) / len(tasks), n, i, t) for i, t in enumerate(tasks)]
    for _, _, _, t in sorted(keyed, key=lambda e: e[:3]):
        t()


class Gather:
    chunks = 4

    @classmethod
    def sems(cls):
        return [dma((cls.chunks, 4))] * 5 + [dma((cls.chunks, 8))] * 2

    def __init__(self, s, src, dst, sems):
        self.s, self.src, self.dst = s, src, dst
        self.zr, self.zu, self.zd, self.ys, self.yr, self.ss, self.sr = sems[:7]
        self.rows = 128 // self.chunks
        self.skip = 0

    def block(self, ch, z, y, c):
        start = self.s.at(z, y, c) * 128 + self.skip + ch * self.rows
        return self.dst.at[pl.ds(pl.multiple_of(start, self.rows), self.rows)]

    def own(self, ch):
        start = pl.multiple_of(self.skip + ch * self.rows, self.rows)
        return self.src.at[pl.ds(start, self.rows)]

    def zcopy(self, ch, zo, up, own=False):
        s = self.s
        dst = self.block(ch, zo, s.y, s.c)
        to = s.at(s.z + 1 if up else s.z - 1, s.y, s.c)
        return send(
            self.own(ch) if own else dst, dst,
            (self.zu if up else self.zd).at[ch, zo], self.zr.at[ch, zo], to,
        )

    def ycopy(self, ch, zo, own=False):
        s = self.s
        dst = self.block(ch, zo, s.y, s.c)
        src = self.own(ch) if own else dst
        return send(src, dst, self.ys.at[ch, zo], self.yr.at[ch, zo], s.at(s.z, 1 - s.y, s.c))

    def scopy(self, ch, zo, yo, own=False):
        s = self.s
        dst = self.block(ch, zo, yo, s.c)
        n = zo * 2 + yo
        src = self.own(ch) if own else dst
        return send(src, dst, self.ss.at[ch, n], self.sr.at[ch, n], s.at(s.z, s.y, 1 - s.c))

    def start(self):
        s = self.s
        for ch in range(self.chunks):
            pl.when(s.z < 3)(lambda: self.zcopy(ch, s.z, True, True).start())
            pl.when(s.z > 0)(lambda: self.zcopy(ch, s.z, False, True).start())
            self.ycopy(ch, s.z, True).start()
            self.scopy(ch, s.z, s.y, True).start()

    def passed_on(self, ch, zo, yo):
        self.scopy(ch, zo, yo).start()

    def z_arrive(self, ch, j):
        s = self.s
        zo = s.arrival(j)
        self.zcopy(ch, zo, True).wait_recv()
        pl.when((zo < s.z) & (s.z < 3))(lambda: self.zcopy(ch, zo, True).start())
        pl.when((zo > s.z) & (s.z > 0))(lambda: self.zcopy(ch, zo, False).start())
        self.ycopy(ch, zo).start()
        self.passed_on(ch, zo, s.y)

    def y_arrive(self, ch, j):
        s = self.s
        zo = s.arrival(j)
        b = self.block(ch, zo, 1 - s.y, s.c)
        send(b, b, self.ys.at[ch, zo], self.yr.at[ch, zo], s.me).wait_recv()
        self.passed_on(ch, zo, 1 - s.y)

    def s_arrive(self, j):
        s = self.s
        zo = s.arrival(j)
        for ch in range(self.chunks):
            for yo in range(2):
                n = zo * 2 + yo
                b = self.block(ch, zo, yo, 1 - s.c)
                send(b, b, self.ss.at[ch, n], self.sr.at[ch, n], s.me).wait_recv()

    def tasks(self, use=None):
        out = []
        for step in range(1, 5):
            for ch in range(self.chunks):
                if step < 4:
                    out.append(functools.partial(self.z_arrive, ch, step))
                out.append(functools.partial(self.y_arrive, ch, step - 1))
                if step == 4 and ch < 3 and use is not None:
                    out.append(functools.partial(use, ch))
            out.append(functools.partial(self.s_arrive, step - 1))
        if use is not None:
            out.append(functools.partial(use, 3))
        return out

    def drain(self):
        s = self.s
        for ch in range(self.chunks):
            for zo in range(4):
                pl.when((s.z < 3) & (zo <= s.z))(lambda: self.zcopy(ch, zo, True).wait_send())
                pl.when((s.z > 0) & (zo >= s.z))(lambda: self.zcopy(ch, zo, False).wait_send())
                self.ycopy(ch, zo).wait_send()
                for yo in range(2):
                    self.scopy(ch, zo, yo).wait_send()


class SharedGather(Gather):
    chunks = 2

    @classmethod
    def sems(cls):
        return Gather.sems.__func__(cls) + [dma((cls.chunks, 8))] * 4

    def __init__(self, s, src, dst, sems):
        super().__init__(s, src, dst, sems)
        self.xs, self.xr, self.ts, self.tr = sems[7:]
        self.rows = 64 // self.chunks
        self.skip = s.dp * 64

    def other(self, ch, z, y, c):
        start = self.s.at(z, y, c) * 128 + (1 - self.s.dp) * 64 + ch * self.rows
        return self.dst.at[pl.ds(pl.multiple_of(start, self.rows), self.rows)]

    def xcopy(self, ch, zo, yo):
        s = self.s
        b = self.block(ch, zo, yo, s.c)
        n = zo * 2 + yo
        return send_over(b, b, self.xs.at[ch, n], self.xr.at[ch, n], s)

    def tcopy(self, ch, zo, yo, own=False):
        s = self.s
        b = self.other(ch, zo, yo, s.c)
        n = zo * 2 + yo
        src = b
        if own:
            start = pl.multiple_of((1 - s.dp) * 64 + ch * self.rows, self.rows)
            src = self.src.at[pl.ds(start, self.rows)]
        return send(src, b, self.ts.at[ch, n], self.tr.at[ch, n], s.at(s.z, s.y, 1 - s.c))

    def start(self):
        super().start()
        for ch in range(self.chunks):
            self.tcopy(ch, self.s.z, self.s.y, True).start()

    def passed_on(self, ch, zo, yo):
        self.xcopy(ch, zo, yo).start()
        self.scopy(ch, zo, yo).start()

    def x_arrive(self, j, yo):
        s = self.s
        zo = s.arrival(j)
        row = s.y if yo == 0 else 1 - s.y
        for ch in range(self.chunks):
            b = self.other(ch, zo, row, s.c)
            n = zo * 2 + row
            send_over(b, b, self.xs.at[ch, n], self.xr.at[ch, n], s).wait_recv()
            self.tcopy(ch, zo, row).start()

    def tasks(self):
        out = super().tasks()
        for j in range(4):
            for yo in range(2):
                if j + yo > 0:
                    out.append(functools.partial(self.x_arrive, j, yo))
        return out

    def finish(self):
        s = self.s
        for ch in range(self.chunks):
            for n in range(8):
                b = self.other(ch, n // 2, n % 2, 1 - s.c)
                send(b, b, self.ts.at[ch, n], self.tr.at[ch, n], s.me).wait_recv()

    def drain(self):
        s = self.s
        super().drain()
        for ch in range(self.chunks):
            for zo in range(4):
                for yo in range(2):
                    self.tcopy(ch, zo, yo).wait_send()
                    far = (s.z != zo) | (s.y != yo)
                    pl.when(far)(lambda: self.xcopy(ch, zo, yo).wait_send())


class Columns:
    @staticmethod
    def sems(parts):
        return [dma((16, parts)), dma((16, parts)), dma((16,)), dma((16,)), dma((parts,))]

    def __init__(self, s, w, dst, parts, sems):
        self.s, self.w, self.dst, self.parts = s, w, dst, parts
        self.e = dst.shape[1] // parts
        self.ps, self.pr, self.xs, self.xr, self.own = sems

    def rows(self, src, half):
        return pl.ds(pl.multiple_of(src * 128 + half * 64, 64), 64)

    def cols(self, p, h):
        return pl.ds(pl.multiple_of(p * 16 * self.e + h * self.e, 128), self.e)

    def copy(self, k, p):
        s = self.s
        to = s.partner(k)
        half = pl.ds(pl.multiple_of(s.dp * 64, 64), 64)
        return send(
            self.w.at[half, self.cols(p, to)],
            self.dst.at[self.rows(s.me, s.dp), pl.ds(p * self.e, self.e)],
            self.ps.at[k, p], self.pr.at[s.me, p], to,
        )

    def local(self, p):
        s = self.s
        return pltpu.make_async_copy(
            self.w.at[:, self.cols(p, s.me)],
            self.dst.at[pl.ds(pl.multiple_of(s.me * 128, 128), 128), pl.ds(p * self.e, self.e)],
            self.own.at[p],
        )

    def begin(self, k):
        for p in range(self.parts):
            (self.copy(k, p) if k else self.local(p)).start()

    def start(self, ahead=16):
        self.ahead = ahead
        for k in range(ahead):
            self.begin(k)

    def over(self, src):
        s = self.s
        b = self.dst.at[self.rows(src, s.dp)]
        return send_over(b, b, self.xs.at[src], self.xr.at[src], s)

    def arrive(self, k):
        s = self.s
        if k + self.ahead - 1 < 16:
            self.begin(k + self.ahead - 1)
        src = s.partner(k)
        for p in range(self.parts):
            b = self.dst.at[self.rows(src, s.dp), pl.ds(p * self.e, self.e)]
            send(b, b, self.ps.at[k, p], self.pr.at[src, p], s.me).wait_recv()
        self.over(src).start()

    def tasks(self):
        return [functools.partial(self.arrive, k) for k in range(1, 16)]

    def finish(self):
        s = self.s
        for k in range(1, 16):
            src = s.partner(k)
            b = self.dst.at[self.rows(src, 1 - s.dp)]
            send_over(b, b, self.xs.at[src], self.xr.at[src], s).wait_recv()
        for p in range(self.parts):
            self.local(p).wait()

    def drain(self):
        s = self.s
        for k in range(1, 16):
            for p in range(self.parts):
                self.copy(k, p).wait_send()
            self.over(s.partner(k)).wait_send()


class Return:
    ahead = 16

    @staticmethod
    def sems(parts):
        return [dma((16, parts))] * 4 + [dma((parts,))]

    def __init__(self, s, src, dst, parts, sems):
        self.s, self.src, self.dst, self.parts = s, src, dst, parts
        self.e = src.shape[2] // parts
        self.ps, self.pr, self.xs, self.xr, self.own = sems

    def place(self, p, h, half):
        cols = pl.ds(pl.multiple_of(p * 16 * self.e + h * self.e, 128), self.e)
        return self.dst.at[pl.ds(pl.multiple_of(half * 64, 64), 64), cols]

    def block(self, h, p):
        return self.src.at[h, :, pl.ds(p * self.e, self.e)]

    def copy(self, k, p):
        s = self.s
        to = s.partner(k)
        return send(
            self.block(to, p), self.place(p, s.me, s.dp), self.ps.at[k, p], self.pr.at[s.me, p], to
        )

    def local(self, p):
        s = self.s
        return pltpu.make_async_copy(self.block(s.me, p), self.place(p, s.me, s.dp), self.own.at[p])

    def over(self, h, p, own=False):
        s = self.s
        dst = self.place(p, h, s.dp)
        src = self.block(s.me, p) if own else dst
        return send_over(src, dst, self.xs.at[h, p], self.xr.at[h, p], s)

    def begin(self, k):
        for p in range(self.parts):
            if k:
                self.copy(k, p).start()
                continue
            self.local(p).start()
            self.over(self.s.me, p, own=True).start()

    def start(self):
        for k in range(16):
            self.begin(k)

    def arrive(self, k):
        s = self.s
        h = s.partner(k)
        for p in range(self.parts):
            b = self.place(p, h, s.dp)
            send(b, b, self.ps.at[k, p], self.pr.at[h, p], s.me).wait_recv()
            self.over(h, p).start()

    def tasks(self):
        return [functools.partial(self.arrive, k) for k in range(1, 16)]

    def finish(self):
        s = self.s
        for p in range(self.parts):
            self.local(p).wait()
        for k in range(16):
            h = s.partner(k)
            for p in range(self.parts):
                b = self.place(p, h, 1 - s.dp)
                send_over(b, b, self.xs.at[h, p], self.xr.at[h, p], s).wait_recv()
        for k in range(16):
            for p in range(self.parts):
                if k:
                    self.copy(k, p).wait_send()
                self.over(s.partner(k), p).wait_send()


class Scatter:
    lag = 3

    @staticmethod
    def scratch(width):
        q = width // 512
        return [
            VM((4, 2, 256, width), bf16), VM((4, 2, 128, width), bf16), VM((4, 2, 128, width), bf16),
            VM((4, 128, width), bf16), VM((5, 128, width), bf16),
            dma((4, q, 2)), dma((4, q, 2)), dma((4, q)), dma((4, q)), dma((4, q)), dma((5, q)),
        ]

    def __init__(self, s, left, right, out, scratch, first=0):
        self.s, self.left, self.right, self.out, self.first = s, left, right, out, first
        self.part, self.sib, self.mid, self.got_y, self.got_z = scratch[:5]
        self.ss, self.sr, self.ys, self.yr, self.zs, self.zr = scratch[5:]
        self.cols = 512
        self.pieces = out.shape[1] // 512
        self.order = [s.arrival(j) for j in (3, 2, 1, 0)]

    def w(self, h):
        return pl.ds(h * self.cols, self.cols)

    def compute(self, k, h, yd, slot):
        tok = pl.multiple_of((self.order[k] * 2 + yd) * 256, 256)
        p = cols_dot(self.left[pl.ds(tok, 256), :], self.right[pl.ds(self.first + h * self.cols, self.cols), :])
        self.part[k, slot, :, self.w(h)] = p.astype(bf16)

    def sib_copy(self, k, h, slot):
        s = self.s
        src = self.part.at[k, slot, pl.ds(pl.multiple_of((1 - s.c) * 128, 128), 128), self.w(h)]
        return send(
            src, self.sib.at[k, slot, :, self.w(h)],
            self.ss.at[k, h, slot], self.sr.at[k, h, slot], s.at(s.z, s.y, 1 - s.c),
        )

    def y_copy(self, k, h):
        s = self.s
        return send(
            self.mid.at[k, 0, :, self.w(h)], self.got_y.at[k, :, self.w(h)],
            self.ys.at[k, h], self.yr.at[k, h], s.at(s.z, 1 - s.y, s.c),
        )

    def z_copy(self, k, h):
        s = self.s
        to = self.order[k]
        up = to > s.z
        hop = jnp.where(up, s.z + 1, s.z - 1)
        slot = jnp.where(up | (hop != to), to, 4)
        return send(
            self.mid.at[k, 1, :, self.w(h)], self.got_z.at[slot, :, self.w(h)],
            self.zs.at[k, h], self.zr.at[slot, h], s.at(hop, s.y, s.c),
        )

    def z_wait(self, slot, h):
        b = self.got_z.at[slot, :, self.w(h)]
        send(b, b, self.zs.at[0, h], self.zr.at[slot, h], self.s.me).wait_recv()

    def fold(self, k, h, slot):
        s = self.s
        self.sib_copy(k, h, slot).wait_recv()
        own = self.part[k, slot, pl.ds(pl.multiple_of(s.c * 128, 128), 128), self.w(h)]
        total = own.astype(f32) + self.sib[k, slot, :, self.w(h)].astype(f32)
        self.mid[k, slot, :, self.w(h)] = total.astype(bf16)

    def after_y(self, k, h):
        s = self.s
        w = self.w(h)
        self.y_copy(k, h).wait_recv()
        total = self.mid[k, 1, :, w].astype(f32) + self.got_y[k, :, w].astype(f32)
        if k == 3:
            self.out[:, w] = total
            return
        to = self.order[k]
        first = jnp.where(to > s.z, s.z == 0, s.z == 3)

        @pl.when(first)
        def _():
            self.mid[k, 1, :, w] = total.astype(bf16)

        @pl.when(jnp.logical_not(first))
        def _():
            self.z_wait(to, h)
            self.mid[k, 1, :, w] = (total + self.got_z[to, :, w].astype(f32)).astype(bf16)

        self.z_copy(k, h).start()

    def tasks(self):
        steps = [(k, h) for k in range(4) for h in range(self.pieces)]
        s = self.s

        def step(i):
            k, h = steps[i]
            self.compute(k, h, 1 - s.y, 0)
            self.sib_copy(k, h, 0).start()
            self.compute(k, h, s.y, 1)
            self.sib_copy(k, h, 1).start()
            self.fold(k, h, 0)
            self.y_copy(k, h).start()
            self.fold(k, h, 1)

        out = []
        for i in range(len(steps) + self.lag):
            if i < len(steps):
                out.append(functools.partial(step, i))
            if i >= self.lag:
                out.append(functools.partial(self.after_y, *steps[i - self.lag]))
        return out

    def finish(self):
        s = self.s
        for h in range(self.pieces):
            w = self.w(h)

            @pl.when(s.z > 0)
            def _():
                self.z_wait(s.z, h)
                self.out[:, w] += self.got_z[s.z, :, w].astype(f32)

            @pl.when(s.z < 3)
            def _():
                self.z_wait(4, h)
                self.out[:, w] += self.got_z[4, :, w].astype(f32)

        for k in range(4):
            for h in range(self.pieces):
                self.sib_copy(k, h, 0).wait_send()
                self.sib_copy(k, h, 1).wait_send()
                self.y_copy(k, h).wait_send()
                if k < 3:
                    self.z_copy(k, h).wait_send()


class Weigh:
    steps = 8

    @classmethod
    def scratch(cls, cols):
        return [
            VM((16, 64, cols), f32), VM((16, 64, cols), bf16), VM((16, 64, cols), bf16),
            dma((cls.steps,)), dma((cls.steps,)),
        ]

    def __init__(self, s, left, right, half, scratch, back=None):
        self.s, self.left, self.right, self.half, self.back = s, left, right, half, back
        self.mine, self.sent, self.got, self.xs, self.xr = scratch

    def at(self, n):
        return self.s.partner(2 * n) // 2

    def copy(self, n):
        i = self.at(n)
        w = pl.ds(2 * i, 2)
        return send_over(self.sent.at[w], self.got.at[w], self.xs.at[i], self.xr.at[i], self.s)

    def compute(self, n):
        i = self.at(n)
        low = self.s.dp == 0
        cols = pl.ds(pl.multiple_of(i * 256, 256), 256)
        got = rows_dot(self.left[:, cols], self.right[...])
        for m in range(2):
            a, b = got[m * 128:m * 128 + 64], got[m * 128 + 64:m * 128 + 128]
            self.mine[2 * i + m] = jnp.where(low, a, b)
            self.sent[2 * i + m] = jnp.where(low, b, a).astype(bf16)
        self.copy(n).start()

    def fold(self, n):
        self.copy(n).wait_recv()
        w = pl.ds(2 * self.at(n), 2)
        self.half[w] = (self.mine[w] + self.got[w].astype(f32)).astype(bf16)
        if self.back is not None:
            self.back.begin(2 * n)
            self.back.begin(2 * n + 1)

    def products(self):
        return [functools.partial(self.compute, i) for i in range(self.steps)]

    def folds(self):
        return [functools.partial(self.fold, i) for i in range(self.steps)]

    def drain(self):
        for i in range(self.steps):
            self.copy(i).wait_send()


def nothing(n):
    return [lambda: None] * n


def halves_of(refs, counts):
    out, at = [], 0
    for n in counts:
        out.append(refs[at:at + n])
        at += n
    return out


def loaded(pairs, sems):
    copies = [pltpu.make_async_copy(a, b, sems.at[i]) for i, (a, b) in enumerate(pairs)]
    for cp in copies:
        cp.start()
    return [cp.wait for cp in copies]


def norm_back(values, upstream, gains_all, which, write):
    whole = values[...].astype(f32)
    width = whole.shape[1]
    factor = lax.rsqrt(jnp.mean(whole * whole, axis=-1, keepdims=True) + epsilon)
    dot_row = jnp.zeros_like(factor)
    for j in range(16):
        w = pl.ds(j * 128, 128)
        scaled = upstream[:, w] * gains_all[j, which:which + 1, :] * values[:, w].astype(f32)
        dot_row = dot_row + jnp.sum(scaled, axis=-1, keepdims=True)
    dot_row = dot_row * (1.0 / width) * factor * factor * factor
    for j in range(16):
        w = pl.ds(j * 128, 128)
        v, u = values[:, w].astype(f32), upstream[:, w]
        grad = factor * (u * gains_all[j, which:which + 1, :]) - v * dot_row
        write(j, grad, jnp.sum(u * v * factor, axis=0, keepdims=True))


def communicate(kernel, name, number, ins, in_specs, outs, out_specs, scratch, flops=0):
    return pl.pallas_call(
        kernel, out_shape=outs, in_specs=in_specs, out_specs=out_specs, scratch_shapes=scratch,
        compiler_params=pltpu.CompilerParams(
            collective_id=number, has_side_effects=True, vmem_limit_bytes=LIMIT
        ),
        cost_estimate=pl.CostEstimate(flops=flops, bytes_accessed=2**24, transcendentals=0),
        name=name,
    )(*ins)


def project_kernel(x, gains, in_w, normed_all, in_cols, gains_all, projected, x_all, normed, row,
                   copies, g_s, g_r, *rest):
    gather_sems, col_sems = halves_of(rest, [7, 5])
    s = Spot()
    greet(s)

    def gain_copy(k):
        return send(gains, gains_all.at[s.me], g_s.at[k], g_r.at[s.me], s.partner(k))

    gather = Gather(s, x, x_all, gather_sems)
    gather.start()
    for k in range(1, 16):
        gain_copy(k).start()
    columns = Columns(s, in_w, in_cols, 3, col_sems)
    columns.start()
    gains_all[s.me] = gains[...]
    x_all[pl.ds(pl.multiple_of(s.me * 128, 128), 128), :] = x[...]

    def gain_row():
        for k in range(1, 16):
            src = s.partner(k)
            b = gains_all.at[src]
            send(b, b, g_s.at[k], g_r.at[src], s.me).wait_recv()
        for j in range(16):
            row[0:1, pl.ds(j * 128, 128)] = gains_all[j, 0:1, :]

    def out_copy(j):
        tok = pl.ds(pl.multiple_of(s.arrival(j) * 512, 512), 512)
        return pltpu.make_async_copy(normed.at[tok], normed_all.at[tok], copies.at[j])

    def use(j):
        if j == 0:
            columns.finish()
            gain_row()
        for n in range(4):
            rows = pl.ds(pl.multiple_of(s.arrival(j) * 512 + n * 128, 128), 128)
            values = x_all[rows, :].astype(f32)
            factor = lax.rsqrt(jnp.mean(values * values, axis=-1, keepdims=True) + epsilon)
            normed[rows, :] = (values * factor * row[0:1, :]).astype(bf16)
        out_copy(j).start()
        tok = pl.ds(pl.multiple_of(s.arrival(j) * 512, 512), 512)
        out = jnp.dot(normed[tok, :], in_cols[...], preferred_element_type=f32)
        projected[tok, :] = out.astype(bf16)

    merged(gather.tasks(use), nothing(2) + columns.tasks() + nothing(8))
    gather.drain()
    columns.drain()
    for k in range(1, 16):
        gain_copy(k).wait_send()
    for j in range(4):
        out_copy(j).wait()


def project(x, gains, in_weight, number):
    tokens, width = x.shape
    return communicate(
        project_kernel, "project", number, (x, gains, in_weight), [vmem(), vmem(), anywhere()],
        [
            jax.ShapeDtypeStruct((16 * tokens, width), bf16),
            jax.ShapeDtypeStruct((width, 3 * DH), bf16),
            jax.ShapeDtypeStruct((16, 8, 128), f32),
            jax.ShapeDtypeStruct((16 * tokens, 3 * DH), bf16),
        ],
        [anywhere(), vmem(), vmem(), vmem()],
        [
            VM((16 * tokens, width), bf16), VM((16 * tokens, width), bf16), VM((8, width), f32),
            dma((4,)), dma((16,)), dma((16,)),
        ] + Gather.sems() + Columns.sems(3),
    )


def kernel_feature(t):
    return jnp.where(t > 0, t + 1.0, jnp.exp(jnp.minimum(t, 0.0)))


def dot_high(left, right, dims=((1,), (0,))):
    return lax.dot_general(
        left, right, (dims, ((), ())), preferred_element_type=f32, precision=highest
    )


def scores_of(query, keys, first):
    raw = cols_dot(query, keys) * (1.0 / math.sqrt(DH))
    row = lax.broadcasted_iota(jnp.int32, raw.shape, 0) + first
    col = lax.broadcasted_iota(jnp.int32, raw.shape, 1)
    return jnp.where(col <= row, raw, -1e30)


class Attend:
    def __init__(self, qkv, keep, mix, local, mem_out, lse, combined, memory, normal):
        self.qkv, self.keep, self.mix = qkv, keep, mix
        self.local, self.mem_out, self.lse, self.combined = local, mem_out, lse, combined
        self.memory, self.normal = memory, normal
        self.segments = qkv.shape[0] // SEG

    def states(self):
        state = jnp.zeros((DH, DH), f32)
        norm = jnp.zeros((1, DH), f32)
        for n in range(self.segments):
            keep = self.keep[n, 0:1, :]
            state, norm = state * keep, norm * keep
            self.memory[n] = state
            self.normal[n, 0:1, :] = norm
            if n + 1 < self.segments:
                rows = pl.ds(n * SEG, SEG)
                fk = kernel_feature(self.qkv[rows, DH:2 * DH].astype(f32)).astype(bf16)
                state = state + rows_dot(fk, self.qkv[rows, 2 * DH:])
                norm = norm + jnp.sum(fk.astype(f32), axis=0, keepdims=True)

    def block(self, n, i):
        rows = pl.ds(n * SEG + i * ROWS, ROWS)
        seen = pl.ds(n * SEG, (i + 1) * ROWS)
        query = self.qkv[rows, :DH]
        scores = scores_of(query, self.qkv[seen, DH:2 * DH], i * ROWS)
        top = jnp.max(scores, axis=-1, keepdims=True)
        expo = jnp.exp(scores - top)
        total = jnp.sum(expo, axis=-1, keepdims=True)
        probs = (expo * (1.0 / total)).astype(bf16)
        local = jnp.dot(probs, self.qkv[seen, 2 * DH:], preferred_element_type=f32)
        fq = kernel_feature(query.astype(f32)).astype(bf16).astype(f32)
        den = jnp.maximum(jnp.sum(fq * self.normal[n, 0:1, :], axis=-1, keepdims=True), 1.0)
        mem_out = dot_high(fq, self.memory[n]) / den
        mix = self.mix[0:1, :]
        self.local[rows, :] = local
        self.mem_out[rows, :] = mem_out
        self.lse[rows, :] = jnp.broadcast_to(top + jnp.log(total), (ROWS, DH))
        self.combined[rows, :] = (mix * mem_out + (1.0 - mix) * local).astype(bf16)

    def blocks(self):
        return [(n, i) for n in range(self.segments) for i in range(SEG // ROWS)]


class AttendBack:
    def __init__(self, qkv, keep, mix, local, mem_out, lse, memory, normal, upstream, grad,
                 mix_grad, dk, dv, state_grad, norm_grad):
        self.qkv, self.keep, self.mix = qkv, keep, mix
        self.local, self.mem_out, self.lse = local, mem_out, lse
        self.memory, self.normal, self.upstream, self.grad = memory, normal, upstream, grad
        self.mix_grad, self.dk, self.dv = mix_grad, dk, dv
        self.state_grad, self.norm_grad = state_grad, norm_grad
        self.segments = qkv.shape[0] // SEG

    def clear(self):
        self.mix_grad[...] = jnp.zeros_like(self.mix_grad)
        self.dk[...] = jnp.zeros_like(self.dk)
        self.dv[...] = jnp.zeros_like(self.dv)
        self.state_grad[...] = jnp.zeros_like(self.state_grad)
        self.norm_grad[...] = jnp.zeros_like(self.norm_grad)

    def block(self, n, i):
        scale = 1.0 / math.sqrt(DH)
        rows = pl.ds(n * SEG + i * ROWS, ROWS)
        seen = pl.ds(n * SEG, (i + 1) * ROWS)
        query = self.qkv[rows, :DH]
        keys = self.qkv[seen, DH:2 * DH]
        values = self.qkv[seen, 2 * DH:]
        up = self.upstream[rows, :].astype(f32)
        mem_out = self.mem_out[rows, :]
        mix = self.mix[0:1, :]
        mixed = jnp.sum(up * (mem_out - self.local[rows, :]), axis=0, keepdims=True)
        self.mix_grad[0:1, :] += mixed * mix * (1.0 - mix)
        memory_grad = up * mix
        local_grad = (up * (1.0 - mix)).astype(bf16)
        query_f = query.astype(f32)
        fq = kernel_feature(query_f).astype(bf16).astype(f32)
        normal = self.normal[n, 0:1, :]
        raw = jnp.sum(fq * normal, axis=-1, keepdims=True)
        den = jnp.maximum(raw, 1.0)
        numer_grad = memory_grad / den
        den_grad = -jnp.sum(memory_grad * mem_out, axis=-1, keepdims=True) / den
        raw_grad = jnp.where(raw > 1.0, den_grad, 0.0)
        fq_grad = dot_high(numer_grad, self.memory[n], ((1,), (1,))) + raw_grad * normal
        if n > 0:
            self.state_grad[n] += dot_high(fq, numer_grad, ((0,), (0,)))
            self.norm_grad[n, 0:1, :] += jnp.sum(raw_grad * fq, axis=0, keepdims=True)
        scores = scores_of(query, keys, i * ROWS)
        probs = jnp.exp(scores - self.lse[rows, 0:1])
        prob_grad = cols_dot(local_grad, values)
        row_term = jnp.sum(probs * prob_grad, axis=-1, keepdims=True)
        score_grad = (probs * (prob_grad - row_term)).astype(bf16)
        query_grad = jnp.dot(score_grad, keys, preferred_element_type=f32) * scale
        query_grad = query_grad + fq_grad * feature_slope(query_f)
        self.grad[rows, :DH] = query_grad.astype(bf16)
        self.dk[seen, :] += rows_dot(score_grad, query) * scale
        self.dv[seen, :] += rows_dot(probs.astype(bf16), local_grad)

    def states(self):
        state = jnp.zeros((DH, DH), f32)
        norm = jnp.zeros((1, DH), f32)
        for n in reversed(range(self.segments)):
            rows = pl.ds(n * SEG, SEG)
            key = self.qkv[rows, DH:2 * DH].astype(f32)
            key_grad = self.dk[rows, :]
            value_grad = self.dv[rows, :]
            if n + 1 < self.segments:
                fk = kernel_feature(key).astype(bf16).astype(f32)
                value = self.qkv[rows, 2 * DH:].astype(f32)
                fk_grad = dot_high(value, state, ((1,), (1,))) + norm
                key_grad = key_grad + fk_grad * feature_slope(key)
                value_grad = value_grad + dot_high(fk, state)
            self.grad[rows, DH:2 * DH] = key_grad.astype(bf16)
            self.grad[rows, 2 * DH:] = value_grad.astype(bf16)
            if n > 0:
                keep = self.keep[n, 0:1, :]
                state = (state + self.state_grad[n]) * keep
                norm = (norm + self.norm_grad[n, 0:1, :]) * keep

    def blocks(self):
        return [(n, i) for n in range(self.segments) for i in range(SEG // ROWS)]


def forward_kernel(qkv, keep, mix, x, gains_all, out_w, cot, gate_up, down,
                   local, mem_out, lse, combined, memory, normal, middle, out_all, cot_all,
                   gate_up_cols, down_cols, hidden_all, act, feed_grad,
                   mixed_tokens, hidden, out_v, cot_v, gate_up_v, down_v, hidden_v, act_v, grad_v,
                   copies, outs, t_s, t_r, *rest):
    sems_o, sems_c, sems_g, sems_d, sems_h = halves_of(rest, [11, 7, 5, 5, 7])
    s = Spot()
    mine = pl.ds(pl.multiple_of(s.me * 128, 128), 128)
    own = [
        pltpu.make_async_copy(out_w, out_v.at[mine], copies.at[0]),
        pltpu.make_async_copy(cot, cot_v.at[mine], copies.at[1]),
    ]
    for cp in own:
        cp.start()
    greet(s)
    gather_o = SharedGather(s, out_w, out_v, sems_o)
    gather_c = Gather(s, cot, cot_v, sems_c)
    gather_h = Gather(s, hidden, hidden_v, sems_h)
    columns_g = Columns(s, gate_up, gate_up_v, 2, sems_g)
    columns_d = Columns(s, down, down_v, 1, sems_d)
    gather_o.start()
    gather_c.start()
    columns_g.start(4)
    attend = Attend(qkv, keep, mix, local, mem_out, lse, combined, memory, normal)

    def token_copy(j):
        return send(
            combined.at[pl.ds(j * 128, 128)],
            mixed_tokens.at[:, pl.ds(pl.multiple_of(s.me * DH, DH), DH)],
            t_s.at[j], t_r.at[s.me], j,
        )

    def block(n, i):
        attend.block(n, i)
        for j in range((n * SEG + i * ROWS) // 128, (n * SEG + (i + 1) * ROWS) // 128):
            pl.when(s.me != j)(lambda: token_copy(j).start())

    compute = [attend.states] + [functools.partial(block, n, i) for n, i in attend.blocks()]
    wholes = [
        pltpu.make_async_copy(a, b, outs.at[4, i])
        for i, (a, b) in enumerate(
            [(out_v, out_all), (cot_v, cot_all), (gate_up_v, gate_up_cols), (down_v, down_cols)]
        )
    ]

    def tokens():
        own[0].wait()
        gather_o.finish()
        mixed_tokens[:, pl.ds(pl.multiple_of(s.me * DH, DH), DH)] = combined[mine, :]
        for k in range(1, 16):
            src = s.partner(k)
            b = mixed_tokens.at[:, pl.ds(pl.multiple_of(src * DH, DH), DH)]
            send(b, b, t_s.at[0], t_r.at[src], s.me).wait_recv()

    def output(j):
        w = pl.ds(j * 512, 512)
        got = jnp.dot(mixed_tokens[...], out_v[:, w], preferred_element_type=f32)
        middle[:, w] = got + x[:, w].astype(f32)

    def norm():
        values = middle[...]
        factor = lax.rsqrt(jnp.mean(values * values, axis=-1, keepdims=True) + epsilon)
        for j in range(16):
            w = pl.ds(j * 128, 128)
            part = (middle[:, w] * factor * gains_all[j, 1:2, :]).astype(bf16)
            hidden[:, w] = part
            hidden_v[mine, w] = part
        gather_h.start()
        wholes[0].start()

    half = act.shape[1]

    def out_copies(j):
        tok = pl.ds(pl.multiple_of(s.arrival(j) * 512, 512), 512)
        pairs = [(hidden_v, hidden_all), (act_v, act), (grad_v, feed_grad)]
        return [
            pltpu.make_async_copy(a.at[tok], b.at[tok], outs.at[j, i]) for i, (a, b) in enumerate(pairs)
        ]

    def use(j):
        if j == 0:
            own[1].wait()
            columns_g.finish()
            columns_d.finish()
            for cp in wholes[1:]:
                cp.start()
        tok = pl.ds(pl.multiple_of(s.arrival(j) * 512, 512), 512)
        act_grad = jnp.dot(cot_v[tok, :], down_v[...], preferred_element_type=f32)
        gate = jnp.dot(hidden_v[tok, :], gate_up_v[:, :half], preferred_element_type=f32)
        up = jnp.dot(hidden_v[tok, :], gate_up_v[:, half:], preferred_element_type=f32)
        sigma = jax.nn.sigmoid(gate)
        silu = gate * sigma
        act_v[tok, :] = (silu * up).astype(bf16)
        slope = sigma * (1.0 + gate * (1.0 - sigma))
        grad_v[tok, :half] = (act_grad * up * slope).astype(bf16)
        grad_v[tok, half:] = (act_grad * silu).astype(bf16)
        for cp in out_copies(j):
            cp.start()

    after = [tokens] + [functools.partial(output, j) for j in range(4)] + [norm]
    c_tasks = gather_c.tasks()
    early = len(c_tasks) * 4 // 5
    merged(gather_o.tasks(), c_tasks[:early], columns_g.tasks(), compute + nothing(len(compute)))
    merged(after, [functools.partial(columns_d.start, 4)])
    merged(
        gather_h.tasks(use),
        c_tasks[early:] + nothing(12),
        nothing(2) + columns_d.tasks() + nothing(8),
    )
    for j in range(16):
        pl.when(s.me != j)(lambda: token_copy(j).wait_send())
    for part in (gather_o, gather_c, gather_h, columns_g, columns_d):
        part.drain()
    for cp in wholes:
        cp.wait()
    for j in range(4):
        for cp in out_copies(j):
            cp.wait()


def forward_of(qkv, keep, mix, x, gains_all, out_weight, cotangent, gate_up, down, number):
    tokens, width = x.shape
    total = qkv.shape[0]
    segments = total // SEG
    half = down.shape[1] // 16
    shape = jax.ShapeDtypeStruct
    rows, cols, fine = (total, width), (width, 2 * half), (total, half)
    return communicate(
        forward_kernel, "forward", number,
        (qkv, keep, mix, x, gains_all, out_weight, cotangent, gate_up, down),
        [vmem()] * 5 + [anywhere()] * 4,
        [
            shape((total, DH), f32), shape((total, DH), f32), shape((total, DH), f32),
            shape((total, DH), bf16), shape((segments, DH, DH), f32), shape((segments, 8, DH), f32),
            shape((tokens, width), f32),
            shape((width, width), bf16), shape(rows, bf16), shape(cols, bf16), shape((width, half), bf16),
            shape(rows, bf16), shape(fine, bf16), shape((total, 2 * half), bf16),
        ],
        [vmem()] * 7 + [anywhere()] * 7,
        [
            VM((tokens, width), bf16), VM((tokens, width), bf16), VM((width, width), bf16),
            VM(rows, bf16), VM(cols, bf16), VM((width, half), bf16), VM(rows, bf16), VM(fine, bf16),
            VM((total, 2 * half), bf16), dma((2,)), dma((5, 4)), dma((16,)), dma((16,)),
        ] + SharedGather.sems() + Gather.sems() + Columns.sems(2) + Columns.sems(1) + Gather.sems(),
    )


def hidden_grad_kernel(feed_grad, gate_up_cols, hidden_all, act, down_cols, out, half, feed_out,
                       grad_v, gate_up_v, hidden_v, act_v, down_v, copies, *rest):
    sems_w, scratch, scratch_f = halves_of(rest, [5, 11, 11])
    s = Spot()
    loads = loaded(
        [(feed_grad, grad_v), (gate_up_cols, gate_up_v), (hidden_all, hidden_v), (act, act_v),
         (down_cols, down_v)],
        copies,
    )
    greet(s, plane=False)
    weigh = Weigh(s, hidden_v, grad_v, half, sems_w)
    scatter = Scatter(s, grad_v, gate_up_v, out, scratch)
    scatter.lag = 2
    filler = Scatter(s, act_v, down_v, feed_out, scratch_f, FILL[0][0])
    merged(
        loads[:2] + scatter.tasks(),
        nothing(1) + loads[2:] + weigh.products() + nothing(8),
        nothing(4) + filler.tasks(),
        nothing(40) + weigh.folds(),
    )
    scatter.finish()
    filler.finish()
    weigh.drain()


def hidden_grad_of(feed_grad, gate_up_cols, hidden_all, act, down_cols, number):
    shape = jax.ShapeDtypeStruct
    total, cols = feed_grad.shape
    width = gate_up_cols.shape[0]
    fill = FILL[0][1]
    return communicate(
        hidden_grad_kernel, "hidden_grad", number,
        (feed_grad, gate_up_cols, hidden_all, act, down_cols), [anywhere()] * 5,
        [
            shape((total // 16, width), f32), shape((16, 64, cols), bf16),
            shape((total // 16, fill), f32),
        ],
        [vmem()] * 3,
        [VM(a.shape, bf16) for a in (feed_grad, gate_up_cols, hidden_all, act, down_cols)] + [dma((5,))]
        + Weigh.scratch(cols) + Scatter.scratch(width) + Scatter.scratch(fill),
    )


def normed_grad_kernel(grad, in_cols, normed_all, x, gains_all, act, down_cols, gains, down_half, combined,
                       attended_all,
                       value_grad, gains_out, feed_out, out_rows, down_rows, in_rows, out_other,
                       attended_v, normed_grad, half, gains_v, got, total, theirs, normed_v, act_v, down_v,
                       copies, x_s, x_r, g_s, g_r,
                       *rest):
    sems_d, sems_i, sems_w, scratch, scratch_f = halves_of(rest, [5, 5, 5, 11, 11])
    s = Spot()
    loads = loaded(
        [(normed_all, normed_v), (act, act_v), (down_cols, down_v), (attended_all, attended_v)], copies
    )
    greet(s)
    back_i = Return(s, half, in_rows, 3, sems_i)
    weigh = Weigh(s, normed_v, grad, half, sems_w, back=back_i)
    back_d = Return(s, down_half, down_rows, 1, sems_d)
    scatter = Scatter(s, grad, in_cols, normed_grad, scratch)
    filler = Scatter(s, act_v, down_v, feed_out, scratch_f, FILL[2][0])
    over = send_over(out_rows, out_other, x_s.at[0], x_r.at[0], s)
    back_d.start()

    def out_product(j):
        w = pl.ds(j * 512, 512)
        out_rows[:, w] = rows_dot(combined[...], attended_v[:, w]).astype(bf16)

    products = [functools.partial(out_product, j) for j in range(4)]

    def gain_copy(k):
        to = s.partner(k)
        return send(gains_v.at[to], got.at[s.me], g_s.at[k], g_r.at[s.me], to)

    def write(j, value, gain):
        value_grad[:, pl.ds(j * 128, 128)] = value
        gains_v[j] = gains[j]
        gains_v[j, 0:1, :] = gain

    merged(
        scatter.tasks(),
        loads[:3] + weigh.products() + nothing(24),
        nothing(5) + weigh.folds() + nothing(12),
        nothing(4) + loads[3:] + products + [over.start] + back_d.tasks() + nothing(5),
        nothing(4) + filler.tasks(),
        nothing(16) + back_i.tasks(),
    )
    scatter.finish()
    norm_back(x, normed_grad, gains_all, 0, write)
    for k in range(1, 16):
        gain_copy(k).start()
    filler.finish()
    back_d.finish()
    back_i.finish()
    weigh.drain()
    over.wait()
    for k in range(1, 16):
        src = s.partner(k)
        b = got.at[src]
        send(b, b, g_s.at[k], g_r.at[src], s.me).wait_recv()
    got[s.me] = gains_v[s.me]
    acc = got[0]
    for k in range(1, 16):
        acc = acc + got[k]
    total[...] = acc
    cp = send_over(total, theirs, x_s.at[1], x_r.at[1], s)
    cp.start()
    for k in range(1, 16):
        gain_copy(k).wait_send()
    cp.wait()
    gains_out[...] = total[...] + theirs[...]


def normed_grad_of(grad, in_cols, normed_all, x, gains_all, act, down_cols, gains, down_half, combined,
                   attended_all, number):
    shape = jax.ShapeDtypeStruct
    total, cols = grad.shape
    tokens, width = x.shape
    fill = FILL[2][1]
    down_rows = shape((DH, 16 * down_half.shape[2]), bf16)
    in_rows = shape((DH, 16 * cols), bf16)
    return communicate(
        normed_grad_kernel, "normed_grad", number,
        (grad, in_cols, normed_all, x, gains_all, act, down_cols, gains, down_half, combined,
         attended_all),
        [vmem()] * 2 + [anywhere()] + [vmem()] * 2 + [anywhere()] * 2 + [vmem(), anywhere(), vmem(), anywhere()],
        [
            shape((tokens, width), f32), shape((8, 128), f32), shape((tokens, fill), f32),
            shape((DH, width), bf16), down_rows, in_rows, shape((DH, width), bf16),
        ],
        [vmem()] * 4 + [anywhere()] * 3,
        [
            VM(attended_all.shape, bf16),
            VM((tokens, width), f32), VM((16, 64, cols), bf16), VM((16, 8, 128), f32),
            VM((16, 8, 128), f32), VM((8, 128), f32), VM((8, 128), f32),
            VM(normed_all.shape, bf16), VM(act.shape, bf16), VM(down_cols.shape, bf16), dma((4,)),
            dma((2,)), dma((2,)), dma((16,)), dma((16,)),
        ] + Return.sems(1) + Return.sems(3) + Weigh.scratch(cols) + Scatter.scratch(width)
        + Scatter.scratch(fill),
    )


def attend_back_kernel(hidden_grad, middle, cot, gains_all, keep, mix, memory, normal, out_all, qkv, local,
                       mem_out, lse, gate_up_half, cot_all, act, down_cols,
                       middle_grad, gains, grad, down_half, feed_out, attended_all, gate_up_rows,
                       attended, out_v, qkv_v, local_v, mem_v, lse_v, cot_v, act_v, down_v, by_token,
                       upstream, mix_grad, dk, dv, state_grad, norm_grad, copies, own_s, h_s, h_r, *rest):
    sems_a, sems_g, sems_w, scratch_f = halves_of(rest, [7, 5, 5, 11])
    s = Spot()
    mine = pl.ds(pl.multiple_of(s.me * 128, 128), 128)
    loads = loaded(
        [(out_all, out_v), (qkv, qkv_v), (local, local_v), (mem_out, mem_v), (lse, lse_v),
         (cot_all, cot_v), (act, act_v), (down_cols, down_v)],
        copies,
    )
    greet(s)
    gains[...] = jnp.zeros_like(gains)

    def write(j, value, gain):
        w = pl.ds(j * 128, 128)
        total = cot[:, w].astype(f32) + value
        middle_grad[:, w] = total
        attended[:, w] = total.astype(bf16)
        gains[j, 1:2, :] = gain

    norm_back(middle, hidden_grad, gains_all, 1, write)
    own = pltpu.make_async_copy(attended, attended_all.at[mine], own_s.at[0])
    own.start()
    gather = Gather(s, attended, attended_all, sems_a)
    back_g = Return(s, gate_up_half, gate_up_rows, 2, sems_g)
    filler = Scatter(s, act_v, down_v, feed_out, scratch_f, FILL[1][0])
    filler.lag = 8
    weigh = Weigh(s, cot_v, act_v, down_half, sems_w)
    attend = AttendBack(qkv_v, keep, mix, local_v, mem_v, lse_v, memory, normal, upstream, grad,
                        mix_grad, dk, dv, state_grad, norm_grad)
    gather.start()
    attend.clear()
    loads[0]()

    def head_copy(j):
        return send(by_token.at[:, pl.ds(j * DH, DH)], upstream.at[mine], h_s.at[j], h_r.at[s.me], j)

    for j in range(4):
        w = pl.ds(j * 512, 512)
        by_token[:, w] = cols_dot(attended[...], out_v[w, :]).astype(bf16)
        for h in range(4 * j, 4 * j + 4):
            pl.when(s.me != h)(lambda: head_copy(h).start())
    upstream[mine, :] = by_token[:, pl.ds(pl.multiple_of(s.me * DH, DH), DH)]
    for wait in loads[1:]:
        wait()

    def arrive(j):
        b = upstream.at[pl.ds(j * 128, 128)]
        pl.when(s.me != j)(lambda: send(b, b, h_s.at[j], h_r.at[j], s.me).wait_recv())

    def block(n, i):
        for j in range((n * SEG + i * ROWS) // 128, (n * SEG + (i + 1) * ROWS) // 128):
            arrive(j)
        attend.block(n, i)

    compute = [functools.partial(block, n, i) for n, i in attend.blocks()] + [attend.states]
    merged(gather.tasks(), nothing(2) + compute, weigh.products() + nothing(12))
    back_g.start()
    merged(filler.tasks(), back_g.tasks(), weigh.folds())
    filler.finish()
    back_g.finish()
    weigh.drain()
    for j in range(16):
        pl.when(s.me != j)(lambda: head_copy(j).wait_send())
    gather.drain()
    own.wait()
    gains[s.me, 2:3, :] = mix_grad[0:1, :]


def attend_backward(hidden_grad, middle, cot, gains_all, keep, mix, memory, normal, out_all, qkv, local,
                    mem_out, lse, gate_up_half, cot_all, act, down_cols, number):
    tokens, width = cot.shape
    total = qkv.shape[0]
    segments = total // SEG
    shape = jax.ShapeDtypeStruct
    whole = (out_all, qkv, local, mem_out, lse, cot_all, act, down_cols)
    return communicate(
        attend_back_kernel, "attend_back", number,
        (hidden_grad, middle, cot, gains_all, keep, mix, memory, normal, out_all, qkv, local, mem_out,
         lse, gate_up_half, cot_all, act, down_cols),
        [vmem()] * 8 + [anywhere()] * 9,
        [
            shape((tokens, width), f32), shape((16, 8, DH), f32), shape((total, 3 * DH), bf16),
            shape((16, 64, act.shape[1]), bf16), shape((tokens, FILL[1][1]), f32),
            shape((total, width), bf16), shape((DH, 16 * gate_up_half.shape[2]), bf16),
        ],
        [vmem()] * 5 + [anywhere()] * 2,
        [VM((tokens, width), bf16)] + [VM(a.shape, a.dtype) for a in whole]
        + [
            VM((tokens, width), bf16), VM((total, DH), bf16), VM((8, DH), f32),
            VM((total, DH), f32), VM((total, DH), f32), VM((segments, DH, DH), f32),
            VM((segments, 8, DH), f32), dma((8,)), dma((1,)), dma((16,)), dma((16,)),
        ] + Gather.sems() + Return.sems(2) + Weigh.scratch(act.shape[1]) + Scatter.scratch(FILL[1][1]),
    )


def body(
    layer_input,
    first_gain,
    in_weight,
    out_weight,
    mix_gate,
    second_gain,
    gate_up,
    down_weight,
    document_starts,
    cotangent,
):
    tokens, width = layer_input.shape
    total = tokens * H
    segments = total // SEG

    own_gains = jnp.zeros((8, tokens), f32)
    own_gains = own_gains.at[0].set(first_gain.astype(f32)).at[1].set(second_gain.astype(f32))
    mix = jnp.broadcast_to(jax.nn.sigmoid(mix_gate.astype(f32))[None], (8, DH))
    numbers = jnp.arange(segments)
    fresh = (numbers == 0) | (document_starts[0] > 0)
    keep = jnp.broadcast_to(jnp.where(fresh, 0.0, 1.0)[:, None, None], (segments, 8, DH))

    normed_all, in_cols, gains_all, qkv = project(layer_input, own_gains, in_weight, 0)
    (local, mem_out, lse, combined, memory, normal, middle, out_all, cot_all, gate_up_cols, down_cols,
     hidden_all, act, feed_grad) = forward_of(
        qkv, keep, mix, layer_input, gains_all, out_weight, cotangent, gate_up, down_weight, 1
    )
    hidden_grad, gate_up_half, feed_out_0 = hidden_grad_of(
        feed_grad, gate_up_cols, hidden_all, act, down_cols, 3
    )

    (middle_grad, gain_grads, projected_grad, down_half, feed_out_1, attended_all,
     gate_up_rows) = attend_backward(
        hidden_grad, middle, cotangent, gains_all, keep, mix, memory, normal, out_all, qkv, local, mem_out,
        lse, gate_up_half, cot_all, act, down_cols, 4,
    )
    (value_grad, gains_out, feed_out_2, out_rows, down_rows, in_rows, out_other) = normed_grad_of(
        projected_grad, in_cols, normed_all, layer_input, gains_all, act, down_cols, gain_grads, down_half,
        combined, attended_all, 5,
    )
    input_grad = middle_grad + value_grad
    feed_out = jnp.concatenate([feed_out_0, feed_out_1, feed_out_2], axis=1)
    layer_output = (middle + feed_out).astype(bf16)

    return (
        layer_output,
        input_grad,
        gains_out[0],
        in_rows.astype(f32),
        out_rows.astype(f32) + out_other.astype(f32),
        gains_out[2],
        gains_out[1],
        gate_up_rows.astype(f32),
        down_rows.astype(f32),
    )


def solution(mesh):
    one_group = mesh.shape[AXIS] == H and mesh.shape["dp"] == 2
    return jax.shard_map(
        body if one_group else body_groups,
        mesh=mesh,
        in_specs=(
            P(("dp", "fsdp"), None),
            P("fsdp"),
            P("fsdp", None),
            P("fsdp", None),
            P("fsdp"),
            P("fsdp"),
            P("fsdp", None),
            P("fsdp", None),
            P("dp", None),
            P(("dp", "fsdp"), None),
        ),
        out_specs=(
            P(("dp", "fsdp"), None),
            P(("dp", "fsdp"), None),
            P("fsdp"),
            P("fsdp", None),
            P("fsdp", None),
            P("fsdp"),
            P("fsdp"),
            P("fsdp", None),
            P("fsdp", None),
        ),
        check_vma=False,
    )
```

```python
import functools
import math

import jax
import jax.numpy as jnp
from jax import lax
from jax.experimental import pallas as pl
from jax.experimental.pallas import tpu as pltpu
from jax.sharding import PartitionSpec as P

H = 16
DH = 128
FF = 8192
SEG = 1024

highest = lax.Precision.HIGHEST
epsilon = 1e-06
f32 = jnp.float32
bf16 = jnp.bfloat16
AXIS = "fsdp"


def feature(values):
    return jax.nn.elu(values) + 1.0


def feature_slope(values):
    return jnp.where(values > 0, 1.0, jnp.exp(jnp.minimum(values, 0.0)))


def norm_forward(values, gain):
    factor = lax.rsqrt(jnp.mean(values * values, axis=-1, keepdims=True) + epsilon)
    return (values * factor * gain, factor)


def norm_backward(values, factor, gain, upstream):
    scaled = upstream * gain
    gain_grad = jnp.sum(upstream * values * factor, axis=0)
    value_grad = factor * scaled - values * (factor * factor * factor) * jnp.mean(
        scaled * values, axis=-1, keepdims=True
    )
    return (value_grad, gain_grad)


def dot(left, right, dims):
    return lax.dot_general(left, right, ((dims[0], dims[1]), ((), ())), preferred_element_type=f32)


def rows_dot(left, right):
    return dot(left, right, ((0,), (0,)))


def cols_dot(left, right):
    return dot(left, right, ((1,), (1,)))


class Layout:
    def __init__(self):
        self.count = lax.axis_size(AXIS)
        self.groups = self.count // H
        self.place = lax.axis_index(AXIS)
        self.head = self.place % H
        self.group = self.place // H
        self.inside = None
        self.across = None
        if self.groups > 1:
            self.inside = [[g * H + j for j in range(H)] for g in range(self.groups)]
            self.across = [[g * H + j for g in range(self.groups)] for j in range(H)]

    def gather(self, block):
        return lax.all_gather(block, AXIS, axis=0, tiled=True, axis_index_groups=self.inside)

    def gather_all(self, block):
        return lax.all_gather(block, AXIS, axis=0, tiled=True)

    def scatter_sum(self, whole):
        return lax.psum_scatter(
            whole, AXIS, scatter_dimension=0, tiled=True, axis_index_groups=self.inside
        )

    def columns(self, block, parts):
        rows, width = block.shape
        each = width // (parts * H)
        if self.groups == 1:
            split = block.reshape(rows, parts, H, each)
            out = lax.all_to_all(split, AXIS, 2, 0, tiled=True)
            return out.reshape(rows * self.count, parts * each)
        whole = self.gather_all(block).reshape(rows * self.count, parts, H, each)
        out = lax.dynamic_index_in_dim(whole, self.head, 2, False)
        return out.reshape(rows * self.count, parts * each)

    def own_rows(self, grad, parts):
        rows, width = grad.shape
        each = width // parts
        if self.groups == 1:
            split = grad.astype(bf16).reshape(rows, parts, 1, each)
            out = lax.all_to_all(split, AXIS, 0, 2, tiled=True)
            return out.reshape(rows // self.count, parts * H * each)
        whole = jnp.zeros((rows, parts, H, each), f32)
        whole = lax.dynamic_update_slice_in_dim(
            whole, grad.reshape(rows, parts, 1, each), self.head, 2
        )
        return lax.psum_scatter(
            whole.reshape(rows, parts * H * each), AXIS, scatter_dimension=0, tiled=True
        )

    def to_tokens(self, by_head):
        tokens, each = by_head.shape
        out = lax.all_to_all(
            by_head.reshape(H, tokens // H, each), AXIS, 0, 0, tiled=False,
            axis_index_groups=self.inside,
        )
        return out.transpose(1, 0, 2).reshape(tokens // H, H * each)

    def to_heads(self, by_token):
        tokens, width = by_token.shape
        split = by_token.reshape(tokens, H, width // H).transpose(1, 0, 2)
        out = lax.all_to_all(
            split, AXIS, 0, 0, tiled=False, axis_index_groups=self.inside
        )
        return out.reshape(H * tokens, width // H)


def carry_forward(layout, delta, count, fresh):
    segments = delta.shape[0]

    def walk(state):
        before = []
        for s in range(segments):
            state = jax.tree.map(lambda a: jnp.where(fresh[s], jnp.zeros_like(a), a), state)
            before.append(state)
            state = (state[0] + delta[s], state[1] + count[s])
        return before, state

    state = (jnp.zeros_like(delta[0]), jnp.zeros_like(count[0]))
    if layout.groups > 1:
        _, last = walk(state)
        renewed = jnp.any(fresh).astype(f32)
        every = jax.tree.map(
            lambda a: lax.all_gather(a, AXIS, axis_index_groups=layout.across), last + (renewed,)
        )
        for g in range(layout.groups - 1):
            keep = every[2][g] < 0.5
            after = jax.tree.map(lambda a, e: jnp.where(keep, a, 0.0) + e[g], state, every[:2])
            state = jax.tree.map(lambda a, b: jnp.where(g < layout.group, b, a), state, after)
    before, _ = walk(state)
    return jnp.stack([b[0] for b in before]), jnp.stack([b[1] for b in before])


def carry_backward(layout, state_grad, norm_grad, fresh):
    segments = state_grad.shape[0]

    def walk(state):
        after = [None] * segments
        for s in reversed(range(segments)):
            after[s] = state
            state = (state[0] + state_grad[s], state[1] + norm_grad[s])
            state = jax.tree.map(lambda a: jnp.where(fresh[s], jnp.zeros_like(a), a), state)
        return after, state

    state = (jnp.zeros_like(state_grad[0]), jnp.zeros_like(norm_grad[0]))
    if layout.groups > 1:
        _, first = walk(state)
        renewed = jnp.any(fresh).astype(f32)
        every = jax.tree.map(
            lambda a: lax.all_gather(a, AXIS, axis_index_groups=layout.across), first + (renewed,)
        )
        for g in reversed(range(1, layout.groups)):
            keep = every[2][g] < 0.5
            before = jax.tree.map(lambda a, e: jnp.where(keep, a, 0.0) + e[g], state, every[:2])
            state = jax.tree.map(lambda a, b: jnp.where(g > layout.group, b, a), state, before)
    after, _ = walk(state)
    return jnp.stack([a[0] for a in after]), jnp.stack([a[1] for a in after])


def body_groups(
    layer_input,
    first_gain,
    in_weight,
    out_weight,
    mix_gate,
    second_gain,
    gate_up,
    down_weight,
    document_starts,
    cotangent,
):
    layout = Layout()
    tokens, width = layer_input.shape
    group_tokens = tokens * H
    segments = group_tokens // SEG
    scale = 1.0 / math.sqrt(DH)

    gains = jnp.stack([first_gain, second_gain])
    gains = lax.all_gather(gains, AXIS, axis=1, tiled=True).astype(f32)
    first_all, second_all = gains[0], gains[1]
    if layout.groups == 1:
        mix_own = mix_gate
    else:
        mix_own = lax.dynamic_slice_in_dim(layout.gather_all(mix_gate), layout.head * DH, DH)
    mix = jax.nn.sigmoid(mix_own.astype(f32))[None]

    inputs = layer_input.astype(f32)
    normed, first_factor = norm_forward(inputs, first_all)
    normed_all = layout.gather(normed.astype(bf16))
    in_cols = layout.columns(in_weight, 3)
    out_all = layout.gather_all(out_weight)
    cot_all = layout.gather(cotangent)
    gate_up_cols = layout.columns(gate_up, 2)
    down_cols = layout.columns(down_weight, 1)

    projected = jnp.dot(normed_all, in_cols, preferred_element_type=f32).astype(bf16)
    by_segment = projected.reshape(segments, SEG, 3, DH)
    query, key, value = by_segment[:, :, 0], by_segment[:, :, 1], by_segment[:, :, 2]
    index = jnp.arange(SEG, dtype=jnp.int32)
    allowed = index[None, :] <= index[:, None]

    def attention_scores():
        raw = jnp.einsum("sqc,skc->sqk", query, key, preferred_element_type=f32) * scale
        return jnp.where(allowed[None], raw, -1e30)

    scores = attention_scores()
    top = jnp.max(scores, axis=-1, keepdims=True)
    expo = jnp.exp(scores - top)
    total = jnp.sum(expo, axis=-1, keepdims=True)
    log_total = top + jnp.log(total)
    probs_low = (expo / total).astype(bf16)
    local_out = jnp.einsum("sqk,skc->sqc", probs_low, value, preferred_element_type=f32)

    query_f, key_f, value_f = query.astype(f32), key.astype(f32), value.astype(f32)
    query_feature = feature(query_f).astype(bf16)
    key_feature = feature(key_f).astype(bf16)
    delta = jnp.einsum("slc,sla->sca", key_feature, value, preferred_element_type=f32)
    count = jnp.sum(key_feature.astype(f32), axis=1)
    numbers = layout.group * segments + jnp.arange(segments)
    fresh = (numbers == 0) | (
        lax.dynamic_slice_in_dim(document_starts[0], layout.group * segments, segments) > 0
    )
    memory, normal = carry_forward(layout, delta, count, fresh)
    query_feature_f = query_feature.astype(f32)
    numerator = jnp.einsum("sie,sej->sij", query_feature_f, memory, precision=highest)
    raw_denom = jnp.einsum("sik,sk->si", query_feature_f, normal, precision=highest)[..., None]
    denom = jnp.maximum(raw_denom, 1.0)
    memory_out = numerator / denom
    combined = mix * memory_out + (1.0 - mix) * local_out
    combined_head = combined.reshape(group_tokens, DH).astype(bf16)
    combined_low = layout.to_tokens(combined_head)
    attended = jnp.dot(combined_low, out_all, preferred_element_type=f32)
    middle = inputs + attended

    hidden, second_factor = norm_forward(middle, second_all)
    hidden_all = layout.gather(hidden.astype(bf16))
    act_grad = jnp.dot(cot_all, down_cols, preferred_element_type=f32)
    both = jnp.dot(hidden_all, gate_up_cols, preferred_element_type=f32)
    half = both.shape[1] // 2
    gate_part, up_part = both[:, :half], both[:, half:]
    sigma = jax.nn.sigmoid(gate_part)
    silu = gate_part * sigma
    activated = (silu * up_part).astype(bf16)
    silu_slope = sigma * (1.0 + gate_part * (1.0 - sigma))
    feed_grad = jnp.concatenate(
        [act_grad * up_part * silu_slope, act_grad * silu], axis=1
    ).astype(bf16)
    feed_out = layout.scatter_sum(cols_dot(activated, down_cols).astype(bf16))
    hidden_grad = layout.scatter_sum(cols_dot(feed_grad, gate_up_cols).astype(bf16))
    layer_output = (middle + feed_out.astype(f32)).astype(bf16)
    gate_up_part = layout.own_rows(rows_dot(hidden_all, feed_grad), 2)
    down_part = layout.own_rows(rows_dot(cot_all, activated), 1)

    upstream = cotangent.astype(f32)
    middle_norm_grad, second_local = norm_backward(
        middle, second_factor, second_all, hidden_grad.astype(f32)
    )
    middle_grad = upstream + middle_norm_grad
    attended_grad = middle_grad.astype(bf16)
    attended_grad_all = layout.gather(attended_grad)
    combined_grad = layout.to_heads(cols_dot(attended_grad, out_all).astype(bf16))
    combined_grad = combined_grad.astype(f32).reshape(segments, SEG, DH)
    out_rows_grad = rows_dot(combined_head, attended_grad_all)
    if layout.groups == 1:
        out_part = out_rows_grad
    else:
        whole = jnp.zeros((H * DH, width), f32)
        whole = lax.dynamic_update_slice_in_dim(whole, out_rows_grad, layout.head * DH, 0)
        out_part = lax.psum_scatter(whole, AXIS, scatter_dimension=0, tiled=True)
    mix_local = jnp.sum(combined_grad * (memory_out - local_out), axis=(0, 1)) * (
        mix * (1.0 - mix)
    ).reshape(DH)

    memory_grad = combined_grad * mix
    local_grad = (combined_grad * (1.0 - mix)).astype(bf16)
    numer_grad = memory_grad / denom
    denom_grad = -jnp.sum(memory_grad * memory_out, axis=-1, keepdims=True) / denom
    raw_grad = jnp.where(raw_denom > 1.0, denom_grad, 0.0)
    query_feature_grad = (
        jnp.einsum("sij,sej->sie", numer_grad, memory, precision=highest)
        + raw_grad * normal[:, None]
    )
    state_grad = jnp.einsum("sie,sij->sej", query_feature_f, numer_grad, precision=highest)
    norm_grad = jnp.sum(raw_grad * query_feature_f, axis=1)
    delta_grad, count_grad = carry_backward(layout, state_grad, norm_grad, fresh)
    key_feature_grad = (
        jnp.einsum("sij,sej->sie", value_f, delta_grad, precision=highest) + count_grad[:, None]
    )
    value_memory_grad = jnp.einsum(
        "sie,sej->sij", key_feature.astype(f32), delta_grad, precision=highest
    )
    query_memory_grad = query_feature_grad * feature_slope(query_f)
    key_memory_grad = key_feature_grad * feature_slope(key_f)

    probs = jnp.exp(attention_scores() - log_total)
    prob_grad = jnp.einsum("sqc,skc->sqk", local_grad, value, preferred_element_type=f32)
    row_term = jnp.sum(probs * prob_grad, axis=-1, keepdims=True)
    score_grad = (probs * (prob_grad - row_term)).astype(bf16)
    query_grad = query_memory_grad + scale * jnp.einsum(
        "sqk,skc->sqc", score_grad, key, preferred_element_type=f32
    )
    key_grad = key_memory_grad + scale * jnp.einsum(
        "sqk,sqc->skc", score_grad, query, preferred_element_type=f32
    )
    value_grad = value_memory_grad + jnp.einsum(
        "sqk,sqc->skc", probs.astype(bf16), local_grad, preferred_element_type=f32
    )
    projected_grad = (
        jnp.stack([query_grad, key_grad, value_grad], axis=2)
        .reshape(group_tokens, 3 * DH)
        .astype(bf16)
    )
    normed_grad = layout.scatter_sum(cols_dot(projected_grad, in_cols).astype(bf16))
    in_part = layout.own_rows(rows_dot(normed_all, projected_grad), 3)
    input_norm_grad, first_local = norm_backward(
        inputs, first_factor, first_all, normed_grad.astype(f32)
    )
    input_grad = middle_grad + input_norm_grad

    gains_part = lax.psum_scatter(
        jnp.stack([first_local, second_local]), AXIS, scatter_dimension=1, tiled=True
    )
    if layout.groups == 1:
        mix_part = mix_local
    else:
        whole = jnp.zeros((H * DH,), f32)
        whole = lax.dynamic_update_slice_in_dim(whole, mix_local, layout.head * DH, 0)
        mix_part = lax.psum_scatter(whole, AXIS, scatter_dimension=0, tiled=True)

    def over_sequences(part):
        return lax.psum(part.astype(bf16), "dp").astype(f32)

    small = over_sequences(jnp.concatenate([gains_part, mix_part[None]]))
    return (
        layer_output,
        input_grad,
        small[0],
        over_sequences(in_part),
        over_sequences(out_part),
        small[2],
        small[1],
        over_sequences(gate_up_part),
        over_sequences(down_part),
    )


MESH = pl.DeviceIdType.MESH
LIMIT = 62 * 2**20
EARLY = 18
FILL = ((0, 512), (512, 1024), (1536, 512))
ROWS = 256
dma = pltpu.SemaphoreType.DMA
VM = pltpu.VMEM


def vmem():
    return pl.BlockSpec(memory_space=pltpu.VMEM)


def anywhere():
    return pl.BlockSpec(memory_space=pl.ANY)


class Spot:
    def __init__(self):
        self.dp = lax.axis_index("dp")
        self.me = lax.axis_index(AXIS)
        self.z = self.me // 4
        self.y = (self.me // 2) % 2
        self.c = self.me % 2

    def at(self, z, y, c):
        return z * 4 + y * 2 + c

    def partner(self, k):
        out = self.me
        for bit in (1, 2, 4, 8):
            if k & bit:
                out = out + bit - 2 * bit * ((self.me // bit) % 2)
        return out

    def arrival(self, j):
        if j == 0:
            return self.z
        ends = jnp.where(self.z == 0, j, 3 - j)
        middle = {1: (0, 3), 2: (2, 1), 3: (3, 0)}[j]
        inner = jnp.where(self.z == 1, middle[0], middle[1])
        return jnp.where((self.z == 0) | (self.z == 3), ends, inner)


def greet(s, plane=True, other=True):
    ids = []
    if plane:
        ids += [{AXIS: (s.me + k) % 16} for k in range(1, 16)]
    else:
        ids += [{AXIS: s.at((s.z + k) % 4, s.y, s.c)} for k in (1, 2, 3)]
        ids += [{AXIS: s.at(s.z, 1 - s.y, s.c)}, {AXIS: s.at(s.z, s.y, 1 - s.c)}]
    if other:
        ids += [{"dp": 1 - s.dp}]
    barrier = pltpu.get_barrier_semaphore()
    for d in ids:
        pl.semaphore_signal(barrier, inc=1, device_id=d, device_id_type=MESH)
    pl.semaphore_wait(barrier, len(ids))


def send(src, dst, ssem, rsem, to):
    return pltpu.make_async_remote_copy(
        src_ref=src, dst_ref=dst, send_sem=ssem, recv_sem=rsem,
        device_id={AXIS: to}, device_id_type=MESH,
    )


def send_over(src, dst, ssem, rsem, s):
    return pltpu.make_async_remote_copy(
        src_ref=src, dst_ref=dst, send_sem=ssem, recv_sem=rsem,
        device_id={"dp": 1 - s.dp}, device_id_type=MESH,
    )


def merged(*lists):
    keyed = []
    for n, tasks in enumerate(lists):
        keyed += [((i + 0.5) / len(tasks), n, i, t) for i, t in enumerate(tasks)]
    for _, _, _, t in sorted(keyed, key=lambda e: e[:3]):
        t()


class Gather:
    chunks = 4

    @classmethod
    def sems(cls):
        return [dma((cls.chunks, 4))] * 5 + [dma((cls.chunks, 8))] * 2

    def __init__(self, s, src, dst, sems):
        self.s, self.src, self.dst = s, src, dst
        self.zr, self.zu, self.zd, self.ys, self.yr, self.ss, self.sr = sems[:7]
        self.rows = 128 // self.chunks
        self.skip = 0

    def block(self, ch, z, y, c):
        start = self.s.at(z, y, c) * 128 + self.skip + ch * self.rows
        return self.dst.at[pl.ds(pl.multiple_of(start, self.rows), self.rows)]

    def own(self, ch):
        start = pl.multiple_of(self.skip + ch * self.rows, self.rows)
        return self.src.at[pl.ds(start, self.rows)]

    def zcopy(self, ch, zo, up, own=False):
        s = self.s
        dst = self.block(ch, zo, s.y, s.c)
        to = s.at(s.z + 1 if up else s.z - 1, s.y, s.c)
        return send(
            self.own(ch) if own else dst, dst,
            (self.zu if up else self.zd).at[ch, zo], self.zr.at[ch, zo], to,
        )

    def ycopy(self, ch, zo, own=False):
        s = self.s
        dst = self.block(ch, zo, s.y, s.c)
        src = self.own(ch) if own else dst
        return send(src, dst, self.ys.at[ch, zo], self.yr.at[ch, zo], s.at(s.z, 1 - s.y, s.c))

    def scopy(self, ch, zo, yo, own=False):
        s = self.s
        dst = self.block(ch, zo, yo, s.c)
        n = zo * 2 + yo
        src = self.own(ch) if own else dst
        return send(src, dst, self.ss.at[ch, n], self.sr.at[ch, n], s.at(s.z, s.y, 1 - s.c))

    def start(self):
        s = self.s
        for ch in range(self.chunks):
            pl.when(s.z < 3)(lambda: self.zcopy(ch, s.z, True, True).start())
            pl.when(s.z > 0)(lambda: self.zcopy(ch, s.z, False, True).start())
            self.ycopy(ch, s.z, True).start()
            self.scopy(ch, s.z, s.y, True).start()

    def passed_on(self, ch, zo, yo):
        self.scopy(ch, zo, yo).start()

    def z_arrive(self, ch, j):
        s = self.s
        zo = s.arrival(j)
        self.zcopy(ch, zo, True).wait_recv()
        pl.when((zo < s.z) & (s.z < 3))(lambda: self.zcopy(ch, zo, True).start())
        pl.when((zo > s.z) & (s.z > 0))(lambda: self.zcopy(ch, zo, False).start())
        self.ycopy(ch, zo).start()
        self.passed_on(ch, zo, s.y)

    def y_arrive(self, ch, j):
        s = self.s
        zo = s.arrival(j)
        b = self.block(ch, zo, 1 - s.y, s.c)
        send(b, b, self.ys.at[ch, zo], self.yr.at[ch, zo], s.me).wait_recv()
        self.passed_on(ch, zo, 1 - s.y)

    def s_arrive(self, j):
        s = self.s
        zo = s.arrival(j)
        for ch in range(self.chunks):
            for yo in range(2):
                n = zo * 2 + yo
                b = self.block(ch, zo, yo, 1 - s.c)
                send(b, b, self.ss.at[ch, n], self.sr.at[ch, n], s.me).wait_recv()

    def tasks(self, use=None):
        out = []
        for step in range(1, 5):
            for ch in range(self.chunks):
                if step < 4:
                    out.append(functools.partial(self.z_arrive, ch, step))
                out.append(functools.partial(self.y_arrive, ch, step - 1))
                if step == 4 and ch < 3 and use is not None:
                    out.append(functools.partial(use, ch))
            out.append(functools.partial(self.s_arrive, step - 1))
        if use is not None:
            out.append(functools.partial(use, 3))
        return out

    def drain(self):
        s = self.s
        for ch in range(self.chunks):
            for zo in range(4):
                pl.when((s.z < 3) & (zo <= s.z))(lambda: self.zcopy(ch, zo, True).wait_send())
                pl.when((s.z > 0) & (zo >= s.z))(lambda: self.zcopy(ch, zo, False).wait_send())
                self.ycopy(ch, zo).wait_send()
                for yo in range(2):
                    self.scopy(ch, zo, yo).wait_send()


class SharedGather(Gather):
    chunks = 2

    @classmethod
    def sems(cls):
        return Gather.sems.__func__(cls) + [dma((cls.chunks, 8))] * 4

    def __init__(self, s, src, dst, sems):
        super().__init__(s, src, dst, sems)
        self.xs, self.xr, self.ts, self.tr = sems[7:]
        self.rows = 64 // self.chunks
        self.skip = s.dp * 64

    def other(self, ch, z, y, c):
        start = self.s.at(z, y, c) * 128 + (1 - self.s.dp) * 64 + ch * self.rows
        return self.dst.at[pl.ds(pl.multiple_of(start, self.rows), self.rows)]

    def xcopy(self, ch, zo, yo):
        s = self.s
        b = self.block(ch, zo, yo, s.c)
        n = zo * 2 + yo
        return send_over(b, b, self.xs.at[ch, n], self.xr.at[ch, n], s)

    def tcopy(self, ch, zo, yo, own=False):
        s = self.s
        b = self.other(ch, zo, yo, s.c)
        n = zo * 2 + yo
        src = b
        if own:
            start = pl.multiple_of((1 - s.dp) * 64 + ch * self.rows, self.rows)
            src = self.src.at[pl.ds(start, self.rows)]
        return send(src, b, self.ts.at[ch, n], self.tr.at[ch, n], s.at(s.z, s.y, 1 - s.c))

    def start(self):
        super().start()
        for ch in range(self.chunks):
            self.tcopy(ch, self.s.z, self.s.y, True).start()

    def passed_on(self, ch, zo, yo):
        self.xcopy(ch, zo, yo).start()
        self.scopy(ch, zo, yo).start()

    def x_arrive(self, j, yo):
        s = self.s
        zo = s.arrival(j)
        row = s.y if yo == 0 else 1 - s.y
        for ch in range(self.chunks):
            b = self.other(ch, zo, row, s.c)
            n = zo * 2 + row
            send_over(b, b, self.xs.at[ch, n], self.xr.at[ch, n], s).wait_recv()
            self.tcopy(ch, zo, row).start()

    def tasks(self):
        out = super().tasks()
        for j in range(4):
            for yo in range(2):
                if j + yo > 0:
                    out.append(functools.partial(self.x_arrive, j, yo))
        return out

    def finish(self):
        s = self.s
        for ch in range(self.chunks):
            for n in range(8):
                b = self.other(ch, n // 2, n % 2, 1 - s.c)
                send(b, b, self.ts.at[ch, n], self.tr.at[ch, n], s.me).wait_recv()

    def drain(self):
        s = self.s
        super().drain()
        for ch in range(self.chunks):
            for zo in range(4):
                for yo in range(2):
                    self.tcopy(ch, zo, yo).wait_send()
                    far = (s.z != zo) | (s.y != yo)
                    pl.when(far)(lambda: self.xcopy(ch, zo, yo).wait_send())


class Columns:
    @staticmethod
    def sems(parts):
        return [dma((16, parts)), dma((16, parts)), dma((16,)), dma((16,)), dma((parts,))]

    def __init__(self, s, w, dst, parts, sems):
        self.s, self.w, self.dst, self.parts = s, w, dst, parts
        self.e = dst.shape[1] // parts
        self.ps, self.pr, self.xs, self.xr, self.own = sems

    def rows(self, src, half):
        return pl.ds(pl.multiple_of(src * 128 + half * 64, 64), 64)

    def cols(self, p, h):
        return pl.ds(pl.multiple_of(p * 16 * self.e + h * self.e, 128), self.e)

    def copy(self, k, p):
        s = self.s
        to = s.partner(k)
        half = pl.ds(pl.multiple_of(s.dp * 64, 64), 64)
        return send(
            self.w.at[half, self.cols(p, to)],
            self.dst.at[self.rows(s.me, s.dp), pl.ds(p * self.e, self.e)],
            self.ps.at[k, p], self.pr.at[s.me, p], to,
        )

    def local(self, p):
        s = self.s
        return pltpu.make_async_copy(
            self.w.at[:, self.cols(p, s.me)],
            self.dst.at[pl.ds(pl.multiple_of(s.me * 128, 128), 128), pl.ds(p * self.e, self.e)],
            self.own.at[p],
        )

    def begin(self, k):
        for p in range(self.parts):
            (self.copy(k, p) if k else self.local(p)).start()

    def start(self, ahead=16):
        self.ahead = ahead
        for k in range(ahead):
            self.begin(k)

    def over(self, src):
        s = self.s
        b = self.dst.at[self.rows(src, s.dp)]
        return send_over(b, b, self.xs.at[src], self.xr.at[src], s)

    def arrive(self, k):
        s = self.s
        if k + self.ahead - 1 < 16:
            self.begin(k + self.ahead - 1)
        src = s.partner(k)
        for p in range(self.parts):
            b = self.dst.at[self.rows(src, s.dp), pl.ds(p * self.e, self.e)]
            send(b, b, self.ps.at[k, p], self.pr.at[src, p], s.me).wait_recv()
        self.over(src).start()

    def tasks(self):
        return [functools.partial(self.arrive, k) for k in range(1, 16)]

    def finish(self):
        s = self.s
        for k in range(1, 16):
            src = s.partner(k)
            b = self.dst.at[self.rows(src, 1 - s.dp)]
            send_over(b, b, self.xs.at[src], self.xr.at[src], s).wait_recv()
        for p in range(self.parts):
            self.local(p).wait()

    def drain(self):
        s = self.s
        for k in range(1, 16):
            for p in range(self.parts):
                self.copy(k, p).wait_send()
            self.over(s.partner(k)).wait_send()


class Return:
    ahead = 16

    @staticmethod
    def sems(parts):
        return [dma((16, parts))] * 4 + [dma((parts,))]

    def __init__(self, s, src, dst, parts, sems):
        self.s, self.src, self.dst, self.parts = s, src, dst, parts
        self.e = src.shape[2] // parts
        self.ps, self.pr, self.xs, self.xr, self.own = sems

    def place(self, p, h, half):
        cols = pl.ds(pl.multiple_of(p * 16 * self.e + h * self.e, 128), self.e)
        return self.dst.at[pl.ds(pl.multiple_of(half * 64, 64), 64), cols]

    def block(self, h, p):
        return self.src.at[h, :, pl.ds(p * self.e, self.e)]

    def copy(self, k, p):
        s = self.s
        to = s.partner(k)
        return send(
            self.block(to, p), self.place(p, s.me, s.dp), self.ps.at[k, p], self.pr.at[s.me, p], to
        )

    def local(self, p):
        s = self.s
        return pltpu.make_async_copy(self.block(s.me, p), self.place(p, s.me, s.dp), self.own.at[p])

    def over(self, h, p, own=False):
        s = self.s
        dst = self.place(p, h, s.dp)
        src = self.block(s.me, p) if own else dst
        return send_over(src, dst, self.xs.at[h, p], self.xr.at[h, p], s)

    def begin(self, k):
        for p in range(self.parts):
            if k:
                self.copy(k, p).start()
                continue
            self.local(p).start()
            self.over(self.s.me, p, own=True).start()

    def start(self):
        for k in range(16):
            self.begin(k)

    def arrive(self, k):
        s = self.s
        h = s.partner(k)
        for p in range(self.parts):
            b = self.place(p, h, s.dp)
            send(b, b, self.ps.at[k, p], self.pr.at[h, p], s.me).wait_recv()
            self.over(h, p).start()

    def tasks(self):
        return [functools.partial(self.arrive, k) for k in range(1, 16)]

    def finish(self):
        s = self.s
        for p in range(self.parts):
            self.local(p).wait()
        for k in range(16):
            h = s.partner(k)
            for p in range(self.parts):
                b = self.place(p, h, 1 - s.dp)
                send_over(b, b, self.xs.at[h, p], self.xr.at[h, p], s).wait_recv()
        for k in range(16):
            for p in range(self.parts):
                if k:
                    self.copy(k, p).wait_send()
                self.over(s.partner(k), p).wait_send()


class Scatter:
    lag = 3

    @staticmethod
    def scratch(width):
        q = width // 512
        return [
            VM((4, 2, 256, width), bf16), VM((4, 2, 128, width), bf16), VM((4, 2, 128, width), bf16),
            VM((4, 128, width), bf16), VM((5, 128, width), bf16),
            dma((4, q, 2)), dma((4, q, 2)), dma((4, q)), dma((4, q)), dma((4, q)), dma((5, q)),
        ]

    def __init__(self, s, left, right, out, scratch, first=0):
        self.s, self.left, self.right, self.out, self.first = s, left, right, out, first
        self.part, self.sib, self.mid, self.got_y, self.got_z = scratch[:5]
        self.ss, self.sr, self.ys, self.yr, self.zs, self.zr = scratch[5:]
        self.cols = 512
        self.pieces = out.shape[1] // 512
        self.order = [s.arrival(j) for j in (3, 2, 1, 0)]

    def w(self, h):
        return pl.ds(h * self.cols, self.cols)

    def compute(self, k, h, yd, slot):
        tok = pl.multiple_of((self.order[k] * 2 + yd) * 256, 256)
        p = cols_dot(self.left[pl.ds(tok, 256), :], self.right[pl.ds(self.first + h * self.cols, self.cols), :])
        self.part[k, slot, :, self.w(h)] = p.astype(bf16)

    def sib_copy(self, k, h, slot):
        s = self.s
        src = self.part.at[k, slot, pl.ds(pl.multiple_of((1 - s.c) * 128, 128), 128), self.w(h)]
        return send(
            src, self.sib.at[k, slot, :, self.w(h)],
            self.ss.at[k, h, slot], self.sr.at[k, h, slot], s.at(s.z, s.y, 1 - s.c),
        )

    def y_copy(self, k, h):
        s = self.s
        return send(
            self.mid.at[k, 0, :, self.w(h)], self.got_y.at[k, :, self.w(h)],
            self.ys.at[k, h], self.yr.at[k, h], s.at(s.z, 1 - s.y, s.c),
        )

    def z_copy(self, k, h):
        s = self.s
        to = self.order[k]
        up = to > s.z
        hop = jnp.where(up, s.z + 1, s.z - 1)
        slot = jnp.where(up | (hop != to), to, 4)
        return send(
            self.mid.at[k, 1, :, self.w(h)], self.got_z.at[slot, :, self.w(h)],
            self.zs.at[k, h], self.zr.at[slot, h], s.at(hop, s.y, s.c),
        )

    def z_wait(self, slot, h):
        b = self.got_z.at[slot, :, self.w(h)]
        send(b, b, self.zs.at[0, h], self.zr.at[slot, h], self.s.me).wait_recv()

    def fold(self, k, h, slot):
        s = self.s
        self.sib_copy(k, h, slot).wait_recv()
        own = self.part[k, slot, pl.ds(pl.multiple_of(s.c * 128, 128), 128), self.w(h)]
        total = own.astype(f32) + self.sib[k, slot, :, self.w(h)].astype(f32)
        self.mid[k, slot, :, self.w(h)] = total.astype(bf16)

    def after_y(self, k, h):
        s = self.s
        w = self.w(h)
        self.y_copy(k, h).wait_recv()
        total = self.mid[k, 1, :, w].astype(f32) + self.got_y[k, :, w].astype(f32)
        if k == 3:
            self.out[:, w] = total
            return
        to = self.order[k]
        first = jnp.where(to > s.z, s.z == 0, s.z == 3)

        @pl.when(first)
        def _():
            self.mid[k, 1, :, w] = total.astype(bf16)

        @pl.when(jnp.logical_not(first))
        def _():
            self.z_wait(to, h)
            self.mid[k, 1, :, w] = (total + self.got_z[to, :, w].astype(f32)).astype(bf16)

        self.z_copy(k, h).start()

    def tasks(self):
        steps = [(k, h) for k in range(4) for h in range(self.pieces)]
        s = self.s

        def step(i):
            k, h = steps[i]
            self.compute(k, h, 1 - s.y, 0)
            self.sib_copy(k, h, 0).start()
            self.compute(k, h, s.y, 1)
            self.sib_copy(k, h, 1).start()
            self.fold(k, h, 0)
            self.y_copy(k, h).start()
            self.fold(k, h, 1)

        out = []
        for i in range(len(steps) + self.lag):
            if i < len(steps):
                out.append(functools.partial(step, i))
            if i >= self.lag:
                out.append(functools.partial(self.after_y, *steps[i - self.lag]))
        return out

    def finish(self):
        s = self.s
        for h in range(self.pieces):
            w = self.w(h)

            @pl.when(s.z > 0)
            def _():
                self.z_wait(s.z, h)
                self.out[:, w] += self.got_z[s.z, :, w].astype(f32)

            @pl.when(s.z < 3)
            def _():
                self.z_wait(4, h)
                self.out[:, w] += self.got_z[4, :, w].astype(f32)

        for k in range(4):
            for h in range(self.pieces):
                self.sib_copy(k, h, 0).wait_send()
                self.sib_copy(k, h, 1).wait_send()
                self.y_copy(k, h).wait_send()
                if k < 3:
                    self.z_copy(k, h).wait_send()


class Weigh:
    steps = 8

    @classmethod
    def scratch(cls, cols):
        return [
            VM((16, 64, cols), f32), VM((16, 64, cols), bf16), VM((16, 64, cols), bf16),
            dma((cls.steps,)), dma((cls.steps,)),
        ]

    def __init__(self, s, left, right, half, scratch, back=None):
        self.s, self.left, self.right, self.half, self.back = s, left, right, half, back
        self.mine, self.sent, self.got, self.xs, self.xr = scratch

    def at(self, n):
        return self.s.partner(2 * n) // 2

    def copy(self, n):
        i = self.at(n)
        w = pl.ds(2 * i, 2)
        return send_over(self.sent.at[w], self.got.at[w], self.xs.at[i], self.xr.at[i], self.s)

    def compute(self, n):
        i = self.at(n)
        low = self.s.dp == 0
        cols = pl.ds(pl.multiple_of(i * 256, 256), 256)
        got = rows_dot(self.left[:, cols], self.right[...])
        for m in range(2):
            a, b = got[m * 128:m * 128 + 64], got[m * 128 + 64:m * 128 + 128]
            self.mine[2 * i + m] = jnp.where(low, a, b)
            self.sent[2 * i + m] = jnp.where(low, b, a).astype(bf16)
        self.copy(n).start()

    def fold(self, n):
        self.copy(n).wait_recv()
        w = pl.ds(2 * self.at(n), 2)
        self.half[w] = (self.mine[w] + self.got[w].astype(f32)).astype(bf16)
        if self.back is not None:
            self.back.begin(2 * n)
            self.back.begin(2 * n + 1)

    def products(self):
        return [functools.partial(self.compute, i) for i in range(self.steps)]

    def folds(self):
        return [functools.partial(self.fold, i) for i in range(self.steps)]

    def drain(self):
        for i in range(self.steps):
            self.copy(i).wait_send()


def nothing(n):
    return [lambda: None] * n


def halves_of(refs, counts):
    out, at = [], 0
    for n in counts:
        out.append(refs[at:at + n])
        at += n
    return out


def loaded(pairs, sems):
    copies = [pltpu.make_async_copy(a, b, sems.at[i]) for i, (a, b) in enumerate(pairs)]
    for cp in copies:
        cp.start()
    return [cp.wait for cp in copies]


def norm_back(values, upstream, gains_all, which, write):
    whole = values[...].astype(f32)
    width = whole.shape[1]
    factor = lax.rsqrt(jnp.mean(whole * whole, axis=-1, keepdims=True) + epsilon)
    dot_row = jnp.zeros_like(factor)
    for j in range(16):
        w = pl.ds(j * 128, 128)
        scaled = upstream[:, w] * gains_all[j, which:which + 1, :] * values[:, w].astype(f32)
        dot_row = dot_row + jnp.sum(scaled, axis=-1, keepdims=True)
    dot_row = dot_row * (1.0 / width) * factor * factor * factor
    for j in range(16):
        w = pl.ds(j * 128, 128)
        v, u = values[:, w].astype(f32), upstream[:, w]
        grad = factor * (u * gains_all[j, which:which + 1, :]) - v * dot_row
        write(j, grad, jnp.sum(u * v * factor, axis=0, keepdims=True))


def communicate(kernel, name, number, ins, in_specs, outs, out_specs, scratch, flops=0):
    return pl.pallas_call(
        kernel, out_shape=outs, in_specs=in_specs, out_specs=out_specs, scratch_shapes=scratch,
        compiler_params=pltpu.CompilerParams(
            collective_id=number, has_side_effects=True, vmem_limit_bytes=LIMIT
        ),
        cost_estimate=pl.CostEstimate(flops=flops, bytes_accessed=2**24, transcendentals=0),
        name=name,
    )(*ins)


def kernel_feature(t):
    return jnp.where(t > 0, t + 1.0, jnp.exp(jnp.minimum(t, 0.0)))


def dot_high(left, right, dims=((1,), (0,))):
    return lax.dot_general(
        left, right, (dims, ((), ())), preferred_element_type=f32, precision=highest
    )


def scores_of(query, keys, first):
    raw = cols_dot(query, keys) * (1.0 / math.sqrt(DH))
    row = lax.broadcasted_iota(jnp.int32, raw.shape, 0) + first
    col = lax.broadcasted_iota(jnp.int32, raw.shape, 1)
    return jnp.where(col <= row, raw, -1e30)


class Attend:
    def __init__(self, qkv, keep, mix, local, mem_out, lse, combined, memory, normal):
        self.qkv, self.keep, self.mix = qkv, keep, mix
        self.local, self.mem_out, self.lse, self.combined = local, mem_out, lse, combined
        self.memory, self.normal = memory, normal
        self.segments = qkv.shape[0] // SEG

    def states(self):
        state = jnp.zeros((DH, DH), f32)
        norm = jnp.zeros((1, DH), f32)
        for n in range(self.segments):
            keep = self.keep[n, 0:1, :]
            state, norm = state * keep, norm * keep
            self.memory[n] = state
            self.normal[n, 0:1, :] = norm
            if n + 1 < self.segments:
                rows = pl.ds(n * SEG, SEG)
                fk = kernel_feature(self.qkv[rows, DH:2 * DH].astype(f32)).astype(bf16)
                state = state + rows_dot(fk, self.qkv[rows, 2 * DH:])
                norm = norm + jnp.sum(fk.astype(f32), axis=0, keepdims=True)

    def block(self, n, i):
        rows = pl.ds(n * SEG + i * ROWS, ROWS)
        seen = pl.ds(n * SEG, (i + 1) * ROWS)
        query = self.qkv[rows, :DH]
        scores = scores_of(query, self.qkv[seen, DH:2 * DH], i * ROWS)
        top = jnp.max(scores, axis=-1, keepdims=True)
        expo = jnp.exp(scores - top)
        total = jnp.sum(expo, axis=-1, keepdims=True)
        probs = (expo * (1.0 / total)).astype(bf16)
        local = jnp.dot(probs, self.qkv[seen, 2 * DH:], preferred_element_type=f32)
        fq = kernel_feature(query.astype(f32)).astype(bf16).astype(f32)
        den = jnp.maximum(jnp.sum(fq * self.normal[n, 0:1, :], axis=-1, keepdims=True), 1.0)
        mem_out = dot_high(fq, self.memory[n]) / den
        mix = self.mix[0:1, :]
        self.local[rows, :] = local
        self.mem_out[rows, :] = mem_out
        self.lse[rows, :] = jnp.broadcast_to(top + jnp.log(total), (ROWS, DH))
        self.combined[rows, :] = (mix * mem_out + (1.0 - mix) * local).astype(bf16)

    def blocks(self):
        return [(n, i) for n in range(self.segments) for i in range(SEG // ROWS)]


class AttendBack:
    def __init__(self, qkv, keep, mix, local, mem_out, lse, memory, normal, upstream, grad,
                 mix_grad, dk, dv, state_grad, norm_grad):
        self.qkv, self.keep, self.mix = qkv, keep, mix
        self.local, self.mem_out, self.lse = local, mem_out, lse
        self.memory, self.normal, self.upstream, self.grad = memory, normal, upstream, grad
        self.mix_grad, self.dk, self.dv = mix_grad, dk, dv
        self.state_grad, self.norm_grad = state_grad, norm_grad
        self.segments = qkv.shape[0] // SEG

    def clear(self):
        self.mix_grad[...] = jnp.zeros_like(self.mix_grad)
        self.dk[...] = jnp.zeros_like(self.dk)
        self.dv[...] = jnp.zeros_like(self.dv)
        self.state_grad[...] = jnp.zeros_like(self.state_grad)
        self.norm_grad[...] = jnp.zeros_like(self.norm_grad)

    def block(self, n, i):
        scale = 1.0 / math.sqrt(DH)
        rows = pl.ds(n * SEG + i * ROWS, ROWS)
        seen = pl.ds(n * SEG, (i + 1) * ROWS)
        query = self.qkv[rows, :DH]
        keys = self.qkv[seen, DH:2 * DH]
        values = self.qkv[seen, 2 * DH:]
        up = self.upstream[rows, :].astype(f32)
        mem_out = self.mem_out[rows, :]
        mix = self.mix[0:1, :]
        mixed = jnp.sum(up * (mem_out - self.local[rows, :]), axis=0, keepdims=True)
        self.mix_grad[0:1, :] += mixed * mix * (1.0 - mix)
        memory_grad = up * mix
        local_grad = (up * (1.0 - mix)).astype(bf16)
        query_f = query.astype(f32)
        fq = kernel_feature(query_f).astype(bf16).astype(f32)
        normal = self.normal[n, 0:1, :]
        raw = jnp.sum(fq * normal, axis=-1, keepdims=True)
        den = jnp.maximum(raw, 1.0)
        numer_grad = memory_grad / den
        den_grad = -jnp.sum(memory_grad * mem_out, axis=-1, keepdims=True) / den
        raw_grad = jnp.where(raw > 1.0, den_grad, 0.0)
        fq_grad = dot_high(numer_grad, self.memory[n], ((1,), (1,))) + raw_grad * normal
        if n > 0:
            self.state_grad[n] += dot_high(fq, numer_grad, ((0,), (0,)))
            self.norm_grad[n, 0:1, :] += jnp.sum(raw_grad * fq, axis=0, keepdims=True)
        scores = scores_of(query, keys, i * ROWS)
        probs = jnp.exp(scores - self.lse[rows, 0:1])
        prob_grad = cols_dot(local_grad, values)
        row_term = jnp.sum(probs * prob_grad, axis=-1, keepdims=True)
        score_grad = (probs * (prob_grad - row_term)).astype(bf16)
        query_grad = jnp.dot(score_grad, keys, preferred_element_type=f32) * scale
        query_grad = query_grad + fq_grad * feature_slope(query_f)
        self.grad[rows, :DH] = query_grad.astype(bf16)
        self.dk[seen, :] += rows_dot(score_grad, query) * scale
        self.dv[seen, :] += rows_dot(probs.astype(bf16), local_grad)

    def states(self):
        state = jnp.zeros((DH, DH), f32)
        norm = jnp.zeros((1, DH), f32)
        for n in reversed(range(self.segments)):
            rows = pl.ds(n * SEG, SEG)
            key = self.qkv[rows, DH:2 * DH].astype(f32)
            key_grad = self.dk[rows, :]
            value_grad = self.dv[rows, :]
            if n + 1 < self.segments:
                fk = kernel_feature(key).astype(bf16).astype(f32)
                value = self.qkv[rows, 2 * DH:].astype(f32)
                fk_grad = dot_high(value, state, ((1,), (1,))) + norm
                key_grad = key_grad + fk_grad * feature_slope(key)
                value_grad = value_grad + dot_high(fk, state)
            self.grad[rows, DH:2 * DH] = key_grad.astype(bf16)
            self.grad[rows, 2 * DH:] = value_grad.astype(bf16)
            if n > 0:
                keep = self.keep[n, 0:1, :]
                state = (state + self.state_grad[n]) * keep
                norm = (norm + self.norm_grad[n, 0:1, :]) * keep

    def blocks(self):
        return [(n, i) for n in range(self.segments) for i in range(SEG // ROWS)]


def forward_kernel(starts, mix_gate, first_gain, second_gain, x, in_w, out_w, cot, gate_up, down,
                   keep, mix, qkv, in_cols, gains_all, local, mem_out, lse, combined, memory, normal, middle,
                   normed_all, out_all, cot_all, gate_up_cols, down_cols, hidden_all, act, feed_grad,
                   gains, x_all, normed, row, mixed_tokens, hidden, out_v, cot_v, gate_up_v, down_v, hidden_v,
                   copies, outs, g_s, g_r, t_s, t_r, *rest):
    sems_o, sems_c, sems_g, sems_d, sems_h, sems_x, sems_i = halves_of(rest, [11, 7, 5, 5, 7, 7, 5])
    s = Spot()
    half = act.shape[1]
    mine = pl.ds(pl.multiple_of(s.me * 128, 128), 128)
    own = [
        pltpu.make_async_copy(out_w, out_v.at[mine], copies.at[0]),
        pltpu.make_async_copy(cot, cot_v.at[mine], copies.at[1]),
    ]
    for cp in own:
        cp.start()
    gains[...] = jnp.zeros_like(gains)
    gains[0:1, :] = first_gain[...].astype(f32)
    gains[1:2, :] = second_gain[...].astype(f32)
    mix[...] = jnp.broadcast_to(jax.nn.sigmoid(mix_gate[...].astype(f32)), mix.shape)
    keep[0] = jnp.zeros(keep.shape[1:], f32)
    for n in range(1, keep.shape[0]):
        kept = jnp.where(starts[0:1, n:n + 1] > 0, 0.0, 1.0)
        keep[n] = jnp.broadcast_to(kept, keep.shape[1:])
    greet(s)

    def gain_copy(k):
        return send(gains, gains_all.at[s.me], g_s.at[k], g_r.at[s.me], s.partner(k))

    gather_x = Gather(s, x, x_all, sems_x)
    columns_i = Columns(s, in_w, in_cols, 3, sems_i)
    gather_x.start()
    for k in range(1, 16):
        gain_copy(k).start()
    columns_i.start()
    gains_all[s.me] = gains[...]
    x_all[mine, :] = x[...]

    def gain_row():
        for k in range(1, 16):
            src = s.partner(k)
            b = gains_all.at[src]
            send(b, b, g_s.at[k], g_r.at[src], s.me).wait_recv()
        for j in range(16):
            row[0:1, pl.ds(j * 128, 128)] = gains_all[j, 0:1, :]

    def normed_copy(j):
        tok = pl.ds(pl.multiple_of(s.arrival(j) * 512, 512), 512)
        return pltpu.make_async_copy(normed.at[tok], normed_all.at[tok], outs.at[j, 3])

    def project(j):
        if j == 0:
            columns_i.finish()
            gain_row()
        for n in range(4):
            rows = pl.ds(pl.multiple_of(s.arrival(j) * 512 + n * 128, 128), 128)
            values = x_all[rows, :].astype(f32)
            factor = lax.rsqrt(jnp.mean(values * values, axis=-1, keepdims=True) + epsilon)
            normed[rows, :] = (values * factor * row[0:1, :]).astype(bf16)
        normed_copy(j).start()
        tok = pl.ds(pl.multiple_of(s.arrival(j) * 512, 512), 512)
        out = jnp.dot(normed[tok, :], in_cols[...], preferred_element_type=f32)
        qkv[tok, :] = out.astype(bf16)

    x_tasks = gather_x.tasks(project)
    gather_o = SharedGather(s, out_w, out_v, sems_o)
    gather_c = Gather(s, cot, cot_v, sems_c)
    gather_h = Gather(s, hidden, hidden_v, sems_h)
    columns_g = Columns(s, gate_up, gate_up_v, 2, sems_g)
    columns_d = Columns(s, down, down_v, 1, sems_d)

    def others():
        gather_o.start()
        gather_c.start()
        columns_g.start(4)

    merged(x_tasks[:EARLY] + [others] + x_tasks[EARLY:27], nothing(2) + columns_i.tasks())
    merged(x_tasks[27:])
    attend = Attend(qkv, keep, mix, local, mem_out, lse, combined, memory, normal)

    def token_copy(j):
        return send(
            combined.at[pl.ds(j * 128, 128)],
            mixed_tokens.at[:, pl.ds(pl.multiple_of(s.me * DH, DH), DH)],
            t_s.at[j], t_r.at[s.me], j,
        )

    def block(n, i):
        attend.block(n, i)
        for j in range((n * SEG + i * ROWS) // 128, (n * SEG + (i + 1) * ROWS) // 128):
            pl.when(s.me != j)(lambda: token_copy(j).start())

    compute = [attend.states] + [functools.partial(block, n, i) for n, i in attend.blocks()]
    wholes = [
        pltpu.make_async_copy(a, b, outs.at[4, i])
        for i, (a, b) in enumerate(
            [(out_v, out_all), (cot_v, cot_all), (gate_up_v, gate_up_cols), (down_v, down_cols)]
        )
    ]

    def tokens():
        own[0].wait()
        gather_o.finish()
        mixed_tokens[:, pl.ds(pl.multiple_of(s.me * DH, DH), DH)] = combined[mine, :]
        for k in range(1, 16):
            src = s.partner(k)
            b = mixed_tokens.at[:, pl.ds(pl.multiple_of(src * DH, DH), DH)]
            send(b, b, t_s.at[0], t_r.at[src], s.me).wait_recv()

    def output(j):
        w = pl.ds(j * 512, 512)
        got = jnp.dot(mixed_tokens[...], out_v[:, w], preferred_element_type=f32)
        middle[:, w] = got + x[:, w].astype(f32)

    def norm():
        values = middle[...]
        factor = lax.rsqrt(jnp.mean(values * values, axis=-1, keepdims=True) + epsilon)
        for j in range(16):
            w = pl.ds(j * 128, 128)
            part = (middle[:, w] * factor * gains_all[j, 1:2, :]).astype(bf16)
            hidden[:, w] = part
            hidden_v[mine, w] = part
        gather_h.start()
        wholes[0].start()

    def out_copies(j):
        tok = pl.ds(pl.multiple_of(s.arrival(j) * 512, 512), 512)
        pairs = [
            (hidden_v.at[tok], hidden_all),
            (normed.at[tok, pl.ds(2 * half, half)], act),
            (normed.at[tok, pl.ds(0, 2 * half)], feed_grad),
        ]
        return [
            pltpu.make_async_copy(a, b.at[tok], outs.at[j, i]) for i, (a, b) in enumerate(pairs)
        ]

    def use(j):
        if j == 0:
            for i in range(4):
                normed_copy(i).wait()
            own[1].wait()
            columns_g.finish()
            columns_d.finish()
            for cp in wholes[1:]:
                cp.start()
        tok = pl.ds(pl.multiple_of(s.arrival(j) * 512, 512), 512)
        act_grad = jnp.dot(cot_v[tok, :], down_v[...], preferred_element_type=f32)
        gate = jnp.dot(hidden_v[tok, :], gate_up_v[:, :half], preferred_element_type=f32)
        up = jnp.dot(hidden_v[tok, :], gate_up_v[:, half:], preferred_element_type=f32)
        sigma = jax.nn.sigmoid(gate)
        silu = gate * sigma
        normed[tok, 2 * half:3 * half] = (silu * up).astype(bf16)
        slope = sigma * (1.0 + gate * (1.0 - sigma))
        normed[tok, :half] = (act_grad * up * slope).astype(bf16)
        normed[tok, half:2 * half] = (act_grad * silu).astype(bf16)
        for cp in out_copies(j):
            cp.start()

    after = [tokens] + [functools.partial(output, j) for j in range(4)] + [norm]
    c_tasks = gather_c.tasks()
    early = len(c_tasks) * 4 // 5
    merged(gather_o.tasks(), c_tasks[:early], columns_g.tasks(), compute + nothing(len(compute)))
    merged(after, [functools.partial(columns_d.start, 4)])
    merged(
        gather_h.tasks(use),
        c_tasks[early:] + nothing(12),
        nothing(2) + columns_d.tasks() + nothing(8),
    )
    for j in range(16):
        pl.when(s.me != j)(lambda: token_copy(j).wait_send())
    for part in (gather_x, columns_i, gather_o, gather_c, gather_h, columns_g, columns_d):
        part.drain()
    for k in range(1, 16):
        gain_copy(k).wait_send()
    for cp in wholes:
        cp.wait()
    for j in range(4):
        for cp in out_copies(j):
            cp.wait()


def forward_of(starts, mix_gate, first_gain, second_gain, x, in_weight, out_weight, cotangent, gate_up, down, number):
    tokens, width = x.shape
    total = tokens * 16
    segments = total // SEG
    half = down.shape[1] // 16
    shape = jax.ShapeDtypeStruct
    rows, cols, fine = (total, width), (width, 2 * half), (total, half)
    return communicate(
        forward_kernel, "forward", number,
        (starts, mix_gate, first_gain, second_gain, x, in_weight, out_weight, cotangent, gate_up, down),
        [vmem()] * 5 + [anywhere()] * 5,
        [
            shape((segments, 8, DH), f32), shape((8, DH), f32),
            shape((total, 3 * DH), bf16), shape((width, 3 * DH), bf16), shape((16, 8, 128), f32),
            shape((total, DH), f32), shape((total, DH), f32), shape((total, DH), f32),
            shape((total, DH), bf16), shape((segments, DH, DH), f32), shape((segments, 8, DH), f32),
            shape((tokens, width), f32),
            shape(rows, bf16), shape((width, width), bf16), shape(rows, bf16), shape(cols, bf16),
            shape((width, half), bf16), shape(rows, bf16), shape(fine, bf16),
            shape((total, 2 * half), bf16),
        ],
        [vmem()] * 12 + [anywhere()] * 8,
        [
            VM((8, tokens), f32), VM(rows, bf16), VM(rows, bf16), VM((8, width), f32),
            VM((tokens, width), bf16), VM((tokens, width), bf16), VM((width, width), bf16),
            VM(rows, bf16), VM(cols, bf16), VM((width, half), bf16), VM(rows, bf16),
            dma((2,)), dma((5, 4)), dma((16,)), dma((16,)), dma((16,)), dma((16,)),
        ] + SharedGather.sems() + Gather.sems() + Columns.sems(2) + Columns.sems(1) + Gather.sems()
        + Gather.sems() + Columns.sems(3),
    )


def hidden_grad_kernel(feed_grad, gate_up_cols, hidden_all, act, down_cols, out, half, feed_out,
                       grad_v, gate_up_v, hidden_v, act_v, down_v, copies, *rest):
    sems_w, scratch, scratch_f = halves_of(rest, [5, 11, 11])
    s = Spot()
    loads = loaded(
        [(feed_grad, grad_v), (gate_up_cols, gate_up_v), (hidden_all, hidden_v), (act, act_v),
         (down_cols, down_v)],
        copies,
    )
    greet(s, plane=False)
    weigh = Weigh(s, hidden_v, grad_v, half, sems_w)
    scatter = Scatter(s, grad_v, gate_up_v, out, scratch)
    scatter.lag = 2
    filler = Scatter(s, act_v, down_v, feed_out, scratch_f, FILL[0][0])
    merged(
        loads[:2] + scatter.tasks(),
        nothing(1) + loads[2:] + weigh.products() + nothing(8),
        nothing(4) + filler.tasks(),
        nothing(40) + weigh.folds(),
    )
    scatter.finish()
    filler.finish()
    weigh.drain()


def hidden_grad_of(feed_grad, gate_up_cols, hidden_all, act, down_cols, number):
    shape = jax.ShapeDtypeStruct
    total, cols = feed_grad.shape
    width = gate_up_cols.shape[0]
    fill = FILL[0][1]
    return communicate(
        hidden_grad_kernel, "hidden_grad", number,
        (feed_grad, gate_up_cols, hidden_all, act, down_cols), [anywhere()] * 5,
        [
            shape((total // 16, width), f32), shape((16, 64, cols), bf16),
            shape((total // 16, fill), f32),
        ],
        [vmem()] * 3,
        [VM(a.shape, bf16) for a in (feed_grad, gate_up_cols, hidden_all, act, down_cols)] + [dma((5,))]
        + Weigh.scratch(cols) + Scatter.scratch(width) + Scatter.scratch(fill),
    )


def normed_grad_kernel(grad, in_cols, normed_all, x, gains_all, act, down_cols, gains, down_half, combined,
                       attended_all,
                       value_grad, gains_out, feed_out, out_rows, down_rows, in_rows, out_other,
                       attended_v, normed_grad, half, gains_v, got, total, theirs, normed_v, act_v, down_v,
                       copies, x_s, x_r, g_s, g_r,
                       *rest):
    sems_d, sems_i, sems_w, scratch, scratch_f = halves_of(rest, [5, 5, 5, 11, 11])
    s = Spot()
    loads = loaded(
        [(normed_all, normed_v), (act, act_v), (down_cols, down_v), (attended_all, attended_v)], copies
    )
    greet(s)
    back_i = Return(s, half, in_rows, 3, sems_i)
    weigh = Weigh(s, normed_v, grad, half, sems_w, back=back_i)
    back_d = Return(s, down_half, down_rows, 1, sems_d)
    scatter = Scatter(s, grad, in_cols, normed_grad, scratch)
    filler = Scatter(s, act_v, down_v, feed_out, scratch_f, FILL[2][0])
    over = send_over(out_rows, out_other, x_s.at[0], x_r.at[0], s)
    back_d.start()

    def out_product(j):
        w = pl.ds(j * 512, 512)
        out_rows[:, w] = rows_dot(combined[...], attended_v[:, w]).astype(bf16)

    products = [functools.partial(out_product, j) for j in range(4)]

    def gain_copy(k):
        to = s.partner(k)
        return send(gains_v.at[to], got.at[s.me], g_s.at[k], g_r.at[s.me], to)

    def write(j, value, gain):
        value_grad[:, pl.ds(j * 128, 128)] = value
        gains_v[j] = gains[j]
        gains_v[j, 0:1, :] = gain

    merged(
        scatter.tasks(),
        loads[:3] + weigh.products() + nothing(24),
        nothing(5) + weigh.folds() + nothing(12),
        nothing(4) + loads[3:] + products + [over.start] + back_d.tasks() + nothing(5),
        nothing(4) + filler.tasks(),
        nothing(16) + back_i.tasks(),
    )
    scatter.finish()
    norm_back(x, normed_grad, gains_all, 0, write)
    for k in range(1, 16):
        gain_copy(k).start()
    filler.finish()
    back_d.finish()
    back_i.finish()
    weigh.drain()
    over.wait()
    for k in range(1, 16):
        src = s.partner(k)
        b = got.at[src]
        send(b, b, g_s.at[k], g_r.at[src], s.me).wait_recv()
    got[s.me] = gains_v[s.me]
    acc = got[0]
    for k in range(1, 16):
        acc = acc + got[k]
    total[...] = acc
    cp = send_over(total, theirs, x_s.at[1], x_r.at[1], s)
    cp.start()
    for k in range(1, 16):
        gain_copy(k).wait_send()
    cp.wait()
    gains_out[...] = total[...] + theirs[...]


def normed_grad_of(grad, in_cols, normed_all, x, gains_all, act, down_cols, gains, down_half, combined,
                   attended_all, number):
    shape = jax.ShapeDtypeStruct
    total, cols = grad.shape
    tokens, width = x.shape
    fill = FILL[2][1]
    down_rows = shape((DH, 16 * down_half.shape[2]), bf16)
    in_rows = shape((DH, 16 * cols), bf16)
    return communicate(
        normed_grad_kernel, "normed_grad", number,
        (grad, in_cols, normed_all, x, gains_all, act, down_cols, gains, down_half, combined,
         attended_all),
        [vmem()] * 2 + [anywhere()] + [vmem()] * 2 + [anywhere()] * 2 + [vmem(), anywhere(), vmem(), anywhere()],
        [
            shape((tokens, width), f32), shape((8, 128), f32), shape((tokens, fill), f32),
            shape((DH, width), bf16), down_rows, in_rows, shape((DH, width), bf16),
        ],
        [vmem()] * 4 + [anywhere()] * 3,
        [
            VM(attended_all.shape, bf16),
            VM((tokens, width), f32), VM((16, 64, cols), bf16), VM((16, 8, 128), f32),
            VM((16, 8, 128), f32), VM((8, 128), f32), VM((8, 128), f32),
            VM(normed_all.shape, bf16), VM(act.shape, bf16), VM(down_cols.shape, bf16), dma((4,)),
            dma((2,)), dma((2,)), dma((16,)), dma((16,)),
        ] + Return.sems(1) + Return.sems(3) + Weigh.scratch(cols) + Scatter.scratch(width)
        + Scatter.scratch(fill),
    )


def attend_back_kernel(hidden_grad, middle, cot, gains_all, keep, mix, memory, normal, out_all, qkv, local,
                       mem_out, lse, gate_up_half, cot_all, act, down_cols,
                       middle_grad, gains, grad, down_half, feed_out, attended_all, gate_up_rows,
                       attended, out_v, qkv_v, local_v, mem_v, lse_v, cot_v, act_v, down_v, by_token,
                       upstream, mix_grad, dk, dv, state_grad, norm_grad, copies, own_s, h_s, h_r, *rest):
    sems_a, sems_g, sems_w, scratch_f = halves_of(rest, [7, 5, 5, 11])
    s = Spot()
    mine = pl.ds(pl.multiple_of(s.me * 128, 128), 128)
    loads = loaded(
        [(out_all, out_v), (qkv, qkv_v), (local, local_v), (mem_out, mem_v), (lse, lse_v),
         (cot_all, cot_v), (act, act_v), (down_cols, down_v)],
        copies,
    )
    greet(s)
    gains[...] = jnp.zeros_like(gains)

    def write(j, value, gain):
        w = pl.ds(j * 128, 128)
        total = cot[:, w].astype(f32) + value
        middle_grad[:, w] = total
        attended[:, w] = total.astype(bf16)
        gains[j, 1:2, :] = gain

    norm_back(middle, hidden_grad, gains_all, 1, write)
    own = pltpu.make_async_copy(attended, attended_all.at[mine], own_s.at[0])
    own.start()
    gather = Gather(s, attended, attended_all, sems_a)
    back_g = Return(s, gate_up_half, gate_up_rows, 2, sems_g)
    filler = Scatter(s, act_v, down_v, feed_out, scratch_f, FILL[1][0])
    filler.lag = 8
    weigh = Weigh(s, cot_v, act_v, down_half, sems_w)
    attend = AttendBack(qkv_v, keep, mix, local_v, mem_v, lse_v, memory, normal, upstream, grad,
                        mix_grad, dk, dv, state_grad, norm_grad)
    gather.start()
    attend.clear()
    loads[0]()

    def head_copy(j):
        return send(by_token.at[:, pl.ds(j * DH, DH)], upstream.at[mine], h_s.at[j], h_r.at[s.me], j)

    for j in range(4):
        w = pl.ds(j * 512, 512)
        by_token[:, w] = cols_dot(attended[...], out_v[w, :]).astype(bf16)
        for h in range(4 * j, 4 * j + 4):
            pl.when(s.me != h)(lambda: head_copy(h).start())
    upstream[mine, :] = by_token[:, pl.ds(pl.multiple_of(s.me * DH, DH), DH)]
    for wait in loads[1:]:
        wait()

    def arrive(j):
        b = upstream.at[pl.ds(j * 128, 128)]
        pl.when(s.me != j)(lambda: send(b, b, h_s.at[j], h_r.at[j], s.me).wait_recv())

    def block(n, i):
        for j in range((n * SEG + i * ROWS) // 128, (n * SEG + (i + 1) * ROWS) // 128):
            arrive(j)
        attend.block(n, i)

    compute = [functools.partial(block, n, i) for n, i in attend.blocks()] + [attend.states]
    merged(gather.tasks(), nothing(2) + compute, weigh.products() + nothing(12))
    back_g.start()
    merged(filler.tasks(), back_g.tasks(), weigh.folds())
    filler.finish()
    back_g.finish()
    weigh.drain()
    for j in range(16):
        pl.when(s.me != j)(lambda: head_copy(j).wait_send())
    gather.drain()
    own.wait()
    gains[s.me, 2:3, :] = mix_grad[0:1, :]


def attend_backward(hidden_grad, middle, cot, gains_all, keep, mix, memory, normal, out_all, qkv, local,
                    mem_out, lse, gate_up_half, cot_all, act, down_cols, number):
    tokens, width = cot.shape
    total = qkv.shape[0]
    segments = total // SEG
    shape = jax.ShapeDtypeStruct
    whole = (out_all, qkv, local, mem_out, lse, cot_all, act, down_cols)
    return communicate(
        attend_back_kernel, "attend_back", number,
        (hidden_grad, middle, cot, gains_all, keep, mix, memory, normal, out_all, qkv, local, mem_out,
         lse, gate_up_half, cot_all, act, down_cols),
        [vmem()] * 8 + [anywhere()] * 9,
        [
            shape((tokens, width), f32), shape((16, 8, DH), f32), shape((total, 3 * DH), bf16),
            shape((16, 64, act.shape[1]), bf16), shape((tokens, FILL[1][1]), f32),
            shape((total, width), bf16), shape((DH, 16 * gate_up_half.shape[2]), bf16),
        ],
        [vmem()] * 5 + [anywhere()] * 2,
        [VM((tokens, width), bf16)] + [VM(a.shape, a.dtype) for a in whole]
        + [
            VM((tokens, width), bf16), VM((total, DH), bf16), VM((8, DH), f32),
            VM((total, DH), f32), VM((total, DH), f32), VM((segments, DH, DH), f32),
            VM((segments, 8, DH), f32), dma((8,)), dma((1,)), dma((16,)), dma((16,)),
        ] + Gather.sems() + Return.sems(2) + Weigh.scratch(act.shape[1]) + Scatter.scratch(FILL[1][1]),
    )


def body(
    layer_input,
    first_gain,
    in_weight,
    out_weight,
    mix_gate,
    second_gain,
    gate_up,
    down_weight,
    document_starts,
    cotangent,
):
    tokens, width = layer_input.shape
    (keep, mix, qkv, in_cols, gains_all, local, mem_out, lse, combined, memory, normal, middle, normed_all,
     out_all, cot_all, gate_up_cols, down_cols, hidden_all, act, feed_grad) = forward_of(
        document_starts, mix_gate.reshape(1, tokens), first_gain.reshape(1, tokens),
        second_gain.reshape(1, tokens), layer_input, in_weight, out_weight, cotangent, gate_up,
        down_weight, 0,
    )
    hidden_grad, gate_up_half, feed_out_0 = hidden_grad_of(
        feed_grad, gate_up_cols, hidden_all, act, down_cols, 3
    )

    (middle_grad, gain_grads, projected_grad, down_half, feed_out_1, attended_all,
     gate_up_rows) = attend_backward(
        hidden_grad, middle, cotangent, gains_all, keep, mix, memory, normal, out_all, qkv, local, mem_out,
        lse, gate_up_half, cot_all, act, down_cols, 4,
    )
    (value_grad, gains_out, feed_out_2, out_rows, down_rows, in_rows, out_other) = normed_grad_of(
        projected_grad, in_cols, normed_all, layer_input, gains_all, act, down_cols, gain_grads, down_half,
        combined, attended_all, 5,
    )
    input_grad = middle_grad + value_grad
    feed_out = jnp.concatenate([feed_out_0, feed_out_1, feed_out_2], axis=1)
    layer_output = (middle + feed_out).astype(bf16)

    return (
        layer_output,
        input_grad,
        gains_out[0],
        in_rows.astype(f32),
        out_rows.astype(f32) + out_other.astype(f32),
        gains_out[2],
        gains_out[1],
        gate_up_rows.astype(f32),
        down_rows.astype(f32),
    )


def solution(mesh):
    one_group = mesh.shape[AXIS] == H and mesh.shape["dp"] == 2
    return jax.shard_map(
        body if one_group else body_groups,
        mesh=mesh,
        in_specs=(
            P(("dp", "fsdp"), None),
            P("fsdp"),
            P("fsdp", None),
            P("fsdp", None),
            P("fsdp"),
            P("fsdp"),
            P("fsdp", None),
            P("fsdp", None),
            P("dp", None),
            P(("dp", "fsdp"), None),
        ),
        out_specs=(
            P(("dp", "fsdp"), None),
            P(("dp", "fsdp"), None),
            P("fsdp"),
            P("fsdp", None),
            P("fsdp", None),
            P("fsdp"),
            P("fsdp"),
            P("fsdp", None),
            P("fsdp", None),
        ),
        check_vma=False,
    )
```

```python
import functools
import math

import jax
import jax.numpy as jnp
from jax import lax
from jax.experimental import pallas as pl
from jax.experimental.pallas import tpu as pltpu
from jax.sharding import PartitionSpec as P

H = 16
DH = 128
FF = 8192
SEG = 1024

highest = lax.Precision.HIGHEST
epsilon = 1e-06
f32 = jnp.float32
bf16 = jnp.bfloat16
AXIS = "fsdp"


def feature(values):
    return jax.nn.elu(values) + 1.0


def feature_slope(values):
    return jnp.where(values > 0, 1.0, jnp.exp(jnp.minimum(values, 0.0)))


def norm_forward(values, gain):
    factor = lax.rsqrt(jnp.mean(values * values, axis=-1, keepdims=True) + epsilon)
    return (values * factor * gain, factor)


def norm_backward(values, factor, gain, upstream):
    scaled = upstream * gain
    gain_grad = jnp.sum(upstream * values * factor, axis=0)
    value_grad = factor * scaled - values * (factor * factor * factor) * jnp.mean(
        scaled * values, axis=-1, keepdims=True
    )
    return (value_grad, gain_grad)


def dot(left, right, dims):
    return lax.dot_general(left, right, ((dims[0], dims[1]), ((), ())), preferred_element_type=f32)


def rows_dot(left, right):
    return dot(left, right, ((0,), (0,)))


def cols_dot(left, right):
    return dot(left, right, ((1,), (1,)))


class Layout:
    def __init__(self):
        self.count = lax.axis_size(AXIS)
        self.groups = self.count // H
        self.place = lax.axis_index(AXIS)
        self.head = self.place % H
        self.group = self.place // H
        self.inside = None
        self.across = None
        if self.groups > 1:
            self.inside = [[g * H + j for j in range(H)] for g in range(self.groups)]
            self.across = [[g * H + j for g in range(self.groups)] for j in range(H)]

    def gather(self, block):
        return lax.all_gather(block, AXIS, axis=0, tiled=True, axis_index_groups=self.inside)

    def gather_all(self, block):
        return lax.all_gather(block, AXIS, axis=0, tiled=True)

    def scatter_sum(self, whole):
        return lax.psum_scatter(
            whole, AXIS, scatter_dimension=0, tiled=True, axis_index_groups=self.inside
        )

    def columns(self, block, parts):
        rows, width = block.shape
        each = width // (parts * H)
        if self.groups == 1:
            split = block.reshape(rows, parts, H, each)
            out = lax.all_to_all(split, AXIS, 2, 0, tiled=True)
            return out.reshape(rows * self.count, parts * each)
        whole = self.gather_all(block).reshape(rows * self.count, parts, H, each)
        out = lax.dynamic_index_in_dim(whole, self.head, 2, False)
        return out.reshape(rows * self.count, parts * each)

    def own_rows(self, grad, parts):
        rows, width = grad.shape
        each = width // parts
        if self.groups == 1:
            split = grad.astype(bf16).reshape(rows, parts, 1, each)
            out = lax.all_to_all(split, AXIS, 0, 2, tiled=True)
            return out.reshape(rows // self.count, parts * H * each)
        whole = jnp.zeros((rows, parts, H, each), f32)
        whole = lax.dynamic_update_slice_in_dim(
            whole, grad.reshape(rows, parts, 1, each), self.head, 2
        )
        return lax.psum_scatter(
            whole.reshape(rows, parts * H * each), AXIS, scatter_dimension=0, tiled=True
        )

    def to_tokens(self, by_head):
        tokens, each = by_head.shape
        out = lax.all_to_all(
            by_head.reshape(H, tokens // H, each), AXIS, 0, 0, tiled=False,
            axis_index_groups=self.inside,
        )
        return out.transpose(1, 0, 2).reshape(tokens // H, H * each)

    def to_heads(self, by_token):
        tokens, width = by_token.shape
        split = by_token.reshape(tokens, H, width // H).transpose(1, 0, 2)
        out = lax.all_to_all(
            split, AXIS, 0, 0, tiled=False, axis_index_groups=self.inside
        )
        return out.reshape(H * tokens, width // H)


def carry_forward(layout, delta, count, fresh):
    segments = delta.shape[0]

    def walk(state):
        before = []
        for s in range(segments):
            state = jax.tree.map(lambda a: jnp.where(fresh[s], jnp.zeros_like(a), a), state)
            before.append(state)
            state = (state[0] + delta[s], state[1] + count[s])
        return before, state

    state = (jnp.zeros_like(delta[0]), jnp.zeros_like(count[0]))
    if layout.groups > 1:
        _, last = walk(state)
        renewed = jnp.any(fresh).astype(f32)
        every = jax.tree.map(
            lambda a: lax.all_gather(a, AXIS, axis_index_groups=layout.across), last + (renewed,)
        )
        for g in range(layout.groups - 1):
            keep = every[2][g] < 0.5
            after = jax.tree.map(lambda a, e: jnp.where(keep, a, 0.0) + e[g], state, every[:2])
            state = jax.tree.map(lambda a, b: jnp.where(g < layout.group, b, a), state, after)
    before, _ = walk(state)
    return jnp.stack([b[0] for b in before]), jnp.stack([b[1] for b in before])


def carry_backward(layout, state_grad, norm_grad, fresh):
    segments = state_grad.shape[0]

    def walk(state):
        after = [None] * segments
        for s in reversed(range(segments)):
            after[s] = state
            state = (state[0] + state_grad[s], state[1] + norm_grad[s])
            state = jax.tree.map(lambda a: jnp.where(fresh[s], jnp.zeros_like(a), a), state)
        return after, state

    state = (jnp.zeros_like(state_grad[0]), jnp.zeros_like(norm_grad[0]))
    if layout.groups > 1:
        _, first = walk(state)
        renewed = jnp.any(fresh).astype(f32)
        every = jax.tree.map(
            lambda a: lax.all_gather(a, AXIS, axis_index_groups=layout.across), first + (renewed,)
        )
        for g in reversed(range(1, layout.groups)):
            keep = every[2][g] < 0.5
            before = jax.tree.map(lambda a, e: jnp.where(keep, a, 0.0) + e[g], state, every[:2])
            state = jax.tree.map(lambda a, b: jnp.where(g > layout.group, b, a), state, before)
    after, _ = walk(state)
    return jnp.stack([a[0] for a in after]), jnp.stack([a[1] for a in after])


def body_groups(
    layer_input,
    first_gain,
    in_weight,
    out_weight,
    mix_gate,
    second_gain,
    gate_up,
    down_weight,
    document_starts,
    cotangent,
):
    layout = Layout()
    tokens, width = layer_input.shape
    group_tokens = tokens * H
    segments = group_tokens // SEG
    scale = 1.0 / math.sqrt(DH)

    gains = jnp.stack([first_gain, second_gain])
    gains = lax.all_gather(gains, AXIS, axis=1, tiled=True).astype(f32)
    first_all, second_all = gains[0], gains[1]
    if layout.groups == 1:
        mix_own = mix_gate
    else:
        mix_own = lax.dynamic_slice_in_dim(layout.gather_all(mix_gate), layout.head * DH, DH)
    mix = jax.nn.sigmoid(mix_own.astype(f32))[None]

    inputs = layer_input.astype(f32)
    normed, first_factor = norm_forward(inputs, first_all)
    normed_all = layout.gather(normed.astype(bf16))
    in_cols = layout.columns(in_weight, 3)
    out_all = layout.gather_all(out_weight)
    cot_all = layout.gather(cotangent)
    gate_up_cols = layout.columns(gate_up, 2)
    down_cols = layout.columns(down_weight, 1)

    projected = jnp.dot(normed_all, in_cols, preferred_element_type=f32).astype(bf16)
    by_segment = projected.reshape(segments, SEG, 3, DH)
    query, key, value = by_segment[:, :, 0], by_segment[:, :, 1], by_segment[:, :, 2]
    index = jnp.arange(SEG, dtype=jnp.int32)
    allowed = index[None, :] <= index[:, None]

    def attention_scores():
        raw = jnp.einsum("sqc,skc->sqk", query, key, preferred_element_type=f32) * scale
        return jnp.where(allowed[None], raw, -1e30)

    scores = attention_scores()
    top = jnp.max(scores, axis=-1, keepdims=True)
    expo = jnp.exp(scores - top)
    total = jnp.sum(expo, axis=-1, keepdims=True)
    log_total = top + jnp.log(total)
    probs_low = (expo / total).astype(bf16)
    local_out = jnp.einsum("sqk,skc->sqc", probs_low, value, preferred_element_type=f32)

    query_f, key_f, value_f = query.astype(f32), key.astype(f32), value.astype(f32)
    query_feature = feature(query_f).astype(bf16)
    key_feature = feature(key_f).astype(bf16)
    delta = jnp.einsum("slc,sla->sca", key_feature, value, preferred_element_type=f32)
    count = jnp.sum(key_feature.astype(f32), axis=1)
    numbers = layout.group * segments + jnp.arange(segments)
    fresh = (numbers == 0) | (
        lax.dynamic_slice_in_dim(document_starts[0], layout.group * segments, segments) > 0
    )
    memory, normal = carry_forward(layout, delta, count, fresh)
    query_feature_f = query_feature.astype(f32)
    numerator = jnp.einsum("sie,sej->sij", query_feature_f, memory, precision=highest)
    raw_denom = jnp.einsum("sik,sk->si", query_feature_f, normal, precision=highest)[..., None]
    denom = jnp.maximum(raw_denom, 1.0)
    memory_out = numerator / denom
    combined = mix * memory_out + (1.0 - mix) * local_out
    combined_head = combined.reshape(group_tokens, DH).astype(bf16)
    combined_low = layout.to_tokens(combined_head)
    attended = jnp.dot(combined_low, out_all, preferred_element_type=f32)
    middle = inputs + attended

    hidden, second_factor = norm_forward(middle, second_all)
    hidden_all = layout.gather(hidden.astype(bf16))
    act_grad = jnp.dot(cot_all, down_cols, preferred_element_type=f32)
    both = jnp.dot(hidden_all, gate_up_cols, preferred_element_type=f32)
    half = both.shape[1] // 2
    gate_part, up_part = both[:, :half], both[:, half:]
    sigma = jax.nn.sigmoid(gate_part)
    silu = gate_part * sigma
    activated = (silu * up_part).astype(bf16)
    silu_slope = sigma * (1.0 + gate_part * (1.0 - sigma))
    feed_grad = jnp.concatenate(
        [act_grad * up_part * silu_slope, act_grad * silu], axis=1
    ).astype(bf16)
    feed_out = layout.scatter_sum(cols_dot(activated, down_cols).astype(bf16))
    hidden_grad = layout.scatter_sum(cols_dot(feed_grad, gate_up_cols).astype(bf16))
    layer_output = (middle + feed_out.astype(f32)).astype(bf16)
    gate_up_part = layout.own_rows(rows_dot(hidden_all, feed_grad), 2)
    down_part = layout.own_rows(rows_dot(cot_all, activated), 1)

    upstream = cotangent.astype(f32)
    middle_norm_grad, second_local = norm_backward(
        middle, second_factor, second_all, hidden_grad.astype(f32)
    )
    middle_grad = upstream + middle_norm_grad
    attended_grad = middle_grad.astype(bf16)
    attended_grad_all = layout.gather(attended_grad)
    combined_grad = layout.to_heads(cols_dot(attended_grad, out_all).astype(bf16))
    combined_grad = combined_grad.astype(f32).reshape(segments, SEG, DH)
    out_rows_grad = rows_dot(combined_head, attended_grad_all)
    if layout.groups == 1:
        out_part = out_rows_grad
    else:
        whole = jnp.zeros((H * DH, width), f32)
        whole = lax.dynamic_update_slice_in_dim(whole, out_rows_grad, layout.head * DH, 0)
        out_part = lax.psum_scatter(whole, AXIS, scatter_dimension=0, tiled=True)
    mix_local = jnp.sum(combined_grad * (memory_out - local_out), axis=(0, 1)) * (
        mix * (1.0 - mix)
    ).reshape(DH)

    memory_grad = combined_grad * mix
    local_grad = (combined_grad * (1.0 - mix)).astype(bf16)
    numer_grad = memory_grad / denom
    denom_grad = -jnp.sum(memory_grad * memory_out, axis=-1, keepdims=True) / denom
    raw_grad = jnp.where(raw_denom > 1.0, denom_grad, 0.0)
    query_feature_grad = (
        jnp.einsum("sij,sej->sie", numer_grad, memory, precision=highest)
        + raw_grad * normal[:, None]
    )
    state_grad = jnp.einsum("sie,sij->sej", query_feature_f, numer_grad, precision=highest)
    norm_grad = jnp.sum(raw_grad * query_feature_f, axis=1)
    delta_grad, count_grad = carry_backward(layout, state_grad, norm_grad, fresh)
    key_feature_grad = (
        jnp.einsum("sij,sej->sie", value_f, delta_grad, precision=highest) + count_grad[:, None]
    )
    value_memory_grad = jnp.einsum(
        "sie,sej->sij", key_feature.astype(f32), delta_grad, precision=highest
    )
    query_memory_grad = query_feature_grad * feature_slope(query_f)
    key_memory_grad = key_feature_grad * feature_slope(key_f)

    probs = jnp.exp(attention_scores() - log_total)
    prob_grad = jnp.einsum("sqc,skc->sqk", local_grad, value, preferred_element_type=f32)
    row_term = jnp.sum(probs * prob_grad, axis=-1, keepdims=True)
    score_grad = (probs * (prob_grad - row_term)).astype(bf16)
    query_grad = query_memory_grad + scale * jnp.einsum(
        "sqk,skc->sqc", score_grad, key, preferred_element_type=f32
    )
    key_grad = key_memory_grad + scale * jnp.einsum(
        "sqk,sqc->skc", score_grad, query, preferred_element_type=f32
    )
    value_grad = value_memory_grad + jnp.einsum(
        "sqk,sqc->skc", probs.astype(bf16), local_grad, preferred_element_type=f32
    )
    projected_grad = (
        jnp.stack([query_grad, key_grad, value_grad], axis=2)
        .reshape(group_tokens, 3 * DH)
        .astype(bf16)
    )
    normed_grad = layout.scatter_sum(cols_dot(projected_grad, in_cols).astype(bf16))
    in_part = layout.own_rows(rows_dot(normed_all, projected_grad), 3)
    input_norm_grad, first_local = norm_backward(
        inputs, first_factor, first_all, normed_grad.astype(f32)
    )
    input_grad = middle_grad + input_norm_grad

    gains_part = lax.psum_scatter(
        jnp.stack([first_local, second_local]), AXIS, scatter_dimension=1, tiled=True
    )
    if layout.groups == 1:
        mix_part = mix_local
    else:
        whole = jnp.zeros((H * DH,), f32)
        whole = lax.dynamic_update_slice_in_dim(whole, mix_local, layout.head * DH, 0)
        mix_part = lax.psum_scatter(whole, AXIS, scatter_dimension=0, tiled=True)

    def over_sequences(part):
        return lax.psum(part.astype(bf16), "dp").astype(f32)

    small = over_sequences(jnp.concatenate([gains_part, mix_part[None]]))
    return (
        layer_output,
        input_grad,
        small[0],
        over_sequences(in_part),
        over_sequences(out_part),
        small[2],
        small[1],
        over_sequences(gate_up_part),
        over_sequences(down_part),
    )


MESH = pl.DeviceIdType.MESH
LIMIT = 62 * 2**20
EARLY = 18
FILL = ((0, 512), (512, 1024), (1536, 512))
ROWS = 256
dma = pltpu.SemaphoreType.DMA
VM = pltpu.VMEM


def vmem():
    return pl.BlockSpec(memory_space=pltpu.VMEM)


def anywhere():
    return pl.BlockSpec(memory_space=pl.ANY)


class Spot:
    def __init__(self):
        self.dp = lax.axis_index("dp")
        self.me = lax.axis_index(AXIS)
        self.z = self.me // 4
        self.y = (self.me // 2) % 2
        self.c = self.me % 2

    def at(self, z, y, c):
        return z * 4 + y * 2 + c

    def partner(self, k):
        out = self.me
        for bit in (1, 2, 4, 8):
            if k & bit:
                out = out + bit - 2 * bit * ((self.me // bit) % 2)
        return out

    def arrival(self, j):
        if j == 0:
            return self.z
        ends = jnp.where(self.z == 0, j, 3 - j)
        middle = {1: (0, 3), 2: (2, 1), 3: (3, 0)}[j]
        inner = jnp.where(self.z == 1, middle[0], middle[1])
        return jnp.where((self.z == 0) | (self.z == 3), ends, inner)


def greet(s, plane=True, other=True):
    ids = []
    if plane:
        ids += [{AXIS: (s.me + k) % 16} for k in range(1, 16)]
    else:
        ids += [{AXIS: s.at((s.z + k) % 4, s.y, s.c)} for k in (1, 2, 3)]
        ids += [{AXIS: s.at(s.z, 1 - s.y, s.c)}, {AXIS: s.at(s.z, s.y, 1 - s.c)}]
    if other:
        ids += [{"dp": 1 - s.dp}]
    barrier = pltpu.get_barrier_semaphore()
    for d in ids:
        pl.semaphore_signal(barrier, inc=1, device_id=d, device_id_type=MESH)
    pl.semaphore_wait(barrier, len(ids))


def send(src, dst, ssem, rsem, to):
    return pltpu.make_async_remote_copy(
        src_ref=src, dst_ref=dst, send_sem=ssem, recv_sem=rsem,
        device_id={AXIS: to}, device_id_type=MESH,
    )


def send_over(src, dst, ssem, rsem, s):
    return pltpu.make_async_remote_copy(
        src_ref=src, dst_ref=dst, send_sem=ssem, recv_sem=rsem,
        device_id={"dp": 1 - s.dp}, device_id_type=MESH,
    )


def merged(*lists):
    keyed = []
    for n, tasks in enumerate(lists):
        keyed += [((i + 0.5) / len(tasks), n, i, t) for i, t in enumerate(tasks)]
    for _, _, _, t in sorted(keyed, key=lambda e: e[:3]):
        t()


class Gather:
    chunks = 4

    @classmethod
    def sems(cls):
        return [dma((cls.chunks, 4))] * 5 + [dma((cls.chunks, 8))] * 2

    def __init__(self, s, src, dst, sems):
        self.s, self.src, self.dst = s, src, dst
        self.zr, self.zu, self.zd, self.ys, self.yr, self.ss, self.sr = sems[:7]
        self.rows = 128 // self.chunks
        self.skip = 0

    def block(self, ch, z, y, c):
        start = self.s.at(z, y, c) * 128 + self.skip + ch * self.rows
        return self.dst.at[pl.ds(pl.multiple_of(start, self.rows), self.rows)]

    def own(self, ch):
        start = pl.multiple_of(self.skip + ch * self.rows, self.rows)
        return self.src.at[pl.ds(start, self.rows)]

    def zcopy(self, ch, zo, up, own=False):
        s = self.s
        dst = self.block(ch, zo, s.y, s.c)
        to = s.at(s.z + 1 if up else s.z - 1, s.y, s.c)
        return send(
            self.own(ch) if own else dst, dst,
            (self.zu if up else self.zd).at[ch, zo], self.zr.at[ch, zo], to,
        )

    def ycopy(self, ch, zo, own=False):
        s = self.s
        dst = self.block(ch, zo, s.y, s.c)
        src = self.own(ch) if own else dst
        return send(src, dst, self.ys.at[ch, zo], self.yr.at[ch, zo], s.at(s.z, 1 - s.y, s.c))

    def scopy(self, ch, zo, yo, own=False):
        s = self.s
        dst = self.block(ch, zo, yo, s.c)
        n = zo * 2 + yo
        src = self.own(ch) if own else dst
        return send(src, dst, self.ss.at[ch, n], self.sr.at[ch, n], s.at(s.z, s.y, 1 - s.c))

    def start(self):
        s = self.s
        for ch in range(self.chunks):
            pl.when(s.z < 3)(lambda: self.zcopy(ch, s.z, True, True).start())
            pl.when(s.z > 0)(lambda: self.zcopy(ch, s.z, False, True).start())
            self.ycopy(ch, s.z, True).start()
            self.scopy(ch, s.z, s.y, True).start()

    def passed_on(self, ch, zo, yo):
        self.scopy(ch, zo, yo).start()

    def z_arrive(self, ch, j):
        s = self.s
        zo = s.arrival(j)
        self.zcopy(ch, zo, True).wait_recv()
        pl.when((zo < s.z) & (s.z < 3))(lambda: self.zcopy(ch, zo, True).start())
        pl.when((zo > s.z) & (s.z > 0))(lambda: self.zcopy(ch, zo, False).start())
        self.ycopy(ch, zo).start()
        self.passed_on(ch, zo, s.y)

    def y_arrive(self, ch, j):
        s = self.s
        zo = s.arrival(j)
        b = self.block(ch, zo, 1 - s.y, s.c)
        send(b, b, self.ys.at[ch, zo], self.yr.at[ch, zo], s.me).wait_recv()
        self.passed_on(ch, zo, 1 - s.y)

    def s_arrive(self, j):
        s = self.s
        zo = s.arrival(j)
        for ch in range(self.chunks):
            for yo in range(2):
                n = zo * 2 + yo
                b = self.block(ch, zo, yo, 1 - s.c)
                send(b, b, self.ss.at[ch, n], self.sr.at[ch, n], s.me).wait_recv()

    def tasks(self, use=None):
        out = []
        for step in range(1, 5):
            for ch in range(self.chunks):
                if step < 4:
                    out.append(functools.partial(self.z_arrive, ch, step))
                out.append(functools.partial(self.y_arrive, ch, step - 1))
                if step == 4 and ch < 3 and use is not None:
                    out.append(functools.partial(use, ch))
            out.append(functools.partial(self.s_arrive, step - 1))
        if use is not None:
            out.append(functools.partial(use, 3))
        return out

    def drain(self):
        s = self.s
        for ch in range(self.chunks):
            for zo in range(4):
                pl.when((s.z < 3) & (zo <= s.z))(lambda: self.zcopy(ch, zo, True).wait_send())
                pl.when((s.z > 0) & (zo >= s.z))(lambda: self.zcopy(ch, zo, False).wait_send())
                self.ycopy(ch, zo).wait_send()
                for yo in range(2):
                    self.scopy(ch, zo, yo).wait_send()


class SharedGather(Gather):
    chunks = 2

    @classmethod
    def sems(cls):
        return Gather.sems.__func__(cls) + [dma((cls.chunks, 8))] * 4

    def __init__(self, s, src, dst, sems):
        super().__init__(s, src, dst, sems)
        self.xs, self.xr, self.ts, self.tr = sems[7:]
        self.rows = 64 // self.chunks
        self.skip = s.dp * 64

    def other(self, ch, z, y, c):
        start = self.s.at(z, y, c) * 128 + (1 - self.s.dp) * 64 + ch * self.rows
        return self.dst.at[pl.ds(pl.multiple_of(start, self.rows), self.rows)]

    def xcopy(self, ch, zo, yo):
        s = self.s
        b = self.block(ch, zo, yo, s.c)
        n = zo * 2 + yo
        return send_over(b, b, self.xs.at[ch, n], self.xr.at[ch, n], s)

    def tcopy(self, ch, zo, yo, own=False):
        s = self.s
        b = self.other(ch, zo, yo, s.c)
        n = zo * 2 + yo
        src = b
        if own:
            start = pl.multiple_of((1 - s.dp) * 64 + ch * self.rows, self.rows)
            src = self.src.at[pl.ds(start, self.rows)]
        return send(src, b, self.ts.at[ch, n], self.tr.at[ch, n], s.at(s.z, s.y, 1 - s.c))

    def start(self):
        super().start()
        for ch in range(self.chunks):
            self.tcopy(ch, self.s.z, self.s.y, True).start()

    def passed_on(self, ch, zo, yo):
        self.xcopy(ch, zo, yo).start()
        self.scopy(ch, zo, yo).start()

    def x_arrive(self, j, yo):
        s = self.s
        zo = s.arrival(j)
        row = s.y if yo == 0 else 1 - s.y
        for ch in range(self.chunks):
            b = self.other(ch, zo, row, s.c)
            n = zo * 2 + row
            send_over(b, b, self.xs.at[ch, n], self.xr.at[ch, n], s).wait_recv()
            self.tcopy(ch, zo, row).start()

    def tasks(self):
        out = super().tasks()
        for j in range(4):
            for yo in range(2):
                if j + yo > 0:
                    out.append(functools.partial(self.x_arrive, j, yo))
        return out

    def finish(self):
        s = self.s
        for ch in range(self.chunks):
            for n in range(8):
                b = self.other(ch, n // 2, n % 2, 1 - s.c)
                send(b, b, self.ts.at[ch, n], self.tr.at[ch, n], s.me).wait_recv()

    def drain(self):
        s = self.s
        super().drain()
        for ch in range(self.chunks):
            for zo in range(4):
                for yo in range(2):
                    self.tcopy(ch, zo, yo).wait_send()
                    far = (s.z != zo) | (s.y != yo)
                    pl.when(far)(lambda: self.xcopy(ch, zo, yo).wait_send())


class Columns:
    @staticmethod
    def sems(parts):
        return [dma((16, parts)), dma((16, parts)), dma((16,)), dma((16,)), dma((parts,))]

    def __init__(self, s, w, dst, parts, sems):
        self.s, self.w, self.dst, self.parts = s, w, dst, parts
        self.e = dst.shape[1] // parts
        self.ps, self.pr, self.xs, self.xr, self.own = sems

    def rows(self, src, half):
        return pl.ds(pl.multiple_of(src * 128 + half * 64, 64), 64)

    def cols(self, p, h):
        return pl.ds(pl.multiple_of(p * 16 * self.e + h * self.e, 128), self.e)

    def copy(self, k, p):
        s = self.s
        to = s.partner(k)
        half = pl.ds(pl.multiple_of(s.dp * 64, 64), 64)
        return send(
            self.w.at[half, self.cols(p, to)],
            self.dst.at[self.rows(s.me, s.dp), pl.ds(p * self.e, self.e)],
            self.ps.at[k, p], self.pr.at[s.me, p], to,
        )

    def local(self, p):
        s = self.s
        return pltpu.make_async_copy(
            self.w.at[:, self.cols(p, s.me)],
            self.dst.at[pl.ds(pl.multiple_of(s.me * 128, 128), 128), pl.ds(p * self.e, self.e)],
            self.own.at[p],
        )

    def begin(self, k):
        for p in range(self.parts):
            (self.copy(k, p) if k else self.local(p)).start()

    def start(self, ahead=16):
        self.ahead = ahead
        for k in range(ahead):
            self.begin(k)

    def over(self, src):
        s = self.s
        b = self.dst.at[self.rows(src, s.dp)]
        return send_over(b, b, self.xs.at[src], self.xr.at[src], s)

    def arrive(self, k):
        s = self.s
        if k + self.ahead - 1 < 16:
            self.begin(k + self.ahead - 1)
        src = s.partner(k)
        for p in range(self.parts):
            b = self.dst.at[self.rows(src, s.dp), pl.ds(p * self.e, self.e)]
            send(b, b, self.ps.at[k, p], self.pr.at[src, p], s.me).wait_recv()
        self.over(src).start()

    def tasks(self):
        return [functools.partial(self.arrive, k) for k in range(1, 16)]

    def finish(self):
        s = self.s
        for k in range(1, 16):
            src = s.partner(k)
            b = self.dst.at[self.rows(src, 1 - s.dp)]
            send_over(b, b, self.xs.at[src], self.xr.at[src], s).wait_recv()
        for p in range(self.parts):
            self.local(p).wait()

    def drain(self):
        s = self.s
        for k in range(1, 16):
            for p in range(self.parts):
                self.copy(k, p).wait_send()
            self.over(s.partner(k)).wait_send()


class Return:
    ahead = 16

    @staticmethod
    def sems(parts):
        return [dma((16, parts))] * 4 + [dma((parts,))]

    def __init__(self, s, src, dst, parts, sems):
        self.s, self.src, self.dst, self.parts = s, src, dst, parts
        self.e = src.shape[2] // parts
        self.ps, self.pr, self.xs, self.xr, self.own = sems

    def place(self, p, h, half):
        cols = pl.ds(pl.multiple_of(p * 16 * self.e + h * self.e, 128), self.e)
        return self.dst.at[pl.ds(pl.multiple_of(half * 64, 64), 64), cols]

    def block(self, h, p):
        return self.src.at[h, :, pl.ds(p * self.e, self.e)]

    def copy(self, k, p):
        s = self.s
        to = s.partner(k)
        return send(
            self.block(to, p), self.place(p, s.me, s.dp), self.ps.at[k, p], self.pr.at[s.me, p], to
        )

    def local(self, p):
        s = self.s
        return pltpu.make_async_copy(self.block(s.me, p), self.place(p, s.me, s.dp), self.own.at[p])

    def over(self, h, p, own=False):
        s = self.s
        dst = self.place(p, h, s.dp)
        src = self.block(s.me, p) if own else dst
        return send_over(src, dst, self.xs.at[h, p], self.xr.at[h, p], s)

    def begin(self, k):
        for p in range(self.parts):
            if k:
                self.copy(k, p).start()
                continue
            self.local(p).start()
            self.over(self.s.me, p, own=True).start()

    def start(self):
        for k in range(16):
            self.begin(k)

    def arrive(self, k):
        s = self.s
        h = s.partner(k)
        for p in range(self.parts):
            b = self.place(p, h, s.dp)
            send(b, b, self.ps.at[k, p], self.pr.at[h, p], s.me).wait_recv()
            self.over(h, p).start()

    def tasks(self):
        return [functools.partial(self.arrive, k) for k in range(1, 16)]

    def finish(self):
        s = self.s
        for p in range(self.parts):
            self.local(p).wait()
        for k in range(16):
            h = s.partner(k)
            for p in range(self.parts):
                b = self.place(p, h, 1 - s.dp)
                send_over(b, b, self.xs.at[h, p], self.xr.at[h, p], s).wait_recv()
        for k in range(16):
            for p in range(self.parts):
                if k:
                    self.copy(k, p).wait_send()
                self.over(s.partner(k), p).wait_send()


class Scatter:
    lag = 3

    @staticmethod
    def scratch(width):
        q = width // 512
        return [
            VM((4, 2, 256, width), bf16), VM((4, 2, 128, width), bf16), VM((4, 2, 128, width), bf16),
            VM((4, 128, width), bf16), VM((5, 128, width), bf16),
            dma((4, q, 2)), dma((4, q, 2)), dma((4, q)), dma((4, q)), dma((4, q)), dma((5, q)),
        ]

    def __init__(self, s, left, right, out, scratch, first=0):
        self.s, self.left, self.right, self.out, self.first = s, left, right, out, first
        self.part, self.sib, self.mid, self.got_y, self.got_z = scratch[:5]
        self.ss, self.sr, self.ys, self.yr, self.zs, self.zr = scratch[5:]
        self.cols = 512
        self.pieces = out.shape[1] // 512
        self.order = [s.arrival(j) for j in (3, 2, 1, 0)]

    def w(self, h):
        return pl.ds(h * self.cols, self.cols)

    def compute(self, k, h, yd, slot):
        tok = pl.multiple_of((self.order[k] * 2 + yd) * 256, 256)
        p = cols_dot(self.left[pl.ds(tok, 256), :], self.right[pl.ds(self.first + h * self.cols, self.cols), :])
        self.part[k, slot, :, self.w(h)] = p.astype(bf16)

    def sib_copy(self, k, h, slot):
        s = self.s
        src = self.part.at[k, slot, pl.ds(pl.multiple_of((1 - s.c) * 128, 128), 128), self.w(h)]
        return send(
            src, self.sib.at[k, slot, :, self.w(h)],
            self.ss.at[k, h, slot], self.sr.at[k, h, slot], s.at(s.z, s.y, 1 - s.c),
        )

    def y_copy(self, k, h):
        s = self.s
        return send(
            self.mid.at[k, 0, :, self.w(h)], self.got_y.at[k, :, self.w(h)],
            self.ys.at[k, h], self.yr.at[k, h], s.at(s.z, 1 - s.y, s.c),
        )

    def z_copy(self, k, h):
        s = self.s
        to = self.order[k]
        up = to > s.z
        hop = jnp.where(up, s.z + 1, s.z - 1)
        slot = jnp.where(up | (hop != to), to, 4)
        return send(
            self.mid.at[k, 1, :, self.w(h)], self.got_z.at[slot, :, self.w(h)],
            self.zs.at[k, h], self.zr.at[slot, h], s.at(hop, s.y, s.c),
        )

    def z_wait(self, slot, h):
        b = self.got_z.at[slot, :, self.w(h)]
        send(b, b, self.zs.at[0, h], self.zr.at[slot, h], self.s.me).wait_recv()

    def fold(self, k, h, slot):
        s = self.s
        self.sib_copy(k, h, slot).wait_recv()
        own = self.part[k, slot, pl.ds(pl.multiple_of(s.c * 128, 128), 128), self.w(h)]
        total = own.astype(f32) + self.sib[k, slot, :, self.w(h)].astype(f32)
        self.mid[k, slot, :, self.w(h)] = total.astype(bf16)

    def after_y(self, k, h):
        s = self.s
        w = self.w(h)
        self.y_copy(k, h).wait_recv()
        total = self.mid[k, 1, :, w].astype(f32) + self.got_y[k, :, w].astype(f32)
        if k == 3:
            self.out[:, w] = total
            return
        to = self.order[k]
        first = jnp.where(to > s.z, s.z == 0, s.z == 3)

        @pl.when(first)
        def _():
            self.mid[k, 1, :, w] = total.astype(bf16)

        @pl.when(jnp.logical_not(first))
        def _():
            self.z_wait(to, h)
            self.mid[k, 1, :, w] = (total + self.got_z[to, :, w].astype(f32)).astype(bf16)

        self.z_copy(k, h).start()

    def tasks(self):
        steps = [(k, h) for k in range(4) for h in range(self.pieces)]
        s = self.s

        def step(i):
            k, h = steps[i]
            self.compute(k, h, 1 - s.y, 0)
            self.sib_copy(k, h, 0).start()
            self.compute(k, h, s.y, 1)
            self.sib_copy(k, h, 1).start()
            self.fold(k, h, 0)
            self.y_copy(k, h).start()
            self.fold(k, h, 1)

        out = []
        for i in range(len(steps) + self.lag):
            if i < len(steps):
                out.append(functools.partial(step, i))
            if i >= self.lag:
                out.append(functools.partial(self.after_y, *steps[i - self.lag]))
        return out

    def finish(self):
        s = self.s
        for h in range(self.pieces):
            w = self.w(h)

            @pl.when(s.z > 0)
            def _():
                self.z_wait(s.z, h)
                self.out[:, w] += self.got_z[s.z, :, w].astype(f32)

            @pl.when(s.z < 3)
            def _():
                self.z_wait(4, h)
                self.out[:, w] += self.got_z[4, :, w].astype(f32)

        for k in range(4):
            for h in range(self.pieces):
                self.sib_copy(k, h, 0).wait_send()
                self.sib_copy(k, h, 1).wait_send()
                self.y_copy(k, h).wait_send()
                if k < 3:
                    self.z_copy(k, h).wait_send()


class Weigh:
    steps = 8

    @classmethod
    def scratch(cls, cols):
        return [
            VM((16, 64, cols), f32), VM((16, 64, cols), bf16), VM((16, 64, cols), bf16),
            dma((cls.steps,)), dma((cls.steps,)),
        ]

    def __init__(self, s, left, right, half, scratch, back=None):
        self.s, self.left, self.right, self.half, self.back = s, left, right, half, back
        self.mine, self.sent, self.got, self.xs, self.xr = scratch

    def at(self, n):
        return self.s.partner(2 * n) // 2

    def copy(self, n):
        i = self.at(n)
        w = pl.ds(2 * i, 2)
        return send_over(self.sent.at[w], self.got.at[w], self.xs.at[i], self.xr.at[i], self.s)

    def compute(self, n):
        i = self.at(n)
        low = self.s.dp == 0
        cols = pl.ds(pl.multiple_of(i * 256, 256), 256)
        got = rows_dot(self.left[:, cols], self.right[...])
        for m in range(2):
            a, b = got[m * 128:m * 128 + 64], got[m * 128 + 64:m * 128 + 128]
            self.mine[2 * i + m] = jnp.where(low, a, b)
            self.sent[2 * i + m] = jnp.where(low, b, a).astype(bf16)
        self.copy(n).start()

    def fold(self, n):
        self.copy(n).wait_recv()
        w = pl.ds(2 * self.at(n), 2)
        self.half[w] = (self.mine[w] + self.got[w].astype(f32)).astype(bf16)
        if self.back is not None:
            self.back.begin(2 * n)
            self.back.begin(2 * n + 1)

    def products(self):
        return [functools.partial(self.compute, i) for i in range(self.steps)]

    def folds(self):
        return [functools.partial(self.fold, i) for i in range(self.steps)]

    def drain(self):
        for i in range(self.steps):
            self.copy(i).wait_send()


def nothing(n):
    return [lambda: None] * n


def halves_of(refs, counts):
    out, at = [], 0
    for n in counts:
        out.append(refs[at:at + n])
        at += n
    return out


def loaded(pairs, sems):
    copies = [pltpu.make_async_copy(a, b, sems.at[i]) for i, (a, b) in enumerate(pairs)]
    for cp in copies:
        cp.start()
    return [cp.wait for cp in copies]


def norm_back(values, upstream, gains_all, which, write):
    whole = values[...].astype(f32)
    width = whole.shape[1]
    factor = lax.rsqrt(jnp.mean(whole * whole, axis=-1, keepdims=True) + epsilon)
    dot_row = jnp.zeros_like(factor)
    for j in range(16):
        w = pl.ds(j * 128, 128)
        scaled = upstream[:, w] * gains_all[j, which:which + 1, :] * values[:, w].astype(f32)
        dot_row = dot_row + jnp.sum(scaled, axis=-1, keepdims=True)
    dot_row = dot_row * (1.0 / width) * factor * factor * factor
    for j in range(16):
        w = pl.ds(j * 128, 128)
        v, u = values[:, w].astype(f32), upstream[:, w]
        grad = factor * (u * gains_all[j, which:which + 1, :]) - v * dot_row
        write(j, grad, jnp.sum(u * v * factor, axis=0, keepdims=True))


def communicate(kernel, name, number, ins, in_specs, outs, out_specs, scratch, flops=0):
    return pl.pallas_call(
        kernel, out_shape=outs, in_specs=in_specs, out_specs=out_specs, scratch_shapes=scratch,
        compiler_params=pltpu.CompilerParams(
            collective_id=number, has_side_effects=True, vmem_limit_bytes=LIMIT
        ),
        cost_estimate=pl.CostEstimate(flops=flops, bytes_accessed=2**24, transcendentals=0),
        name=name,
    )(*ins)


def kernel_feature(t):
    return jnp.where(t > 0, t + 1.0, jnp.exp(jnp.minimum(t, 0.0)))


def dot_high(left, right, dims=((1,), (0,))):
    return lax.dot_general(
        left, right, (dims, ((), ())), preferred_element_type=f32, precision=highest
    )


def scores_of(query, keys, first):
    raw = cols_dot(query, keys) * (1.0 / math.sqrt(DH))
    row = lax.broadcasted_iota(jnp.int32, raw.shape, 0) + first
    col = lax.broadcasted_iota(jnp.int32, raw.shape, 1)
    return jnp.where(col <= row, raw, -1e30)


class Attend:
    def __init__(self, qkv, keep, mix, local, mem_out, lse, combined, memory, normal):
        self.qkv, self.keep, self.mix = qkv, keep, mix
        self.local, self.mem_out, self.lse, self.combined = local, mem_out, lse, combined
        self.memory, self.normal = memory, normal
        self.segments = qkv.shape[0] // SEG

    def states(self):
        state = jnp.zeros((DH, DH), f32)
        norm = jnp.zeros((1, DH), f32)
        for n in range(self.segments):
            keep = self.keep[n, 0:1, :]
            state, norm = state * keep, norm * keep
            self.memory[n] = state
            self.normal[n, 0:1, :] = norm
            if n + 1 < self.segments:
                rows = pl.ds(n * SEG, SEG)
                fk = kernel_feature(self.qkv[rows, DH:2 * DH].astype(f32)).astype(bf16)
                state = state + rows_dot(fk, self.qkv[rows, 2 * DH:])
                norm = norm + jnp.sum(fk.astype(f32), axis=0, keepdims=True)

    def block(self, n, i):
        rows = pl.ds(n * SEG + i * ROWS, ROWS)
        seen = pl.ds(n * SEG, (i + 1) * ROWS)
        query = self.qkv[rows, :DH]
        scores = scores_of(query, self.qkv[seen, DH:2 * DH], i * ROWS)
        top = jnp.max(scores, axis=-1, keepdims=True)
        expo = jnp.exp(scores - top)
        total = jnp.sum(expo, axis=-1, keepdims=True)
        probs = (expo * (1.0 / total)).astype(bf16)
        local = jnp.dot(probs, self.qkv[seen, 2 * DH:], preferred_element_type=f32)
        fq = kernel_feature(query.astype(f32)).astype(bf16).astype(f32)
        den = jnp.maximum(jnp.sum(fq * self.normal[n, 0:1, :], axis=-1, keepdims=True), 1.0)
        mem_out = dot_high(fq, self.memory[n]) / den
        mix = self.mix[0:1, :]
        self.local[rows, :] = local
        self.mem_out[rows, :] = mem_out
        self.lse[rows, :] = jnp.broadcast_to(top + jnp.log(total), (ROWS, DH))
        self.combined[rows, :] = (mix * mem_out + (1.0 - mix) * local).astype(bf16)

    def blocks(self):
        return [(n, i) for n in range(self.segments) for i in range(SEG // ROWS)]


class AttendBack:
    def __init__(self, qkv, keep, mix, local, mem_out, lse, memory, normal, upstream, grad,
                 mix_grad, dk, dv, state_grad, norm_grad):
        self.qkv, self.keep, self.mix = qkv, keep, mix
        self.local, self.mem_out, self.lse = local, mem_out, lse
        self.memory, self.normal, self.upstream, self.grad = memory, normal, upstream, grad
        self.mix_grad, self.dk, self.dv = mix_grad, dk, dv
        self.state_grad, self.norm_grad = state_grad, norm_grad
        self.segments = qkv.shape[0] // SEG

    def clear(self):
        self.mix_grad[...] = jnp.zeros_like(self.mix_grad)
        self.dk[...] = jnp.zeros_like(self.dk)
        self.dv[...] = jnp.zeros_like(self.dv)
        self.state_grad[...] = jnp.zeros_like(self.state_grad)
        self.norm_grad[...] = jnp.zeros_like(self.norm_grad)

    def block(self, n, i):
        scale = 1.0 / math.sqrt(DH)
        rows = pl.ds(n * SEG + i * ROWS, ROWS)
        seen = pl.ds(n * SEG, (i + 1) * ROWS)
        query = self.qkv[rows, :DH]
        keys = self.qkv[seen, DH:2 * DH]
        values = self.qkv[seen, 2 * DH:]
        up = self.upstream[rows, :].astype(f32)
        mem_out = self.mem_out[rows, :]
        mix = self.mix[0:1, :]
        mixed = jnp.sum(up * (mem_out - self.local[rows, :]), axis=0, keepdims=True)
        self.mix_grad[0:1, :] += mixed * mix * (1.0 - mix)
        memory_grad = up * mix
        local_grad = (up * (1.0 - mix)).astype(bf16)
        query_f = query.astype(f32)
        fq = kernel_feature(query_f).astype(bf16).astype(f32)
        normal = self.normal[n, 0:1, :]
        raw = jnp.sum(fq * normal, axis=-1, keepdims=True)
        den = jnp.maximum(raw, 1.0)
        numer_grad = memory_grad / den
        den_grad = -jnp.sum(memory_grad * mem_out, axis=-1, keepdims=True) / den
        raw_grad = jnp.where(raw > 1.0, den_grad, 0.0)
        fq_grad = dot_high(numer_grad, self.memory[n], ((1,), (1,))) + raw_grad * normal
        if n > 0:
            self.state_grad[n] += dot_high(fq, numer_grad, ((0,), (0,)))
            self.norm_grad[n, 0:1, :] += jnp.sum(raw_grad * fq, axis=0, keepdims=True)
        scores = scores_of(query, keys, i * ROWS)
        probs = jnp.exp(scores - self.lse[rows, 0:1])
        prob_grad = cols_dot(local_grad, values)
        row_term = jnp.sum(probs * prob_grad, axis=-1, keepdims=True)
        score_grad = (probs * (prob_grad - row_term)).astype(bf16)
        query_grad = jnp.dot(score_grad, keys, preferred_element_type=f32) * scale
        query_grad = query_grad + fq_grad * feature_slope(query_f)
        self.grad[rows, :DH] = query_grad.astype(bf16)
        self.dk[seen, :] += rows_dot(score_grad, query) * scale
        self.dv[seen, :] += rows_dot(probs.astype(bf16), local_grad)

    def states(self):
        state = jnp.zeros((DH, DH), f32)
        norm = jnp.zeros((1, DH), f32)
        for n in reversed(range(self.segments)):
            rows = pl.ds(n * SEG, SEG)
            key = self.qkv[rows, DH:2 * DH].astype(f32)
            key_grad = self.dk[rows, :]
            value_grad = self.dv[rows, :]
            if n + 1 < self.segments:
                fk = kernel_feature(key).astype(bf16).astype(f32)
                value = self.qkv[rows, 2 * DH:].astype(f32)
                fk_grad = dot_high(value, state, ((1,), (1,))) + norm
                key_grad = key_grad + fk_grad * feature_slope(key)
                value_grad = value_grad + dot_high(fk, state)
            self.grad[rows, DH:2 * DH] = key_grad.astype(bf16)
            self.grad[rows, 2 * DH:] = value_grad.astype(bf16)
            if n > 0:
                keep = self.keep[n, 0:1, :]
                state = (state + self.state_grad[n]) * keep
                norm = (norm + self.norm_grad[n, 0:1, :]) * keep

    def blocks(self):
        return [(n, i) for n in range(self.segments) for i in range(SEG // ROWS)]


def forward_kernel(starts, mix_gate, first_gain, second_gain, x, in_w, out_w, cot, gate_up, down,
                   keep, mix, qkv, in_cols, gains_all, local, mem_out, lse, combined, memory, normal, middle,
                   normed_all, out_all, cot_all, gate_up_cols, down_cols, hidden_all, act, feed_grad,
                   gains, x_all, normed, row, mixed_tokens, hidden, out_v, cot_v, gate_up_v, down_v, hidden_v,
                   copies, outs, g_s, g_r, t_s, t_r, *rest):
    sems_o, sems_c, sems_g, sems_d, sems_h, sems_x, sems_i = halves_of(rest, [11, 7, 5, 5, 7, 7, 5])
    s = Spot()
    half = act.shape[1]
    mine = pl.ds(pl.multiple_of(s.me * 128, 128), 128)
    own = [
        pltpu.make_async_copy(out_w, out_v.at[mine], copies.at[0]),
        pltpu.make_async_copy(cot, cot_v.at[mine], copies.at[1]),
    ]
    for cp in own:
        cp.start()
    gains[...] = jnp.zeros_like(gains)
    gains[0:1, :] = first_gain[...].astype(f32)
    gains[1:2, :] = second_gain[...].astype(f32)
    mix[...] = jnp.broadcast_to(jax.nn.sigmoid(mix_gate[...].astype(f32)), mix.shape)
    keep[0] = jnp.zeros(keep.shape[1:], f32)
    for n in range(1, keep.shape[0]):
        kept = jnp.where(starts[0:1, n:n + 1] > 0, 0.0, 1.0)
        keep[n] = jnp.broadcast_to(kept, keep.shape[1:])
    greet(s)

    def gain_copy(k):
        return send(gains, gains_all.at[s.me], g_s.at[k], g_r.at[s.me], s.partner(k))

    gather_x = Gather(s, x, x_all, sems_x)
    columns_i = Columns(s, in_w, in_cols, 3, sems_i)
    gather_x.start()
    for k in range(1, 16):
        gain_copy(k).start()
    columns_i.start()
    gains_all[s.me] = gains[...]
    x_all[mine, :] = x[...]

    def gain_row():
        for k in range(1, 16):
            src = s.partner(k)
            b = gains_all.at[src]
            send(b, b, g_s.at[k], g_r.at[src], s.me).wait_recv()
        for j in range(16):
            row[0:1, pl.ds(j * 128, 128)] = gains_all[j, 0:1, :]

    def normed_copy(j):
        tok = pl.ds(pl.multiple_of(s.arrival(j) * 512, 512), 512)
        return pltpu.make_async_copy(normed.at[tok], normed_all.at[tok], outs.at[j, 3])

    def project(j):
        if j == 0:
            columns_i.finish()
            gain_row()
        for n in range(4):
            rows = pl.ds(pl.multiple_of(s.arrival(j) * 512 + n * 128, 128), 128)
            values = x_all[rows, :].astype(f32)
            factor = lax.rsqrt(jnp.mean(values * values, axis=-1, keepdims=True) + epsilon)
            normed[rows, :] = (values * factor * row[0:1, :]).astype(bf16)
        normed_copy(j).start()
        tok = pl.ds(pl.multiple_of(s.arrival(j) * 512, 512), 512)
        out = jnp.dot(normed[tok, :], in_cols[...], preferred_element_type=f32)
        qkv[tok, :] = out.astype(bf16)

    x_tasks = gather_x.tasks(project)
    gather_o = SharedGather(s, out_w, out_v, sems_o)
    gather_c = Gather(s, cot, cot_v, sems_c)
    gather_h = Gather(s, hidden, hidden_v, sems_h)
    columns_g = Columns(s, gate_up, gate_up_v, 2, sems_g)
    columns_d = Columns(s, down, down_v, 1, sems_d)

    def others():
        gather_o.start()
        gather_c.start()
        columns_g.start(4)

    merged(x_tasks[:EARLY] + [others] + x_tasks[EARLY:27], nothing(2) + columns_i.tasks())
    merged(x_tasks[27:])
    attend = Attend(qkv, keep, mix, local, mem_out, lse, combined, memory, normal)

    def token_copy(j):
        return send(
            combined.at[pl.ds(j * 128, 128)],
            mixed_tokens.at[:, pl.ds(pl.multiple_of(s.me * DH, DH), DH)],
            t_s.at[j], t_r.at[s.me], j,
        )

    def block(n, i):
        attend.block(n, i)
        for j in range((n * SEG + i * ROWS) // 128, (n * SEG + (i + 1) * ROWS) // 128):
            pl.when(s.me != j)(lambda: token_copy(j).start())

    compute = [attend.states] + [functools.partial(block, n, i) for n, i in attend.blocks()]
    wholes = [
        pltpu.make_async_copy(a, b, outs.at[4, i])
        for i, (a, b) in enumerate(
            [(out_v, out_all), (cot_v, cot_all), (gate_up_v, gate_up_cols), (down_v, down_cols)]
        )
    ]

    def tokens():
        own[0].wait()
        gather_o.finish()
        mixed_tokens[:, pl.ds(pl.multiple_of(s.me * DH, DH), DH)] = combined[mine, :]
        for k in range(1, 16):
            src = s.partner(k)
            b = mixed_tokens.at[:, pl.ds(pl.multiple_of(src * DH, DH), DH)]
            send(b, b, t_s.at[0], t_r.at[src], s.me).wait_recv()

    def output(j):
        w = pl.ds(j * 512, 512)
        got = jnp.dot(mixed_tokens[...], out_v[:, w], preferred_element_type=f32)
        middle[:, w] = got + x[:, w].astype(f32)

    def norm():
        values = middle[...]
        factor = lax.rsqrt(jnp.mean(values * values, axis=-1, keepdims=True) + epsilon)
        for j in range(16):
            w = pl.ds(j * 128, 128)
            part = (middle[:, w] * factor * gains_all[j, 1:2, :]).astype(bf16)
            hidden[:, w] = part
            hidden_v[mine, w] = part
        gather_h.start()
        wholes[0].start()

    def out_copies(j):
        tok = pl.ds(pl.multiple_of(s.arrival(j) * 512, 512), 512)
        pairs = [
            (hidden_v.at[tok], hidden_all),
            (normed.at[tok, pl.ds(2 * half, half)], act),
            (normed.at[tok, pl.ds(0, 2 * half)], feed_grad),
        ]
        return [
            pltpu.make_async_copy(a, b.at[tok], outs.at[j, i]) for i, (a, b) in enumerate(pairs)
        ]

    def use(j):
        if j == 0:
            for i in range(4):
                normed_copy(i).wait()
            own[1].wait()
            columns_g.finish()
            columns_d.finish()
            for cp in wholes[1:]:
                cp.start()
        tok = pl.ds(pl.multiple_of(s.arrival(j) * 512, 512), 512)
        act_grad = jnp.dot(cot_v[tok, :], down_v[...], preferred_element_type=f32)
        gate = jnp.dot(hidden_v[tok, :], gate_up_v[:, :half], preferred_element_type=f32)
        up = jnp.dot(hidden_v[tok, :], gate_up_v[:, half:], preferred_element_type=f32)
        sigma = jax.nn.sigmoid(gate)
        silu = gate * sigma
        normed[tok, 2 * half:3 * half] = (silu * up).astype(bf16)
        slope = sigma * (1.0 + gate * (1.0 - sigma))
        normed[tok, :half] = (act_grad * up * slope).astype(bf16)
        normed[tok, half:2 * half] = (act_grad * silu).astype(bf16)
        for cp in out_copies(j):
            cp.start()

    after = [tokens] + [functools.partial(output, j) for j in range(4)] + [norm]
    c_tasks = gather_c.tasks()
    early = len(c_tasks) * 4 // 5
    merged(gather_o.tasks(), c_tasks[:early], columns_g.tasks(), compute + nothing(len(compute)))
    merged(after, [functools.partial(columns_d.start, 4)])
    merged(
        gather_h.tasks(use),
        c_tasks[early:] + nothing(12),
        nothing(2) + columns_d.tasks() + nothing(8),
    )
    for j in range(16):
        pl.when(s.me != j)(lambda: token_copy(j).wait_send())
    for part in (gather_x, columns_i, gather_o, gather_c, gather_h, columns_g, columns_d):
        part.drain()
    for k in range(1, 16):
        gain_copy(k).wait_send()
    for cp in wholes:
        cp.wait()
    for j in range(4):
        for cp in out_copies(j):
            cp.wait()


def forward_of(starts, mix_gate, first_gain, second_gain, x, in_weight, out_weight, cotangent, gate_up, down, number):
    tokens, width = x.shape
    total = tokens * 16
    segments = total // SEG
    half = down.shape[1] // 16
    shape = jax.ShapeDtypeStruct
    rows, cols, fine = (total, width), (width, 2 * half), (total, half)
    return communicate(
        forward_kernel, "forward", number,
        (starts, mix_gate, first_gain, second_gain, x, in_weight, out_weight, cotangent, gate_up, down),
        [vmem()] * 5 + [anywhere()] * 5,
        [
            shape((segments, 8, DH), f32), shape((8, DH), f32),
            shape((total, 3 * DH), bf16), shape((width, 3 * DH), bf16), shape((16, 8, 128), f32),
            shape((total, DH), f32), shape((total, DH), f32), shape((total, DH), f32),
            shape((total, DH), bf16), shape((segments, DH, DH), f32), shape((segments, 8, DH), f32),
            shape((tokens, width), f32),
            shape(rows, bf16), shape((width, width), bf16), shape(rows, bf16), shape(cols, bf16),
            shape((width, half), bf16), shape(rows, bf16), shape(fine, bf16),
            shape((total, 2 * half), bf16),
        ],
        [vmem()] * 12 + [anywhere()] * 8,
        [
            VM((8, tokens), f32), VM(rows, bf16), VM(rows, bf16), VM((8, width), f32),
            VM((tokens, width), bf16), VM((tokens, width), bf16), VM((width, width), bf16),
            VM(rows, bf16), VM(cols, bf16), VM((width, half), bf16), VM(rows, bf16),
            dma((2,)), dma((5, 4)), dma((16,)), dma((16,)), dma((16,)), dma((16,)),
        ] + SharedGather.sems() + Gather.sems() + Columns.sems(2) + Columns.sems(1) + Gather.sems()
        + Gather.sems() + Columns.sems(3),
    )


def hidden_grad_kernel(feed_grad, gate_up_cols, hidden_all, act, down_cols, out, half, feed_out,
                       grad_v, gate_up_v, hidden_v, act_v, down_v, copies, *rest):
    sems_w, scratch, scratch_f = halves_of(rest, [5, 11, 11])
    s = Spot()
    loads = loaded(
        [(feed_grad, grad_v), (gate_up_cols, gate_up_v), (hidden_all, hidden_v), (act, act_v),
         (down_cols, down_v)],
        copies,
    )
    greet(s, plane=False)
    weigh = Weigh(s, hidden_v, grad_v, half, sems_w)
    scatter = Scatter(s, grad_v, gate_up_v, out, scratch)
    scatter.lag = 2
    filler = Scatter(s, act_v, down_v, feed_out, scratch_f, FILL[0][0])
    merged(
        loads[:2] + scatter.tasks(),
        nothing(1) + loads[2:] + weigh.products() + nothing(8),
        nothing(4) + filler.tasks(),
        nothing(40) + weigh.folds(),
    )
    scatter.finish()
    filler.finish()
    weigh.drain()


def hidden_grad_of(feed_grad, gate_up_cols, hidden_all, act, down_cols, number):
    shape = jax.ShapeDtypeStruct
    total, cols = feed_grad.shape
    width = gate_up_cols.shape[0]
    fill = FILL[0][1]
    return communicate(
        hidden_grad_kernel, "hidden_grad", number,
        (feed_grad, gate_up_cols, hidden_all, act, down_cols), [anywhere()] * 5,
        [
            shape((total // 16, width), f32), shape((16, 64, cols), bf16),
            shape((total // 16, fill), f32),
        ],
        [vmem()] * 3,
        [VM(a.shape, bf16) for a in (feed_grad, gate_up_cols, hidden_all, act, down_cols)] + [dma((5,))]
        + Weigh.scratch(cols) + Scatter.scratch(width) + Scatter.scratch(fill),
    )


def normed_grad_kernel(grad, in_cols, normed_all, x, gains_all, act, down_cols, gains, down_half, combined,
                       attended_all,
                       value_grad, gains_out, feed_out, out_rows, down_rows, in_rows, out_other,
                       attended_v, normed_grad, half, gains_v, got, total, theirs, normed_v, act_v, down_v,
                       copies, x_s, x_r, g_s, g_r,
                       *rest):
    sems_d, sems_i, sems_w, scratch, scratch_f = halves_of(rest, [5, 5, 5, 11, 11])
    s = Spot()
    loads = loaded(
        [(normed_all, normed_v), (act, act_v), (down_cols, down_v), (attended_all, attended_v)], copies
    )
    greet(s)
    back_i = Return(s, half, in_rows, 3, sems_i)
    weigh = Weigh(s, normed_v, grad, half, sems_w, back=back_i)
    back_d = Return(s, down_half, down_rows, 1, sems_d)
    scatter = Scatter(s, grad, in_cols, normed_grad, scratch)
    filler = Scatter(s, act_v, down_v, feed_out, scratch_f, FILL[2][0])
    over = send_over(out_rows, out_other, x_s.at[0], x_r.at[0], s)
    back_d.start()

    def out_product(j):
        w = pl.ds(j * 512, 512)
        out_rows[:, w] = rows_dot(combined[...], attended_v[:, w]).astype(bf16)

    products = [functools.partial(out_product, j) for j in range(4)]

    def gain_copy(k):
        to = s.partner(k)
        return send(gains_v.at[to], got.at[s.me], g_s.at[k], g_r.at[s.me], to)

    def write(j, value, gain):
        value_grad[:, pl.ds(j * 128, 128)] = value
        gains_v[j] = gains[j]
        gains_v[j, 0:1, :] = gain

    merged(
        scatter.tasks(),
        loads[:3] + weigh.products() + nothing(24),
        nothing(5) + weigh.folds() + nothing(12),
        back_d.tasks() + loads[3:] + products + [over.start] + nothing(9),
        nothing(4) + filler.tasks(),
        nothing(16) + back_i.tasks(),
    )
    scatter.finish()
    norm_back(x, normed_grad, gains_all, 0, write)
    for k in range(1, 16):
        gain_copy(k).start()
    filler.finish()
    back_d.finish()
    back_i.finish()
    weigh.drain()
    over.wait()
    for k in range(1, 16):
        src = s.partner(k)
        b = got.at[src]
        send(b, b, g_s.at[k], g_r.at[src], s.me).wait_recv()
    got[s.me] = gains_v[s.me]
    acc = got[0]
    for k in range(1, 16):
        acc = acc + got[k]
    total[...] = acc
    cp = send_over(total, theirs, x_s.at[1], x_r.at[1], s)
    cp.start()
    for k in range(1, 16):
        gain_copy(k).wait_send()
    cp.wait()
    gains_out[...] = total[...] + theirs[...]


def normed_grad_of(grad, in_cols, normed_all, x, gains_all, act, down_cols, gains, down_half, combined,
                   attended_all, number):
    shape = jax.ShapeDtypeStruct
    total, cols = grad.shape
    tokens, width = x.shape
    fill = FILL[2][1]
    down_rows = shape((DH, 16 * down_half.shape[2]), bf16)
    in_rows = shape((DH, 16 * cols), bf16)
    return communicate(
        normed_grad_kernel, "normed_grad", number,
        (grad, in_cols, normed_all, x, gains_all, act, down_cols, gains, down_half, combined,
         attended_all),
        [vmem()] * 2 + [anywhere()] + [vmem()] * 2 + [anywhere()] * 2 + [vmem(), anywhere(), vmem(), anywhere()],
        [
            shape((tokens, width), f32), shape((8, 128), f32), shape((tokens, fill), f32),
            shape((DH, width), bf16), down_rows, in_rows, shape((DH, width), bf16),
        ],
        [vmem()] * 4 + [anywhere()] * 3,
        [
            VM(attended_all.shape, bf16),
            VM((tokens, width), f32), VM((16, 64, cols), bf16), VM((16, 8, 128), f32),
            VM((16, 8, 128), f32), VM((8, 128), f32), VM((8, 128), f32),
            VM(normed_all.shape, bf16), VM(act.shape, bf16), VM(down_cols.shape, bf16), dma((4,)),
            dma((2,)), dma((2,)), dma((16,)), dma((16,)),
        ] + Return.sems(1) + Return.sems(3) + Weigh.scratch(cols) + Scatter.scratch(width)
        + Scatter.scratch(fill),
    )


def attend_back_kernel(hidden_grad, middle, cot, gains_all, keep, mix, memory, normal, out_all, qkv, local,
                       mem_out, lse, gate_up_half, cot_all, act, down_cols,
                       middle_grad, gains, grad, down_half, feed_out, attended_all, gate_up_rows,
                       attended, out_v, qkv_v, local_v, mem_v, lse_v, cot_v, act_v, down_v, by_token,
                       upstream, mix_grad, dk, dv, state_grad, norm_grad, copies, own_s, h_s, h_r, *rest):
    sems_a, sems_g, sems_w, scratch_f = halves_of(rest, [7, 5, 5, 11])
    s = Spot()
    mine = pl.ds(pl.multiple_of(s.me * 128, 128), 128)
    loads = loaded(
        [(out_all, out_v), (qkv, qkv_v), (local, local_v), (mem_out, mem_v), (lse, lse_v),
         (cot_all, cot_v), (act, act_v), (down_cols, down_v)],
        copies,
    )
    greet(s)
    gains[...] = jnp.zeros_like(gains)

    def write(j, value, gain):
        w = pl.ds(j * 128, 128)
        total = cot[:, w].astype(f32) + value
        middle_grad[:, w] = total
        attended[:, w] = total.astype(bf16)
        gains[j, 1:2, :] = gain

    norm_back(middle, hidden_grad, gains_all, 1, write)
    own = pltpu.make_async_copy(attended, attended_all.at[mine], own_s.at[0])
    own.start()
    gather = Gather(s, attended, attended_all, sems_a)
    back_g = Return(s, gate_up_half, gate_up_rows, 2, sems_g)
    filler = Scatter(s, act_v, down_v, feed_out, scratch_f, FILL[1][0])
    filler.lag = 8
    weigh = Weigh(s, cot_v, act_v, down_half, sems_w)
    attend = AttendBack(qkv_v, keep, mix, local_v, mem_v, lse_v, memory, normal, upstream, grad,
                        mix_grad, dk, dv, state_grad, norm_grad)
    gather.start()
    attend.clear()
    loads[0]()

    def head_copy(j):
        return send(by_token.at[:, pl.ds(j * DH, DH)], upstream.at[mine], h_s.at[j], h_r.at[s.me], j)

    for j in range(4):
        w = pl.ds(j * 512, 512)
        by_token[:, w] = cols_dot(attended[...], out_v[w, :]).astype(bf16)
        for h in range(4 * j, 4 * j + 4):
            pl.when(s.me != h)(lambda: head_copy(h).start())
    upstream[mine, :] = by_token[:, pl.ds(pl.multiple_of(s.me * DH, DH), DH)]
    for wait in loads[1:]:
        wait()

    def arrive(j):
        b = upstream.at[pl.ds(j * 128, 128)]
        pl.when(s.me != j)(lambda: send(b, b, h_s.at[j], h_r.at[j], s.me).wait_recv())

    def block(n, i):
        for j in range((n * SEG + i * ROWS) // 128, (n * SEG + (i + 1) * ROWS) // 128):
            arrive(j)
        attend.block(n, i)

    compute = [functools.partial(block, n, i) for n, i in attend.blocks()] + [attend.states]
    merged(gather.tasks(), nothing(2) + compute, weigh.products() + nothing(12))
    back_g.start()
    merged(filler.tasks(), back_g.tasks(), weigh.folds())
    filler.finish()
    back_g.finish()
    weigh.drain()
    for j in range(16):
        pl.when(s.me != j)(lambda: head_copy(j).wait_send())
    gather.drain()
    own.wait()
    gains[s.me, 2:3, :] = mix_grad[0:1, :]


def attend_backward(hidden_grad, middle, cot, gains_all, keep, mix, memory, normal, out_all, qkv, local,
                    mem_out, lse, gate_up_half, cot_all, act, down_cols, number):
    tokens, width = cot.shape
    total = qkv.shape[0]
    segments = total // SEG
    shape = jax.ShapeDtypeStruct
    whole = (out_all, qkv, local, mem_out, lse, cot_all, act, down_cols)
    return communicate(
        attend_back_kernel, "attend_back", number,
        (hidden_grad, middle, cot, gains_all, keep, mix, memory, normal, out_all, qkv, local, mem_out,
         lse, gate_up_half, cot_all, act, down_cols),
        [vmem()] * 8 + [anywhere()] * 9,
        [
            shape((tokens, width), f32), shape((16, 8, DH), f32), shape((total, 3 * DH), bf16),
            shape((16, 64, act.shape[1]), bf16), shape((tokens, FILL[1][1]), f32),
            shape((total, width), bf16), shape((DH, 16 * gate_up_half.shape[2]), bf16),
        ],
        [vmem()] * 5 + [anywhere()] * 2,
        [VM((tokens, width), bf16)] + [VM(a.shape, a.dtype) for a in whole]
        + [
            VM((tokens, width), bf16), VM((total, DH), bf16), VM((8, DH), f32),
            VM((total, DH), f32), VM((total, DH), f32), VM((segments, DH, DH), f32),
            VM((segments, 8, DH), f32), dma((8,)), dma((1,)), dma((16,)), dma((16,)),
        ] + Gather.sems() + Return.sems(2) + Weigh.scratch(act.shape[1]) + Scatter.scratch(FILL[1][1]),
    )


def body(
    layer_input,
    first_gain,
    in_weight,
    out_weight,
    mix_gate,
    second_gain,
    gate_up,
    down_weight,
    document_starts,
    cotangent,
):
    tokens, width = layer_input.shape
    (keep, mix, qkv, in_cols, gains_all, local, mem_out, lse, combined, memory, normal, middle, normed_all,
     out_all, cot_all, gate_up_cols, down_cols, hidden_all, act, feed_grad) = forward_of(
        document_starts, mix_gate.reshape(1, tokens), first_gain.reshape(1, tokens),
        second_gain.reshape(1, tokens), layer_input, in_weight, out_weight, cotangent, gate_up,
        down_weight, 0,
    )
    hidden_grad, gate_up_half, feed_out_0 = hidden_grad_of(
        feed_grad, gate_up_cols, hidden_all, act, down_cols, 3
    )

    (middle_grad, gain_grads, projected_grad, down_half, feed_out_1, attended_all,
     gate_up_rows) = attend_backward(
        hidden_grad, middle, cotangent, gains_all, keep, mix, memory, normal, out_all, qkv, local, mem_out,
        lse, gate_up_half, cot_all, act, down_cols, 4,
    )
    (value_grad, gains_out, feed_out_2, out_rows, down_rows, in_rows, out_other) = normed_grad_of(
        projected_grad, in_cols, normed_all, layer_input, gains_all, act, down_cols, gain_grads, down_half,
        combined, attended_all, 5,
    )
    input_grad = middle_grad + value_grad
    feed_out = jnp.concatenate([feed_out_0, feed_out_1, feed_out_2], axis=1)
    layer_output = (middle + feed_out).astype(bf16)

    return (
        layer_output,
        input_grad,
        gains_out[0],
        in_rows.astype(f32),
        out_rows.astype(f32) + out_other.astype(f32),
        gains_out[2],
        gains_out[1],
        gate_up_rows.astype(f32),
        down_rows.astype(f32),
    )


def solution(mesh):
    one_group = mesh.shape[AXIS] == H and mesh.shape["dp"] == 2
    return jax.shard_map(
        body if one_group else body_groups,
        mesh=mesh,
        in_specs=(
            P(("dp", "fsdp"), None),
            P("fsdp"),
            P("fsdp", None),
            P("fsdp", None),
            P("fsdp"),
            P("fsdp"),
            P("fsdp", None),
            P("fsdp", None),
            P("dp", None),
            P(("dp", "fsdp"), None),
        ),
        out_specs=(
            P(("dp", "fsdp"), None),
            P(("dp", "fsdp"), None),
            P("fsdp"),
            P("fsdp", None),
            P("fsdp", None),
            P("fsdp"),
            P("fsdp"),
            P("fsdp", None),
            P("fsdp", None),
        ),
        check_vma=False,
    )
```
